32 devices in a mesh: wide: 16 (over z, y, x), narrow: 2 (over core).
Axes of the slice: x: 2, y: 2, z: 4, core: 2. Of those that a mesh axis runs over, the one named last changes fastest.
Arguments:
- tokens: bfloat16 [8192, 768], P(('wide', 'narrow')), may hold values from -6 to 6
- seg_ids: int32 [8192], P(('wide', 'narrow')), may hold values from 0 to 1, as said below
- frame_ids: int32 [8192], P(('wide', 'narrow')), may hold values from 0 to 15, as said below
- patch_ids: int32 [8192], P(('wide', 'narrow')), may hold values from 0 to 15
- timesteps: int32 [64], P(('wide', 'narrow')), may hold values from 0 to 999
- w_ada: bfloat16 [768, 6912], P(('wide', 'narrow')), may hold values from -0.21875 to 0.21875
- b_ada: bfloat16 [6912], P(('wide', 'narrow')), may hold values from -3 to 3
- w_qkv_spatial: bfloat16 [768, 2304], P(('wide', 'narrow')), may hold values from -0.21875 to 0.21875
- w_out_spatial: bfloat16 [768, 768], P(('wide', 'narrow')), may hold values from -0.4375 to 0.4375
- w_qkv_temporal: bfloat16 [768, 2304], P(('wide', 'narrow')), may hold values from -0.21875 to 0.21875
- w_out_temporal: bfloat16 [768, 768], P(('wide', 'narrow')), may hold values from -0.4375 to 0.4375
- w_up: bfloat16 [768, 3072], P(('wide', 'narrow')), may hold values from -0.21875 to 0.21875
- w_down: bfloat16 [3072, 768], P(('wide', 'narrow')), may hold values from -0.109375 to 0.109375
- cotangent: bfloat16 [8192, 768], P(('wide', 'narrow')), may hold values from -6 to 6
Outputs:
- layer_out: bfloat16 [8192, 768], P(('wide', 'narrow'))
- grad_tokens: float32 [8192, 768], P(('wide', 'narrow'))
- grad_w_ada: float32 [768, 6912], P(('wide', 'narrow'))
- grad_b_ada: float32 [6912], P(('wide', 'narrow'))
- grad_qkv_spatial: float32 [768, 2304], P(('wide', 'narrow'))
- grad_out_spatial: float32 [768, 768], P(('wide', 'narrow'))
- grad_qkv_temporal: float32 [768, 2304], P(('wide', 'narrow'))
- grad_out_temporal: float32 [768, 768], P(('wide', 'narrow'))
- grad_w_up: float32 [768, 3072], P(('wide', 'narrow'))
- grad_w_down: float32 [3072, 768], P(('wide', 'narrow'))
The draws below stay inside these ranges and needn't reach their ends.
Inputs may be any that keep to these rules, and one draw needn't show every extreme that they name: `seg_ids`: on each device its 256 tokens belong to clips numbered from 0 without gaps; each clip has 8 or 16 frames of 16 patches, 16 frames on a device together; each triple of clip, frame and patch number occurs exactly once on a device, in no particular order. `frame_ids`: frame numbers of a clip run from 0 to its frame count minus 1.
All inputs are finite; a program needn't handle non-finite values.
Results may differ from the reference program's by a relative error of at most 0.02.
Values may be sent and summed in bfloat16 or wider, within the bound.
A program may use at most 320 MiB of HBM per device.

```python
import math
import jax
import jax.numpy as jnp
import numpy as np
from jax import lax

D = 768
HEADS = 12
HEAD_DIM = 64
FF = 3072
PATCHES = 16
FRAMES_DEV = 16
TOK_DEV = 256
CLIPS_DEV = 2
TOKENS = 8192
CLIPS = 64
DEVICES = 32


def clip_layout(key):
    unit_count = FRAMES_DEV // 8
    unit_ids = np.arange(unit_count)
    four_bits = jax.random.randint(jax.random.fold_in(key, 1), (DEVICES, unit_count), 0, 2)
    two_bits = jax.random.randint(jax.random.fold_in(key, 2), (DEVICES, unit_count), 0, 2)
    four_bits = four_bits.at[0].set(1).at[1].set(0)
    two_bits = two_bits.at[0].set(1).at[1].set(0)
    complete = unit_ids // 4 * 4 + 4 <= unit_count
    four_whole = (four_bits[:, unit_ids // 4] == 1) & jnp.asarray(complete)[None, :]
    two_whole = two_bits[:, unit_ids // 2] == 1
    even_unit = jnp.asarray(unit_ids % 2 == 0)[None, :]
    starts = jnp.asarray(unit_ids % 4 == 0)[None, :] | even_unit & ~four_whole | ~even_unit & ~four_whole & ~two_whole
    unit_index = jnp.asarray(unit_ids, jnp.int32)[None, :]
    clip_of_unit = jnp.cumsum(starts.astype(jnp.int32), axis=1) - 1
    first_unit = lax.cummax(jnp.where(starts, unit_index, 0), axis=1)
    offset_unit = unit_index - first_unit
    frame_slots = np.arange(FRAMES_DEV)
    clip_of_frame = clip_of_unit[:, frame_slots // 8]
    frame_in_clip = 8 * offset_unit[:, frame_slots // 8] + jnp.asarray(frame_slots % 8, jnp.int32)[None, :]
    grid_shape = (DEVICES, FRAMES_DEV, PATCHES)
    segments = jnp.broadcast_to(clip_of_frame[:, :, None], grid_shape).reshape(DEVICES, TOK_DEV)
    frames = jnp.broadcast_to(frame_in_clip[:, :, None], grid_shape).reshape(DEVICES, TOK_DEV)
    patch_pos = jnp.broadcast_to(jnp.arange(PATCHES, dtype=jnp.int32)[None, None, :], grid_shape).reshape(DEVICES, TOK_DEV)
    orders = jax.vmap(lambda item: jax.random.permutation(item, TOK_DEV))(jax.random.split(jax.random.fold_in(key, 3), DEVICES))

    def reorder(values):
        return jnp.take_along_axis(values, orders, axis=1).reshape(-1).astype(jnp.int32)
    return (reorder(segments), reorder(frames), reorder(patch_pos))


def draw_seg_ids(key, part):
    layout = clip_layout(key)
    return layout[0]


def draw_frame_ids(key, part):
    layout = clip_layout(key)
    return layout[1]


def draw_patch_ids(key, part):
    layout = clip_layout(key)
    return layout[2]


def place_ends(values, own_key, low, top_value):
    extent = values.shape
    spot = [jax.random.randint(jax.random.fold_in(own_key, axis), (), 0, extent[axis]) for axis in range(len(extent))]
    values = values.at[tuple(spot)].set(low)
    longest = extent.index(max(extent))
    spot[longest] = (spot[longest] + 1) % extent[longest]
    return values.at[tuple(spot)].set(top_value)


def steps_of(key, shape, shards, low, largest):
    loudness = 1.0
    for axis_at, blocks in shards:
        steps = jax.random.uniform(jax.random.fold_in(jax.random.fold_in(key, 6), axis_at), (blocks,), jnp.float32, low / len(shards), largest / len(shards))
        loudness = loudness * jnp.repeat(jnp.exp(steps), shape[axis_at] // blocks).reshape((-1,) + (1,) * (len(shape) - 1 - axis_at))
    return loudness


def noise(rng, shape, scale, reach, cuts=(), kind=jnp.bfloat16):
    values = jax.random.normal(rng, shape, jnp.float32) * scale
    if len(cuts) > 0:
        values = steps_of(rng, shape, cuts, -0.22, 0.18) * values
    return jnp.clip(values, min=-reach, max=reach).astype(kind)


def setup_inputs(seed: int = 0) -> dict:
    keys = jax.random.split(jax.random.key(seed), 15)
    tokens = noise(keys[0], (TOKENS, D), 1.0, 6.0, ((0, 32),))
    seg_ids = draw_seg_ids(jax.random.fold_in(keys[14], 71), 0)
    frame_ids = draw_frame_ids(jax.random.fold_in(keys[14], 71), 0)
    patch_ids = draw_patch_ids(jax.random.fold_in(keys[14], 71), 0)
    timesteps = place_ends(jax.random.randint(keys[4], (CLIPS,), 0, 1000), jax.random.fold_in(keys[4], 1), 0, 999).astype(jnp.int32)
    w_ada = noise(keys[5], (D, 9 * D), D ** -0.5, 0.21875, ((0, 32),))
    b_ada = noise(keys[6], (9 * D,), 0.5, 3.0, ((0, 32),))
    w_qkv_spatial = noise(keys[7], (D, 3 * D), D ** -0.5, 0.21875, ((0, 32),))
    w_out_spatial = noise(keys[8], (D, D), (D // 4) ** -0.5, 0.4375, ((0, 32),))
    w_qkv_temporal = noise(keys[9], (D, 3 * D), D ** -0.5, 0.21875, ((0, 32),))
    w_out_temporal = noise(keys[10], (D, D), (D // 4) ** -0.5, 0.4375, ((0, 32),))
    w_up = noise(keys[11], (D, FF), D ** -0.5, 0.21875, ((0, 32),))
    w_down = noise(keys[12], (FF, D), FF ** -0.5, 0.109375, ((0, 32),))
    cotangent = noise(keys[13], (TOKENS, D), 1.0, 6.0, ((0, 32),))
    return dict(tokens=tokens, seg_ids=seg_ids, frame_ids=frame_ids, patch_ids=patch_ids, timesteps=timesteps, w_ada=w_ada, b_ada=b_ada, w_qkv_spatial=w_qkv_spatial, w_out_spatial=w_out_spatial, w_qkv_temporal=w_qkv_temporal, w_out_temporal=w_out_temporal, w_up=w_up, w_down=w_down, cotangent=cotangent)


EPSILON = 1e-06
FREQ_BASE = 10000.0
MASKED = -1e+30
HIGH_PRECISION = lax.Precision.HIGHEST

@jax.custom_vjp
def low(v):
    return lax.optimization_barrier(v.astype(jnp.bfloat16)).astype(jnp.float32)

@jax.custom_vjp
def low_back(v):
    return v

def low_keep(v):
    return (low(v), None)

def low_pass(kept, grad):
    return (grad,)

def back_keep(v):
    return (v, None)

def back_low(kept, grad):
    return (low(grad),)
low.defvjp(low_keep, low_pass)
low_back.defvjp(back_keep, back_low)

def time_embed(step_ids, width):
    half_width = width // 2
    frequency = jnp.exp(-math.log(FREQ_BASE) * jnp.arange(half_width, dtype=jnp.float32) / half_width)
    angles = step_ids.astype(jnp.float32)[:, None] * frequency[None, :]
    return jnp.concatenate([jnp.cos(angles), jnp.sin(angles)], axis=1)

def layer_norm(stream):
    center = stream - lax.optimization_barrier(jnp.mean(stream, axis=-1, keepdims=True))
    return center * lax.rsqrt(lax.optimization_barrier(jnp.mean(center * center, axis=-1, keepdims=True)) + EPSILON)

def attend(normed, w_qkv, w_out, allowed):
    row_count = normed.shape[0]
    qkv_rows = low(low_back(jnp.dot(normed, w_qkv, precision=HIGH_PRECISION)))
    qkv_rows = qkv_rows.reshape(row_count, 3, HEADS, HEAD_DIM)
    scores = jnp.einsum('qhd,khd->hqk', qkv_rows[:, 0], qkv_rows[:, 1], precision=HIGH_PRECISION) * HEAD_DIM ** (-0.5)
    scores = jnp.where(allowed[None], low_back(scores), MASKED)
    attn_prob = jax.nn.softmax(scores, axis=-1)
    attended = jnp.einsum('hqk,khd->qhd', low(attn_prob), qkv_rows[:, 2], precision=HIGH_PRECISION)
    merged = low(low_back(attended.reshape(row_count, HEADS * HEAD_DIM)))
    return low_back(jnp.dot(merged, w_out, precision=HIGH_PRECISION))

def block(stream, segments, frame_pos, patch_pos, modulation, weights):
    w_qkv_s, w_out_s, w_qkv_t, w_out_t, up_full, down_full = weights
    token_mod = jnp.take(modulation, segments, axis=0).reshape(-1, 3, 3, D)
    same_clip = segments[:, None] == segments[None, :]
    spatial = same_clip & (frame_pos[:, None] == frame_pos[None, :])
    temporal = same_clip & (patch_pos[:, None] == patch_pos[None, :])
    normed = low(layer_norm(stream) * (1.0 + token_mod[:, 0, 1]) + token_mod[:, 0, 0])
    stream = stream + token_mod[:, 0, 2] * attend(normed, w_qkv_s, w_out_s, spatial)
    normed = low(layer_norm(stream) * (1.0 + token_mod[:, 1, 1]) + token_mod[:, 1, 0])
    stream = stream + token_mod[:, 1, 2] * attend(normed, w_qkv_t, w_out_t, temporal)
    normed = low(layer_norm(stream) * (1.0 + token_mod[:, 2, 1]) + token_mod[:, 2, 0])
    hidden = low(jax.nn.gelu(low_back(jnp.dot(normed, up_full, precision=HIGH_PRECISION))))
    return stream + token_mod[:, 2, 2] * low_back(jnp.dot(hidden, down_full, precision=HIGH_PRECISION))

def reference(tokens, seg_ids, frame_ids, patch_ids, timesteps, w_ada, b_ada, w_qkv_spatial, w_out_spatial, w_qkv_temporal, w_out_temporal, w_up, w_down, cotangent):
    params = tuple((weight.astype(jnp.float32) for weight in (w_ada, b_ada, w_qkv_spatial, w_out_spatial, w_qkv_temporal, w_out_temporal, w_up, w_down)))
    cond_low = low(jax.nn.silu(time_embed(timesteps, D)))
    checked = jax.checkpoint(block)

    def forward(stream, weights):
        modulation = low_back(jnp.dot(cond_low, weights[0], precision=HIGH_PRECISION)) + weights[1]
        items = (stream.reshape(DEVICES, TOK_DEV, D), seg_ids.reshape(DEVICES, TOK_DEV), frame_ids.reshape(DEVICES, TOK_DEV), patch_ids.reshape(DEVICES, TOK_DEV), modulation.reshape(DEVICES, CLIPS_DEV, 9 * D))

        def advance(carry, item):
            return (carry, checked(item[0], item[1], item[2], item[3], item[4], weights[2:]))
        _, blocks_out = lax.scan(advance, jnp.zeros((), jnp.float32), items)
        return blocks_out.reshape(TOKENS, D)
    result, pullback = jax.vjp(forward, tokens.astype(jnp.float32), params)
    grad_input, grad_list = pullback(cotangent.astype(jnp.float32))
    return (result.astype(jnp.bfloat16), grad_input, grad_list[0], grad_list[1], grad_list[2], grad_list[3], grad_list[4], grad_list[5], grad_list[6], grad_list[7])
```

```python
from functools import partial
import math

import jax
import jax.numpy as jnp
from jax import lax
from jax.sharding import PartitionSpec as P

HEADS = 12


EPSILON = 1e-06
FREQ_BASE = 10000.0
MASKED = -1e30


def time_embed(step_ids, width):
    half_width = width // 2
    frequency = jnp.exp(
        -math.log(FREQ_BASE) * jnp.arange(half_width, dtype=jnp.float32) / half_width
    )
    angles = step_ids.astype(jnp.float32)[:, None] * frequency[None, :]
    return jnp.concatenate([jnp.cos(angles), jnp.sin(angles)], axis=1)


def contract_rows(left, right):
    return lax.dot_general(
        left, right, (((0,), (0,)), ((), ())), preferred_element_type=jnp.float32
    )


def contract_cols(left, right):
    return lax.dot_general(
        left, right, (((1,), (1,)), ((), ())), preferred_element_type=jnp.float32
    )


def exact_rows(left, right):
    return lax.dot_general(
        left,
        right,
        (((0,), (0,)), ((), ())),
        precision=lax.Precision.HIGHEST,
        preferred_element_type=jnp.float32,
    )


def layer_norm_apply(stream):
    center = stream - jnp.mean(stream, axis=-1, keepdims=True)
    inverse_deviation = lax.rsqrt(jnp.mean(center * center, axis=-1, keepdims=True) + EPSILON)
    return (center * inverse_deviation, inverse_deviation)


def layer_norm_reverse(normalized_gradient, standardized_input, inverse_deviation, row_scales):
    input_gradient = normalized_gradient * (1.0 + row_scales)
    mean_removed = input_gradient - jnp.mean(input_gradient, axis=-1, keepdims=True)
    return inverse_deviation * (
        mean_removed
        - standardized_input * jnp.mean(input_gradient * standardized_input, axis=-1, keepdims=True)
    )


def sublayer_mod(one_hot, modulation, sublayer, width):
    table = modulation[:, 3 * width * sublayer : 3 * width * (sublayer + 1)]
    rows_mod = jnp.dot(
        one_hot, table, precision=lax.Precision.HIGHEST, preferred_element_type=jnp.float32
    )
    return (rows_mod[:, :width], rows_mod[:, width : 2 * width], rows_mod[:, 2 * width :])


def head_probs(allowed, scale, queries, key_vecs):
    scores = contract_cols(queries, key_vecs) * scale
    scores = jnp.where(allowed, scores, MASKED)
    return jax.nn.softmax(scores, axis=-1)


def head_forward(allowed, scale, item):
    queries, key_vecs, val_vecs = item
    attn_prob = head_probs(allowed, scale, queries, key_vecs)
    return jnp.dot(attn_prob.astype(jnp.bfloat16), val_vecs, preferred_element_type=jnp.float32)


def head_backward(allowed, scale, item):
    queries, key_vecs, val_vecs, grad_att = item
    attn_prob = head_probs(allowed, scale, queries, key_vecs)
    grad_val = contract_rows(attn_prob.astype(jnp.bfloat16), grad_att)
    grad_prob = contract_cols(grad_att, val_vecs)
    grad_score = attn_prob * (grad_prob - jnp.sum(attn_prob * grad_prob, axis=-1, keepdims=True))
    score_low = grad_score.astype(jnp.bfloat16)
    grad_query = jnp.dot(score_low, key_vecs, preferred_element_type=jnp.float32) * scale
    grad_key = contract_rows(score_low, queries) * scale
    return (grad_query, grad_key, grad_val)


def split_heads(qkv_rows, head_count):
    row_count = qkv_rows.shape[0]
    return qkv_rows.reshape(row_count, 3, head_count, -1).transpose(1, 2, 0, 3)


def attention_forward(normed, w_qkv, w_out, allowed, head_count):
    row_count = normed.shape[0]
    qkv_rows = jnp.dot(normed, w_qkv, preferred_element_type=jnp.float32).astype(jnp.bfloat16)
    split_qkv = split_heads(qkv_rows, head_count)
    scale = split_qkv.shape[-1] ** (-0.5)
    attended = lax.map(
        partial(head_forward, allowed, scale), (split_qkv[0], split_qkv[1], split_qkv[2])
    )
    merged = attended.transpose(1, 0, 2).reshape(row_count, -1).astype(jnp.bfloat16)
    branch = jnp.dot(merged, w_out, preferred_element_type=jnp.float32)
    return (branch, qkv_rows, merged)


def attention_backward(grad_branch, qkv_rows, w_qkv, w_out, allowed, head_count):
    row_count = qkv_rows.shape[0]
    grad_merged = contract_cols(grad_branch, w_out).astype(jnp.bfloat16)
    grad_heads = grad_merged.reshape(row_count, head_count, -1).transpose(1, 0, 2)
    split_qkv = split_heads(qkv_rows, head_count)
    scale = split_qkv.shape[-1] ** (-0.5)
    grad_query, grad_key, grad_val = lax.map(
        partial(head_backward, allowed, scale),
        (split_qkv[0], split_qkv[1], split_qkv[2], grad_heads),
    )
    grad_qkv = (
        jnp.stack([grad_query, grad_key, grad_val])
        .transpose(2, 0, 1, 3)
        .reshape(row_count, -1)
        .astype(jnp.bfloat16)
    )
    normalized_gradient = contract_cols(grad_qkv, w_qkv)
    return (normalized_gradient, grad_qkv)


def on_device(
    tokens,
    seg_ids,
    frame_ids,
    patch_ids,
    timesteps,
    w_ada,
    b_ada,
    w_qkv_spatial,
    w_out_spatial,
    w_qkv_temporal,
    w_out_temporal,
    w_up,
    w_down,
    cotangent,
):
    axes = ("wide", "narrow")
    gathered = (
        None,
        None,
        lax.all_gather(w_qkv_spatial, axes, axis=0, tiled=True),
        lax.all_gather(w_out_spatial, axes, axis=0, tiled=True),
        lax.all_gather(w_qkv_temporal, axes, axis=0, tiled=True),
        lax.all_gather(w_out_temporal, axes, axis=0, tiled=True),
        lax.all_gather(w_up, axes, axis=0, tiled=True),
        lax.all_gather(w_down, axes, axis=0, tiled=True),
    )
    width = tokens.shape[1]
    head_count = HEADS
    clip_count = timesteps.shape[0]
    row_count = w_ada.shape[0]
    place = lax.axis_index(axes)
    all_steps = lax.all_gather(timesteps, axes, axis=0, tiled=True)
    cond_all = jax.nn.silu(time_embed(all_steps, width)).astype(jnp.bfloat16)
    cond_rows = lax.dynamic_slice_in_dim(cond_all, place * row_count, row_count, axis=1)
    all_bias = lax.all_gather(b_ada, axes, axis=0, tiled=True)
    modulation = lax.psum_scatter(
        jnp.dot(cond_rows, w_ada, preferred_element_type=jnp.float32),
        axes,
        scatter_dimension=0,
        tiled=True,
    ) + all_bias.astype(jnp.float32)
    one_hot = (seg_ids[:, None] == jnp.arange(clip_count, dtype=jnp.int32)[None, :]).astype(
        jnp.float32
    )
    offset_first, scale_first, gate_a = sublayer_mod(one_hot, modulation, 0, width)
    offset_second, scale_second, gate_b = sublayer_mod(one_hot, modulation, 1, width)
    offset_third, scale_third, gate_c = sublayer_mod(one_hot, modulation, 2, width)
    same_clip = seg_ids[:, None] == seg_ids[None, :]
    spatial_mask = same_clip & (frame_ids[:, None] == frame_ids[None, :])
    temporal_mask = same_clip & (patch_ids[:, None] == patch_ids[None, :])
    residual_first = tokens.astype(jnp.float32)
    standardized_first, inverse_deviation_first = layer_norm_apply(residual_first)
    normalized_first = (standardized_first * (1.0 + scale_first) + offset_first).astype(
        jnp.bfloat16
    )
    branch_a, qkv_a, merged_a = attention_forward(
        normalized_first, gathered[2], gathered[3], spatial_mask, head_count
    )
    residual_second = residual_first + gate_a * branch_a
    standardized_second, inverse_deviation_second = layer_norm_apply(residual_second)
    normalized_second = (standardized_second * (1.0 + scale_second) + offset_second).astype(
        jnp.bfloat16
    )
    branch_b, qkv_b, merged_b = attention_forward(
        normalized_second, gathered[4], gathered[5], temporal_mask, head_count
    )
    residual_third = residual_second + gate_b * branch_b
    standardized_third, inverse_deviation_third = layer_norm_apply(residual_third)
    normalized_third = (standardized_third * (1.0 + scale_third) + offset_third).astype(
        jnp.bfloat16
    )
    pre_act = jnp.dot(normalized_third, gathered[6], preferred_element_type=jnp.float32)
    act_out, gelu_pull = jax.vjp(jax.nn.gelu, pre_act)
    hidden = act_out.astype(jnp.bfloat16)
    branch_c = jnp.dot(hidden, gathered[7], preferred_element_type=jnp.float32)
    result = residual_third + gate_c * branch_c
    back_weights = gathered
    output_gradient = cotangent.astype(jnp.float32)
    gate_gradient_third = output_gradient * branch_c
    grad_branch_c = (gate_c * output_gradient).astype(jnp.bfloat16)
    grad_hidden = contract_cols(grad_branch_c, back_weights[7])
    grad_pre = gelu_pull(grad_hidden)[0].astype(jnp.bfloat16)
    normalized_gradient_third = contract_cols(grad_pre, back_weights[6])
    residual_gradient = output_gradient + layer_norm_reverse(
        normalized_gradient_third, standardized_third, inverse_deviation_third, scale_third
    )
    gate_gradient_second = residual_gradient * branch_b
    grad_branch_b = (gate_b * residual_gradient).astype(jnp.bfloat16)
    normalized_gradient_second, grad_qkv_t = attention_backward(
        grad_branch_b, qkv_b, back_weights[4], back_weights[5], temporal_mask, head_count
    )
    residual_gradient = residual_gradient + layer_norm_reverse(
        normalized_gradient_second, standardized_second, inverse_deviation_second, scale_second
    )
    gate_gradient_first = residual_gradient * branch_a
    grad_branch_a = (gate_a * residual_gradient).astype(jnp.bfloat16)
    normalized_gradient_first, grad_qkv_s = attention_backward(
        grad_branch_a, qkv_a, back_weights[2], back_weights[3], spatial_mask, head_count
    )
    residual_gradient = residual_gradient + layer_norm_reverse(
        normalized_gradient_first, standardized_first, inverse_deviation_first, scale_first
    )
    grad_mod = jnp.concatenate(
        [
            exact_rows(
                one_hot,
                jnp.concatenate(
                    [
                        normalized_gradient_first,
                        normalized_gradient_first * standardized_first,
                        gate_gradient_first,
                    ],
                    axis=1,
                ),
            ),
            exact_rows(
                one_hot,
                jnp.concatenate(
                    [
                        normalized_gradient_second,
                        normalized_gradient_second * standardized_second,
                        gate_gradient_second,
                    ],
                    axis=1,
                ),
            ),
            exact_rows(
                one_hot,
                jnp.concatenate(
                    [
                        normalized_gradient_third,
                        normalized_gradient_third * standardized_third,
                        gate_gradient_third,
                    ],
                    axis=1,
                ),
            ),
        ],
        axis=1,
    )
    grad_mod_low = grad_mod.astype(jnp.bfloat16)
    all_grad_mod = lax.all_gather(grad_mod_low, axes, axis=0, tiled=True)
    bias_share = lax.psum_scatter(
        jnp.sum(grad_mod, axis=0), axes, scatter_dimension=0, tiled=True
    )

    def share(left, right):
        return lax.psum_scatter(
            contract_rows(left, right).astype(jnp.bfloat16),
            axes,
            scatter_dimension=0,
            tiled=True,
        ).astype(jnp.float32)

    return (
        result.astype(jnp.bfloat16),
        residual_gradient,
        contract_rows(cond_rows, all_grad_mod),
        bias_share,
        share(normalized_first, grad_qkv_s),
        share(merged_a, grad_branch_a),
        share(normalized_second, grad_qkv_t),
        share(merged_b, grad_branch_b),
        share(normalized_third, grad_pre),
        share(hidden, grad_branch_c),
    )


def solution(mesh):
    placed = (
        P(("wide", "narrow"), None),
        P(("wide", "narrow")),
        P(("wide", "narrow")),
        P(("wide", "narrow")),
        P(("wide", "narrow")),
        P(("wide", "narrow"), None),
        P(("wide", "narrow")),
        P(("wide", "narrow"), None),
        P(("wide", "narrow"), None),
        P(("wide", "narrow"), None),
        P(("wide", "narrow"), None),
        P(("wide", "narrow"), None),
        P(("wide", "narrow"), None),
        P(("wide", "narrow"), None),
    )
    return jax.shard_map(
        on_device,
        mesh=mesh,
        in_specs=placed,
        out_specs=(
            P(("wide", "narrow"), None),
            P(("wide", "narrow"), None),
            P(("wide", "narrow"), None),
            P(("wide", "narrow")),
            P(("wide", "narrow"), None),
            P(("wide", "narrow"), None),
            P(("wide", "narrow"), None),
            P(("wide", "narrow"), None),
            P(("wide", "narrow"), None),
            P(("wide", "narrow"), None),
        ),
        check_vma=False,
    )
```

```python
from functools import partial
import math

import jax
import jax.numpy as jnp
from jax import lax
from jax.experimental import pallas as pl
from jax.experimental.pallas import tpu as pltpu
from jax.sharding import PartitionSpec as P

HEADS = 12


EPSILON = 1e-06
FREQ_BASE = 10000.0
MASKED = -1e30


def time_embed(step_ids, width):
    half_width = width // 2
    frequency = jnp.exp(
        -math.log(FREQ_BASE) * jnp.arange(half_width, dtype=jnp.float32) / half_width
    )
    angles = step_ids.astype(jnp.float32)[:, None] * frequency[None, :]
    return jnp.concatenate([jnp.cos(angles), jnp.sin(angles)], axis=1)


def contract_rows(left, right):
    return lax.dot_general(
        left, right, (((0,), (0,)), ((), ())), preferred_element_type=jnp.float32
    )


def contract_cols(left, right):
    return lax.dot_general(
        left, right, (((1,), (1,)), ((), ())), preferred_element_type=jnp.float32
    )


def exact_rows(left, right):
    return lax.dot_general(
        left,
        right,
        (((0,), (0,)), ((), ())),
        precision=lax.Precision.HIGHEST,
        preferred_element_type=jnp.float32,
    )


def layer_norm_apply(stream):
    center = stream - jnp.mean(stream, axis=-1, keepdims=True)
    inverse_deviation = lax.rsqrt(jnp.mean(center * center, axis=-1, keepdims=True) + EPSILON)
    return (center * inverse_deviation, inverse_deviation)


def layer_norm_reverse(normalized_gradient, standardized_input, inverse_deviation, row_scales):
    input_gradient = normalized_gradient * (1.0 + row_scales)
    mean_removed = input_gradient - jnp.mean(input_gradient, axis=-1, keepdims=True)
    return inverse_deviation * (
        mean_removed
        - standardized_input * jnp.mean(input_gradient * standardized_input, axis=-1, keepdims=True)
    )


def sublayer_mod(one_hot, modulation, sublayer, width):
    table = modulation[:, 3 * width * sublayer : 3 * width * (sublayer + 1)]
    rows_mod = jnp.dot(
        one_hot, table, precision=lax.Precision.HIGHEST, preferred_element_type=jnp.float32
    )
    return (rows_mod[:, :width], rows_mod[:, width : 2 * width], rows_mod[:, 2 * width :])


def head_probs(allowed, scale, queries, key_vecs):
    scores = contract_cols(queries, key_vecs) * scale
    scores = jnp.where(allowed, scores, MASKED)
    return jax.nn.softmax(scores, axis=-1)


def head_forward(allowed, scale, item):
    queries, key_vecs, val_vecs = item
    attn_prob = head_probs(allowed, scale, queries, key_vecs)
    return jnp.dot(attn_prob.astype(jnp.bfloat16), val_vecs, preferred_element_type=jnp.float32)


def head_backward(allowed, scale, item):
    queries, key_vecs, val_vecs, grad_att = item
    attn_prob = head_probs(allowed, scale, queries, key_vecs)
    grad_val = contract_rows(attn_prob.astype(jnp.bfloat16), grad_att)
    grad_prob = contract_cols(grad_att, val_vecs)
    grad_score = attn_prob * (grad_prob - jnp.sum(attn_prob * grad_prob, axis=-1, keepdims=True))
    score_low = grad_score.astype(jnp.bfloat16)
    grad_query = jnp.dot(score_low, key_vecs, preferred_element_type=jnp.float32) * scale
    grad_key = contract_rows(score_low, queries) * scale
    return (grad_query, grad_key, grad_val)


def split_heads(qkv_rows, head_count):
    row_count = qkv_rows.shape[0]
    return qkv_rows.reshape(row_count, 3, head_count, -1).transpose(1, 2, 0, 3)


def attention_forward(normed, w_qkv, w_out, allowed, head_count):
    row_count = normed.shape[0]
    qkv_rows = jnp.dot(normed, w_qkv, preferred_element_type=jnp.float32).astype(jnp.bfloat16)
    split_qkv = split_heads(qkv_rows, head_count)
    scale = split_qkv.shape[-1] ** (-0.5)
    attended = lax.map(
        partial(head_forward, allowed, scale), (split_qkv[0], split_qkv[1], split_qkv[2])
    )
    merged = attended.transpose(1, 0, 2).reshape(row_count, -1).astype(jnp.bfloat16)
    branch = jnp.dot(merged, w_out, preferred_element_type=jnp.float32)
    return (branch, qkv_rows, merged)


def attention_backward(grad_branch, qkv_rows, w_qkv, w_out, allowed, head_count):
    row_count = qkv_rows.shape[0]
    grad_merged = contract_cols(grad_branch, w_out).astype(jnp.bfloat16)
    grad_heads = grad_merged.reshape(row_count, head_count, -1).transpose(1, 0, 2)
    split_qkv = split_heads(qkv_rows, head_count)
    scale = split_qkv.shape[-1] ** (-0.5)
    grad_query, grad_key, grad_val = lax.map(
        partial(head_backward, allowed, scale),
        (split_qkv[0], split_qkv[1], split_qkv[2], grad_heads),
    )
    grad_qkv = (
        jnp.stack([grad_query, grad_key, grad_val])
        .transpose(2, 0, 1, 3)
        .reshape(row_count, -1)
        .astype(jnp.bfloat16)
    )
    normalized_gradient = contract_cols(grad_qkv, w_qkv)
    return (normalized_gradient, grad_qkv)


MESH = pl.DeviceIdType.MESH


class Spot:
    def __init__(self):
        chip = lax.axis_index("wide")
        core = lax.axis_index("narrow")
        z, y, x = lax.div(chip, 4), lax.rem(lax.div(chip, 2), 2), lax.rem(chip, 2)
        half = lax.div(z, 2)
        toward = 1 - 2 * half
        self.chip, self.core, self.z, self.y, self.x = chip, core, z, y, x
        self.half = half
        self.middle = z + half * (3 - 2 * z)
        self.is_middle = self.middle == 1
        self.is_end = self.middle == 0
        self.plane = 2 * y + x
        self.inner = ((z + toward) * 4 + self.plane, core)
        self.outer = ((z - toward) * 4 + self.plane, core)
        self.first_plane = 2 * lax.rem(y + core, 2) + lax.rem(x + 1 - core, 2)
        self.second_plane = 2 * lax.rem(y + 1 - core, 2) + lax.rem(x + core, 2)
        self.far_plane = 3 - self.plane
        self.first = (z * 4 + self.first_plane, core)
        self.second = (z * 4 + self.second_plane, core)
        self.twin = (chip, 1 - core)

    def layer(self, mirrored):
        return mirrored + self.half * (3 - 2 * mirrored)

    def arrival(self, k):
        return (self.z, self.layer(1 - self.middle), self.layer(2), self.layer(3))[k]


def greet(spot):
    barrier = pltpu.get_barrier_semaphore()
    for device in (spot.twin, spot.inner, spot.first, spot.second):
        pl.semaphore_signal(barrier, inc=1, device_id=device, device_id_type=MESH)

    @pl.when(spot.is_middle)
    def _():
        pl.semaphore_signal(barrier, inc=1, device_id=spot.outer, device_id_type=MESH)
        pl.semaphore_wait(barrier, 5)

    @pl.when(spot.is_end)
    def _():
        pl.semaphore_wait(barrier, 4)


class Gather:
    def __init__(self, spot, shard, held, stage, apart, stage_sems, send, recv):
        self.spot, self.shard, self.held = spot, shard, held
        self.stage, self.apart, self.stage_sems = stage, apart, stage_sems
        self.send, self.recv = send, recv
        self.rows = held.shape[1] // 16
        self.width = held.shape[2]

    def block(self, z, plane):
        start = pl.multiple_of((z * 4 + plane) * self.rows, 16)
        return self.held.at[self.spot.core, pl.ds(start, self.rows), :]

    def layer_rows(self, half, z):
        start = pl.multiple_of(z * 4 * self.rows, 16)
        return self.held.at[half, pl.ds(start, 4 * self.rows), :]

    def copy(self, ref, send, recv, device):
        return pltpu.make_async_remote_copy(
            src_ref=ref,
            dst_ref=ref,
            send_sem=self.send.at[send],
            recv_sem=self.recv.at[recv],
            device_id=device,
            device_id_type=MESH,
        )

    def swap(self):
        rows = self.rows // 2
        core = self.spot.core
        start = pl.multiple_of(core * rows, 8)
        return pltpu.make_async_remote_copy(
            src_ref=self.apart,
            dst_ref=self.stage.at[pl.ds(start, rows), :],
            send_sem=self.stage_sems.at[0],
            recv_sem=self.stage_sems.at[1],
            device_id=self.spot.twin,
            device_id_type=MESH,
        )

    def open(self):
        rows, core = self.rows // 2, self.spot.core
        theirs = pl.multiple_of((1 - core) * self.width, 128)
        ours = pl.multiple_of(core * self.width, 128)
        self.apart[...] = self.shard[:, pl.ds(theirs, self.width)].astype(jnp.float32)
        self.swap().start()
        self.stage[pl.ds(pl.multiple_of(core * rows, 8), rows), :] = self.shard[
            :, pl.ds(ours, self.width)
        ].astype(jnp.float32)

    def own(self):
        self.swap().wait_recv()
        start = pl.multiple_of(self.spot.chip * self.rows, 16)
        self.held[self.spot.core, pl.ds(start, self.rows), :] = self.stage[...].astype(jnp.bfloat16)
        self.z_own(True).start()
        pl.when(self.spot.is_middle)(lambda: self.z_own(False).start())
        self.first_copy(0).start()
        self.second_copy(0).start()

    def z_own(self, inward):
        spot = self.spot
        return self.copy(
            self.block(spot.z, spot.plane),
            0 if inward else 1,
            spot.z,
            spot.inner if inward else spot.outer,
        )

    def z_pass(self, k):
        spot = self.spot
        z = spot.arrival(k)
        return self.copy(
            self.block(z, spot.plane), 1 + k, z, spot.inner if k == 1 else spot.outer
        )

    def first_copy(self, k):
        z = self.spot.arrival(k)
        return self.copy(self.block(z, self.spot.plane), 5 + k, 4 + z, self.spot.first)

    def second_copy(self, k):
        z = self.spot.arrival(k)
        return self.copy(self.block(z, self.spot.plane), 9 + k, 8 + z, self.spot.second)

    def second_pass(self, k):
        z = self.spot.arrival(k)
        return self.copy(self.block(z, self.spot.first_plane), 13 + k, 12 + z, self.spot.second)

    def twin_copy(self, k):
        z = self.spot.arrival(k)
        return self.copy(self.layer_rows(self.spot.core, z), 17 + k, 16 + z, self.spot.twin)

    def along_z(self, k):
        spot = self.spot
        z = spot.arrival(k)
        self.copy(self.block(z, spot.plane), 0, z, spot.inner).wait_recv()
        pl.when(spot.is_middle)(lambda: self.z_pass(k).start())
        self.first_copy(k).start()
        self.second_copy(k).start()

    def along_first(self, k):
        spot = self.spot
        z = spot.arrival(k)
        self.copy(self.block(z, spot.first_plane), 0, 4 + z, spot.first).wait_recv()
        self.second_pass(k).start()

    def along_second(self, k):
        spot = self.spot
        z = spot.arrival(k)
        self.copy(self.block(z, spot.second_plane), 0, 8 + z, spot.second).wait_recv()
        self.copy(self.block(z, spot.far_plane), 0, 12 + z, spot.second).wait_recv()
        self.twin_copy(k).start()

    def from_twin(self, k):
        z = self.spot.arrival(k)
        self.copy(self.layer_rows(1 - self.spot.core, z), 0, 16 + z, self.spot.twin).wait_recv()

    def events(self):
        return [
            (0.0, self.own),
            (2.5, lambda: self.along_first(0)),
            (2.6, lambda: self.along_z(1)),
            (4.0, lambda: self.along_z(2)),
            (5.0, lambda: self.along_first(1)),
            (5.5, lambda: self.along_z(3)),
            (6.0, lambda: self.along_second(0)),
            (7.0, lambda: self.along_first(2)),
            (8.0, lambda: self.along_second(1)),
            (9.0, lambda: self.along_first(3)),
            (10.5, lambda: self.along_second(2)),
            (13.0, lambda: self.along_second(3)),
        ]

    def landed(self):
        for k in range(4):
            self.from_twin(k)

    def drain(self):
        spot = self.spot
        self.swap().wait_send()
        self.z_own(True).wait_send()

        @pl.when(spot.is_middle)
        def _():
            self.z_own(False).wait_send()
            for k in (1, 2, 3):
                self.z_pass(k).wait_send()

        for k in range(4):
            self.first_copy(k).wait_send()
            self.second_copy(k).wait_send()
            self.second_pass(k).wait_send()
            self.twin_copy(k).wait_send()


def gather_kernel(*refs):
    shards, held = refs[:6], refs[6:12]
    stage, apart = refs[12:18], refs[18:24]
    stage_sems, send, recv = refs[24:]
    spot = Spot()
    gathers = [
        Gather(spot, shards[i], held[i], stage[i], apart[i], stage_sems.at[i], send.at[i], recv.at[i])
        for i in range(6)
    ]
    greet(spot)
    events = []
    start = 0.0
    for i, gather in enumerate(gathers):
        unit = gather.rows * gather.width / (48 * 1152)
        for place, (at, action) in enumerate(gather.events()):
            when = start + at * unit if place else start - 10
            events.append((when, i, place, action))
        start += 12 * unit
    events.sort(key=lambda e: e[:3])
    for gather in gathers:
        gather.open()
    for _, _, _, action in events:
        action()
    for gather in gathers:
        gather.landed()
    for gather in gathers:
        gather.drain()


def gather_weights(shards):
    dims = [(16 * 2 * s.shape[0], s.shape[1] // 2) for s in shards]
    return pl.pallas_call(
        gather_kernel,
        out_shape=[jax.ShapeDtypeStruct((2, r, n), jnp.bfloat16) for r, n in dims],
        in_specs=[pl.BlockSpec(memory_space=pltpu.VMEM)] * 6,
        out_specs=[pl.BlockSpec(memory_space=pltpu.VMEM)] * 6,
        scratch_shapes=[pltpu.VMEM((r // 16, n), jnp.float32) for r, n in dims]
        + [pltpu.VMEM((r // 32, n), jnp.float32) for r, n in dims]
        + [
            pltpu.SemaphoreType.DMA((6, 2)),
            pltpu.SemaphoreType.DMA((6, 21)),
            pltpu.SemaphoreType.DMA((6, 20)),
        ],
        compiler_params=pltpu.CompilerParams(
            collective_id=0, has_side_effects=True, vmem_limit_bytes=60 * 2**20
        ),
    )(*shards)


def on_device(
    tokens,
    seg_ids,
    frame_ids,
    patch_ids,
    timesteps,
    w_ada,
    b_ada,
    w_qkv_spatial,
    w_out_spatial,
    w_qkv_temporal,
    w_out_temporal,
    w_up,
    w_down,
    cotangent,
    on_grid,
):
    axes = ("wide", "narrow")
    shards = (w_qkv_spatial, w_out_spatial, w_qkv_temporal, w_out_temporal, w_up, w_down)
    if on_grid:
        halves = gather_weights(shards)
        gathered = (None, None) + tuple(jnp.concatenate([h[0], h[1]], axis=1) for h in halves)
    else:
        gathered = (None, None) + tuple(
            lax.all_gather(s, axes, axis=0, tiled=True) for s in shards
        )
    width = tokens.shape[1]
    head_count = HEADS
    clip_count = timesteps.shape[0]
    row_count = w_ada.shape[0]
    place = lax.axis_index(axes)
    all_steps = lax.all_gather(timesteps, axes, axis=0, tiled=True)
    cond_all = jax.nn.silu(time_embed(all_steps, width)).astype(jnp.bfloat16)
    cond_rows = lax.dynamic_slice_in_dim(cond_all, place * row_count, row_count, axis=1)
    all_bias = lax.all_gather(b_ada, axes, axis=0, tiled=True)
    modulation = lax.psum_scatter(
        jnp.dot(cond_rows, w_ada, preferred_element_type=jnp.float32),
        axes,
        scatter_dimension=0,
        tiled=True,
    ) + all_bias.astype(jnp.float32)
    one_hot = (seg_ids[:, None] == jnp.arange(clip_count, dtype=jnp.int32)[None, :]).astype(
        jnp.float32
    )
    offset_first, scale_first, gate_a = sublayer_mod(one_hot, modulation, 0, width)
    offset_second, scale_second, gate_b = sublayer_mod(one_hot, modulation, 1, width)
    offset_third, scale_third, gate_c = sublayer_mod(one_hot, modulation, 2, width)
    same_clip = seg_ids[:, None] == seg_ids[None, :]
    spatial_mask = same_clip & (frame_ids[:, None] == frame_ids[None, :])
    temporal_mask = same_clip & (patch_ids[:, None] == patch_ids[None, :])
    residual_first = tokens.astype(jnp.float32)
    standardized_first, inverse_deviation_first = layer_norm_apply(residual_first)
    normalized_first = (standardized_first * (1.0 + scale_first) + offset_first).astype(
        jnp.bfloat16
    )
    branch_a, qkv_a, merged_a = attention_forward(
        normalized_first, gathered[2], gathered[3], spatial_mask, head_count
    )
    residual_second = residual_first + gate_a * branch_a
    standardized_second, inverse_deviation_second = layer_norm_apply(residual_second)
    normalized_second = (standardized_second * (1.0 + scale_second) + offset_second).astype(
        jnp.bfloat16
    )
    branch_b, qkv_b, merged_b = attention_forward(
        normalized_second, gathered[4], gathered[5], temporal_mask, head_count
    )
    residual_third = residual_second + gate_b * branch_b
    standardized_third, inverse_deviation_third = layer_norm_apply(residual_third)
    normalized_third = (standardized_third * (1.0 + scale_third) + offset_third).astype(
        jnp.bfloat16
    )
    pre_act = jnp.dot(normalized_third, gathered[6], preferred_element_type=jnp.float32)
    act_out, gelu_pull = jax.vjp(jax.nn.gelu, pre_act)
    hidden = act_out.astype(jnp.bfloat16)
    branch_c = jnp.dot(hidden, gathered[7], preferred_element_type=jnp.float32)
    result = residual_third + gate_c * branch_c
    back_weights = gathered
    output_gradient = cotangent.astype(jnp.float32)
    gate_gradient_third = output_gradient * branch_c
    grad_branch_c = (gate_c * output_gradient).astype(jnp.bfloat16)
    grad_hidden = contract_cols(grad_branch_c, back_weights[7])
    grad_pre = gelu_pull(grad_hidden)[0].astype(jnp.bfloat16)
    normalized_gradient_third = contract_cols(grad_pre, back_weights[6])
    residual_gradient = output_gradient + layer_norm_reverse(
        normalized_gradient_third, standardized_third, inverse_deviation_third, scale_third
    )
    gate_gradient_second = residual_gradient * branch_b
    grad_branch_b = (gate_b * residual_gradient).astype(jnp.bfloat16)
    normalized_gradient_second, grad_qkv_t = attention_backward(
        grad_branch_b, qkv_b, back_weights[4], back_weights[5], temporal_mask, head_count
    )
    residual_gradient = residual_gradient + layer_norm_reverse(
        normalized_gradient_second, standardized_second, inverse_deviation_second, scale_second
    )
    gate_gradient_first = residual_gradient * branch_a
    grad_branch_a = (gate_a * residual_gradient).astype(jnp.bfloat16)
    normalized_gradient_first, grad_qkv_s = attention_backward(
        grad_branch_a, qkv_a, back_weights[2], back_weights[3], spatial_mask, head_count
    )
    residual_gradient = residual_gradient + layer_norm_reverse(
        normalized_gradient_first, standardized_first, inverse_deviation_first, scale_first
    )
    grad_mod = jnp.concatenate(
        [
            exact_rows(
                one_hot,
                jnp.concatenate(
                    [
                        normalized_gradient_first,
                        normalized_gradient_first * standardized_first,
                        gate_gradient_first,
                    ],
                    axis=1,
                ),
            ),
            exact_rows(
                one_hot,
                jnp.concatenate(
                    [
                        normalized_gradient_second,
                        normalized_gradient_second * standardized_second,
                        gate_gradient_second,
                    ],
                    axis=1,
                ),
            ),
            exact_rows(
                one_hot,
                jnp.concatenate(
                    [
                        normalized_gradient_third,
                        normalized_gradient_third * standardized_third,
                        gate_gradient_third,
                    ],
                    axis=1,
                ),
            ),
        ],
        axis=1,
    )
    grad_mod_low = grad_mod.astype(jnp.bfloat16)
    all_grad_mod = lax.all_gather(grad_mod_low, axes, axis=0, tiled=True)
    bias_share = lax.psum_scatter(
        jnp.sum(grad_mod, axis=0), axes, scatter_dimension=0, tiled=True
    )

    def share(left, right):
        return lax.psum_scatter(
            contract_rows(left, right).astype(jnp.bfloat16),
            axes,
            scatter_dimension=0,
            tiled=True,
        ).astype(jnp.float32)

    return (
        result.astype(jnp.bfloat16),
        residual_gradient,
        contract_rows(cond_rows, all_grad_mod),
        bias_share,
        share(normalized_first, grad_qkv_s),
        share(merged_a, grad_branch_a),
        share(normalized_second, grad_qkv_t),
        share(merged_b, grad_branch_b),
        share(normalized_third, grad_pre),
        share(hidden, grad_branch_c),
    )


def solution(mesh):
    placed = (
        P(("wide", "narrow"), None),
        P(("wide", "narrow")),
        P(("wide", "narrow")),
        P(("wide", "narrow")),
        P(("wide", "narrow")),
        P(("wide", "narrow"), None),
        P(("wide", "narrow")),
        P(("wide", "narrow"), None),
        P(("wide", "narrow"), None),
        P(("wide", "narrow"), None),
        P(("wide", "narrow"), None),
        P(("wide", "narrow"), None),
        P(("wide", "narrow"), None),
        P(("wide", "narrow"), None),
    )
    on_grid = dict(mesh.shape) == {"wide": 16, "narrow": 2}
    return jax.shard_map(
        partial(on_device, on_grid=on_grid),
        mesh=mesh,
        in_specs=placed,
        out_specs=(
            P(("wide", "narrow"), None),
            P(("wide", "narrow"), None),
            P(("wide", "narrow"), None),
            P(("wide", "narrow")),
            P(("wide", "narrow"), None),
            P(("wide", "narrow"), None),
            P(("wide", "narrow"), None),
            P(("wide", "narrow"), None),
            P(("wide", "narrow"), None),
            P(("wide", "narrow"), None),
        ),
        check_vma=False,
    )
```

```python
from functools import partial
import math

import jax
import jax.numpy as jnp
from jax import lax
from jax.experimental import pallas as pl
from jax.experimental.pallas import tpu as pltpu
from jax.sharding import PartitionSpec as P

HEADS = 12


EPSILON = 1e-06
FREQ_BASE = 10000.0
MASKED = -1e30


def time_embed(step_ids, width):
    half_width = width // 2
    frequency = jnp.exp(
        -math.log(FREQ_BASE) * jnp.arange(half_width, dtype=jnp.float32) / half_width
    )
    angles = step_ids.astype(jnp.float32)[:, None] * frequency[None, :]
    return jnp.concatenate([jnp.cos(angles), jnp.sin(angles)], axis=1)


def contract_rows(left, right):
    return lax.dot_general(
        left, right, (((0,), (0,)), ((), ())), preferred_element_type=jnp.float32
    )


def contract_cols(left, right):
    return lax.dot_general(
        left, right, (((1,), (1,)), ((), ())), preferred_element_type=jnp.float32
    )


def exact_rows(left, right):
    return lax.dot_general(
        left,
        right,
        (((0,), (0,)), ((), ())),
        precision=lax.Precision.HIGHEST,
        preferred_element_type=jnp.float32,
    )


def layer_norm_apply(stream):
    center = stream - jnp.mean(stream, axis=-1, keepdims=True)
    inverse_deviation = lax.rsqrt(jnp.mean(center * center, axis=-1, keepdims=True) + EPSILON)
    return (center * inverse_deviation, inverse_deviation)


def layer_norm_reverse(normalized_gradient, standardized_input, inverse_deviation, row_scales):
    input_gradient = normalized_gradient * (1.0 + row_scales)
    mean_removed = input_gradient - jnp.mean(input_gradient, axis=-1, keepdims=True)
    return inverse_deviation * (
        mean_removed
        - standardized_input * jnp.mean(input_gradient * standardized_input, axis=-1, keepdims=True)
    )


def sublayer_mod(one_hot, modulation, sublayer, width):
    table = modulation[:, 3 * width * sublayer : 3 * width * (sublayer + 1)]
    rows_mod = jnp.dot(
        one_hot, table, precision=lax.Precision.HIGHEST, preferred_element_type=jnp.float32
    )
    return (rows_mod[:, :width], rows_mod[:, width : 2 * width], rows_mod[:, 2 * width :])


def head_probs(allowed, scale, queries, key_vecs):
    scores = contract_cols(queries, key_vecs) * scale
    scores = jnp.where(allowed, scores, MASKED)
    return jax.nn.softmax(scores, axis=-1)


def head_forward(allowed, scale, item):
    queries, key_vecs, val_vecs = item
    attn_prob = head_probs(allowed, scale, queries, key_vecs)
    return jnp.dot(attn_prob.astype(jnp.bfloat16), val_vecs, preferred_element_type=jnp.float32)


def head_backward(allowed, scale, item):
    queries, key_vecs, val_vecs, grad_att = item
    attn_prob = head_probs(allowed, scale, queries, key_vecs)
    grad_val = contract_rows(attn_prob.astype(jnp.bfloat16), grad_att)
    grad_prob = contract_cols(grad_att, val_vecs)
    grad_score = attn_prob * (grad_prob - jnp.sum(attn_prob * grad_prob, axis=-1, keepdims=True))
    score_low = grad_score.astype(jnp.bfloat16)
    grad_query = jnp.dot(score_low, key_vecs, preferred_element_type=jnp.float32) * scale
    grad_key = contract_rows(score_low, queries) * scale
    return (grad_query, grad_key, grad_val)


def split_heads(qkv_rows, head_count):
    row_count = qkv_rows.shape[0]
    return qkv_rows.reshape(row_count, 3, head_count, -1).transpose(1, 2, 0, 3)


def attention_forward(normed, w_qkv, w_out, allowed, head_count):
    row_count = normed.shape[0]
    qkv_rows = jnp.dot(normed, w_qkv, preferred_element_type=jnp.float32).astype(jnp.bfloat16)
    split_qkv = split_heads(qkv_rows, head_count)
    scale = split_qkv.shape[-1] ** (-0.5)
    attended = lax.map(
        partial(head_forward, allowed, scale), (split_qkv[0], split_qkv[1], split_qkv[2])
    )
    merged = attended.transpose(1, 0, 2).reshape(row_count, -1).astype(jnp.bfloat16)
    branch = jnp.dot(merged, w_out, preferred_element_type=jnp.float32)
    return (branch, qkv_rows, merged)


def attention_backward(grad_branch, qkv_rows, w_qkv, w_out, allowed, head_count):
    row_count = qkv_rows.shape[0]
    grad_merged = contract_cols(grad_branch, w_out).astype(jnp.bfloat16)
    grad_heads = grad_merged.reshape(row_count, head_count, -1).transpose(1, 0, 2)
    split_qkv = split_heads(qkv_rows, head_count)
    scale = split_qkv.shape[-1] ** (-0.5)
    grad_query, grad_key, grad_val = lax.map(
        partial(head_backward, allowed, scale),
        (split_qkv[0], split_qkv[1], split_qkv[2], grad_heads),
    )
    grad_qkv = (
        jnp.stack([grad_query, grad_key, grad_val])
        .transpose(2, 0, 1, 3)
        .reshape(row_count, -1)
        .astype(jnp.bfloat16)
    )
    normalized_gradient = contract_cols(grad_qkv, w_qkv)
    return (normalized_gradient, grad_qkv)


MESH = pl.DeviceIdType.MESH


class Spot:
    def __init__(self):
        chip = lax.axis_index("wide")
        core = lax.axis_index("narrow")
        z, y, x = lax.div(chip, 4), lax.rem(lax.div(chip, 2), 2), lax.rem(chip, 2)
        half = lax.div(z, 2)
        toward = 1 - 2 * half
        self.chip, self.core, self.z, self.y, self.x = chip, core, z, y, x
        self.half = half
        self.middle = z + half * (3 - 2 * z)
        self.is_middle = self.middle == 1
        self.is_end = self.middle == 0
        self.plane = 2 * y + x
        self.inner = ((z + toward) * 4 + self.plane, core)
        self.outer = ((z - toward) * 4 + self.plane, core)
        self.first_plane = 2 * lax.rem(y + core, 2) + lax.rem(x + 1 - core, 2)
        self.second_plane = 2 * lax.rem(y + 1 - core, 2) + lax.rem(x + core, 2)
        self.far_plane = 3 - self.plane
        self.first = (z * 4 + self.first_plane, core)
        self.second = (z * 4 + self.second_plane, core)
        self.twin = (chip, 1 - core)

    def layer(self, mirrored):
        return mirrored + self.half * (3 - 2 * mirrored)

    def arrival(self, k):
        return (self.z, self.layer(1 - self.middle), self.layer(2), self.layer(3))[k]


def greet(spot):
    barrier = pltpu.get_barrier_semaphore()
    for device in (spot.twin, spot.inner, spot.first, spot.second):
        pl.semaphore_signal(barrier, inc=1, device_id=device, device_id_type=MESH)

    @pl.when(spot.is_middle)
    def _():
        pl.semaphore_signal(barrier, inc=1, device_id=spot.outer, device_id_type=MESH)
        pl.semaphore_wait(barrier, 5)

    @pl.when(spot.is_end)
    def _():
        pl.semaphore_wait(barrier, 4)


def remote(src, dst, send, recv, device):
    return pltpu.make_async_remote_copy(
        src_ref=src,
        dst_ref=dst,
        send_sem=send,
        recv_sem=recv,
        device_id=device,
        device_id_type=MESH,
    )


class Gather:
    def __init__(self, spot, held, stage, apart, swap_sems, send, recv):
        self.spot, self.held = spot, held
        self.stage, self.apart, self.swap_sems = stage, apart, swap_sems
        self.send, self.recv = send, recv
        self.whole = apart.shape[1] == 48

    def block(self, z, plane):
        return self.held.at[self.spot.core, z * 4 + plane]

    def layer_blocks(self, half, z):
        return self.held.at[half, pl.ds(z * 4, 4)]

    def copy(self, ref, send, recv, device):
        return remote(ref, ref, self.send.at[send], self.recv.at[recv], device)

    def mine(self):
        core = self.spot.core
        if self.whole:
            return self.stage.at[pl.ds(2 * core, 2)]
        return self.stage.at[:, pl.ds(pl.multiple_of(core * 24, 8), 24), :]

    def swap(self):
        return remote(
            self.apart, self.mine(), self.swap_sems.at[0], self.swap_sems.at[1], self.spot.twin
        )

    def open(self, piece):
        core = self.spot.core
        for chunk in range(self.apart.shape[0]):
            self.apart[chunk] = piece(1 - core, chunk).astype(jnp.float32)
        self.swap().start()
        place = self.mine()
        for chunk in range(self.apart.shape[0]):
            place[chunk] = piece(core, chunk).astype(jnp.float32)

    def own(self):
        spot = self.spot
        self.swap().wait_recv()
        self.held[spot.core, spot.chip] = self.stage[...].astype(jnp.bfloat16)
        self.z_own(True).start()
        pl.when(spot.is_middle)(lambda: self.z_own(False).start())
        self.first_copy(0).start()
        self.second_copy(0).start()

    def z_own(self, inward):
        spot = self.spot
        return self.copy(
            self.block(spot.z, spot.plane),
            0 if inward else 1,
            spot.z,
            spot.inner if inward else spot.outer,
        )

    def z_pass(self, k):
        spot = self.spot
        z = spot.arrival(k)
        return self.copy(
            self.block(z, spot.plane), 1 + k, z, spot.inner if k == 1 else spot.outer
        )

    def first_copy(self, k):
        z = self.spot.arrival(k)
        return self.copy(self.block(z, self.spot.plane), 5 + k, 4 + z, self.spot.first)

    def second_copy(self, k):
        z = self.spot.arrival(k)
        return self.copy(self.block(z, self.spot.plane), 9 + k, 8 + z, self.spot.second)

    def second_pass(self, k):
        z = self.spot.arrival(k)
        return self.copy(self.block(z, self.spot.first_plane), 13 + k, 12 + z, self.spot.second)

    def twin_copy(self, k):
        z = self.spot.arrival(k)
        return self.copy(self.layer_blocks(self.spot.core, z), 17 + k, 16 + z, self.spot.twin)

    def along_z(self, k):
        spot = self.spot
        z = spot.arrival(k)
        self.copy(self.block(z, spot.plane), 0, z, spot.inner).wait_recv()
        pl.when(spot.is_middle)(lambda: self.z_pass(k).start())
        self.first_copy(k).start()
        self.second_copy(k).start()

    def along_first(self, k):
        spot = self.spot
        z = spot.arrival(k)
        self.copy(self.block(z, spot.first_plane), 0, 4 + z, spot.first).wait_recv()
        self.second_pass(k).start()

    def along_second(self, k):
        spot = self.spot
        z = spot.arrival(k)
        self.copy(self.block(z, spot.second_plane), 0, 8 + z, spot.second).wait_recv()
        self.copy(self.block(z, spot.far_plane), 0, 12 + z, spot.second).wait_recv()
        self.twin_copy(k).start()

    def from_twin(self, k):
        z = self.spot.arrival(k)
        self.copy(self.layer_blocks(1 - self.spot.core, z), 0, 16 + z, self.spot.twin).wait_recv()

    def landed(self):
        for k in range(4):
            self.from_twin(k)

    def drain(self):
        spot = self.spot
        self.z_own(True).wait_send()

        @pl.when(spot.is_middle)
        def _():
            self.z_own(False).wait_send()
            for k in (1, 2, 3):
                self.z_pass(k).wait_send()

        for k in range(4):
            self.first_copy(k).wait_send()
            self.second_copy(k).wait_send()
            self.second_pass(k).wait_send()
            self.twin_copy(k).wait_send()


class LineSum:
    def __init__(self, spot, part, slot, send, recv):
        self.spot, self.part, self.slot = spot, part, slot
        self.send, self.recv = send, recv

    def layer(self, k):
        spot = self.spot
        return (spot.layer(3), spot.layer(2), spot.layer(1 - spot.middle), spot.z)[k]

    def copy(self, k, slot, device):
        return remote(
            self.part(self.layer(k)), self.slot(slot), self.send.at[k], self.recv.at[slot], device
        )

    def from_end(self, k):
        return self.copy(k, k, self.spot.inner)

    def from_middle(self, k):
        return self.copy(k, 3 + k, self.spot.inner) if k < 2 else self.copy(2, 3, self.spot.outer)

    def arrived(self, slot):
        self.copy(0, slot, self.spot.inner).wait_recv()
        return self.slot(slot)

    def step(self, k):
        spot = self.spot

        @pl.when(spot.is_end)
        def _():
            self.from_end(k).start()

        @pl.when(spot.is_middle)
        def _():
            source, part = self.arrived((0, 1, 3)[k]), self.part(self.layer(k))
            for i in range(part.shape[0]):
                part[i] += source[i]
            self.from_middle(k).start()

    def total(self, put):
        def add(*slots):
            sources = [self.arrived(slot) for slot in slots]
            part = self.part(self.spot.z)
            for i in range(part.shape[0]):
                value = part[i].astype(jnp.float32)
                for source in sources:
                    value += source[i].astype(jnp.float32)
                put(i, value)

        pl.when(self.spot.is_end)(lambda: add(3))
        pl.when(self.spot.is_middle)(lambda: add(2, 4))

    def drain(self):
        for k in range(3):
            self.from_end(k).wait_send()


class LineGather:
    def __init__(self, spot, part, send, recv):
        self.spot, self.part = spot, part
        self.send, self.recv = send, recv

    def copy(self, z, send, device):
        ref = self.part(z)
        return remote(ref, ref, self.send.at[send], self.recv.at[z], device)

    def own(self, inward):
        spot = self.spot
        return self.copy(spot.z, 0 if inward else 1, spot.inner if inward else spot.outer)

    def onward(self, k):
        spot = self.spot
        return self.copy(spot.arrival(k), 1 + k, spot.inner if k == 1 else spot.outer)

    def open(self):
        self.own(True).start()
        pl.when(self.spot.is_middle)(lambda: self.own(False).start())

    def step(self, k):
        self.copy(self.spot.arrival(k), 0, self.spot.inner).wait_recv()
        pl.when(self.spot.is_middle)(lambda: self.onward(k).start())

    def drain(self):
        self.own(True).wait_send()

        @pl.when(self.spot.is_middle)
        def _():
            self.own(False).wait_send()
            for k in (1, 2, 3):
                self.onward(k).wait_send()


class Scatter:
    def __init__(
        self, spot, sums, from_second, from_first, from_z, final, theirs, send, recv, credit, owed
    ):
        self.spot, self.sums = spot, sums
        self.from_second, self.from_first = from_second, from_first
        self.final, self.theirs = final, theirs
        self.send, self.recv, self.credit = send, recv, credit
        self.owed, self.whole = owed, theirs.shape[1] == 48
        self.line = LineSum(
            spot,
            lambda z: sums.at[pl.ds(16 * z, 4)],
            lambda i: from_z.at[i],
            send.at[pl.ds(8, 3)],
            recv.at[pl.ds(8, 5)],
        )

    def place(self, chip):
        spot = self.spot
        z, y, x = chip // 4, (chip // 2) % 2, chip % 2
        other_y, other_x = lax.rem(spot.y + y, 2), lax.rem(spot.x + x, 2)
        second = other_y * (1 - spot.core) + other_x * spot.core
        first = other_x * (1 - spot.core) + other_y * spot.core
        return 16 * z + 8 * second + 4 * first

    def second_copy(self, k):
        z = self.line.layer(k)
        return remote(
            self.sums.at[pl.ds(16 * z + 8, 8)],
            self.from_second.at[z],
            self.send.at[k],
            self.recv.at[z],
            self.spot.second,
        )

    def first_copy(self, k):
        z = self.line.layer(k)
        return remote(
            self.sums.at[pl.ds(16 * z + 4, 4)],
            self.from_first.at[z],
            self.send.at[4 + k],
            self.recv.at[4 + z],
            self.spot.first,
        )

    def swap(self):
        core = self.spot.core
        if self.whole:
            src = self.final.at[pl.ds(2 * (1 - core), 2)]
        else:
            src = self.final.at[:, pl.ds(pl.multiple_of((1 - core) * 24, 8), 24), :]
        return remote(src, self.theirs, self.send.at[11], self.recv.at[13], self.spot.twin)

    def start(self):
        spot = self.spot
        if self.owed:
            for kind in range(3):
                pl.semaphore_wait(self.credit.at[kind], 1)
            pl.when(spot.is_middle)(lambda: pl.semaphore_wait(self.credit.at[3], 1))
        for k in range(4):
            self.second_copy(k).start()

    def add_second(self, k):
        z = self.line.layer(k)
        self.second_copy(k).wait_recv()
        for i in (4, 5, 6, 7, 0, 1, 2, 3):
            self.sums[16 * z + i] += self.from_second[z, i]
            if i == 7:
                self.first_copy(k).start()

    def add_first(self, k):
        z = self.line.layer(k)
        self.first_copy(k).wait_recv()
        for i in range(4):
            self.sums[16 * z + i] += self.from_first[z, i]
        if k < 3:
            self.line.step(k)

    def finish(self):
        def put(i, value):
            self.final[i] = value

        self.line.total(put)
        self.swap().start()

    def store(self, put):
        core = self.spot.core
        for chunk in range(self.theirs.shape[0]):
            if self.whole:
                mine = self.final[2 * core + chunk]
            else:
                mine = self.final[chunk, pl.ds(pl.multiple_of(core * 24, 8), 24), :]
            put(core, chunk, mine)
        self.swap().wait_recv()
        for chunk in range(self.theirs.shape[0]):
            put(1 - core, chunk, self.theirs[chunk])

    def drain(self):
        for k in range(4):
            self.second_copy(k).wait_send()
            self.first_copy(k).wait_send()
        self.line.drain()

    def release(self):
        spot, credit = self.spot, self.credit

        def tell(kind, device):
            pl.semaphore_signal(credit.at[kind], inc=1, device_id=device, device_id_type=MESH)

        tell(0, spot.second)
        tell(1, spot.first)

        @pl.when(spot.is_end)
        def _():
            tell(3, spot.inner)

        @pl.when(spot.is_middle)
        def _():
            tell(2, spot.inner)
            tell(2, spot.outer)


class Plan:
    def __init__(self):
        self.clock, self.waiting, self.count = 0.0, [], 0

    def at(self, time, action):
        self.waiting.append((time, self.count, action))
        self.count += 1

    def flush(self):
        while self.waiting:
            first = min(self.waiting, key=lambda entry: entry[:2])
            if first[0] > self.clock:
                return
            self.waiting.remove(first)
            first[2]()

    def run(self, cost, action):
        self.flush()
        action()
        self.clock += cost

    def until(self, time):
        while self.waiting and min(entry[0] for entry in self.waiting) <= time:
            self.clock = max(self.clock, min(entry[0] for entry in self.waiting))
            self.flush()
        self.clock = max(self.clock, time)


def dot(left, right):
    return jnp.dot(left, right, preferred_element_type=jnp.float32)


GATHER_STEPS = (
    (2.5, "first", 0),
    (2.6, "z", 1),
    (4.0, "z", 2),
    (5.0, "first", 1),
    (5.5, "z", 3),
    (6.0, "second", 0),
    (7.0, "first", 2),
    (8.0, "second", 1),
    (9.0, "first", 3),
    (10.5, "second", 2),
    (13.0, "second", 3),
)
SCATTER_STEPS = (
    (2.0, "second", 0),
    (4.0, "second", 1),
    (5.5, "first", 0),
    (6.0, "second", 2),
    (7.5, "first", 1),
    (8.0, "second", 3),
    (9.5, "first", 2),
    (11.0, "first", 3),
    (13.0, "finish", 0),
)
UNIT = 1.6
GROUPS = ("spatial", "temporal", "up", "down")


def layer_kernel(
    tokens,
    cotangent,
    ids_row,
    ids_col,
    steps,
    bias,
    w_ada,
    w_qkv_s,
    w_out_s,
    w_qkv_t,
    w_out_t,
    w_up,
    w_down,
    o_layer,
    o_tokens,
    o_ada,
    o_bias,
    o_qkv_s,
    o_out_s,
    o_qkv_t,
    o_out_t,
    o_up,
    o_down,
    held,
    stage,
    apart,
    apart_down,
    sums,
    from_second,
    from_first,
    from_z,
    all_steps,
    cond,
    mod_half,
    mod,
    tally,
    rows_mod,
    all_rows_mod,
    xhat,
    deviation,
    normed,
    attended,
    turned,
    hidden_turned,
    qkv,
    probs,
    branch,
    stream,
    grad,
    hidden,
    slope,
    grad_pre_twin,
    gated,
    gated_twin,
    grad_attended,
    grad_qkv_twin,
    disallowed,
    swap_sems,
    gather_send,
    gather_recv,
    scatter_send,
    scatter_recv,
    credit,
    twin_send,
    twin_recv,
    step_send,
    step_recv,
    mod_send,
    mod_recv,
    row_send,
    row_recv,
):
    width, tok = tokens.shape[1], tokens.shape[0]
    f32, bf16 = jnp.float32, jnp.bfloat16
    spot = Spot()
    core = spot.core
    grad_qkv, grad_normed = hidden, stream
    greet(spot)

    def attention_piece(w_qkv, w_out):
        def piece(half, chunk):
            if chunk < 3:
                return w_qkv[:, pl.ds(pl.multiple_of(half * 1152 + chunk * 384, 128), 384)]
            return w_out[:, pl.ds(pl.multiple_of(half * 384, 128), 384)]

        return piece

    def up_piece(half, chunk):
        return w_up[:, pl.ds(pl.multiple_of(half * 1536 + chunk * 384, 128), 384)]

    def down_piece(half, chunk):
        return w_down[chunk * 48 : chunk * 48 + 48, pl.ds(pl.multiple_of(half * 384, 128), 384)]

    pieces = (
        attention_piece(w_qkv_s, w_out_s),
        attention_piece(w_qkv_t, w_out_t),
        up_piece,
        down_piece,
    )
    gathers = [
        Gather(
            spot,
            held.at[g],
            stage.at[g],
            apart.at[g] if g < 3 else apart_down,
            swap_sems.at[g],
            gather_send.at[g],
            gather_recv.at[g],
        )
        for g in range(4)
    ]
    scatters = [
        Scatter(
            spot,
            sums.at[n % 2],
            from_second.at[n % 2],
            from_first.at[n % 2],
            from_z.at[n % 2],
            stage.at[3 - n],
            apart_down if n == 0 else apart.at[3 - n],
            scatter_send.at[n],
            scatter_recv.at[n],
            credit.at[n % 2],
            n >= 2,
        )
        for n in range(4)
    ]

    def put_attention(o_qkv, o_out):
        def put(half, chunk, rows):
            if chunk < 3:
                o_qkv[:, pl.ds(pl.multiple_of(half * 1152 + chunk * 384, 128), 384)] = rows
            else:
                o_out[:, pl.ds(pl.multiple_of(half * 384, 128), 384)] = rows

        return put

    def put_up(half, chunk, rows):
        o_up[:, pl.ds(pl.multiple_of(half * 1536 + chunk * 384, 128), 384)] = rows

    def put_down(half, chunk, rows):
        o_down[chunk * 48 : chunk * 48 + 48, pl.ds(pl.multiple_of(half * 384, 128), 384)] = rows

    puts = (put_down, put_up, put_attention(o_qkv_t, o_out_t), put_attention(o_qkv_s, o_out_s))

    def to_twin(index, src, dst):
        return remote(src, dst, twin_send.at[index], twin_recv.at[index], spot.twin)

    def turned_copy(i):
        return to_twin(i, turned.at[i, 0], turned.at[i, 1])

    def hidden_copy():
        return to_twin(5, hidden_turned.at[0], hidden_turned.at[1])

    def gated_copy(j):
        theirs = pl.multiple_of((1 - core) * 384, 128)
        return to_twin(6 + j, gated.at[j, :, pl.ds(theirs, 384)], gated_twin.at[j])

    def grad_pre_copy():
        theirs = pl.multiple_of((1 - core) * 1536, 128)
        return to_twin(9, slope.at[:, pl.ds(theirs, 1536)], grad_pre_twin)

    def grad_qkv_copy(j):
        theirs = pl.multiple_of((1 - core) * 1152, 128)
        return to_twin(10 + j, grad_qkv.at[:, pl.ds(theirs, 1152)], grad_qkv_twin.at[j])

    def step_copy(index, ref, device):
        return remote(ref, ref, step_send.at[index], step_recv.at[index], device)

    def step_pair(plane):
        return all_steps.at[spot.z, plane]

    step_line = LineGather(
        spot, lambda z: all_steps.at[z], step_send.at[pl.ds(4, 5)], step_recv.at[pl.ds(4, 4)]
    )

    def steps_open():
        all_steps[spot.z, spot.plane, core] = steps[...]
        step_copy(0, all_steps.at[spot.z, spot.plane, core], spot.twin).start()

    def steps_first():
        step_copy(0, all_steps.at[spot.z, spot.plane, 1 - core], spot.twin).wait_recv()
        step_copy(1, step_pair(spot.plane), spot.first).start()
        step_copy(2, step_pair(spot.plane), spot.second).start()

    def steps_second():
        step_copy(1, step_pair(spot.first_plane), spot.first).wait_recv()
        step_copy(3, step_pair(spot.first_plane), spot.second).start()

    def steps_z():
        step_copy(2, step_pair(spot.second_plane), spot.second).wait_recv()
        step_copy(3, step_pair(spot.far_plane), spot.second).wait_recv()
        step_line.open()

    def steps_drain():
        step_copy(0, all_steps.at[spot.z, spot.plane, core], spot.twin).wait_send()
        for index in (1, 2, 3):
            step_copy(index, step_pair(spot.plane), spot.first).wait_send()
        step_line.drain()

    def make_cond():
        flat = all_steps[...].reshape(256, 128)
        clip = lax.broadcasted_iota(jnp.int32, (64, 256), 0)
        column = lax.broadcasted_iota(jnp.int32, (64, 256), 1)
        wanted = 8 * lax.shift_right_logical(clip, 1) + (clip & 1)
        times = jnp.dot(
            (column == wanted).astype(f32),
            flat,
            precision=lax.Precision.HIGHEST,
            preferred_element_type=f32,
        )
        first = (spot.chip * 2 + core) * 24
        half_width = width // 2
        feature = first + lax.broadcasted_iota(jnp.int32, (64, 128), 1)
        place = jnp.where(feature < half_width, feature, feature - half_width).astype(f32)
        angle = times * jnp.exp(-math.log(FREQ_BASE) * place / half_width)
        value = jnp.where(feature < half_width, jnp.cos(angle), jnp.sin(angle))
        cond[...] = (value / (1.0 + jnp.exp(-value))).astype(bf16)

    spare = sums.at[1]
    mod_out, mod_in, mod_sum = (spare.at[pl.ds(i, 12)] for i in (0, 12, 24))
    mod_first, mod_second, mod_one, mod_two = (spare.at[pl.ds(i, 3)] for i in (51, 54, 57, 60))
    mod_line = LineSum(
        spot,
        lambda z: spare.at[pl.ds(24 + 3 * z, 3)],
        lambda i: spare.at[pl.ds(36 + 3 * i, 3)],
        mod_send.at[pl.ds(0, 3)],
        mod_recv.at[pl.ds(0, 5)],
    )

    def mod_copy(index):
        src, dst, device = (
            (mod_out, mod_in, spot.twin),
            (mod_one, mod_first, spot.first),
            (mod_two, mod_second, spot.second),
            (mod_half.at[core], mod_half.at[core], spot.twin),
        )[index]
        return remote(src, dst, mod_send.at[3 + index], mod_recv.at[5 + index], device)

    def mod_partial(half, chunk):
        columns = pl.ds(pl.multiple_of(half * 3456 + chunk * 384, 128), 384)
        return dot(cond[:, :24], w_ada[:, columns]) + bias[:, columns]

    def mod_twin():
        for chunk in range(9):
            value = mod_partial(1 - core, chunk).astype(bf16)
            for z in range(4):
                mod_out[3 * z + chunk // 3, 16 * (chunk % 3) : 16 * (chunk % 3) + 16] = value[
                    16 * z : 16 * z + 16
                ]
        mod_copy(0).start()

    def mod_own():
        mod_copy(0).wait_recv()
        for chunk in range(9):
            value = mod_partial(core, chunk)
            rows = slice(16 * (chunk % 3), 16 * (chunk % 3) + 16)
            for z in range(4):
                at = 3 * z + chunk // 3
                mod_sum[at, rows] = (
                    value[16 * z : 16 * z + 16] + mod_in[at, rows].astype(f32)
                ).astype(bf16)

    def mod_along_first():
        def put(i, value):
            mod_one[i] = value.astype(bf16)

        mod_line.total(put)
        mod_copy(1).start()

    def mod_along_second():
        mod_copy(1).wait_recv()
        for i in range(3):
            mod_two[i] = mod_one[i] + mod_first[i]
        mod_copy(2).start()

    def mod_to_twin():
        mod_copy(2).wait_recv()
        for chunk in range(9):
            at, rows = chunk // 3, slice(16 * (chunk % 3), 16 * (chunk % 3) + 16)
            mod_half[core, :, 384 * chunk : 384 * chunk + 384] = mod_two[at, rows].astype(
                f32
            ) + mod_second[at, rows].astype(f32)
        mod_copy(3).start()

    def mod_rows():
        remote(
            mod_half.at[1 - core], mod_half.at[1 - core], mod_send.at[6], mod_recv.at[8], spot.twin
        ).wait_recv()
        row = lax.broadcasted_iota(jnp.int32, (16, 384), 0)
        for clip in range(2):
            chosen = row == 4 * spot.plane + 2 * core + clip
            for chunk in range(18):
                at = 384 * (chunk % 9)
                value = mod_half[chunk // 9, :, at : at + 384]
                mod[clip : clip + 1, 384 * chunk : 384 * chunk + 384] = jnp.sum(
                    jnp.where(chosen, value, 0.0), axis=0, keepdims=True
                )

    def mod_drain():
        mod_line.drain()
        for index in range(4):
            mod_copy(index).wait_send()

    row_line = LineGather(
        spot,
        lambda z: all_rows_mod.at[core, z],
        row_send.at[pl.ds(4, 5)],
        row_recv.at[pl.ds(4, 4)],
    )

    def row_copy(index):
        src, dst, device = (
            (rows_mod.at[1], rows_mod.at[2], spot.twin),
            (rows_mod.at[0], rows_mod.at[3], spot.first),
            (rows_mod.at[5], rows_mod.at[4], spot.second),
            (all_rows_mod.at[core], all_rows_mod.at[core], spot.twin),
        )[index]
        return remote(src, dst, row_send.at[index], row_recv.at[index], device)

    def row_value(half):
        columns = pl.ds(pl.multiple_of(half * 3456, 128), 3456)
        row = lax.broadcasted_iota(jnp.int32, (16, 3456), 0)
        mine = 4 * spot.plane + 2 * core
        value = jnp.where(row == mine, tally[0:1, columns], 0.0)
        return jnp.where(row == mine + 1, tally[1:2, columns], value).astype(bf16)

    def rows_open():
        rows_mod[1] = row_value(1 - core)
        row_copy(0).start()

    def rows_first():
        row_copy(0).wait_recv()
        rows_mod[0] = row_value(core) + rows_mod[2]
        row_copy(1).start()

    def rows_second():
        row_copy(1).wait_recv()
        rows_mod[5] = rows_mod[0] + rows_mod[3]
        row_copy(2).start()

    def rows_z():
        row_copy(2).wait_recv()
        all_rows_mod[core, spot.z] = rows_mod[5] + rows_mod[4]
        row_line.open()

    def rows_twin():
        row_copy(3).start()

    def ada_half(half):
        for chunk in range(9):
            value = all_rows_mod[half, :, :, 384 * chunk : 384 * chunk + 384].reshape(64, 384)
            columns = pl.ds(pl.multiple_of(half * 3456 + 384 * chunk, 128), 384)
            o_ada[:, columns] = contract_rows(cond[...], value)[:24]
            o_bias[:, columns] = jnp.sum(value.astype(f32), axis=0, keepdims=True)

    def rows_last():
        remote(
            all_rows_mod.at[1 - core],
            all_rows_mod.at[1 - core],
            row_send.at[3],
            row_recv.at[3],
            spot.twin,
        ).wait_recv()
        ada_half(1 - core)

    def rows_drain():
        for index in range(4):
            row_copy(index).wait_send()
        row_line.drain()

    def by_rows(action):
        @pl.loop(0, tok // 64)
        def _(i):
            action(pl.ds(pl.multiple_of(i * 64, 64), 64))

    def mod_part(j, component, rows):
        at = (3 * j + component) * width
        second = ids_col[rows, 2:3] == 1
        return jnp.where(second, mod[1:2, at : at + width], mod[0:1, at : at + width])

    def count(j, component, rows, value):
        at = (3 * j + component) * width
        second = ids_col[rows, 2:3] == 1
        tally[0:1, at : at + width] += jnp.sum(jnp.where(second, 0.0, value), axis=0, keepdims=True)
        tally[1:2, at : at + width] += jnp.sum(jnp.where(second, value, 0.0), axis=0, keepdims=True)

    def masks():
        for j in range(2):
            same = ids_col[:, j : j + 1] == ids_row[j : j + 1, :]
            disallowed[j] = jnp.where(same, 0.0, MASKED)
        tally[...] = jnp.zeros_like(tally)

    def standardize(j):
        def action(rows):
            if j == 0:
                stream[rows] = tokens[rows].astype(f32)
            value = stream[rows]
            center = value - jnp.mean(value, axis=-1, keepdims=True)
            inverse = lax.rsqrt(jnp.mean(center * center, axis=-1, keepdims=True) + EPSILON)
            xhat[j, rows] = (center * inverse).astype(bf16)
            deviation[rows, j : j + 1] = inverse

        by_rows(action)

    def modulate(j):
        def action(rows):
            normed[rows] = (
                xhat[j, rows].astype(f32) * (1.0 + mod_part(j, 1, rows)) + mod_part(j, 0, rows)
            ).astype(bf16)

        by_rows(action)

    def turn(i, source):
        for at in range(0, tok, 128):
            turned[i, 0, :, at : at + 128] = source[at : at + 128, :].T
        turned_copy(i).start()

    def weight(g, half, chunk):
        return held[g, half, :, chunk].reshape(width, 384)

    def project(j):
        @pl.loop(0, 6)
        def _(i):
            half, chunk = lax.div(i, 3), lax.rem(i, 3)
            columns = pl.ds(pl.multiple_of(i * 384, 128), 384)
            qkv[j, :, columns] = dot(normed[...], weight(j, half, chunk)).astype(bf16)

    def head_lanes():
        lane = lax.broadcasted_iota(jnp.int32, (1, 128), 1)
        return lane < 64, lane >= 64

    def head_columns(pair):
        return [pl.ds(pl.multiple_of(part * 768 + pair * 128, 128), 128) for part in range(3)]

    def attend(j, first, last):
        @pl.loop(first, last)
        def _(pair):
            at_q, at_k, at_v = head_columns(pair)
            queries, keys, values = qkv[j, :, at_q], qkv[j, :, at_k], qkv[j, :, at_v]
            results = []
            for head, lanes in enumerate(head_lanes()):
                scaled = jnp.where(lanes, queries, 0.0) * bf16(0.125)
                scores = contract_cols(scaled, keys) + disallowed[j]
                scores = jnp.exp(scores - jnp.max(scores, axis=-1, keepdims=True))
                low = (scores * (1.0 / jnp.sum(scores, axis=-1, keepdims=True))).astype(bf16)
                probs[j, 2 * pair + head] = low
                results.append(dot(low, values))
            attended[:, at_q] = jnp.where(head_lanes()[0], results[0], results[1]).astype(bf16)

    def join(j):
        @pl.loop(0, 2)
        def _(half):
            columns = pl.ds(pl.multiple_of(half * 384, 128), 384)
            branch[j, :, columns] = dot(attended[...], weight(j, half, 3)).astype(bf16)

    def add_branch(j):
        def action(rows):
            stream[rows] += mod_part(j, 2, rows) * branch[j, rows].astype(f32)

        by_rows(action)

    def expand(first, last):
        @pl.loop(first, last)
        def _(i):
            columns = pl.ds(pl.multiple_of(i * 384, 128), 384)
            matrix = weight(2, lax.div(i, 4), lax.rem(i, 4))
            for at in range(0, tok, 128):
                rows = slice(at, at + 128)
                pre = dot(normed[rows], matrix)
                square = pre * pre
                root = math.sqrt(2.0 / math.pi)
                bent = jnp.tanh(root * (pre + 0.044715 * (square * pre)))
                value = (0.5 * pre * (1.0 + bent)).astype(bf16)
                hidden[rows, columns] = value
                hidden_turned[0, columns, rows] = value.T
                slope[rows, columns] = (
                    0.5 * (1.0 + bent)
                    + 0.5 * pre * (1.0 - bent * bent) * (root * (1.0 + 3 * 0.044715 * square))
                ).astype(bf16)

    def gate(j):
        def action(rows):
            value = cotangent[rows].astype(f32) if j == 2 else grad[rows]
            if j == 2:
                grad[rows] = value
            else:
                count(j, 2, rows, value * branch[j, rows].astype(f32))
            gated[j, rows] = (mod_part(j, 2, rows) * value).astype(bf16)

        by_rows(action)
        gated_copy(j).start()

    def own_columns(first, width_of_half):
        return pl.ds(pl.multiple_of(core * width_of_half + first, 128), 384)

    def down_terms(first, last):
        scatter = scatters[0]
        for z in range(first, last):
            rows = slice(768 * z, 768 * z + 768)
            value = dot(hidden_turned[0, rows], gated[2, :, own_columns(0, 384)]) + dot(
                hidden_turned[1, rows], gated_twin[2]
            )
            value = value.astype(bf16).reshape(4, 4, 48, 384)
            for plane in range(4):
                sums[0, pl.ds(scatter.place(4 * z + plane), 4)] = value[plane]

    def column_terms(n, chunk, left, right, right_twin):
        value = dot(turned[left, 0], right) + dot(turned[left, 1], right_twin)
        value = value.astype(bf16).reshape(16, 48, 384)
        for chip in range(16):
            sums[n % 2, scatters[n].place(chip) + chunk] = value[chip]

    def up_terms(chunk):
        column_terms(
            1,
            chunk,
            4,
            slope[:, own_columns(384 * chunk, 1536)],
            grad_pre_twin[:, 384 * chunk : 384 * chunk + 384],
        )

    def out_terms(j):
        column_terms(3 - j, 3, 2 * j + 1, gated[j, :, own_columns(0, 384)], gated_twin[j])

    def qkv_terms(j, chunk):
        column_terms(
            3 - j,
            chunk,
            2 * j,
            grad_qkv[:, own_columns(384 * chunk, 1152)],
            grad_qkv_twin[j, :, 384 * chunk : 384 * chunk + 384],
        )

    def contract():
        @pl.loop(0, 2)
        def _(half):
            columns = pl.ds(pl.multiple_of(half * 384, 128), 384)
            matrix = held[3, half].reshape(3072, 384)
            normed[:, columns] = dot(hidden[...], matrix).astype(bf16)

    def close():
        def action(rows):
            value = normed[rows].astype(f32)
            o_layer[rows] = (stream[rows] + mod_part(2, 2, rows) * value).astype(bf16)
            count(2, 2, rows, cotangent[rows].astype(f32) * value)

        by_rows(action)

    def grad_hidden(first, last):
        @pl.loop(first, last)
        def _(i):
            columns = pl.ds(pl.multiple_of(i * 384, 128), 384)
            value = sum(
                contract_cols(
                    gated[2, :, 384 * half : 384 * half + 384],
                    held[3, half, pl.ds(2 * i, 2)].reshape(384, 384),
                )
                for half in range(2)
            )
            slope[:, columns] = (slope[:, columns].astype(f32) * value).astype(bf16)

    def back_project(g, chunks, source, first, last):
        @pl.loop(first, last)
        def _(i):
            columns = pl.ds(pl.multiple_of(i * 384, 128), 384)
            value = contract_cols(
                source[:, columns], weight(g, lax.div(i, chunks), lax.rem(i, chunks))
            )

            @pl.when(i == 0)
            def _():
                grad_normed[...] = value

            @pl.when(i > 0)
            def _():
                grad_normed[...] += value

    def norm_back(j):
        def action(rows):
            value, unit = grad_normed[rows], xhat[j, rows].astype(f32)
            count(j, 0, rows, value)
            count(j, 1, rows, value * unit)
            scaled = value * (1.0 + mod_part(j, 1, rows))
            inner = jnp.mean(scaled * unit, axis=-1, keepdims=True)
            scaled = scaled - jnp.mean(scaled, axis=-1, keepdims=True)
            total = grad[rows] + deviation[rows, j : j + 1] * (scaled - unit * inner)
            if j == 0:
                o_tokens[rows] = total
            else:
                grad[rows] = total

        by_rows(action)

    def split(j):
        value = sum(
            contract_cols(gated[j, :, 384 * half : 384 * half + 384], weight(j, half, 3))
            for half in range(2)
        )
        grad_attended[...] = value.astype(bf16)

    def attend_back(j, first, last):
        @pl.loop(first, last)
        def _(pair):
            at_q, at_k, at_v = head_columns(pair)
            queries, keys, values = qkv[j, :, at_q], qkv[j, :, at_k], qkv[j, :, at_v]
            given = grad_attended[:, at_q]
            grad_q, grad_k, grad_v = [], 0.0, 0.0
            for head, lanes in enumerate(head_lanes()):
                part = jnp.where(lanes, given, 0.0).astype(bf16)
                low = probs[j, 2 * pair + head]
                product = low.astype(f32) * contract_cols(part, values)
                total = jnp.sum(product, axis=-1, keepdims=True)
                scores = ((product - low.astype(f32) * total) * 0.125).astype(bf16)
                grad_v += contract_rows(low, part)
                grad_k += contract_rows(scores, jnp.where(lanes, queries, 0.0).astype(bf16))
                grad_q.append(dot(scores, keys))
            grad_qkv[:, at_q] = jnp.where(head_lanes()[0], grad_q[0], grad_q[1]).astype(bf16)
            grad_qkv[:, at_k] = grad_k.astype(bf16)
            grad_qkv[:, at_v] = grad_v.astype(bf16)

    plan = Plan()
    run = plan.run
    for g, gather in enumerate(gathers):
        gather.open(pieces[g])
        begin = 1.0 + 12 * UNIT * g
        plan.at(begin - (2 * UNIT if g else 0.5), gather.own)
        kinds = {"z": gather.along_z, "first": gather.along_first, "second": gather.along_second}
        for at, kind, k in GATHER_STEPS:
            plan.at(begin + at * UNIT, partial(kinds[kind], k))

    def landed(g):
        plan.until(2.0 + UNIT * (12 * g + 14.5))
        gathers[g].landed()

    steps_open()
    plan.at(2.0, steps_first)
    plan.at(4.0, steps_second)
    plan.at(6.0, steps_z)
    for k in (1, 2, 3):
        plan.at(6.0 + 2 * k, partial(step_line.step, k))
    plan.at(12.1, make_cond)
    plan.at(12.5, mod_twin)
    plan.at(14.5, mod_own)
    plan.at(15.5, lambda: mod_line.step(0))
    plan.at(16.5, lambda: mod_line.step(1))
    plan.at(20.0, lambda: mod_line.step(2))
    plan.at(25.0, mod_along_first)
    plan.at(28.5, mod_along_second)
    plan.at(32.0, mod_to_twin)

    run(1.0, masks)
    run(1.0, lambda: standardize(0))
    plan.until(34.0)
    mod_rows()
    landed(0)
    for j in range(2):
        if j:
            run(1.0, lambda: standardize(1))
            landed(1)
        run(1.0, lambda: modulate(j))
        run(2.0, lambda: project(j))
        run(0.5, lambda: turn(2 * j, normed))
        for pair in range(0, 6, 2):
            run(1.5, lambda: attend(j, pair, pair + 2))
        run(0.7, lambda: join(j))
        run(0.5, lambda: add_branch(j))
        run(0.5, lambda: turn(2 * j + 1, attended))
    run(1.0, lambda: standardize(2))
    run(1.0, lambda: modulate(2))
    run(0.5, lambda: turn(4, normed))
    run(1.0, lambda: gate(2))
    landed(2)
    for i in range(0, 8, 2):
        run(1.2, lambda: expand(i, i + 2))
    steps_drain()
    mod_drain()
    for gather in gathers:
        gather.swap().wait_send()
    run(0.0, lambda: hidden_copy().start())

    link = [0.0]

    def begin_scatter(n):
        scatters[n].start()
        begin = max(plan.clock, link[0])
        link[0] = begin + 12 * UNIT
        kinds = {"second": scatters[n].add_second, "first": scatters[n].add_first}
        for at, kind, k in SCATTER_STEPS:
            action = scatters[n].finish if kind == "finish" else partial(kinds[kind], k)
            plan.at(begin + at * UNIT, action)
        return begin + 13 * UNIT + 0.1

    plan.until(plan.clock + 2.0)
    gated_copy(2).wait_recv()
    hidden_copy().wait_recv()
    for z in range(4):
        run(0.7, lambda: down_terms(z, z + 1))
    ends = [begin_scatter(0)]
    landed(3)
    for i in range(0, 8, 2):
        run(0.6, lambda: grad_hidden(i, i + 2))
    run(0.0, lambda: grad_pre_copy().start())
    run(2.0, contract)
    run(1.0, close)
    plan.flush()
    grad_pre_copy().wait_recv()
    turned_copy(4).wait_recv()
    for chunk in range(4):
        run(0.7, lambda: up_terms(chunk))
    ends.append(begin_scatter(1))
    for i in range(0, 8, 2):
        run(0.7, lambda: back_project(2, 4, slope, i, i + 2))
    run(1.5, lambda: norm_back(2))

    def retire(n):
        scatters[n].drain()
        scatters[n].store(puts[n])
        scatters[n].swap().wait_send()
        if n < 2:
            scatters[n].release()

    for j in (1, 0):
        n = 3 - j
        run(1.0, lambda: gate(j))
        run(1.0, lambda: split(j))
        for pair in range(0, 6, 2):
            run(2.5, lambda: attend_back(j, pair, pair + 2))
        run(0.0, lambda: grad_qkv_copy(j).start())
        plan.until(ends[n - 2])
        retire(n - 2)
        turned_copy(2 * j + 1).wait_recv()
        gated_copy(j).wait_recv()
        run(0.7, lambda: out_terms(j))
        turned_copy(2 * j).wait_recv()
        grad_qkv_copy(j).wait_recv()
        for chunk in range(3):
            run(0.7, lambda: qkv_terms(j, chunk))
        ends.append(begin_scatter(n))
        for i in range(0, 6, 2):
            run(0.7, lambda: back_project(j, 3, grad_qkv, i, i + 2))
        run(1.5, lambda: norm_back(j))
        grad_qkv_copy(j).wait_send()
    now = plan.clock
    plan.at(now, rows_open)
    plan.at(now + 2.0, rows_first)
    plan.at(now + 5.0, rows_second)
    plan.at(now + 8.0, rows_z)
    plan.at(now + 11.0, lambda: row_line.step(1))
    plan.at(now + 14.0, lambda: row_line.step(2))
    plan.at(now + 17.0, lambda: row_line.step(3))
    plan.at(now + 17.1, rows_twin)
    plan.at(now + 17.2, lambda: ada_half(core))
    plan.at(now + 18.5, rows_last)
    plan.at(ends[2], lambda: retire(2))
    plan.until(1e6)
    retire(3)
    rows_drain()
    for gather in gathers:
        gather.drain()
    for i in range(5):
        turned_copy(i).wait_send()
    hidden_copy().wait_send()
    for j in range(3):
        gated_copy(j).wait_send()
    grad_pre_copy().wait_send()


def layer(tokens, cotangent, ids_row, ids_col, steps, bias, w_ada, *shards):
    f32, bf16 = jnp.float32, jnp.bfloat16
    tok, width = tokens.shape
    block = (4, 48, 384)
    dma, vmem = pltpu.SemaphoreType.DMA, pltpu.VMEM
    return pl.pallas_call(
        layer_kernel,
        out_shape=[
            jax.ShapeDtypeStruct((tok, width), bf16),
            jax.ShapeDtypeStruct((tok, width), f32),
            jax.ShapeDtypeStruct(w_ada.shape, f32),
            jax.ShapeDtypeStruct((1, w_ada.shape[1]), f32),
        ]
        + [jax.ShapeDtypeStruct(shard.shape, f32) for shard in shards],
        in_specs=[pl.BlockSpec(memory_space=vmem)] * 13,
        out_specs=[pl.BlockSpec(memory_space=vmem)] * 10,
        scratch_shapes=[
            vmem((4, 2, 16) + block, bf16),
            vmem((4,) + block, f32),
            vmem((3, 4, 24, 384), f32),
            vmem((2, 48, 384), f32),
            vmem((2, 64, 48, 384), bf16),
            vmem((2, 4, 8, 48, 384), bf16),
            vmem((2, 4) + block, bf16),
            vmem((2, 5) + block, bf16),
            vmem((4, 4, 2, 8, 128), f32),
            vmem((64, 128), bf16),
            vmem((2, 16, 3456), f32),
            vmem((8, 6912), f32),
            vmem((8, 6912), f32),
            vmem((6, 16, 3456), bf16),
            vmem((2, 4, 16, 3456), bf16),
            vmem((3, tok, width), bf16),
            vmem((tok, 128), f32),
            vmem((tok, width), bf16),
            vmem((tok, width), bf16),
            vmem((5, 2, width, tok), bf16),
            vmem((2, 4 * width, tok), bf16),
            vmem((2, tok, 3 * width), bf16),
            vmem((2, HEADS, tok, tok), bf16),
            vmem((2, tok, width), bf16),
            vmem((tok, width), f32),
            vmem((tok, width), f32),
            vmem((tok, 4 * width), bf16),
            vmem((tok, 4 * width), bf16),
            vmem((tok, 2 * width), bf16),
            vmem((3, tok, width), bf16),
            vmem((3, tok, width // 2), bf16),
            vmem((tok, width), bf16),
            vmem((2, tok, 3 * width // 2), bf16),
            vmem((2, tok, tok), f32),
            dma((4, 2)),
            dma((4, 21)),
            dma((4, 20)),
            dma((4, 12)),
            dma((4, 14)),
            pltpu.SemaphoreType.REGULAR((2, 4)),
            dma((12,)),
            dma((12,)),
            dma((9,)),
            dma((8,)),
            dma((7,)),
            dma((9,)),
            dma((9,)),
            dma((8,)),
        ],
        compiler_params=pltpu.CompilerParams(
            collective_id=0, has_side_effects=True, vmem_limit_bytes=64 * 2**20
        ),
    )(tokens, cotangent, ids_row, ids_col, steps, bias, w_ada, *shards)


def on_grid(
    tokens,
    seg_ids,
    frame_ids,
    patch_ids,
    timesteps,
    w_ada,
    b_ada,
    w_qkv_spatial,
    w_out_spatial,
    w_qkv_temporal,
    w_out_temporal,
    w_up,
    w_down,
    cotangent,
):
    place = lax.axis_index(("wide", "narrow"))
    share = b_ada.shape[0]
    ids = jnp.stack([seg_ids * 16 + frame_ids, seg_ids * 16 + patch_ids, seg_ids])
    steps = jnp.broadcast_to(
        jnp.pad(timesteps.astype(jnp.float32), (0, 6))[:, None], (8, 128)
    )
    bias = lax.dynamic_update_slice(
        jnp.zeros((1, w_ada.shape[1]), jnp.float32),
        b_ada.astype(jnp.float32)[None],
        (0, place * share),
    )
    shards = (w_qkv_spatial, w_out_spatial, w_qkv_temporal, w_out_temporal, w_up, w_down)
    outs = layer(tokens, cotangent, ids, ids.T, steps, bias, w_ada, *shards)
    bias_share = lax.dynamic_slice(outs[3][0], (place * share,), (share,))
    return (*outs[:3], bias_share, *outs[4:])


def on_device(
    tokens,
    seg_ids,
    frame_ids,
    patch_ids,
    timesteps,
    w_ada,
    b_ada,
    w_qkv_spatial,
    w_out_spatial,
    w_qkv_temporal,
    w_out_temporal,
    w_up,
    w_down,
    cotangent,
):
    axes = ("wide", "narrow")
    gathered = (
        None,
        None,
        lax.all_gather(w_qkv_spatial, axes, axis=0, tiled=True),
        lax.all_gather(w_out_spatial, axes, axis=0, tiled=True),
        lax.all_gather(w_qkv_temporal, axes, axis=0, tiled=True),
        lax.all_gather(w_out_temporal, axes, axis=0, tiled=True),
        lax.all_gather(w_up, axes, axis=0, tiled=True),
        lax.all_gather(w_down, axes, axis=0, tiled=True),
    )
    width = tokens.shape[1]
    head_count = HEADS
    clip_count = timesteps.shape[0]
    row_count = w_ada.shape[0]
    place = lax.axis_index(axes)
    all_steps = lax.all_gather(timesteps, axes, axis=0, tiled=True)
    cond_all = jax.nn.silu(time_embed(all_steps, width)).astype(jnp.bfloat16)
    cond_rows = lax.dynamic_slice_in_dim(cond_all, place * row_count, row_count, axis=1)
    all_bias = lax.all_gather(b_ada, axes, axis=0, tiled=True)
    modulation = lax.psum_scatter(
        jnp.dot(cond_rows, w_ada, preferred_element_type=jnp.float32),
        axes,
        scatter_dimension=0,
        tiled=True,
    ) + all_bias.astype(jnp.float32)
    one_hot = (seg_ids[:, None] == jnp.arange(clip_count, dtype=jnp.int32)[None, :]).astype(
        jnp.float32
    )
    offset_first, scale_first, gate_a = sublayer_mod(one_hot, modulation, 0, width)
    offset_second, scale_second, gate_b = sublayer_mod(one_hot, modulation, 1, width)
    offset_third, scale_third, gate_c = sublayer_mod(one_hot, modulation, 2, width)
    same_clip = seg_ids[:, None] == seg_ids[None, :]
    spatial_mask = same_clip & (frame_ids[:, None] == frame_ids[None, :])
    temporal_mask = same_clip & (patch_ids[:, None] == patch_ids[None, :])
    residual_first = tokens.astype(jnp.float32)
    standardized_first, inverse_deviation_first = layer_norm_apply(residual_first)
    normalized_first = (standardized_first * (1.0 + scale_first) + offset_first).astype(
        jnp.bfloat16
    )
    branch_a, qkv_a, merged_a = attention_forward(
        normalized_first, gathered[2], gathered[3], spatial_mask, head_count
    )
    residual_second = residual_first + gate_a * branch_a
    standardized_second, inverse_deviation_second = layer_norm_apply(residual_second)
    normalized_second = (standardized_second * (1.0 + scale_second) + offset_second).astype(
        jnp.bfloat16
    )
    branch_b, qkv_b, merged_b = attention_forward(
        normalized_second, gathered[4], gathered[5], temporal_mask, head_count
    )
    residual_third = residual_second + gate_b * branch_b
    standardized_third, inverse_deviation_third = layer_norm_apply(residual_third)
    normalized_third = (standardized_third * (1.0 + scale_third) + offset_third).astype(
        jnp.bfloat16
    )
    pre_act = jnp.dot(normalized_third, gathered[6], preferred_element_type=jnp.float32)
    act_out, gelu_pull = jax.vjp(jax.nn.gelu, pre_act)
    hidden = act_out.astype(jnp.bfloat16)
    branch_c = jnp.dot(hidden, gathered[7], preferred_element_type=jnp.float32)
    result = residual_third + gate_c * branch_c
    back_weights = gathered
    output_gradient = cotangent.astype(jnp.float32)
    gate_gradient_third = output_gradient * branch_c
    grad_branch_c = (gate_c * output_gradient).astype(jnp.bfloat16)
    grad_hidden = contract_cols(grad_branch_c, back_weights[7])
    grad_pre = gelu_pull(grad_hidden)[0].astype(jnp.bfloat16)
    normalized_gradient_third = contract_cols(grad_pre, back_weights[6])
    residual_gradient = output_gradient + layer_norm_reverse(
        normalized_gradient_third, standardized_third, inverse_deviation_third, scale_third
    )
    gate_gradient_second = residual_gradient * branch_b
    grad_branch_b = (gate_b * residual_gradient).astype(jnp.bfloat16)
    normalized_gradient_second, grad_qkv_t = attention_backward(
        grad_branch_b, qkv_b, back_weights[4], back_weights[5], temporal_mask, head_count
    )
    residual_gradient = residual_gradient + layer_norm_reverse(
        normalized_gradient_second, standardized_second, inverse_deviation_second, scale_second
    )
    gate_gradient_first = residual_gradient * branch_a
    grad_branch_a = (gate_a * residual_gradient).astype(jnp.bfloat16)
    normalized_gradient_first, grad_qkv_s = attention_backward(
        grad_branch_a, qkv_a, back_weights[2], back_weights[3], spatial_mask, head_count
    )
    residual_gradient = residual_gradient + layer_norm_reverse(
        normalized_gradient_first, standardized_first, inverse_deviation_first, scale_first
    )
    grad_mod = jnp.concatenate(
        [
            exact_rows(
                one_hot,
                jnp.concatenate(
                    [
                        normalized_gradient_first,
                        normalized_gradient_first * standardized_first,
                        gate_gradient_first,
                    ],
                    axis=1,
                ),
            ),
            exact_rows(
                one_hot,
                jnp.concatenate(
                    [
                        normalized_gradient_second,
                        normalized_gradient_second * standardized_second,
                        gate_gradient_second,
                    ],
                    axis=1,
                ),
            ),
            exact_rows(
                one_hot,
                jnp.concatenate(
                    [
                        normalized_gradient_third,
                        normalized_gradient_third * standardized_third,
                        gate_gradient_third,
                    ],
                    axis=1,
                ),
            ),
        ],
        axis=1,
    )
    grad_mod_low = grad_mod.astype(jnp.bfloat16)
    all_grad_mod = lax.all_gather(grad_mod_low, axes, axis=0, tiled=True)
    bias_share = lax.psum_scatter(
        jnp.sum(grad_mod, axis=0), axes, scatter_dimension=0, tiled=True
    )

    def share(left, right):
        return lax.psum_scatter(
            contract_rows(left, right).astype(jnp.bfloat16),
            axes,
            scatter_dimension=0,
            tiled=True,
        ).astype(jnp.float32)

    return (
        result.astype(jnp.bfloat16),
        residual_gradient,
        contract_rows(cond_rows, all_grad_mod),
        bias_share,
        share(normalized_first, grad_qkv_s),
        share(merged_a, grad_branch_a),
        share(normalized_second, grad_qkv_t),
        share(merged_b, grad_branch_b),
        share(normalized_third, grad_pre),
        share(hidden, grad_branch_c),
    )


def solution(mesh):
    placed = (
        P(("wide", "narrow"), None),
        P(("wide", "narrow")),
        P(("wide", "narrow")),
        P(("wide", "narrow")),
        P(("wide", "narrow")),
        P(("wide", "narrow"), None),
        P(("wide", "narrow")),
        P(("wide", "narrow"), None),
        P(("wide", "narrow"), None),
        P(("wide", "narrow"), None),
        P(("wide", "narrow"), None),
        P(("wide", "narrow"), None),
        P(("wide", "narrow"), None),
        P(("wide", "narrow"), None),
    )
    grid = dict(mesh.shape) == {"wide": 16, "narrow": 2}
    return jax.shard_map(
        on_grid if grid else on_device,
        mesh=mesh,
        in_specs=placed,
        out_specs=(
            P(("wide", "narrow"), None),
            P(("wide", "narrow"), None),
            P(("wide", "narrow"), None),
            P(("wide", "narrow")),
            P(("wide", "narrow"), None),
            P(("wide", "narrow"), None),
            P(("wide", "narrow"), None),
            P(("wide", "narrow"), None),
            P(("wide", "narrow"), None),
            P(("wide", "narrow"), None),
        ),
        check_vma=False,
    )
```

```python
from functools import partial
import math

import jax
import jax.numpy as jnp
from jax import lax
from jax.experimental import pallas as pl
from jax.experimental.pallas import tpu as pltpu
from jax.sharding import PartitionSpec as P

HEADS = 12


EPSILON = 1e-06
FREQ_BASE = 10000.0
MASKED = -1e30


def time_embed(step_ids, width):
    half_width = width // 2
    frequency = jnp.exp(
        -math.log(FREQ_BASE) * jnp.arange(half_width, dtype=jnp.float32) / half_width
    )
    angles = step_ids.astype(jnp.float32)[:, None] * frequency[None, :]
    return jnp.concatenate([jnp.cos(angles), jnp.sin(angles)], axis=1)


def contract_rows(left, right):
    return lax.dot_general(
        left, right, (((0,), (0,)), ((), ())), preferred_element_type=jnp.float32
    )


def contract_cols(left, right):
    return lax.dot_general(
        left, right, (((1,), (1,)), ((), ())), preferred_element_type=jnp.float32
    )


def exact_rows(left, right):
    return lax.dot_general(
        left,
        right,
        (((0,), (0,)), ((), ())),
        precision=lax.Precision.HIGHEST,
        preferred_element_type=jnp.float32,
    )


def layer_norm_apply(stream):
    center = stream - jnp.mean(stream, axis=-1, keepdims=True)
    inverse_deviation = lax.rsqrt(jnp.mean(center * center, axis=-1, keepdims=True) + EPSILON)
    return (center * inverse_deviation, inverse_deviation)


def layer_norm_reverse(normalized_gradient, standardized_input, inverse_deviation, row_scales):
    input_gradient = normalized_gradient * (1.0 + row_scales)
    mean_removed = input_gradient - jnp.mean(input_gradient, axis=-1, keepdims=True)
    return inverse_deviation * (
        mean_removed
        - standardized_input * jnp.mean(input_gradient * standardized_input, axis=-1, keepdims=True)
    )


def sublayer_mod(one_hot, modulation, sublayer, width):
    table = modulation[:, 3 * width * sublayer : 3 * width * (sublayer + 1)]
    rows_mod = jnp.dot(
        one_hot, table, precision=lax.Precision.HIGHEST, preferred_element_type=jnp.float32
    )
    return (rows_mod[:, :width], rows_mod[:, width : 2 * width], rows_mod[:, 2 * width :])


def head_probs(allowed, scale, queries, key_vecs):
    scores = contract_cols(queries, key_vecs) * scale
    scores = jnp.where(allowed, scores, MASKED)
    return jax.nn.softmax(scores, axis=-1)


def head_forward(allowed, scale, item):
    queries, key_vecs, val_vecs = item
    attn_prob = head_probs(allowed, scale, queries, key_vecs)
    return jnp.dot(attn_prob.astype(jnp.bfloat16), val_vecs, preferred_element_type=jnp.float32)


def head_backward(allowed, scale, item):
    queries, key_vecs, val_vecs, grad_att = item
    attn_prob = head_probs(allowed, scale, queries, key_vecs)
    grad_val = contract_rows(attn_prob.astype(jnp.bfloat16), grad_att)
    grad_prob = contract_cols(grad_att, val_vecs)
    grad_score = attn_prob * (grad_prob - jnp.sum(attn_prob * grad_prob, axis=-1, keepdims=True))
    score_low = grad_score.astype(jnp.bfloat16)
    grad_query = jnp.dot(score_low, key_vecs, preferred_element_type=jnp.float32) * scale
    grad_key = contract_rows(score_low, queries) * scale
    return (grad_query, grad_key, grad_val)


def split_heads(qkv_rows, head_count):
    row_count = qkv_rows.shape[0]
    return qkv_rows.reshape(row_count, 3, head_count, -1).transpose(1, 2, 0, 3)


def attention_forward(normed, w_qkv, w_out, allowed, head_count):
    row_count = normed.shape[0]
    qkv_rows = jnp.dot(normed, w_qkv, preferred_element_type=jnp.float32).astype(jnp.bfloat16)
    split_qkv = split_heads(qkv_rows, head_count)
    scale = split_qkv.shape[-1] ** (-0.5)
    attended = lax.map(
        partial(head_forward, allowed, scale), (split_qkv[0], split_qkv[1], split_qkv[2])
    )
    merged = attended.transpose(1, 0, 2).reshape(row_count, -1).astype(jnp.bfloat16)
    branch = jnp.dot(merged, w_out, preferred_element_type=jnp.float32)
    return (branch, qkv_rows, merged)


def attention_backward(grad_branch, qkv_rows, w_qkv, w_out, allowed, head_count):
    row_count = qkv_rows.shape[0]
    grad_merged = contract_cols(grad_branch, w_out).astype(jnp.bfloat16)
    grad_heads = grad_merged.reshape(row_count, head_count, -1).transpose(1, 0, 2)
    split_qkv = split_heads(qkv_rows, head_count)
    scale = split_qkv.shape[-1] ** (-0.5)
    grad_query, grad_key, grad_val = lax.map(
        partial(head_backward, allowed, scale),
        (split_qkv[0], split_qkv[1], split_qkv[2], grad_heads),
    )
    grad_qkv = (
        jnp.stack([grad_query, grad_key, grad_val])
        .transpose(2, 0, 1, 3)
        .reshape(row_count, -1)
        .astype(jnp.bfloat16)
    )
    normalized_gradient = contract_cols(grad_qkv, w_qkv)
    return (normalized_gradient, grad_qkv)


MESH = pl.DeviceIdType.MESH


class Spot:
    def __init__(self):
        chip = lax.axis_index("wide")
        core = lax.axis_index("narrow")
        z, y, x = lax.div(chip, 4), lax.rem(lax.div(chip, 2), 2), lax.rem(chip, 2)
        half = lax.div(z, 2)
        toward = 1 - 2 * half
        self.chip, self.core, self.z, self.y, self.x = chip, core, z, y, x
        self.half = half
        self.middle = z + half * (3 - 2 * z)
        self.is_middle = self.middle == 1
        self.is_end = self.middle == 0
        self.plane = 2 * y + x
        self.inner = ((z + toward) * 4 + self.plane, core)
        self.outer = ((z - toward) * 4 + self.plane, core)
        self.first_plane = 2 * lax.rem(y + core, 2) + lax.rem(x + 1 - core, 2)
        self.second_plane = 2 * lax.rem(y + 1 - core, 2) + lax.rem(x + core, 2)
        self.far_plane = 3 - self.plane
        self.first = (z * 4 + self.first_plane, core)
        self.second = (z * 4 + self.second_plane, core)
        self.twin = (chip, 1 - core)

    def layer(self, mirrored):
        return mirrored + self.half * (3 - 2 * mirrored)

    def arrival(self, k):
        return (self.z, self.layer(1 - self.middle), self.layer(2), self.layer(3))[k]


def greet(spot):
    barrier = pltpu.get_barrier_semaphore()
    for device in (spot.twin, spot.inner, spot.first, spot.second):
        pl.semaphore_signal(barrier, inc=1, device_id=device, device_id_type=MESH)

    @pl.when(spot.is_middle)
    def _():
        pl.semaphore_signal(barrier, inc=1, device_id=spot.outer, device_id_type=MESH)
        pl.semaphore_wait(barrier, 5)

    @pl.when(spot.is_end)
    def _():
        pl.semaphore_wait(barrier, 4)


def remote(src, dst, send, recv, device):
    return pltpu.make_async_remote_copy(
        src_ref=src,
        dst_ref=dst,
        send_sem=send,
        recv_sem=recv,
        device_id=device,
        device_id_type=MESH,
    )


class LineSum:
    def __init__(self, spot, part, slot, send, recv):
        self.spot, self.part, self.slot = spot, part, slot
        self.send, self.recv = send, recv

    def layer(self, k):
        spot = self.spot
        return (spot.layer(3), spot.layer(2), spot.layer(1 - spot.middle), spot.z)[k]

    def copy(self, k, slot, device):
        return remote(
            self.part(self.layer(k)), self.slot(slot), self.send.at[k], self.recv.at[slot], device
        )

    def from_end(self, k):
        return self.copy(k, k, self.spot.inner)

    def from_middle(self, k):
        return self.copy(k, 3 + k, self.spot.inner) if k < 2 else self.copy(2, 3, self.spot.outer)

    def arrived(self, slot):
        self.copy(0, slot, self.spot.inner).wait_recv()
        return self.slot(slot)

    def send_end(self, k):
        pl.when(self.spot.is_end)(lambda: self.from_end(k).start())

    def send_middle(self, k):
        @pl.when(self.spot.is_middle)
        def _():
            source, part = self.arrived((0, 1, 3)[k]), self.part(self.layer(k))
            for i in range(part.shape[0]):
                part[i] += source[i]
            self.from_middle(k).start()

    def total(self, put):
        def add(*slots):
            sources = [self.arrived(slot) for slot in slots]
            part = self.part(self.spot.z)
            for i in range(part.shape[0]):
                value = part[i].astype(jnp.float32)
                for source in sources:
                    value += source[i].astype(jnp.float32)
                put(i, value)

        pl.when(self.spot.is_end)(lambda: add(3))
        pl.when(self.spot.is_middle)(lambda: add(2, 4))

    def drain(self):
        for k in range(3):
            self.from_end(k).wait_send()


class LineGather:
    def __init__(self, spot, part, send, recv):
        self.spot, self.part = spot, part
        self.send, self.recv = send, recv

    def copy(self, z, send, device):
        ref = self.part(z)
        return remote(ref, ref, self.send.at[send], self.recv.at[z], device)

    def own(self, inward):
        spot = self.spot
        return self.copy(spot.z, 0 if inward else 1, spot.inner if inward else spot.outer)

    def onward(self, k):
        spot = self.spot
        return self.copy(spot.arrival(k), 1 + k, spot.inner if k == 1 else spot.outer)

    def open(self):
        self.own(True).start()
        pl.when(self.spot.is_middle)(lambda: self.own(False).start())

    def get(self, k):
        self.copy(self.spot.arrival(k), 0, self.spot.inner).wait_recv()

    def pass_on(self, k):
        @pl.when(self.spot.is_middle)
        def _():
            self.get(k)
            self.onward(k).start()

    def take(self, k):
        pl.when(self.spot.is_end)(lambda: self.get(k))

    def drain(self):
        self.own(True).wait_send()

        @pl.when(self.spot.is_middle)
        def _():
            self.own(False).wait_send()
            for k in (1, 2, 3):
                self.onward(k).wait_send()


class Gather:
    def __init__(self, spot, held, stage, apart, swap_sems, send, recv):
        self.spot, self.held = spot, held
        self.stage, self.apart, self.swap_sems = stage, apart, swap_sems
        self.send, self.recv = send, recv
        self.whole = apart.shape[1] == 48
        self.line = LineGather(
            spot,
            lambda z: held.at[spot.core, pl.ds(4 * z, 4), 3],
            send.at[pl.ds(24, 5)],
            recv.at[pl.ds(23, 4)],
        )

    def block(self, z, plane):
        return self.held.at[self.spot.core, z * 4 + plane, 0:3]

    def last(self, plane):
        return self.held.at[self.spot.core, self.spot.z * 4 + plane, 3]

    def copy(self, ref, send, recv, device):
        return remote(ref, ref, self.send.at[send], self.recv.at[recv], device)

    def mine(self):
        core = self.spot.core
        if self.whole:
            return self.stage.at[pl.ds(2 * core, 2)]
        return self.stage.at[:, pl.ds(pl.multiple_of(core * 24, 8), 24), :]

    def swap(self):
        return remote(
            self.apart, self.mine(), self.swap_sems.at[0], self.swap_sems.at[1], self.spot.twin
        )

    def open(self, piece):
        core = self.spot.core
        for chunk in range(self.apart.shape[0]):
            self.apart[chunk] = piece(1 - core, chunk).astype(jnp.float32)
        self.swap().start()
        place = self.mine()
        for chunk in range(self.apart.shape[0]):
            place[chunk] = piece(core, chunk).astype(jnp.float32)

    def own(self):
        spot = self.spot
        self.swap().wait_recv()
        self.held[spot.core, spot.chip] = self.stage[...].astype(jnp.bfloat16)
        self.z_own(True).start()
        pl.when(spot.is_middle)(lambda: self.z_own(False).start())
        self.last_first().start()
        self.last_second(False).start()

    def z_own(self, inward):
        spot = self.spot
        return self.copy(
            self.block(spot.z, spot.plane),
            0 if inward else 1,
            spot.z,
            spot.inner if inward else spot.outer,
        )

    def z_pass(self, k):
        spot = self.spot
        z = spot.arrival(k)
        return self.copy(
            self.block(z, spot.plane), 1 + k, z, spot.inner if k == 1 else spot.outer
        )

    def first_copy(self, k):
        z = self.spot.arrival(k)
        return self.copy(self.block(z, self.spot.plane), 5 + k, 4 + z, self.spot.first)

    def second_copy(self, k):
        z = self.spot.arrival(k)
        return self.copy(self.block(z, self.spot.plane), 9 + k, 8 + z, self.spot.second)

    def second_pass(self, k):
        z = self.spot.arrival(k)
        return self.copy(self.block(z, self.spot.first_plane), 13 + k, 12 + z, self.spot.second)

    def twin_copy(self, half, k):
        z = self.spot.arrival(k)
        ref = self.held.at[half, pl.ds(z * 4, 4), 0:3]
        return self.copy(ref, 17 + k, 16 + z, self.spot.twin)

    def last_first(self):
        return self.copy(self.last(self.spot.plane), 21, 20, self.spot.first)

    def last_second(self, onward):
        spot = self.spot
        plane = spot.first_plane if onward else spot.plane
        return self.copy(self.last(plane), 23 if onward else 22, 22 if onward else 21, spot.second)

    def last_twin(self, half, k):
        z = self.spot.arrival(k)
        ref = self.held.at[half, pl.ds(z * 4, 4), 3]
        return self.copy(ref, 29 + k, 27 + z, self.spot.twin)

    def get(self, k):
        spot = self.spot
        z = spot.arrival(k)
        self.copy(self.block(z, spot.plane), 0, z, spot.inner).wait_recv()

    def pass_on(self, k):
        @pl.when(self.spot.is_middle)
        def _():
            self.get(k)
            self.z_pass(k).start()

    def spread(self, k):
        if k:
            pl.when(self.spot.is_end)(lambda: self.get(k))
        self.first_copy(k).start()
        self.second_copy(k).start()

    def along_first(self, k):
        spot = self.spot
        z = spot.arrival(k)
        self.copy(self.block(z, spot.first_plane), 0, 4 + z, spot.first).wait_recv()
        self.second_pass(k).start()

    def along_second(self, k):
        spot = self.spot
        z = spot.arrival(k)
        self.copy(self.block(z, spot.second_plane), 0, 8 + z, spot.second).wait_recv()
        self.copy(self.block(z, spot.far_plane), 0, 12 + z, spot.second).wait_recv()
        self.twin_copy(spot.core, k).start()

    def last_along_first(self):
        spot = self.spot
        self.copy(self.last(spot.first_plane), 0, 20, spot.first).wait_recv()
        self.last_second(True).start()

    def last_along_second(self):
        spot = self.spot
        self.copy(self.last(spot.second_plane), 0, 21, spot.second).wait_recv()
        self.copy(self.last(spot.far_plane), 0, 22, spot.second).wait_recv()
        self.line.open()
        self.last_twin(spot.core, 0).start()

    def last_along_z(self, k):
        self.line.take(k)
        self.last_twin(self.spot.core, k).start()

    def landed(self):
        for k in range(4):
            self.twin_copy(1 - self.spot.core, k).wait_recv()
            self.last_twin(1 - self.spot.core, k).wait_recv()

    def drain(self):
        spot = self.spot
        self.z_own(True).wait_send()

        @pl.when(spot.is_middle)
        def _():
            self.z_own(False).wait_send()
            for k in (1, 2, 3):
                self.z_pass(k).wait_send()

        for k in range(4):
            self.first_copy(k).wait_send()
            self.second_copy(k).wait_send()
            self.second_pass(k).wait_send()
            self.twin_copy(spot.core, k).wait_send()
            self.last_twin(spot.core, k).wait_send()
        self.last_first().wait_send()
        self.last_second(False).wait_send()
        self.last_second(True).wait_send()
        self.line.drain()


class Scatter:
    def __init__(
        self, spot, sums, from_second, from_first, from_z, last_pair, last_one, last_z, final,
        theirs, send, recv, credit, owed,
    ):
        self.spot, self.sums = spot, sums
        self.from_second, self.from_first = from_second, from_first
        self.last_pair, self.last_one = last_pair, last_one
        self.final, self.theirs = final, theirs
        self.send, self.recv, self.credit = send, recv, credit
        self.owed, self.whole = owed, theirs.shape[1] == 48
        self.line = LineSum(
            spot,
            lambda z: sums.at[pl.ds(12 * z, 3)],
            lambda i: from_z.at[i],
            send.at[pl.ds(8, 3)],
            recv.at[pl.ds(8, 5)],
        )
        self.last_line = LineSum(
            spot,
            lambda z: sums.at[pl.ds(48 + 4 * z, 4)],
            lambda i: last_z.at[i],
            send.at[pl.ds(12, 3)],
            recv.at[pl.ds(14, 5)],
        )

    def place(self, chip, chunk):
        spot = self.spot
        z, y, x = chip // 4, (chip // 2) % 2, chip % 2
        other_y, other_x = lax.rem(spot.y + y, 2), lax.rem(spot.x + x, 2)
        second = other_y * (1 - spot.core) + other_x * spot.core
        first = other_x * (1 - spot.core) + other_y * spot.core
        block = 4 * z + 2 * second + first
        return 48 + block if chunk == 3 else 3 * block + chunk

    def second_copy(self, k):
        z = self.line.layer(k)
        return remote(
            self.sums.at[pl.ds(12 * z + 6, 6)],
            self.from_second.at[z],
            self.send.at[k],
            self.recv.at[z],
            self.spot.second,
        )

    def first_copy(self, k):
        z = self.line.layer(k)
        return remote(
            self.sums.at[pl.ds(12 * z + 3, 3)],
            self.from_first.at[z],
            self.send.at[4 + k],
            self.recv.at[4 + z],
            self.spot.first,
        )

    def last_second_copy(self):
        return remote(
            self.sums.at[pl.ds(48 + 4 * self.spot.z + 2, 2)],
            self.last_pair,
            self.send.at[15],
            self.recv.at[19],
            self.spot.second,
        )

    def last_first_copy(self):
        return remote(
            self.sums.at[48 + 4 * self.spot.z + 1],
            self.last_one,
            self.send.at[16],
            self.recv.at[20],
            self.spot.first,
        )

    def swap(self):
        core = self.spot.core
        if self.whole:
            src = self.final.at[pl.ds(2 * (1 - core), 2)]
        else:
            src = self.final.at[:, pl.ds(pl.multiple_of((1 - core) * 24, 8), 24), :]
        return remote(src, self.theirs, self.send.at[11], self.recv.at[13], self.spot.twin)

    def wait_credit(self):
        spot = self.spot
        if self.owed:
            for kind in range(3):
                pl.semaphore_wait(self.credit.at[kind], 1)
            pl.when(spot.is_middle)(lambda: pl.semaphore_wait(self.credit.at[3], 1))

    def add_second(self, k):
        z = self.line.layer(k)
        self.second_copy(k).wait_recv()
        for i in (3, 4, 5, 0, 1, 2):
            self.sums[12 * z + i] += self.from_second[z, i]
            if i == 5:
                self.first_copy(k).start()

    def add_first(self, k):
        z = self.line.layer(k)
        self.first_copy(k).wait_recv()
        for i in range(3):
            self.sums[12 * z + i] += self.from_first[z, i]
        if k < 3:
            self.line.send_end(k)

    def finish(self):
        def put(i, value):
            self.final[i] = value

        self.line.total(put)

    def last_total(self):
        at = 48 + 4 * self.spot.z

        def put(i, value):
            self.sums[at + i] = value.astype(jnp.bfloat16)

        self.last_line.total(put)
        self.last_second_copy().start()

    def last_add_second(self):
        at = 48 + 4 * self.spot.z
        self.last_second_copy().wait_recv()
        self.sums[at + 1] += self.last_pair[1]
        self.last_first_copy().start()
        self.sums[at] += self.last_pair[0]

    def last_finish(self):
        self.last_first_copy().wait_recv()
        self.final[3] = self.sums[48 + 4 * self.spot.z].astype(jnp.float32) + self.last_one[
            ...
        ].astype(jnp.float32)

    def store(self, put):
        core = self.spot.core
        for chunk in range(self.theirs.shape[0]):
            if self.whole:
                mine = self.final[2 * core + chunk]
            else:
                mine = self.final[chunk, pl.ds(pl.multiple_of(core * 24, 8), 24), :]
            put(core, chunk, mine)
        self.swap().wait_recv()
        for chunk in range(self.theirs.shape[0]):
            put(1 - core, chunk, self.theirs[chunk])
        self.swap().wait_send()

    def drain(self):
        for k in range(4):
            self.second_copy(k).wait_send()
            self.first_copy(k).wait_send()
        self.line.drain()
        self.last_line.drain()
        self.last_second_copy().wait_send()
        self.last_first_copy().wait_send()

    def release(self):
        spot, credit = self.spot, self.credit

        def tell(kind, device):
            pl.semaphore_signal(credit.at[kind], inc=1, device_id=device, device_id_type=MESH)

        tell(0, spot.second)
        tell(1, spot.first)

        @pl.when(spot.is_end)
        def _():
            tell(3, spot.inner)

        @pl.when(spot.is_middle)
        def _():
            tell(2, spot.inner)
            tell(2, spot.outer)


ORDER = (
    ("masks",), ("standardize", 0), ("steps", 0), ("own", 0), ("gs", 0, 0), ("steps", 1), ("own", 1), ("lx", 0),
    ("gs", 1, 0), ("gz", 0, 1), ("gz", 0, 2), ("steps", 2), ("gx", 0, 0), ("lx", 1), ("ly", 0), ("gz", 1, 1),
    ("gz", 1, 2), ("gs", 0, 1), ("stepp", 1), ("gz", 0, 3), ("gx", 1, 0), ("stepp", 2), ("stepz", 1), ("gy", 0, 0),
    ("gs", 0, 2), ("lp", 0, 1), ("lp", 0, 2), ("gx", 0, 1), ("lz", 0, 1), ("gy", 1, 0), ("gs", 1, 1), ("gz", 1, 3),
    ("stepp", 3), ("gx", 0, 2), ("gy", 0, 1), ("gs", 1, 2), ("stepz", 2), ("lp", 0, 3), ("gx", 1, 1), ("gy", 0, 2),
    ("gs", 0, 3), ("lz", 0, 2), ("ly", 1), ("gx", 1, 2), ("gy", 1, 1), ("stepz", 3), ("cond",), ("modpart", 0),
    ("lp", 1, 2), ("gx", 0, 3), ("lp", 1, 1), ("gs", 1, 3), ("lz", 0, 3), ("gy", 1, 2), ("modpart", 1), ("mode", 0),
    ("mode", 1), ("mode", 2), ("gy", 0, 3), ("gx", 1, 3), ("lz", 1, 1), ("lp", 1, 3), ("gy", 1, 3), ("lz", 1, 2),
    ("modz", 0), ("own", 2), ("gs", 2, 0), ("lx", 2), ("modz", 1), ("lz", 1, 3), ("modz", 2), ("gx", 2, 0),
    ("own", 3), ("gs", 3, 0), ("gz", 2, 2), ("gy", 2, 0), ("lx", 3), ("gz", 2, 1), ("gs", 2, 1), ("modfirst",),
    ("ly", 2), ("gz", 3, 1), ("gx", 3, 0), ("gz", 3, 2), ("gx", 2, 1), ("lp", 2, 1), ("gs", 2, 2), ("gz", 2, 3),
    ("modsecond",), ("gy", 3, 0), ("lz", 2, 1), ("gy", 2, 1), ("gs", 3, 1), ("lp", 2, 2), ("gx", 2, 2), ("gz", 3, 3),
    ("modrows",), ("gs", 3, 2), ("modulate", 0), ("gate", 2), ("ly", 3), ("lp", 2, 3), ("landed", 0), ("project", 0),
    ("gx", 3, 1), ("gy", 2, 2), ("lz", 2, 2), ("gx", 3, 2), ("turnn", 0), ("gs", 2, 3), ("attend", 0, 0),
    ("lp", 3, 1), ("lp", 3, 2), ("attend", 0, 1), ("gy", 3, 1), ("gy", 3, 2), ("lz", 3, 1), ("gs", 3, 3),
    ("attend", 0, 2), ("gx", 2, 3), ("join", 0), ("lp", 3, 3), ("gx", 3, 3), ("add", 0), ("lz", 2, 3), ("turna", 0),
    ("standardize", 1), ("modulate", 1), ("gy", 2, 3), ("landed", 1), ("project", 1), ("lz", 3, 2), ("gy", 3, 3),
    ("turnn", 1), ("attend", 1, 0), ("lz", 3, 3), ("attend", 1, 1), ("attend", 1, 2), ("join", 1), ("add", 1),
    ("turna", 1), ("standardize", 2), ("modulate", 2), ("turnn", 2), ("landed", 2), ("expand", 0), ("expand", 1),
    ("expand", 2), ("expand", 3), ("sendh",), ("needh",), ("cwait", 0), ("downt", 0), ("downt", 1), ("downt", 2),
    ("downt", 3), ("te", 0, 0), ("ss", 0, 0), ("landed", 3), ("ghid", 0), ("te", 0, 1), ("ss", 0, 1), ("ghid", 1),
    ("ghid", 2), ("ghid", 3), ("te", 0, 2), ("ss", 0, 2), ("sendp",), ("sy", 0, 0), ("tz", 0, 0), ("sy", 0, 1),
    ("needp",), ("cwait", 1), ("upt", 3), ("te", 1, 0), ("upt", 0), ("tz", 0, 1), ("ss", 0, 3), ("upt", 1),
    ("sy", 0, 2), ("upt", 2), ("tz", 0, 2), ("contract",), ("sx", 0, 0), ("sx", 0, 1), ("ss", 1, 0), ("close",),
    ("back2", 0), ("back2", 1), ("sy", 0, 3), ("ttot", 0), ("tz", 1, 0), ("sx", 0, 2), ("back2", 2), ("ss", 1, 1),
    ("back2", 3), ("sz", 0, 0), ("normb", 2), ("sy", 1, 0), ("te", 1, 1), ("sx", 0, 3), ("gate", 1), ("ty", 0),
    ("sz", 0, 1), ("split", 1), ("te", 1, 2), ("ss", 1, 2), ("attb", 1, 0), ("sy", 1, 1), ("sz", 0, 2),
    ("attb", 1, 1), ("tx", 0), ("sx", 1, 0), ("tz", 1, 1), ("tz", 1, 2), ("ss", 1, 3), ("attb", 1, 2), ("sy", 1, 2),
    ("sfin", 0), ("swap", 0), ("sx", 1, 1), ("sendq", 1), ("retire", 0), ("ttot", 1), ("sy", 1, 3), ("sz", 1, 0),
    ("sx", 1, 2), ("cwait", 2), ("needq", 1), ("outt", 1), ("te", 2, 0), ("qkvt", 1, 0), ("ty", 1), ("qkvt", 1, 1),
    ("sz", 1, 1), ("sx", 1, 3), ("qkvt", 1, 2), ("te", 2, 1), ("ss", 2, 0), ("back", 1, 0), ("tx", 1), ("sz", 1, 2),
    ("ss", 2, 1), ("back", 1, 1), ("back", 1, 2), ("ss", 2, 2), ("normb", 1), ("te", 2, 2), ("sy", 2, 0),
    ("tz", 2, 0), ("sentq", 1), ("gate", 0), ("sfin", 1), ("swap", 1), ("split", 0), ("sy", 2, 1), ("attb", 0, 0),
    ("tz", 2, 1), ("ss", 2, 3), ("attb", 0, 1), ("sy", 2, 2), ("tz", 2, 2), ("sx", 2, 0), ("attb", 0, 2),
    ("sx", 2, 1), ("sendq", 0), ("retire", 1), ("sy", 2, 3), ("sx", 2, 2), ("sz", 2, 0), ("cwait", 3), ("needq", 0),
    ("outt", 0), ("ttot", 2), ("te", 3, 0), ("qkvt", 0, 0), ("sx", 2, 3), ("qkvt", 0, 1), ("sz", 2, 1),
    ("qkvt", 0, 2), ("ty", 2), ("te", 3, 1), ("ss", 3, 0), ("back", 0, 0), ("sz", 2, 2), ("ss", 3, 1), ("back", 0, 1),
    ("tx", 2), ("back", 0, 2), ("te", 3, 2), ("normb", 0), ("rows", 0), ("tz", 3, 0), ("sy", 3, 0), ("sfin", 2),
    ("swap", 2), ("ss", 3, 2), ("sentq", 0), ("sy", 3, 1), ("tz", 3, 1), ("retire", 2), ("rows", 1), ("sx", 3, 0),
    ("tz", 3, 2), ("ss", 3, 3), ("sy", 3, 2), ("sx", 3, 1), ("sz", 3, 0), ("rows", 2), ("ttot", 3), ("sy", 3, 3),
    ("sz", 3, 1), ("sx", 3, 2), ("sz", 3, 2), ("ty", 3), ("rowp", 1), ("rowz", 1), ("rowp", 2), ("sx", 3, 3),
    ("tx", 3), ("sfin", 3), ("swap", 3), ("retire", 3), ("rowz", 2), ("rowp", 3), ("rowz", 3), ("rowt",), ("ada", 0),
    ("ada", 1),
)


def dot(left, right):
    return jnp.dot(left, right, preferred_element_type=jnp.float32)


def layer_kernel(
    tokens,
    cotangent,
    ids_row,
    ids_col,
    steps,
    bias,
    w_ada,
    w_qkv_s,
    w_out_s,
    w_qkv_t,
    w_out_t,
    w_up,
    w_down,
    o_layer,
    o_tokens,
    o_ada,
    o_bias,
    o_qkv_s,
    o_out_s,
    o_qkv_t,
    o_out_t,
    o_up,
    o_down,
    held,
    stage,
    apart,
    apart_down,
    sums,
    from_second,
    from_first,
    from_z,
    last_pair,
    last_one,
    last_z,
    all_steps,
    cond,
    mod,
    tally,
    rows_mod,
    all_rows_mod,
    xhat,
    deviation,
    normed,
    attended,
    turned,
    hidden_turned,
    qkv,
    probs,
    branch,
    stream,
    grad,
    hidden,
    slope,
    grad_pre_twin,
    gated,
    gated_twin,
    grad_attended,
    grad_qkv_twin,
    disallowed,
    swap_sems,
    gather_send,
    gather_recv,
    scatter_send,
    scatter_recv,
    credit,
    twin_send,
    twin_recv,
    step_send,
    step_recv,
    mod_send,
    mod_recv,
    row_send,
    row_recv,
):
    width, tok = tokens.shape[1], tokens.shape[0]
    f32, bf16 = jnp.float32, jnp.bfloat16
    spot = Spot()
    core = spot.core
    grad_qkv, grad_normed = hidden, stream
    greet(spot)

    def attention_piece(w_qkv, w_out):
        def piece(half, chunk):
            if chunk < 3:
                return w_qkv[:, pl.ds(pl.multiple_of(half * 1152 + chunk * 384, 128), 384)]
            return w_out[:, pl.ds(pl.multiple_of(half * 384, 128), 384)]

        return piece

    def up_piece(half, chunk):
        return w_up[:, pl.ds(pl.multiple_of(half * 1536 + chunk * 384, 128), 384)]

    def down_piece(half, chunk):
        return w_down[chunk * 48 : chunk * 48 + 48, pl.ds(pl.multiple_of(half * 384, 128), 384)]

    pieces = (
        attention_piece(w_qkv_s, w_out_s),
        attention_piece(w_qkv_t, w_out_t),
        up_piece,
        down_piece,
    )
    gathers = [
        Gather(
            spot,
            held.at[g],
            stage.at[g],
            apart.at[g] if g < 3 else apart_down,
            swap_sems.at[g],
            gather_send.at[g],
            gather_recv.at[g],
        )
        for g in range(4)
    ]
    scatters = [
        Scatter(
            spot,
            sums.at[n % 2],
            from_second.at[n % 2],
            from_first.at[n % 2],
            from_z.at[n % 2],
            last_pair.at[n % 2],
            last_one.at[n % 2],
            last_z.at[n % 2],
            stage.at[3 - n],
            apart_down if n == 0 else apart.at[3 - n],
            scatter_send.at[n],
            scatter_recv.at[n],
            credit.at[n % 2],
            n >= 2,
        )
        for n in range(4)
    ]

    def put_attention(o_qkv, o_out):
        def put(half, chunk, rows):
            if chunk < 3:
                o_qkv[:, pl.ds(pl.multiple_of(half * 1152 + chunk * 384, 128), 384)] = rows
            else:
                o_out[:, pl.ds(pl.multiple_of(half * 384, 128), 384)] = rows

        return put

    def put_up(half, chunk, rows):
        o_up[:, pl.ds(pl.multiple_of(half * 1536 + chunk * 384, 128), 384)] = rows

    def put_down(half, chunk, rows):
        o_down[chunk * 48 : chunk * 48 + 48, pl.ds(pl.multiple_of(half * 384, 128), 384)] = rows

    puts = (put_down, put_up, put_attention(o_qkv_t, o_out_t), put_attention(o_qkv_s, o_out_s))

    def to_twin(index, src, dst):
        return remote(src, dst, twin_send.at[index], twin_recv.at[index], spot.twin)

    def turned_copy(i):
        return to_twin(i, turned.at[i, 0], turned.at[i, 1])

    def hidden_copy():
        return to_twin(5, hidden_turned.at[0], hidden_turned.at[1])

    def gated_copy(j):
        theirs = pl.multiple_of((1 - core) * 384, 128)
        return to_twin(6 + j, gated.at[j, :, pl.ds(theirs, 384)], gated_twin.at[j])

    def grad_pre_copy():
        theirs = pl.multiple_of((1 - core) * 1536, 128)
        return to_twin(9, slope.at[:, pl.ds(theirs, 1536)], grad_pre_twin)

    def grad_qkv_copy(j):
        theirs = pl.multiple_of((1 - core) * 1152, 128)
        return to_twin(10 + j, grad_qkv.at[:, pl.ds(theirs, 1152)], grad_qkv_twin.at[j])

    def step_copy(index, ref, device):
        return remote(ref, ref, step_send.at[index], step_recv.at[index], device)

    def step_pair(plane):
        return all_steps.at[spot.z, plane]

    step_line = LineGather(
        spot, lambda z: all_steps.at[z], step_send.at[pl.ds(4, 5)], step_recv.at[pl.ds(4, 4)]
    )

    def steps_open():
        all_steps[spot.z, spot.plane, core] = steps[...]
        step_copy(0, all_steps.at[spot.z, spot.plane, core], spot.twin).start()

    def steps_first():
        step_copy(0, all_steps.at[spot.z, spot.plane, 1 - core], spot.twin).wait_recv()
        step_copy(1, step_pair(spot.plane), spot.first).start()
        step_copy(2, step_pair(spot.plane), spot.second).start()

    def steps_second():
        step_copy(1, step_pair(spot.first_plane), spot.first).wait_recv()
        step_copy(3, step_pair(spot.first_plane), spot.second).start()

    def steps_z():
        step_copy(2, step_pair(spot.second_plane), spot.second).wait_recv()
        step_copy(3, step_pair(spot.far_plane), spot.second).wait_recv()
        step_line.open()

    def steps_drain():
        step_copy(0, all_steps.at[spot.z, spot.plane, core], spot.twin).wait_send()
        for index in (1, 2, 3):
            step_copy(index, step_pair(spot.plane), spot.first).wait_send()
        step_line.drain()

    def make_cond():
        flat = all_steps[...].reshape(256, 128)
        clip = lax.broadcasted_iota(jnp.int32, (64, 256), 0)
        column = lax.broadcasted_iota(jnp.int32, (64, 256), 1)
        wanted = 64 * ((clip >> 3) & 3) + 16 * ((clip >> 1) & 3) + 8 * (clip >> 5) + (clip & 1)
        times = jnp.dot(
            (column == wanted).astype(f32),
            flat,
            precision=lax.Precision.HIGHEST,
            preferred_element_type=f32,
        )
        first = (spot.chip * 2 + core) * 24
        half_width = width // 2
        feature = first + lax.broadcasted_iota(jnp.int32, (64, 128), 1)
        place = jnp.where(feature < half_width, feature, feature - half_width).astype(f32)
        angle = times * jnp.exp(-math.log(FREQ_BASE) * place / half_width)
        value = jnp.where(feature < half_width, jnp.cos(angle), jnp.sin(angle))
        cond[...] = (value / (1.0 + jnp.exp(-value))).astype(bf16)

    spare = sums.at[1]
    mod_out, mod_in, mod_sum = (spare.at[pl.ds(i, 12)] for i in (0, 12, 24))
    mod_first, mod_second, mod_one, mod_two = (spare.at[pl.ds(i, 3)] for i in (51, 54, 57, 60))
    mod_line = LineSum(
        spot,
        lambda z: spare.at[pl.ds(24 + 3 * z, 3)],
        lambda i: spare.at[pl.ds(36 + 3 * i, 3)],
        mod_send.at[pl.ds(0, 3)],
        mod_recv.at[pl.ds(0, 5)],
    )

    def mod_copy(index):
        src, dst, device = (
            (mod_out, mod_in, spot.twin),
            (mod_one, mod_first, spot.first),
            (mod_two, mod_second, spot.second),
        )[index]
        return remote(src, dst, mod_send.at[3 + index], mod_recv.at[5 + index], device)

    def mod_partial(owner, chunk):
        rows = cond[pl.ds(pl.multiple_of(32 * owner, 32), 32), :24]
        left, right = (
            dot(rows, w_ada[:, at : at + 384]) + bias[:, at : at + 384]
            for at in (384 * chunk, 3456 + 384 * chunk)
        )
        for z in range(4):
            part = slice(8 * z, 8 * z + 8)
            yield 3 * z + chunk // 3, jnp.concatenate([left[part], right[part]], axis=0)

    def mod_twin():
        for chunk in range(9):
            rows = slice(16 * (chunk % 3), 16 * (chunk % 3) + 16)
            for at, value in mod_partial(1 - core, chunk):
                mod_out[at, rows] = value.astype(bf16)
        mod_copy(0).start()

    def mod_own():
        mod_copy(0).wait_recv()
        for chunk in range(9):
            rows = slice(16 * (chunk % 3), 16 * (chunk % 3) + 16)
            for at, value in mod_partial(core, chunk):
                mod_sum[at, rows] = (value + mod_in[at, rows].astype(f32)).astype(bf16)

    def mod_along_first():
        def put(i, value):
            mod_one[i] = value.astype(bf16)

        mod_line.total(put)
        mod_copy(1).start()

    def mod_along_second():
        mod_copy(1).wait_recv()
        for i in range(3):
            mod_two[i] = mod_one[i] + mod_first[i]
        mod_copy(2).start()

    def mod_rows():
        mod_copy(2).wait_recv()
        row = lax.broadcasted_iota(jnp.int32, (16, 384), 0)
        for chunk in range(9):
            at, rows = chunk // 3, slice(16 * (chunk % 3), 16 * (chunk % 3) + 16)
            value = mod_two[at, rows].astype(f32) + mod_second[at, rows].astype(f32)
            for clip in range(2):
                for half in range(2):
                    chosen = row == 8 * half + 2 * spot.plane + clip
                    column = 3456 * half + 384 * chunk
                    mod[clip : clip + 1, column : column + 384] = jnp.sum(
                        jnp.where(chosen, value, 0.0), axis=0, keepdims=True
                    )

    def mod_drain():
        mod_line.drain()
        for index in range(3):
            mod_copy(index).wait_send()

    row_line = LineGather(
        spot,
        lambda z: all_rows_mod.at[core, z],
        row_send.at[pl.ds(4, 5)],
        row_recv.at[pl.ds(4, 4)],
    )

    def row_copy(index):
        src, dst, device = (
            (rows_mod.at[0], rows_mod.at[1], spot.first),
            (rows_mod.at[2], rows_mod.at[3], spot.second),
            (all_rows_mod.at[core], all_rows_mod.at[core], spot.twin),
        )[index]
        return remote(src, dst, row_send.at[index], row_recv.at[index], device)

    def rows_first():
        row = lax.broadcasted_iota(jnp.int32, (16, 384), 0)
        for chunk in range(9):
            value = 0.0
            for clip in range(2):
                for half in range(2):
                    chosen = row == 8 * half + 2 * spot.plane + clip
                    column = 3456 * half + 384 * chunk
                    value += jnp.where(chosen, tally[clip : clip + 1, column : column + 384], 0.0)
            rows_mod[0, :, 384 * chunk : 384 * chunk + 384] = value.astype(bf16)
        row_copy(0).start()

    def rows_second():
        row_copy(0).wait_recv()
        rows_mod[2] = rows_mod[0] + rows_mod[1]
        row_copy(1).start()

    def rows_z():
        row_copy(1).wait_recv()
        all_rows_mod[core, spot.z] = rows_mod[2] + rows_mod[3]
        row_line.open()

    def rows_twin():
        row_copy(2).start()

    def ada(owner):
        rows = cond[pl.ds(pl.multiple_of(32 * owner, 32), 32), :]
        for chunk in range(9):
            value = all_rows_mod[owner, :, :, 384 * chunk : 384 * chunk + 384].astype(f32)
            for half in range(2):
                part = value[:, 8 * half : 8 * half + 8].reshape(32, 384)
                columns = slice(3456 * half + 384 * chunk, 3456 * half + 384 * chunk + 384)
                product = contract_rows(rows, part.astype(bf16))[:24]
                total = jnp.sum(part, axis=0, keepdims=True)
                yield columns, product, total

    def ada_own():
        for columns, product, total in ada(core):
            o_ada[:, columns] = product
            o_bias[:, columns] = total

    def ada_twin():
        theirs = all_rows_mod.at[1 - core]
        remote(theirs, theirs, row_send.at[2], row_recv.at[2], spot.twin).wait_recv()
        for columns, product, total in ada(1 - core):
            o_ada[:, columns] += product
            o_bias[:, columns] += total

    def rows_drain():
        for index in range(3):
            row_copy(index).wait_send()
        row_line.drain()

    def by_rows(action):
        @pl.loop(0, tok // 64)
        def _(i):
            action(pl.ds(pl.multiple_of(i * 64, 64), 64))

    def mod_part(j, component, rows):
        at = (3 * j + component) * width
        second = ids_col[rows, 2:3] == 1
        return jnp.where(second, mod[1:2, at : at + width], mod[0:1, at : at + width])

    def count(j, component, rows, value):
        at = (3 * j + component) * width
        second = ids_col[rows, 2:3] == 1
        tally[0:1, at : at + width] += jnp.sum(jnp.where(second, 0.0, value), axis=0, keepdims=True)
        tally[1:2, at : at + width] += jnp.sum(jnp.where(second, value, 0.0), axis=0, keepdims=True)

    def masks():
        for j in range(2):
            same = ids_col[:, j : j + 1] == ids_row[j : j + 1, :]
            disallowed[j] = jnp.where(same, 0.0, MASKED)
        tally[...] = jnp.zeros_like(tally)

    def standardize(j):
        def action(rows):
            if j == 0:
                stream[rows] = tokens[rows].astype(f32)
            value = stream[rows]
            center = value - jnp.mean(value, axis=-1, keepdims=True)
            inverse = lax.rsqrt(jnp.mean(center * center, axis=-1, keepdims=True) + EPSILON)
            xhat[j, rows] = (center * inverse).astype(bf16)
            deviation[rows, j : j + 1] = inverse

        by_rows(action)

    def modulate(j):
        def action(rows):
            normed[rows] = (
                xhat[j, rows].astype(f32) * (1.0 + mod_part(j, 1, rows)) + mod_part(j, 0, rows)
            ).astype(bf16)

        by_rows(action)

    def turn(i, source):
        for at in range(0, tok, 128):
            turned[i, 0, :, at : at + 128] = source[at : at + 128, :].T
        turned_copy(i).start()

    def weight(g, half, chunk):
        return held[g, half, :, chunk].reshape(width, 384)

    def project(j):
        @pl.loop(0, 6)
        def _(i):
            half, chunk = lax.div(i, 3), lax.rem(i, 3)
            columns = pl.ds(pl.multiple_of(i * 384, 128), 384)
            qkv[j, :, columns] = dot(normed[...], weight(j, half, chunk)).astype(bf16)

    def head_lanes():
        lane = lax.broadcasted_iota(jnp.int32, (1, 128), 1)
        return lane < 64, lane >= 64

    def head_columns(pair):
        return [pl.ds(pl.multiple_of(part * 768 + pair * 128, 128), 128) for part in range(3)]

    def attend(j, first, last):
        @pl.loop(first, last)
        def _(pair):
            at_q, at_k, at_v = head_columns(pair)
            queries, keys, values = qkv[j, :, at_q], qkv[j, :, at_k], qkv[j, :, at_v]
            results = []
            for head, lanes in enumerate(head_lanes()):
                scaled = jnp.where(lanes, queries, 0.0) * bf16(0.125)
                scores = contract_cols(scaled, keys) + disallowed[j]
                scores = jnp.exp(scores - jnp.max(scores, axis=-1, keepdims=True))
                low = (scores * (1.0 / jnp.sum(scores, axis=-1, keepdims=True))).astype(bf16)
                probs[j, 2 * pair + head] = low
                results.append(dot(low, values))
            attended[:, at_q] = jnp.where(head_lanes()[0], results[0], results[1]).astype(bf16)

    def join(j):
        @pl.loop(0, 2)
        def _(half):
            columns = pl.ds(pl.multiple_of(half * 384, 128), 384)
            branch[j, :, columns] = dot(attended[...], weight(j, half, 3)).astype(bf16)

    def add_branch(j):
        def action(rows):
            stream[rows] += mod_part(j, 2, rows) * branch[j, rows].astype(f32)

        by_rows(action)

    def expand(first, last):
        @pl.loop(first, last)
        def _(i):
            columns = pl.ds(pl.multiple_of(i * 384, 128), 384)
            matrix = weight(2, lax.div(i, 4), lax.rem(i, 4))
            for at in range(0, tok, 128):
                rows = slice(at, at + 128)
                pre = dot(normed[rows], matrix)
                square = pre * pre
                root = math.sqrt(2.0 / math.pi)
                bent = jnp.tanh(root * (pre + 0.044715 * (square * pre)))
                value = (0.5 * pre * (1.0 + bent)).astype(bf16)
                hidden[rows, columns] = value
                hidden_turned[0, columns, rows] = value.T
                slope[rows, columns] = (
                    0.5 * (1.0 + bent)
                    + 0.5 * pre * (1.0 - bent * bent) * (root * (1.0 + 3 * 0.044715 * square))
                ).astype(bf16)

    def gate(j):
        def action(rows):
            value = cotangent[rows].astype(f32) if j == 2 else grad[rows]
            if j == 2:
                grad[rows] = value
            else:
                count(j, 2, rows, value * branch[j, rows].astype(f32))
            gated[j, rows] = (mod_part(j, 2, rows) * value).astype(bf16)

        by_rows(action)
        gated_copy(j).start()

    def own_columns(first, width_of_half):
        return pl.ds(pl.multiple_of(core * width_of_half + first, 128), 384)

    def down_terms(z):
        scatter = scatters[0]
        rows = slice(768 * z, 768 * z + 768)
        value = dot(hidden_turned[0, rows], gated[2, :, own_columns(0, 384)]) + dot(
            hidden_turned[1, rows], gated_twin[2]
        )
        value = value.astype(bf16).reshape(4, 4, 48, 384)
        for plane in range(4):
            sums[0, pl.ds(scatter.place(4 * z + plane, 0), 3)] = value[plane, :3]
            sums[0, scatter.place(4 * z + plane, 3)] = value[plane, 3]

    def column_terms(n, chunk, left, right, right_twin):
        value = dot(turned[left, 0], right) + dot(turned[left, 1], right_twin)
        value = value.astype(bf16).reshape(16, 48, 384)
        for chip in range(16):
            sums[n % 2, scatters[n].place(chip, chunk)] = value[chip]

    def up_terms(chunk):
        column_terms(
            1,
            chunk,
            4,
            slope[:, own_columns(384 * chunk, 1536)],
            grad_pre_twin[:, 384 * chunk : 384 * chunk + 384],
        )

    def out_terms(j):
        column_terms(3 - j, 3, 2 * j + 1, gated[j, :, own_columns(0, 384)], gated_twin[j])

    def qkv_terms(j, chunk):
        column_terms(
            3 - j,
            chunk,
            2 * j,
            grad_qkv[:, own_columns(384 * chunk, 1152)],
            grad_qkv_twin[j, :, 384 * chunk : 384 * chunk + 384],
        )

    def contract():
        @pl.loop(0, 2)
        def _(half):
            columns = pl.ds(pl.multiple_of(half * 384, 128), 384)
            matrix = held[3, half].reshape(3072, 384)
            normed[:, columns] = dot(hidden[...], matrix).astype(bf16)

    def close():
        def action(rows):
            value = normed[rows].astype(f32)
            o_layer[rows] = (stream[rows] + mod_part(2, 2, rows) * value).astype(bf16)
            count(2, 2, rows, cotangent[rows].astype(f32) * value)

        by_rows(action)

    def grad_hidden(first, last):
        @pl.loop(first, last)
        def _(i):
            columns = pl.ds(pl.multiple_of(i * 384, 128), 384)
            value = sum(
                contract_cols(
                    gated[2, :, 384 * half : 384 * half + 384],
                    held[3, half, pl.ds(2 * i, 2)].reshape(384, 384),
                )
                for half in range(2)
            )
            slope[:, columns] = (slope[:, columns].astype(f32) * value).astype(bf16)

    def back_project(g, chunks, source, first, last):
        @pl.loop(first, last)
        def _(i):
            columns = pl.ds(pl.multiple_of(i * 384, 128), 384)
            value = contract_cols(
                source[:, columns], weight(g, lax.div(i, chunks), lax.rem(i, chunks))
            )

            @pl.when(i == 0)
            def _():
                grad_normed[...] = value

            @pl.when(i > 0)
            def _():
                grad_normed[...] += value

    def norm_back(j):
        def action(rows):
            value, unit = grad_normed[rows], xhat[j, rows].astype(f32)
            count(j, 0, rows, value)
            count(j, 1, rows, value * unit)
            scaled = value * (1.0 + mod_part(j, 1, rows))
            inner = jnp.mean(scaled * unit, axis=-1, keepdims=True)
            scaled = scaled - jnp.mean(scaled, axis=-1, keepdims=True)
            total = grad[rows] + deviation[rows, j : j + 1] * (scaled - unit * inner)
            if j == 0:
                o_tokens[rows] = total
            else:
                grad[rows] = total

        by_rows(action)

    def split(j):
        value = sum(
            contract_cols(gated[j, :, 384 * half : 384 * half + 384], weight(j, half, 3))
            for half in range(2)
        )
        grad_attended[...] = value.astype(bf16)

    def attend_back(j, first, last):
        @pl.loop(first, last)
        def _(pair):
            at_q, at_k, at_v = head_columns(pair)
            queries, keys, values = qkv[j, :, at_q], qkv[j, :, at_k], qkv[j, :, at_v]
            given = grad_attended[:, at_q]
            grad_q, grad_k, grad_v = [], 0.0, 0.0
            for head, lanes in enumerate(head_lanes()):
                part = jnp.where(lanes, given, 0.0).astype(bf16)
                low = probs[j, 2 * pair + head]
                product = low.astype(f32) * contract_cols(part, values)
                total = jnp.sum(product, axis=-1, keepdims=True)
                scores = ((product - low.astype(f32) * total) * 0.125).astype(bf16)
                grad_v += contract_rows(low, part)
                grad_k += contract_rows(scores, jnp.where(lanes, queries, 0.0).astype(bf16))
                grad_q.append(dot(scores, keys))
            grad_qkv[:, at_q] = jnp.where(head_lanes()[0], grad_q[0], grad_q[1]).astype(bf16)
            grad_qkv[:, at_k] = grad_k.astype(bf16)
            grad_qkv[:, at_v] = grad_v.astype(bf16)

    def each_twin_copy():
        for i in range(5):
            yield turned_copy(i)
        yield hidden_copy()
        for j in range(3):
            yield gated_copy(j)
        yield grad_pre_copy()

    def forward_drain():
        steps_drain()
        mod_drain()
        for gather in gathers:
            gather.swap().wait_send()

    def send_hidden():
        forward_drain()
        hidden_copy().start()

    def retire(n):
        scatters[n].store(puts[n])
        scatters[n].drain()
        if n < 2:
            scatters[n].release()

    def swap(n):
        scatters[n].swap().start()

    def need(copy, *indices):
        copy(*indices).wait_recv()

    steps_of = {
        "steps": (steps_first, steps_second, steps_z),
        "stepp": step_line.pass_on,
        "stepz": step_line.take,
        "cond": make_cond,
        "modpart": (mod_twin, mod_own),
        "mode": mod_line.send_end,
        "modz": mod_line.send_middle,
        "modfirst": mod_along_first,
        "modsecond": mod_along_second,
        "modrows": mod_rows,
        "own": lambda g: gathers[g].own(),
        "gz": lambda g, k: gathers[g].pass_on(k),
        "gs": lambda g, k: gathers[g].spread(k),
        "gx": lambda g, k: gathers[g].along_first(k),
        "gy": lambda g, k: gathers[g].along_second(k),
        "lx": lambda g: gathers[g].last_along_first(),
        "ly": lambda g: gathers[g].last_along_second(),
        "lp": lambda g, k: gathers[g].line.pass_on(k),
        "lz": lambda g, k: gathers[g].last_along_z(k),
        "landed": lambda g: gathers[g].landed(),
        "cwait": lambda n: scatters[n].wait_credit(),
        "ss": lambda n, k: scatters[n].second_copy(k).start(),
        "sy": lambda n, k: scatters[n].add_second(k),
        "sx": lambda n, k: scatters[n].add_first(k),
        "sz": lambda n, k: scatters[n].line.send_middle(k),
        "sfin": lambda n: scatters[n].finish(),
        "te": lambda n, k: scatters[n].last_line.send_end(k),
        "tz": lambda n, k: scatters[n].last_line.send_middle(k),
        "ttot": lambda n: scatters[n].last_total(),
        "ty": lambda n: scatters[n].last_add_second(),
        "tx": lambda n: scatters[n].last_finish(),
        "swap": swap,
        "retire": retire,
        "rows": (rows_first, rows_second, rows_z),
        "rowp": row_line.pass_on,
        "rowz": row_line.take,
        "rowt": rows_twin,
        "ada": (ada_own, ada_twin),
        "masks": masks,
        "standardize": standardize,
        "modulate": modulate,
        "project": project,
        "turnn": lambda j: turn(2 * j, normed),
        "turna": lambda j: turn(2 * j + 1, attended),
        "attend": lambda j, i: attend(j, 2 * i, 2 * i + 2),
        "join": join,
        "add": add_branch,
        "gate": gate,
        "expand": lambda i: expand(2 * i, 2 * i + 2),
        "sendh": send_hidden,
        "needh": lambda: (need(gated_copy, 2), need(hidden_copy)),
        "downt": down_terms,
        "ghid": lambda i: grad_hidden(2 * i, 2 * i + 2),
        "sendp": lambda: grad_pre_copy().start(),
        "contract": contract,
        "close": close,
        "needp": lambda: (need(grad_pre_copy), need(turned_copy, 4)),
        "upt": up_terms,
        "back2": lambda i: back_project(2, 4, slope, 2 * i, 2 * i + 2),
        "normb": norm_back,
        "split": split,
        "attb": lambda j, i: attend_back(j, 2 * i, 2 * i + 2),
        "sendq": lambda j: grad_qkv_copy(j).start(),
        "needq": lambda j: (
            need(turned_copy, 2 * j + 1),
            need(gated_copy, j),
            need(turned_copy, 2 * j),
            need(grad_qkv_copy, j),
        ),
        "outt": out_terms,
        "qkvt": qkv_terms,
        "back": lambda j, i: back_project(j, 3, grad_qkv, 2 * i, 2 * i + 2),
        "sentq": lambda j: grad_qkv_copy(j).wait_send(),
    }
    for g, gather in enumerate(gathers):
        gather.open(pieces[g])
    steps_open()
    for name, *indices in ORDER:
        step = steps_of[name]
        if isinstance(step, tuple):
            step[indices[0]]()
        else:
            step(*indices)
    rows_drain()
    for gather in gathers:
        gather.drain()
    for copy in each_twin_copy():
        copy.wait_send()


def layer(tokens, cotangent, ids_row, ids_col, steps, bias, w_ada, *shards):
    f32, bf16 = jnp.float32, jnp.bfloat16
    tok, width = tokens.shape
    block = (4, 48, 384)
    dma, vmem = pltpu.SemaphoreType.DMA, pltpu.VMEM
    return pl.pallas_call(
        layer_kernel,
        out_shape=[
            jax.ShapeDtypeStruct((tok, width), bf16),
            jax.ShapeDtypeStruct((tok, width), f32),
            jax.ShapeDtypeStruct(w_ada.shape, f32),
            jax.ShapeDtypeStruct((1, w_ada.shape[1]), f32),
        ]
        + [jax.ShapeDtypeStruct(shard.shape, f32) for shard in shards],
        in_specs=[pl.BlockSpec(memory_space=vmem)] * 13,
        out_specs=[pl.BlockSpec(memory_space=vmem)] * 10,
        scratch_shapes=[
            vmem((4, 2, 16) + block, bf16),
            vmem((4,) + block, f32),
            vmem((3, 4, 24, 384), f32),
            vmem((2, 48, 384), f32),
            vmem((2, 64, 48, 384), bf16),
            vmem((2, 4, 6, 48, 384), bf16),
            vmem((2, 4, 3, 48, 384), bf16),
            vmem((2, 5, 3, 48, 384), bf16),
            vmem((2, 2, 48, 384), bf16),
            vmem((2, 48, 384), bf16),
            vmem((2, 5) + block, bf16),
            vmem((4, 4, 2, 8, 128), f32),
            vmem((64, 128), bf16),
            vmem((8, 6912), f32),
            vmem((8, 6912), f32),
            vmem((4, 16, 3456), bf16),
            vmem((2, 4, 16, 3456), bf16),
            vmem((3, tok, width), bf16),
            vmem((tok, 128), f32),
            vmem((tok, width), bf16),
            vmem((tok, width), bf16),
            vmem((5, 2, width, tok), bf16),
            vmem((2, 4 * width, tok), bf16),
            vmem((2, tok, 3 * width), bf16),
            vmem((2, HEADS, tok, tok), bf16),
            vmem((2, tok, width), bf16),
            vmem((tok, width), f32),
            vmem((tok, width), f32),
            vmem((tok, 4 * width), bf16),
            vmem((tok, 4 * width), bf16),
            vmem((tok, 2 * width), bf16),
            vmem((3, tok, width), bf16),
            vmem((3, tok, width // 2), bf16),
            vmem((tok, width), bf16),
            vmem((2, tok, 3 * width // 2), bf16),
            vmem((2, tok, tok), f32),
            dma((4, 2)),
            dma((4, 33)),
            dma((4, 31)),
            dma((4, 17)),
            dma((4, 21)),
            pltpu.SemaphoreType.REGULAR((2, 4)),
            dma((12,)),
            dma((12,)),
            dma((9,)),
            dma((8,)),
            dma((6,)),
            dma((8,)),
            dma((9,)),
            dma((8,)),
        ],
        compiler_params=pltpu.CompilerParams(
            collective_id=0, has_side_effects=True, vmem_limit_bytes=64 * 2**20
        ),
    )(tokens, cotangent, ids_row, ids_col, steps, bias, w_ada, *shards)


def on_grid(
    tokens,
    seg_ids,
    frame_ids,
    patch_ids,
    timesteps,
    w_ada,
    b_ada,
    w_qkv_spatial,
    w_out_spatial,
    w_qkv_temporal,
    w_out_temporal,
    w_up,
    w_down,
    cotangent,
):
    place = lax.axis_index(("wide", "narrow"))
    share = b_ada.shape[0]
    ids = jnp.stack([seg_ids * 16 + frame_ids, seg_ids * 16 + patch_ids, seg_ids])
    steps = jnp.broadcast_to(
        jnp.pad(timesteps.astype(jnp.float32), (0, 6))[:, None], (8, 128)
    )
    bias = lax.dynamic_update_slice(
        jnp.zeros((1, w_ada.shape[1]), jnp.float32),
        b_ada.astype(jnp.float32)[None],
        (0, place * share),
    )
    shards = (w_qkv_spatial, w_out_spatial, w_qkv_temporal, w_out_temporal, w_up, w_down)
    outs = layer(tokens, cotangent, ids, ids.T, steps, bias, w_ada, *shards)
    bias_share = lax.dynamic_slice(outs[3][0], (place * share,), (share,))
    return (*outs[:3], bias_share, *outs[4:])


def on_device(
    tokens,
    seg_ids,
    frame_ids,
    patch_ids,
    timesteps,
    w_ada,
    b_ada,
    w_qkv_spatial,
    w_out_spatial,
    w_qkv_temporal,
    w_out_temporal,
    w_up,
    w_down,
    cotangent,
):
    axes = ("wide", "narrow")
    gathered = (
        None,
        None,
        lax.all_gather(w_qkv_spatial, axes, axis=0, tiled=True),
        lax.all_gather(w_out_spatial, axes, axis=0, tiled=True),
        lax.all_gather(w_qkv_temporal, axes, axis=0, tiled=True),
        lax.all_gather(w_out_temporal, axes, axis=0, tiled=True),
        lax.all_gather(w_up, axes, axis=0, tiled=True),
        lax.all_gather(w_down, axes, axis=0, tiled=True),
    )
    width = tokens.shape[1]
    head_count = HEADS
    clip_count = timesteps.shape[0]
    row_count = w_ada.shape[0]
    place = lax.axis_index(axes)
    all_steps = lax.all_gather(timesteps, axes, axis=0, tiled=True)
    cond_all = jax.nn.silu(time_embed(all_steps, width)).astype(jnp.bfloat16)
    cond_rows = lax.dynamic_slice_in_dim(cond_all, place * row_count, row_count, axis=1)
    all_bias = lax.all_gather(b_ada, axes, axis=0, tiled=True)
    modulation = lax.psum_scatter(
        jnp.dot(cond_rows, w_ada, preferred_element_type=jnp.float32),
        axes,
        scatter_dimension=0,
        tiled=True,
    ) + all_bias.astype(jnp.float32)
    one_hot = (seg_ids[:, None] == jnp.arange(clip_count, dtype=jnp.int32)[None, :]).astype(
        jnp.float32
    )
    offset_first, scale_first, gate_a = sublayer_mod(one_hot, modulation, 0, width)
    offset_second, scale_second, gate_b = sublayer_mod(one_hot, modulation, 1, width)
    offset_third, scale_third, gate_c = sublayer_mod(one_hot, modulation, 2, width)
    same_clip = seg_ids[:, None] == seg_ids[None, :]
    spatial_mask = same_clip & (frame_ids[:, None] == frame_ids[None, :])
    temporal_mask = same_clip & (patch_ids[:, None] == patch_ids[None, :])
    residual_first = tokens.astype(jnp.float32)
    standardized_first, inverse_deviation_first = layer_norm_apply(residual_first)
    normalized_first = (standardized_first * (1.0 + scale_first) + offset_first).astype(
        jnp.bfloat16
    )
    branch_a, qkv_a, merged_a = attention_forward(
        normalized_first, gathered[2], gathered[3], spatial_mask, head_count
    )
    residual_second = residual_first + gate_a * branch_a
    standardized_second, inverse_deviation_second = layer_norm_apply(residual_second)
    normalized_second = (standardized_second * (1.0 + scale_second) + offset_second).astype(
        jnp.bfloat16
    )
    branch_b, qkv_b, merged_b = attention_forward(
        normalized_second, gathered[4], gathered[5], temporal_mask, head_count
    )
    residual_third = residual_second + gate_b * branch_b
    standardized_third, inverse_deviation_third = layer_norm_apply(residual_third)
    normalized_third = (standardized_third * (1.0 + scale_third) + offset_third).astype(
        jnp.bfloat16
    )
    pre_act = jnp.dot(normalized_third, gathered[6], preferred_element_type=jnp.float32)
    act_out, gelu_pull = jax.vjp(jax.nn.gelu, pre_act)
    hidden = act_out.astype(jnp.bfloat16)
    branch_c = jnp.dot(hidden, gathered[7], preferred_element_type=jnp.float32)
    result = residual_third + gate_c * branch_c
    back_weights = gathered
    output_gradient = cotangent.astype(jnp.float32)
    gate_gradient_third = output_gradient * branch_c
    grad_branch_c = (gate_c * output_gradient).astype(jnp.bfloat16)
    grad_hidden = contract_cols(grad_branch_c, back_weights[7])
    grad_pre = gelu_pull(grad_hidden)[0].astype(jnp.bfloat16)
    normalized_gradient_third = contract_cols(grad_pre, back_weights[6])
    residual_gradient = output_gradient + layer_norm_reverse(
        normalized_gradient_third, standardized_third, inverse_deviation_third, scale_third
    )
    gate_gradient_second = residual_gradient * branch_b
    grad_branch_b = (gate_b * residual_gradient).astype(jnp.bfloat16)
    normalized_gradient_second, grad_qkv_t = attention_backward(
        grad_branch_b, qkv_b, back_weights[4], back_weights[5], temporal_mask, head_count
    )
    residual_gradient = residual_gradient + layer_norm_reverse(
        normalized_gradient_second, standardized_second, inverse_deviation_second, scale_second
    )
    gate_gradient_first = residual_gradient * branch_a
    grad_branch_a = (gate_a * residual_gradient).astype(jnp.bfloat16)
    normalized_gradient_first, grad_qkv_s = attention_backward(
        grad_branch_a, qkv_a, back_weights[2], back_weights[3], spatial_mask, head_count
    )
    residual_gradient = residual_gradient + layer_norm_reverse(
        normalized_gradient_first, standardized_first, inverse_deviation_first, scale_first
    )
    grad_mod = jnp.concatenate(
        [
            exact_rows(
                one_hot,
                jnp.concatenate(
                    [
                        normalized_gradient_first,
                        normalized_gradient_first * standardized_first,
                        gate_gradient_first,
                    ],
                    axis=1,
                ),
            ),
            exact_rows(
                one_hot,
                jnp.concatenate(
                    [
                        normalized_gradient_second,
                        normalized_gradient_second * standardized_second,
                        gate_gradient_second,
                    ],
                    axis=1,
                ),
            ),
            exact_rows(
                one_hot,
                jnp.concatenate(
                    [
                        normalized_gradient_third,
                        normalized_gradient_third * standardized_third,
                        gate_gradient_third,
                    ],
                    axis=1,
                ),
            ),
        ],
        axis=1,
    )
    grad_mod_low = grad_mod.astype(jnp.bfloat16)
    all_grad_mod = lax.all_gather(grad_mod_low, axes, axis=0, tiled=True)
    bias_share = lax.psum_scatter(
        jnp.sum(grad_mod, axis=0), axes, scatter_dimension=0, tiled=True
    )

    def share(left, right):
        return lax.psum_scatter(
            contract_rows(left, right).astype(jnp.bfloat16),
            axes,
            scatter_dimension=0,
            tiled=True,
        ).astype(jnp.float32)

    return (
        result.astype(jnp.bfloat16),
        residual_gradient,
        contract_rows(cond_rows, all_grad_mod),
        bias_share,
        share(normalized_first, grad_qkv_s),
        share(merged_a, grad_branch_a),
        share(normalized_second, grad_qkv_t),
        share(merged_b, grad_branch_b),
        share(normalized_third, grad_pre),
        share(hidden, grad_branch_c),
    )


def solution(mesh):
    placed = (
        P(("wide", "narrow"), None),
        P(("wide", "narrow")),
        P(("wide", "narrow")),
        P(("wide", "narrow")),
        P(("wide", "narrow")),
        P(("wide", "narrow"), None),
        P(("wide", "narrow")),
        P(("wide", "narrow"), None),
        P(("wide", "narrow"), None),
        P(("wide", "narrow"), None),
        P(("wide", "narrow"), None),
        P(("wide", "narrow"), None),
        P(("wide", "narrow"), None),
        P(("wide", "narrow"), None),
    )
    grid = dict(mesh.shape) == {"wide": 16, "narrow": 2}
    return jax.shard_map(
        on_grid if grid else on_device,
        mesh=mesh,
        in_specs=placed,
        out_specs=(
            P(("wide", "narrow"), None),
            P(("wide", "narrow"), None),
            P(("wide", "narrow"), None),
            P(("wide", "narrow")),
            P(("wide", "narrow"), None),
            P(("wide", "narrow"), None),
            P(("wide", "narrow"), None),
            P(("wide", "narrow"), None),
            P(("wide", "narrow"), None),
            P(("wide", "narrow"), None),
        ),
        check_vma=False,
    )
```

```python
from functools import partial
import math

import jax
import jax.numpy as jnp
from jax import lax
from jax.experimental import pallas as pl
from jax.experimental.pallas import tpu as pltpu
from jax.sharding import PartitionSpec as P

HEADS = 12


EPSILON = 1e-06
FREQ_BASE = 10000.0
MASKED = -1e30


def time_embed(step_ids, width):
    half_width = width // 2
    frequency = jnp.exp(
        -math.log(FREQ_BASE) * jnp.arange(half_width, dtype=jnp.float32) / half_width
    )
    angles = step_ids.astype(jnp.float32)[:, None] * frequency[None, :]
    return jnp.concatenate([jnp.cos(angles), jnp.sin(angles)], axis=1)


def contract_rows(left, right):
    return lax.dot_general(
        left, right, (((0,), (0,)), ((), ())), preferred_element_type=jnp.float32
    )


def contract_cols(left, right):
    return lax.dot_general(
        left, right, (((1,), (1,)), ((), ())), preferred_element_type=jnp.float32
    )


def exact_rows(left, right):
    return lax.dot_general(
        left,
        right,
        (((0,), (0,)), ((), ())),
        precision=lax.Precision.HIGHEST,
        preferred_element_type=jnp.float32,
    )


def layer_norm_apply(stream):
    center = stream - jnp.mean(stream, axis=-1, keepdims=True)
    inverse_deviation = lax.rsqrt(jnp.mean(center * center, axis=-1, keepdims=True) + EPSILON)
    return (center * inverse_deviation, inverse_deviation)


def layer_norm_reverse(normalized_gradient, standardized_input, inverse_deviation, row_scales):
    input_gradient = normalized_gradient * (1.0 + row_scales)
    mean_removed = input_gradient - jnp.mean(input_gradient, axis=-1, keepdims=True)
    return inverse_deviation * (
        mean_removed
        - standardized_input * jnp.mean(input_gradient * standardized_input, axis=-1, keepdims=True)
    )


def sublayer_mod(one_hot, modulation, sublayer, width):
    table = modulation[:, 3 * width * sublayer : 3 * width * (sublayer + 1)]
    rows_mod = jnp.dot(
        one_hot, table, precision=lax.Precision.HIGHEST, preferred_element_type=jnp.float32
    )
    return (rows_mod[:, :width], rows_mod[:, width : 2 * width], rows_mod[:, 2 * width :])


def head_probs(allowed, scale, queries, key_vecs):
    scores = contract_cols(queries, key_vecs) * scale
    scores = jnp.where(allowed, scores, MASKED)
    return jax.nn.softmax(scores, axis=-1)


def head_forward(allowed, scale, item):
    queries, key_vecs, val_vecs = item
    attn_prob = head_probs(allowed, scale, queries, key_vecs)
    return jnp.dot(attn_prob.astype(jnp.bfloat16), val_vecs, preferred_element_type=jnp.float32)


def head_backward(allowed, scale, item):
    queries, key_vecs, val_vecs, grad_att = item
    attn_prob = head_probs(allowed, scale, queries, key_vecs)
    grad_val = contract_rows(attn_prob.astype(jnp.bfloat16), grad_att)
    grad_prob = contract_cols(grad_att, val_vecs)
    grad_score = attn_prob * (grad_prob - jnp.sum(attn_prob * grad_prob, axis=-1, keepdims=True))
    score_low = grad_score.astype(jnp.bfloat16)
    grad_query = jnp.dot(score_low, key_vecs, preferred_element_type=jnp.float32) * scale
    grad_key = contract_rows(score_low, queries) * scale
    return (grad_query, grad_key, grad_val)


def split_heads(qkv_rows, head_count):
    row_count = qkv_rows.shape[0]
    return qkv_rows.reshape(row_count, 3, head_count, -1).transpose(1, 2, 0, 3)


def attention_forward(normed, w_qkv, w_out, allowed, head_count):
    row_count = normed.shape[0]
    qkv_rows = jnp.dot(normed, w_qkv, preferred_element_type=jnp.float32).astype(jnp.bfloat16)
    split_qkv = split_heads(qkv_rows, head_count)
    scale = split_qkv.shape[-1] ** (-0.5)
    attended = lax.map(
        partial(head_forward, allowed, scale), (split_qkv[0], split_qkv[1], split_qkv[2])
    )
    merged = attended.transpose(1, 0, 2).reshape(row_count, -1).astype(jnp.bfloat16)
    branch = jnp.dot(merged, w_out, preferred_element_type=jnp.float32)
    return (branch, qkv_rows, merged)


def attention_backward(grad_branch, qkv_rows, w_qkv, w_out, allowed, head_count):
    row_count = qkv_rows.shape[0]
    grad_merged = contract_cols(grad_branch, w_out).astype(jnp.bfloat16)
    grad_heads = grad_merged.reshape(row_count, head_count, -1).transpose(1, 0, 2)
    split_qkv = split_heads(qkv_rows, head_count)
    scale = split_qkv.shape[-1] ** (-0.5)
    grad_query, grad_key, grad_val = lax.map(
        partial(head_backward, allowed, scale),
        (split_qkv[0], split_qkv[1], split_qkv[2], grad_heads),
    )
    grad_qkv = (
        jnp.stack([grad_query, grad_key, grad_val])
        .transpose(2, 0, 1, 3)
        .reshape(row_count, -1)
        .astype(jnp.bfloat16)
    )
    normalized_gradient = contract_cols(grad_qkv, w_qkv)
    return (normalized_gradient, grad_qkv)


MESH = pl.DeviceIdType.MESH


class Spot:
    def __init__(self):
        chip = lax.axis_index("wide")
        core = lax.axis_index("narrow")
        z, y, x = lax.div(chip, 4), lax.rem(lax.div(chip, 2), 2), lax.rem(chip, 2)
        half = lax.div(z, 2)
        toward = 1 - 2 * half
        self.chip, self.core, self.z, self.y, self.x = chip, core, z, y, x
        self.half = half
        self.middle = z + half * (3 - 2 * z)
        self.is_middle = self.middle == 1
        self.is_end = self.middle == 0
        self.plane = 2 * y + x
        self.inner = ((z + toward) * 4 + self.plane, core)
        self.outer = ((z - toward) * 4 + self.plane, core)
        self.first_plane = 2 * lax.rem(y + core, 2) + lax.rem(x + 1 - core, 2)
        self.second_plane = 2 * lax.rem(y + 1 - core, 2) + lax.rem(x + core, 2)
        self.far_plane = 3 - self.plane
        self.first = (z * 4 + self.first_plane, core)
        self.second = (z * 4 + self.second_plane, core)
        self.far = (z * 4 + self.far_plane, core)
        self.twin = (chip, 1 - core)
        self.mates = (
            (self.first_plane, self.first),
            (self.second_plane, self.second),
            (self.far_plane, self.far),
        )
        self.line = [
            (lax.rem(z + j, 4), (lax.rem(z + j, 4) * 4 + self.plane, core)) for j in (1, 2, 3)
        ]

    def layer(self, mirrored):
        return mirrored + self.half * (3 - 2 * mirrored)

    def arrival(self, k):
        return (self.z, self.layer(1 - self.middle), self.layer(2), self.layer(3))[k]


def greet(spot):
    barrier = pltpu.get_barrier_semaphore()
    for device in [spot.twin] + [device for _, device in spot.mates + tuple(spot.line)]:
        pl.semaphore_signal(barrier, inc=1, device_id=device, device_id_type=MESH)
    pl.semaphore_wait(barrier, 7)


def remote(src, dst, send, recv, device):
    return pltpu.make_async_remote_copy(
        src_ref=src,
        dst_ref=dst,
        send_sem=send,
        recv_sem=recv,
        device_id=device,
        device_id_type=MESH,
    )


class Exchange:
    def __init__(self, places, mine, src, dst, send, recv):
        self.places, self.mine = places, mine
        self.src, self.dst = src, dst
        self.send, self.recv = send, recv

    def copy(self, i):
        place, device = self.places[i]
        return remote(
            self.src(place), self.dst(self.mine), self.send.at[i], self.recv.at[self.mine], device
        )

    def start(self):
        for i in range(3):
            self.copy(i).start()

    def arrive(self):
        for place, device in self.places:
            ref = self.dst(place)
            remote(ref, ref, self.send.at[0], self.recv.at[place], device).wait_recv()

    def drain(self):
        for i in range(3):
            self.copy(i).wait_send()


class LineSum:
    def __init__(self, spot, part, slot, send, recv):
        self.spot, self.part, self.slot = spot, part, slot
        self.send, self.recv = send, recv

    def layer(self, k):
        spot = self.spot
        return (spot.layer(3), spot.layer(2), spot.layer(1 - spot.middle), spot.z)[k]

    def copy(self, k, slot, device):
        return remote(
            self.part(self.layer(k)), self.slot(slot), self.send.at[k], self.recv.at[slot], device
        )

    def from_end(self, k):
        return self.copy(k, k, self.spot.inner)

    def from_middle(self, k):
        return self.copy(k, 3 + k, self.spot.inner) if k < 2 else self.copy(2, 3, self.spot.outer)

    def arrived(self, slot):
        self.copy(0, slot, self.spot.inner).wait_recv()
        return self.slot(slot)

    def send_end(self, k):
        pl.when(self.spot.is_end)(lambda: self.from_end(k).start())

    def send_middle(self, k):
        @pl.when(self.spot.is_middle)
        def _():
            source, part = self.arrived((0, 1, 3)[k]), self.part(self.layer(k))
            for i in range(part.shape[0]):
                part[i] += source[i]
            self.from_middle(k).start()

    def total(self, put):
        def add(*slots):
            sources = [self.arrived(slot) for slot in slots]
            part = self.part(self.spot.z)
            for i in range(part.shape[0]):
                value = part[i].astype(jnp.float32)
                for source in sources:
                    value += source[i].astype(jnp.float32)
                put(i, value)

        pl.when(self.spot.is_end)(lambda: add(3))
        pl.when(self.spot.is_middle)(lambda: add(2, 4))

    def drain(self):
        for k in range(3):
            self.from_end(k).wait_send()


class LineGather:
    def __init__(self, spot, part, send, recv):
        self.spot, self.part = spot, part
        self.send, self.recv = send, recv

    def copy(self, z, send, device):
        ref = self.part(z)
        return remote(ref, ref, self.send.at[send], self.recv.at[z], device)

    def own(self, inward):
        spot = self.spot
        return self.copy(spot.z, 0 if inward else 1, spot.inner if inward else spot.outer)

    def onward(self, k):
        spot = self.spot
        return self.copy(spot.arrival(k), 1 + k, spot.inner if k == 1 else spot.outer)

    def open(self):
        self.own(True).start()
        pl.when(self.spot.is_middle)(lambda: self.own(False).start())

    def get(self, k):
        self.copy(self.spot.arrival(k), 0, self.spot.inner).wait_recv()

    def pass_on(self, k):
        @pl.when(self.spot.is_middle)
        def _():
            self.get(k)
            self.onward(k).start()

    def take(self, k):
        pl.when(self.spot.is_end)(lambda: self.get(k))

    def drain(self):
        self.own(True).wait_send()

        @pl.when(self.spot.is_middle)
        def _():
            self.own(False).wait_send()
            for k in (1, 2, 3):
                self.onward(k).wait_send()


class Gather:
    def __init__(self, spot, held, stage, apart, swap_sems, send, recv):
        self.spot, self.held = spot, held
        self.stage, self.apart, self.swap_sems = stage, apart, swap_sems
        self.send, self.recv = send, recv
        self.whole = apart.shape[1] == 48
        self.line = LineGather(
            spot,
            lambda z: held.at[spot.core, pl.ds(4 * z, 4), 3],
            send.at[pl.ds(24, 5)],
            recv.at[pl.ds(23, 4)],
        )

    def block(self, z, plane):
        return self.held.at[self.spot.core, z * 4 + plane, 0:3]

    def last(self, plane):
        return self.held.at[self.spot.core, self.spot.z * 4 + plane, 3]

    def copy(self, ref, send, recv, device):
        return remote(ref, ref, self.send.at[send], self.recv.at[recv], device)

    def mine(self):
        core = self.spot.core
        if self.whole:
            return self.stage.at[pl.ds(2 * core, 2)]
        return self.stage.at[:, pl.ds(pl.multiple_of(core * 24, 8), 24), :]

    def swap(self):
        return remote(
            self.apart, self.mine(), self.swap_sems.at[0], self.swap_sems.at[1], self.spot.twin
        )

    def open(self, piece):
        core = self.spot.core
        for chunk in range(self.apart.shape[0]):
            self.apart[chunk] = piece(1 - core, chunk).astype(jnp.float32)
        self.swap().start()
        place = self.mine()
        for chunk in range(self.apart.shape[0]):
            place[chunk] = piece(core, chunk).astype(jnp.float32)

    def own(self):
        spot = self.spot
        self.swap().wait_recv()
        self.held[spot.core, spot.chip] = self.stage[...].astype(jnp.bfloat16)
        self.z_own(True).start()
        pl.when(spot.is_middle)(lambda: self.z_own(False).start())
        self.last_first().start()
        self.last_second(False).start()

    def z_own(self, inward):
        spot = self.spot
        return self.copy(
            self.block(spot.z, spot.plane),
            0 if inward else 1,
            spot.z,
            spot.inner if inward else spot.outer,
        )

    def z_pass(self, k):
        spot = self.spot
        z = spot.arrival(k)
        return self.copy(
            self.block(z, spot.plane), 1 + k, z, spot.inner if k == 1 else spot.outer
        )

    def first_copy(self, k):
        z = self.spot.arrival(k)
        return self.copy(self.block(z, self.spot.plane), 5 + k, 4 + z, self.spot.first)

    def second_copy(self, k):
        z = self.spot.arrival(k)
        return self.copy(self.block(z, self.spot.plane), 9 + k, 8 + z, self.spot.second)

    def second_pass(self, k):
        z = self.spot.arrival(k)
        return self.copy(self.block(z, self.spot.first_plane), 13 + k, 12 + z, self.spot.second)

    def twin_copy(self, half, k):
        z = self.spot.arrival(k)
        ref = self.held.at[half, pl.ds(z * 4, 4), 0:3]
        return self.copy(ref, 17 + k, 16 + z, self.spot.twin)

    def last_first(self):
        return self.copy(self.last(self.spot.plane), 21, 20, self.spot.first)

    def last_second(self, onward):
        spot = self.spot
        plane = spot.first_plane if onward else spot.plane
        return self.copy(self.last(plane), 23 if onward else 22, 22 if onward else 21, spot.second)

    def last_twin(self, half, k):
        z = self.spot.arrival(k)
        ref = self.held.at[half, pl.ds(z * 4, 4), 3]
        return self.copy(ref, 29 + k, 27 + z, self.spot.twin)

    def get(self, k):
        spot = self.spot
        z = spot.arrival(k)
        self.copy(self.block(z, spot.plane), 0, z, spot.inner).wait_recv()

    def pass_on(self, k):
        @pl.when(self.spot.is_middle)
        def _():
            self.get(k)
            self.z_pass(k).start()

    def spread(self, k):
        if k:
            pl.when(self.spot.is_end)(lambda: self.get(k))
        self.first_copy(k).start()
        self.second_copy(k).start()

    def along_first(self, k):
        spot = self.spot
        z = spot.arrival(k)
        self.copy(self.block(z, spot.first_plane), 0, 4 + z, spot.first).wait_recv()
        self.second_pass(k).start()

    def along_second(self, k):
        spot = self.spot
        z = spot.arrival(k)
        self.copy(self.block(z, spot.second_plane), 0, 8 + z, spot.second).wait_recv()
        self.copy(self.block(z, spot.far_plane), 0, 12 + z, spot.second).wait_recv()
        self.twin_copy(spot.core, k).start()

    def last_along_first(self):
        spot = self.spot
        self.copy(self.last(spot.first_plane), 0, 20, spot.first).wait_recv()
        self.last_second(True).start()

    def last_along_second(self):
        spot = self.spot
        self.copy(self.last(spot.second_plane), 0, 21, spot.second).wait_recv()
        self.copy(self.last(spot.far_plane), 0, 22, spot.second).wait_recv()
        self.line.open()
        self.last_twin(spot.core, 0).start()

    def last_along_z(self, k):
        self.line.take(k)
        self.last_twin(self.spot.core, k).start()

    def landed(self):
        for k in range(4):
            self.twin_copy(1 - self.spot.core, k).wait_recv()
            self.last_twin(1 - self.spot.core, k).wait_recv()

    def drain(self):
        spot = self.spot
        self.z_own(True).wait_send()

        @pl.when(spot.is_middle)
        def _():
            self.z_own(False).wait_send()
            for k in (1, 2, 3):
                self.z_pass(k).wait_send()

        for k in range(4):
            self.first_copy(k).wait_send()
            self.second_copy(k).wait_send()
            self.second_pass(k).wait_send()
            self.twin_copy(spot.core, k).wait_send()
            self.last_twin(spot.core, k).wait_send()
        self.last_first().wait_send()
        self.last_second(False).wait_send()
        self.last_second(True).wait_send()
        self.line.drain()


class Scatter:
    def __init__(
        self, spot, sums, from_second, from_first, from_z, last_pair, last_one, last_z, final,
        theirs, send, recv, credit, owed,
    ):
        self.spot, self.sums = spot, sums
        self.from_second, self.from_first = from_second, from_first
        self.last_pair, self.last_one = last_pair, last_one
        self.final, self.theirs = final, theirs
        self.send, self.recv, self.credit = send, recv, credit
        self.owed, self.whole = owed, theirs.shape[1] == 48
        self.line = LineSum(
            spot,
            lambda z: sums.at[pl.ds(12 * z, 3)],
            lambda i: from_z.at[i],
            send.at[pl.ds(8, 3)],
            recv.at[pl.ds(8, 5)],
        )
        self.last_line = LineSum(
            spot,
            lambda z: sums.at[pl.ds(48 + 4 * z, 4)],
            lambda i: last_z.at[i],
            send.at[pl.ds(12, 3)],
            recv.at[pl.ds(14, 5)],
        )

    def place(self, chip, chunk):
        spot = self.spot
        z, y, x = chip // 4, (chip // 2) % 2, chip % 2
        other_y, other_x = lax.rem(spot.y + y, 2), lax.rem(spot.x + x, 2)
        second = other_y * (1 - spot.core) + other_x * spot.core
        first = other_x * (1 - spot.core) + other_y * spot.core
        block = 4 * z + 2 * second + first
        return 48 + block if chunk == 3 else 3 * block + chunk

    def second_copy(self, k):
        z = self.line.layer(k)
        return remote(
            self.sums.at[pl.ds(12 * z + 6, 6)],
            self.from_second.at[z],
            self.send.at[k],
            self.recv.at[z],
            self.spot.second,
        )

    def first_copy(self, k):
        z = self.line.layer(k)
        return remote(
            self.sums.at[pl.ds(12 * z + 3, 3)],
            self.from_first.at[z],
            self.send.at[4 + k],
            self.recv.at[4 + z],
            self.spot.first,
        )

    def last_second_copy(self):
        return remote(
            self.sums.at[pl.ds(48 + 4 * self.spot.z + 2, 2)],
            self.last_pair,
            self.send.at[15],
            self.recv.at[19],
            self.spot.second,
        )

    def last_first_copy(self):
        return remote(
            self.sums.at[48 + 4 * self.spot.z + 1],
            self.last_one,
            self.send.at[16],
            self.recv.at[20],
            self.spot.first,
        )

    def swap(self):
        core = self.spot.core
        if self.whole:
            src = self.final.at[pl.ds(2 * (1 - core), 2)]
        else:
            src = self.final.at[:, pl.ds(pl.multiple_of((1 - core) * 24, 8), 24), :]
        return remote(src, self.theirs, self.send.at[11], self.recv.at[13], self.spot.twin)

    def wait_credit(self):
        spot = self.spot
        if self.owed:
            for kind in range(3):
                pl.semaphore_wait(self.credit.at[kind], 1)
            pl.when(spot.is_middle)(lambda: pl.semaphore_wait(self.credit.at[3], 1))

    def add_second(self, k):
        z = self.line.layer(k)
        self.second_copy(k).wait_recv()
        for i in (3, 4, 5, 0, 1, 2):
            self.sums[12 * z + i] += self.from_second[z, i]
            if i == 5:
                self.first_copy(k).start()

    def add_first(self, k):
        z = self.line.layer(k)
        self.first_copy(k).wait_recv()
        for i in range(3):
            self.sums[12 * z + i] += self.from_first[z, i]
        if k < 3:
            self.line.send_end(k)

    def finish(self):
        def put(i, value):
            self.final[i] = value

        self.line.total(put)

    def last_total(self):
        at = 48 + 4 * self.spot.z

        def put(i, value):
            self.sums[at + i] = value.astype(jnp.bfloat16)

        self.last_line.total(put)
        self.last_second_copy().start()

    def last_add_second(self):
        at = 48 + 4 * self.spot.z
        self.last_second_copy().wait_recv()
        self.sums[at + 1] += self.last_pair[1]
        self.last_first_copy().start()
        self.sums[at] += self.last_pair[0]

    def last_finish(self):
        self.last_first_copy().wait_recv()
        self.final[3] = self.sums[48 + 4 * self.spot.z].astype(jnp.float32) + self.last_one[
            ...
        ].astype(jnp.float32)

    def store(self, put):
        core = self.spot.core
        for chunk in range(self.theirs.shape[0]):
            if self.whole:
                mine = self.final[2 * core + chunk]
            else:
                mine = self.final[chunk, pl.ds(pl.multiple_of(core * 24, 8), 24), :]
            put(core, chunk, mine)
        self.swap().wait_recv()
        for chunk in range(self.theirs.shape[0]):
            put(1 - core, chunk, self.theirs[chunk])
        self.swap().wait_send()

    def drain(self):
        for k in range(4):
            self.second_copy(k).wait_send()
            self.first_copy(k).wait_send()
        self.line.drain()
        self.last_line.drain()
        self.last_second_copy().wait_send()
        self.last_first_copy().wait_send()

    def release(self):
        spot, credit = self.spot, self.credit

        def tell(kind, device):
            pl.semaphore_signal(credit.at[kind], inc=1, device_id=device, device_id_type=MESH)

        tell(0, spot.second)
        tell(1, spot.first)

        @pl.when(spot.is_end)
        def _():
            tell(3, spot.inner)

        @pl.when(spot.is_middle)
        def _():
            tell(2, spot.inner)
            tell(2, spot.outer)


(
    DO_STEPS, DO_COND, DO_MODT, DO_MODZ, DO_MODM, DO_MODROWS, DO_OWN, DO_GZ, DO_GS, DO_GX, DO_GY,
    DO_LX, DO_LY, DO_LP, DO_LZ, DO_LANDED, DO_CWAIT, DO_SS, DO_SY, DO_SX, DO_SZ, DO_SFIN, DO_TE,
    DO_TZ, DO_TTOT, DO_TY, DO_TX, DO_SWAP, DO_RETIRE, DO_ROWM, DO_ROWZ, DO_ROWT, DO_ROWD, DO_MASKS,
    DO_STANDARDIZE, DO_MODULATE, DO_PROJECT, DO_TURNN, DO_TURNA, DO_ATTEND, DO_JOIN, DO_ADD,
    DO_GATE, DO_EXPAND, DO_SENDH, DO_NEEDH, DO_DOWNT, DO_GHID, DO_SENDP, DO_CONTRACT, DO_CLOSE,
    DO_NEEDP, DO_UPT, DO_BACK2, DO_NORMB, DO_SPLIT, DO_ATTB, DO_SENDQ, DO_NEEDG, DO_NEEDQ, DO_OUTT,
    DO_QKVT, DO_BACK, DO_SENTQ,
) = range(64)

ORDER = (
    (DO_MASKS,), (DO_STANDARDIZE, 0), (DO_STEPS, 0), (DO_OWN, 0), (DO_GS, 0, 0), (DO_OWN, 1), (DO_GS, 1, 0),
    (DO_STEPS, 1), (DO_LX, 0), (DO_GZ, 0, 1), (DO_GZ, 0, 2), (DO_GX, 0, 0), (DO_LX, 1), (DO_GZ, 1, 1), (DO_GZ, 1, 2),
    (DO_GS, 0, 1), (DO_GZ, 0, 3), (DO_LY, 0), (DO_COND,), (DO_MODT, 0), (DO_MODT, 1), (DO_MODZ, 0), (DO_GX, 0, 1),
    (DO_GZ, 1, 3), (DO_GY, 0, 0), (DO_GX, 1, 0), (DO_MODZ, 1), (DO_GS, 0, 2), (DO_LP, 0, 1), (DO_LP, 0, 2),
    (DO_GS, 0, 3), (DO_GY, 0, 1), (DO_LZ, 0, 1), (DO_GY, 1, 0), (DO_GS, 1, 1), (DO_MODM, 0), (DO_GX, 0, 2),
    (DO_GX, 0, 3), (DO_GX, 1, 1), (DO_LY, 1), (DO_MODROWS, 0), (DO_GS, 1, 2), (DO_MODULATE, 0), (DO_MODM, 1),
    (DO_GY, 0, 2), (DO_LP, 0, 3), (DO_GY, 0, 3), (DO_LZ, 0, 2), (DO_GS, 1, 3), (DO_GY, 1, 1), (DO_LP, 1, 1),
    (DO_LP, 1, 2), (DO_GX, 1, 2), (DO_LZ, 1, 1), (DO_OWN, 2), (DO_MODROWS, 1), (DO_GS, 2, 0), (DO_LZ, 0, 3),
    (DO_LP, 1, 3), (DO_GX, 1, 3), (DO_LANDED, 0), (DO_PROJECT, 0), (DO_LX, 2), (DO_GY, 1, 2), (DO_LZ, 1, 2),
    (DO_TURNN, 0), (DO_GZ, 2, 1), (DO_GZ, 2, 2), (DO_ATTEND, 0, 0), (DO_GX, 2, 0), (DO_ATTEND, 0, 1), (DO_GS, 2, 1),
    (DO_GY, 1, 3), (DO_LY, 2), (DO_ATTEND, 0, 2), (DO_GZ, 2, 3), (DO_LZ, 1, 3), (DO_GY, 2, 0), (DO_JOIN, 0),
    (DO_GS, 2, 2), (DO_ADD, 0), (DO_TURNA, 0), (DO_STANDARDIZE, 1), (DO_GX, 2, 1), (DO_MODULATE, 1), (DO_GATE, 2),
    (DO_LP, 2, 1), (DO_LP, 2, 2), (DO_LZ, 2, 1), (DO_LANDED, 1), (DO_PROJECT, 1), (DO_GX, 2, 2), (DO_TURNN, 1),
    (DO_GS, 2, 3), (DO_GY, 2, 1), (DO_ATTEND, 1, 0), (DO_OWN, 3), (DO_ATTEND, 1, 1), (DO_LP, 2, 3), (DO_GS, 3, 0),
    (DO_GY, 2, 2), (DO_LZ, 2, 2), (DO_ATTEND, 1, 2), (DO_LX, 3), (DO_GX, 2, 3), (DO_JOIN, 1), (DO_GZ, 3, 1),
    (DO_GZ, 3, 2), (DO_GS, 3, 1), (DO_ADD, 1), (DO_TURNA, 1), (DO_STANDARDIZE, 2), (DO_MODULATE, 2), (DO_GX, 3, 0),
    (DO_LY, 3), (DO_TURNN, 2), (DO_LZ, 2, 3), (DO_GY, 2, 3), (DO_GZ, 3, 3), (DO_GX, 3, 1), (DO_GS, 3, 2),
    (DO_LANDED, 2), (DO_EXPAND, 0), (DO_GY, 3, 0), (DO_SENDH, 0), (DO_EXPAND, 1), (DO_LP, 3, 1), (DO_LP, 3, 2),
    (DO_LZ, 3, 1), (DO_SENDH, 1), (DO_EXPAND, 2), (DO_GY, 3, 1), (DO_SENDH, 2), (DO_GX, 3, 2), (DO_EXPAND, 3),
    (DO_GS, 3, 3), (DO_SENDH, 3), (DO_CWAIT, 0), (DO_NEEDH, 0), (DO_DOWNT, 0), (DO_NEEDH, 1), (DO_DOWNT, 1),
    (DO_NEEDH, 2), (DO_DOWNT, 2), (DO_LP, 3, 3), (DO_GY, 3, 2), (DO_LZ, 3, 2), (DO_NEEDH, 3), (DO_DOWNT, 3),
    (DO_SS, 0, 0), (DO_TE, 0, 0), (DO_GX, 3, 3), (DO_TE, 0, 1), (DO_SS, 0, 1), (DO_TE, 0, 2), (DO_LZ, 3, 3),
    (DO_SY, 0, 0), (DO_SS, 0, 2), (DO_TZ, 0, 0), (DO_GY, 3, 3), (DO_LANDED, 3), (DO_GHID, 0), (DO_GHID, 1),
    (DO_TZ, 0, 1), (DO_SY, 0, 1), (DO_SENDP,), (DO_GHID, 2), (DO_SX, 0, 0), (DO_SS, 0, 3), (DO_GHID, 3),
    (DO_TZ, 0, 2), (DO_NEEDP,), (DO_CWAIT, 1), (DO_SY, 0, 2), (DO_UPT, 3), (DO_UPT, 0), (DO_TE, 1, 0), (DO_SX, 0, 1),
    (DO_UPT, 1), (DO_UPT, 2), (DO_SS, 1, 0), (DO_CONTRACT,), (DO_SZ, 0, 0), (DO_SX, 0, 2), (DO_SY, 0, 3), (DO_CLOSE,),
    (DO_TTOT, 0), (DO_SS, 1, 1), (DO_BACK2, 0), (DO_TZ, 1, 0), (DO_BACK2, 1), (DO_SY, 1, 0), (DO_BACK2, 2),
    (DO_TE, 1, 1), (DO_SX, 0, 3), (DO_SZ, 0, 1), (DO_SZ, 0, 2), (DO_TY, 0), (DO_SS, 1, 2), (DO_BACK2, 3),
    (DO_NORMB, 2), (DO_TE, 1, 2), (DO_GATE, 1), (DO_SS, 1, 3), (DO_SPLIT, 1), (DO_SX, 1, 0), (DO_SY, 1, 1),
    (DO_ATTB, 1, 0), (DO_TX, 0), (DO_TZ, 1, 1), (DO_TZ, 1, 2), (DO_SFIN, 0), (DO_SWAP, 0), (DO_SY, 1, 2),
    (DO_ATTB, 1, 1), (DO_RETIRE, 0), (DO_SX, 1, 1), (DO_CWAIT, 2), (DO_NEEDG, 1), (DO_OUTT, 1), (DO_SY, 1, 3),
    (DO_SZ, 1, 0), (DO_ATTB, 1, 2), (DO_TTOT, 1), (DO_TE, 2, 0), (DO_SX, 1, 2), (DO_SENDQ, 1), (DO_BACK, 1, 0),
    (DO_SX, 1, 3), (DO_SZ, 1, 1), (DO_NEEDQ, 1), (DO_QKVT, 1, 0), (DO_QKVT, 1, 1), (DO_TY, 1), (DO_SZ, 1, 2),
    (DO_QKVT, 1, 2), (DO_TE, 2, 1), (DO_SS, 2, 0), (DO_BACK, 1, 1), (DO_BACK, 1, 2), (DO_TZ, 2, 0), (DO_SS, 2, 1),
    (DO_TX, 1), (DO_NORMB, 1), (DO_ROWM, 1), (DO_TE, 2, 2), (DO_SFIN, 1), (DO_SWAP, 1), (DO_SENTQ, 1), (DO_GATE, 0),
    (DO_SY, 2, 0), (DO_SPLIT, 0), (DO_ATTB, 0, 0), (DO_TZ, 2, 1), (DO_TZ, 2, 2), (DO_SY, 2, 1), (DO_ATTB, 0, 1),
    (DO_ROWZ, 1), (DO_SS, 2, 2), (DO_RETIRE, 1), (DO_SX, 2, 0), (DO_CWAIT, 3), (DO_NEEDG, 0), (DO_OUTT, 0),
    (DO_SS, 2, 3), (DO_ATTB, 0, 2), (DO_TTOT, 2), (DO_SX, 2, 1), (DO_SENDQ, 0), (DO_BACK, 0, 0), (DO_SY, 2, 2),
    (DO_NEEDQ, 0), (DO_QKVT, 0, 0), (DO_QKVT, 0, 1), (DO_QKVT, 0, 2), (DO_TE, 3, 0), (DO_SY, 2, 3), (DO_BACK, 0, 1),
    (DO_TY, 2), (DO_SS, 3, 0), (DO_BACK, 0, 2), (DO_SX, 2, 2), (DO_ROWT, 1), (DO_SZ, 2, 0), (DO_NORMB, 0),
    (DO_ROWM, 0), (DO_SX, 2, 3), (DO_SZ, 2, 1), (DO_SS, 3, 1), (DO_ROWD, 1), (DO_SENTQ, 0), (DO_TX, 2), (DO_TE, 3, 1),
    (DO_SY, 3, 0), (DO_TZ, 3, 0), (DO_SZ, 2, 2), (DO_SS, 3, 2), (DO_ROWZ, 0), (DO_SS, 3, 3), (DO_SY, 3, 1),
    (DO_SX, 3, 0), (DO_SFIN, 2), (DO_SWAP, 2), (DO_TZ, 3, 1), (DO_RETIRE, 2), (DO_SY, 3, 2), (DO_TE, 3, 2),
    (DO_TZ, 3, 2), (DO_SX, 3, 1), (DO_ROWT, 0), (DO_SZ, 3, 0), (DO_ROWD, 0), (DO_SY, 3, 3), (DO_SX, 3, 2),
    (DO_TTOT, 3), (DO_SX, 3, 3), (DO_SZ, 3, 1), (DO_SZ, 3, 2), (DO_TY, 3), (DO_TX, 3), (DO_SFIN, 3), (DO_SWAP, 3),
    (DO_RETIRE, 3),
)


def dot(left, right):
    return jnp.dot(left, right, preferred_element_type=jnp.float32)


def layer_kernel(
    tokens,
    cotangent,
    steps,
    seg_ids,
    frame_ids,
    patch_ids,
    b_ada,
    w_ada,
    w_qkv_s,
    w_out_s,
    w_qkv_t,
    w_out_t,
    w_up,
    w_down,
    o_layer,
    o_tokens,
    cond,
    all_rows_mod,
    o_qkv_s,
    o_out_s,
    o_qkv_t,
    o_out_t,
    o_up,
    o_down,
    held,
    stage,
    apart,
    apart_down,
    sums,
    from_second,
    from_first,
    from_z,
    last_pair,
    last_one,
    last_z,
    all_steps,
    bias,
    ids,
    mod,
    tally,
    rows_mod,
    xhat,
    deviation,
    normed,
    attended,
    turned,
    hidden_turned,
    qkv,
    probs,
    branch,
    stream,
    grad,
    hidden,
    slope,
    grad_pre_twin,
    gated,
    gated_twin,
    grad_attended,
    grad_qkv_twin,
    disallowed,
    swap_sems,
    gather_send,
    gather_recv,
    scatter_send,
    scatter_recv,
    credit,
    twin_send,
    twin_recv,
    step_send,
    step_recv,
    mod_send,
    mod_recv,
    row_send,
    row_recv,
):
    width, tok = tokens.shape[1], tokens.shape[0]
    f32, bf16 = jnp.float32, jnp.bfloat16
    spot = Spot()
    core = spot.core
    grad_qkv, grad_normed = hidden, stream
    greet(spot)

    def attention_piece(w_qkv, w_out):
        def piece(half, chunk):
            if chunk < 3:
                return w_qkv[:, pl.ds(pl.multiple_of(half * 1152 + chunk * 384, 128), 384)]
            return w_out[:, pl.ds(pl.multiple_of(half * 384, 128), 384)]

        return piece

    def up_piece(half, chunk):
        return w_up[:, pl.ds(pl.multiple_of(half * 1536 + chunk * 384, 128), 384)]

    def down_piece(half, chunk):
        return w_down[chunk * 48 : chunk * 48 + 48, pl.ds(pl.multiple_of(half * 384, 128), 384)]

    pieces = (
        attention_piece(w_qkv_s, w_out_s),
        attention_piece(w_qkv_t, w_out_t),
        up_piece,
        down_piece,
    )
    gathers = [
        Gather(
            spot,
            held.at[g],
            stage.at[g],
            apart.at[g] if g < 3 else apart_down,
            swap_sems.at[g],
            gather_send.at[g],
            gather_recv.at[g],
        )
        for g in range(4)
    ]
    scatters = [
        Scatter(
            spot,
            sums.at[n % 2],
            from_second.at[n % 2],
            from_first.at[n % 2],
            from_z.at[n % 2],
            last_pair.at[n % 2],
            last_one.at[n % 2],
            last_z.at[n % 2],
            stage.at[3 - n],
            apart_down if n == 0 else apart.at[3 - n],
            scatter_send.at[n],
            scatter_recv.at[n],
            credit.at[n % 2],
            n >= 2,
        )
        for n in range(4)
    ]

    def put_attention(o_qkv, o_out):
        def put(half, chunk, rows):
            if chunk < 3:
                o_qkv[:, pl.ds(pl.multiple_of(half * 1152 + chunk * 384, 128), 384)] = rows
            else:
                o_out[:, pl.ds(pl.multiple_of(half * 384, 128), 384)] = rows

        return put

    def put_up(half, chunk, rows):
        o_up[:, pl.ds(pl.multiple_of(half * 1536 + chunk * 384, 128), 384)] = rows

    def put_down(half, chunk, rows):
        o_down[chunk * 48 : chunk * 48 + 48, pl.ds(pl.multiple_of(half * 384, 128), 384)] = rows

    puts = (put_down, put_up, put_attention(o_qkv_t, o_out_t), put_attention(o_qkv_s, o_out_s))

    def to_twin(index, src, dst):
        return remote(src, dst, twin_send.at[index], twin_recv.at[index], spot.twin)

    def turned_copy(i):
        return to_twin(i, turned.at[i, 0], turned.at[i, 1])

    def hidden_copy(i):
        rows = pl.ds(768 * i, 768)
        return to_twin(12 + i, hidden_turned.at[0, rows], hidden_turned.at[1, rows])

    def gated_copy(j):
        theirs = pl.multiple_of((1 - core) * 384, 128)
        return to_twin(6 + j, gated.at[j, :, pl.ds(theirs, 384)], gated_twin.at[j])

    def grad_pre_copy():
        theirs = pl.multiple_of((1 - core) * 1536, 128)
        return to_twin(9, slope.at[:, pl.ds(theirs, 1536)], grad_pre_twin)

    def grad_qkv_copy(j):
        theirs = pl.multiple_of((1 - core) * 1152, 128)
        return to_twin(10 + j, grad_qkv.at[:, pl.ds(theirs, 1152)], grad_qkv_twin.at[j])

    def step_twin(owner):
        ref = all_steps.at[spot.z, spot.plane, owner]
        return remote(ref, ref, step_send.at[0], step_recv.at[0], spot.twin)

    step_line = Exchange(
        spot.line,
        spot.z,
        lambda z: all_steps.at[spot.z, spot.plane],
        lambda z: all_steps.at[z, spot.plane],
        step_send.at[pl.ds(1, 3)],
        step_recv.at[pl.ds(4, 4)],
    )
    step_mates = Exchange(
        spot.mates,
        spot.plane,
        lambda plane: all_steps.at[:, spot.plane],
        lambda plane: all_steps.at[:, plane],
        step_send.at[pl.ds(4, 3)],
        step_recv.at[pl.ds(8, 4)],
    )

    def steps_open():
        row = lax.broadcasted_iota(jnp.int32, (8, 128), 0)
        value = jnp.where(row == 0, steps[0, 0], jnp.where(row == 1, steps[0, 1], 0))
        all_steps[spot.z, spot.plane, core] = value.astype(f32)
        step_twin(core).start()

    def steps_line():
        step_twin(1 - core).wait_recv()
        step_line.start()

    def steps_mates():
        step_line.arrive()
        step_mates.start()

    def steps_drain():
        step_twin(core).wait_send()
        step_line.drain()
        step_mates.drain()

    def make_cond():
        step_mates.arrive()
        flat = all_steps[...].reshape(256, 128)
        clip = lax.broadcasted_iota(jnp.int32, (64, 256), 0)
        column = lax.broadcasted_iota(jnp.int32, (64, 256), 1)
        wanted = 64 * ((clip >> 3) & 3) + 16 * ((clip >> 1) & 3) + 8 * (clip >> 5) + (clip & 1)
        times = jnp.dot(
            (column == wanted).astype(f32),
            flat,
            precision=lax.Precision.HIGHEST,
            preferred_element_type=f32,
        )
        first = (spot.chip * 2 + core) * 24
        half_width = width // 2
        feature = first + lax.broadcasted_iota(jnp.int32, (64, 128), 1)
        place = jnp.where(feature < half_width, feature, feature - half_width).astype(f32)
        angle = times * jnp.exp(-math.log(FREQ_BASE) * place / half_width)
        value = jnp.where(feature < half_width, jnp.cos(angle), jnp.sin(angle))
        cond[...] = (value / (1.0 + jnp.exp(-value))).astype(bf16)

    parts = (range(0, 1), range(1, 3))

    def columns_of(j, half, chunk):
        at = 2304 * j + 1152 * half + 384 * chunk
        return slice(at, at + 384)

    def rows_of(chunk):
        return slice(16 * chunk, 16 * chunk + 16)

    class ModPart:
        def __init__(self, part):
            self.part, self.n = part, len(parts[part])
            base, n = 21 * part, self.n
            self.out, self.into, self.sum = (sums.at[1, pl.ds(base + 4 * n * i, 4 * n)] for i in range(3))
            self.own = sums.at[1, pl.ds(base + 16 * n, n)]
            self.line = Exchange(
                spot.line,
                spot.z,
                lambda z: sums.at[1, pl.ds(base + 8 * n + n * z, n)],
                lambda z: sums.at[1, pl.ds(base + 12 * n + n * z, n)],
                mod_send.at[part, pl.ds(1, 3)],
                mod_recv.at[part, pl.ds(4, 4)],
            )
            self.mates = Exchange(
                spot.mates,
                spot.plane,
                lambda plane: self.own,
                lambda plane: sums.at[1, pl.ds(base + 17 * n + n * plane, n)],
                mod_send.at[part, pl.ds(4, 3)],
                mod_recv.at[part, pl.ds(8, 4)],
            )

        def swap(self):
            part = self.part
            return remote(self.out, self.into, mod_send.at[part, 0], mod_recv.at[part, 0], spot.twin)

        def terms(self, owner):
            rows = cond[pl.ds(pl.multiple_of(32 * owner, 32), 32), :24]
            for i, j in enumerate(parts[self.part]):
                for chunk in range(3):
                    left, right = (
                        dot(rows, w_ada[:, columns_of(j, half, chunk)])
                        + bias[0:1, columns_of(j, half, chunk)]
                        for half in range(2)
                    )
                    for z in range(4):
                        own = slice(8 * z, 8 * z + 8)
                        block = jnp.concatenate([left[own], right[own]], axis=0)
                        yield self.n * z + i, rows_of(chunk), block

        def for_twin(self):
            for at, rows, value in self.terms(1 - core):
                self.out[at, rows] = value.astype(bf16)
            self.swap().start()

        def for_line(self):
            self.swap().wait_recv()
            for at, rows, value in self.terms(core):
                self.sum[at, rows] = (value + self.into[at, rows].astype(f32)).astype(bf16)
            self.line.start()

        def for_mates(self):
            self.line.arrive()
            for i in range(self.n):
                value = self.line.src(spot.z)[i].astype(f32)
                for z, _ in spot.line:
                    value += self.line.dst(z)[i].astype(f32)
                self.own[i] = value.astype(bf16)
            self.mates.start()

        def done(self):
            self.mates.arrive()
            row = lax.broadcasted_iota(jnp.int32, (16, 384), 0)
            for i, j in enumerate(parts[self.part]):
                for chunk in range(3):
                    value = self.own[i, rows_of(chunk)].astype(f32)
                    for plane, _ in spot.mates:
                        value += self.mates.dst(plane)[i, rows_of(chunk)].astype(f32)
                    for clip in range(2):
                        for half in range(2):
                            chosen = row == 8 * half + 2 * spot.plane + clip
                            mod[clip : clip + 1, columns_of(j, half, chunk)] = jnp.sum(
                                jnp.where(chosen, value, 0.0), axis=0, keepdims=True
                            )

        def drain(self):
            self.swap().wait_send()
            self.line.drain()
            self.mates.drain()

    class RowPart:
        def __init__(self, part):
            self.part, n = part, len(parts[part])
            self.subs = subs = pl.ds(parts[part][0], n)
            self.mates = Exchange(
                spot.mates,
                spot.plane,
                lambda plane: rows_mod.at[spot.plane, subs],
                lambda plane: rows_mod.at[plane, subs],
                row_send.at[part, pl.ds(4, 3)],
                row_recv.at[part, pl.ds(8, 4)],
            )
            self.line = Exchange(
                spot.line,
                spot.z,
                lambda z: all_rows_mod.at[core, spot.z, subs],
                lambda z: all_rows_mod.at[core, z, subs],
                row_send.at[part, pl.ds(1, 3)],
                row_recv.at[part, pl.ds(4, 4)],
            )

        def swap(self, owner):
            ref = all_rows_mod.at[owner, :, self.subs]
            return remote(ref, ref, row_send.at[self.part, 0], row_recv.at[self.part, 0], spot.twin)

        def for_mates(self):
            row = lax.broadcasted_iota(jnp.int32, (16, 384), 0)
            for j in parts[self.part]:
                for chunk in range(3):
                    value = 0.0
                    for clip in range(2):
                        for half in range(2):
                            chosen = row == 8 * half + 2 * spot.plane + clip
                            own = tally[clip : clip + 1, columns_of(j, half, chunk)]
                            value += jnp.where(chosen, own, 0.0)
                    rows_mod[spot.plane, j, :, 384 * chunk : 384 * chunk + 384] = value.astype(bf16)
            self.mates.start()

        def for_line(self):
            self.mates.arrive()
            for j in parts[self.part]:
                all_rows_mod[core, spot.z, j] = (rows_mod[0, j] + rows_mod[1, j]) + (
                    rows_mod[2, j] + rows_mod[3, j]
                )
            self.line.start()

        def for_twin(self):
            self.line.arrive()
            self.swap(core).start()

        def done(self):
            self.swap(1 - core).wait_recv()

        def drain(self):
            self.swap(core).wait_send()
            self.mates.drain()
            self.line.drain()

    mod_parts = [ModPart(part) for part in range(2)]
    row_parts = [RowPart(part) for part in range(2)]

    def by_rows(action):
        @pl.loop(0, tok // 64)
        def _(i):
            action(pl.ds(pl.multiple_of(i * 64, 64), 64))

    def mod_part(j, component, rows):
        at = (3 * j + component) * width
        second = ids[rows, 2:3] == 1.0
        return jnp.where(second, mod[1:2, at : at + width], mod[0:1, at : at + width])

    def count(j, component, rows, value):
        at = (3 * j + component) * width
        second = ids[rows, 2:3] == 1.0
        tally[0:1, at : at + width] += jnp.sum(jnp.where(second, 0.0, value), axis=0, keepdims=True)
        tally[1:2, at : at + width] += jnp.sum(jnp.where(second, value, 0.0), axis=0, keepdims=True)

    def masks():
        spatial = (seg_ids[...] * 16 + frame_ids[...]).astype(f32)
        temporal = (seg_ids[...] * 16 + patch_ids[...]).astype(f32)
        row = lax.broadcasted_iota(jnp.int32, (8, tok), 0)
        second = seg_ids[...].astype(f32)
        stacked = jnp.where(row == 0, spatial, jnp.where(row == 1, temporal, second))
        ids[...] = stacked.T
        for j, keys in enumerate((spatial, temporal)):
            disallowed[j] = jnp.where(ids[:, j : j + 1] == keys, 0.0, MASKED)
        tally[...] = jnp.zeros_like(tally)
        share = b_ada.shape[1]
        bias[...] = jnp.zeros_like(bias)
        bias[0:1, :share] = b_ada[...].astype(f32)
        bias[...] = pltpu.roll(bias[...], (2 * spot.chip + core) * share, 1)

    def standardize(j):
        def action(rows):
            if j == 0:
                stream[rows] = tokens[rows].astype(f32)
            value = stream[rows]
            center = value - jnp.mean(value, axis=-1, keepdims=True)
            inverse = lax.rsqrt(jnp.mean(center * center, axis=-1, keepdims=True) + EPSILON)
            xhat[j, rows] = (center * inverse).astype(bf16)
            deviation[rows, j : j + 1] = inverse

        by_rows(action)

    def modulate(j):
        def action(rows):
            normed[rows] = (
                xhat[j, rows].astype(f32) * (1.0 + mod_part(j, 1, rows)) + mod_part(j, 0, rows)
            ).astype(bf16)

        by_rows(action)

    def turn(i, source):
        for at in range(0, tok, 128):
            turned[i, 0, :, at : at + 128] = source[at : at + 128, :].T
        turned_copy(i).start()

    def weight(g, half, chunk):
        return held[g, half, :, chunk].reshape(width, 384)

    def project(j):
        @pl.loop(0, 6)
        def _(i):
            half, chunk = lax.div(i, 3), lax.rem(i, 3)
            columns = pl.ds(pl.multiple_of(i * 384, 128), 384)
            qkv[j, :, columns] = dot(normed[...], weight(j, half, chunk)).astype(bf16)

    def head_lanes():
        lane = lax.broadcasted_iota(jnp.int32, (1, 128), 1)
        return lane < 64, lane >= 64

    def head_columns(pair):
        return [pl.ds(pl.multiple_of(part * 768 + pair * 128, 128), 128) for part in range(3)]

    def attend(j, first, last):
        @pl.loop(first, last)
        def _(pair):
            at_q, at_k, at_v = head_columns(pair)
            queries, keys, values = qkv[j, :, at_q], qkv[j, :, at_k], qkv[j, :, at_v]
            results = []
            for head, lanes in enumerate(head_lanes()):
                scaled = jnp.where(lanes, queries, 0.0) * bf16(0.125)
                scores = contract_cols(scaled, keys) + disallowed[j]
                scores = jnp.exp(scores - jnp.max(scores, axis=-1, keepdims=True))
                low = (scores * (1.0 / jnp.sum(scores, axis=-1, keepdims=True))).astype(bf16)
                probs[j, 2 * pair + head] = low
                results.append(dot(low, values))
            attended[:, at_q] = jnp.where(head_lanes()[0], results[0], results[1]).astype(bf16)

    def join(j):
        @pl.loop(0, 2)
        def _(half):
            columns = pl.ds(pl.multiple_of(half * 384, 128), 384)
            branch[j, :, columns] = dot(attended[...], weight(j, half, 3)).astype(bf16)

    def add_branch(j):
        def action(rows):
            stream[rows] += mod_part(j, 2, rows) * branch[j, rows].astype(f32)

        by_rows(action)

    def expand(first, last):
        @pl.loop(first, last)
        def _(i):
            columns = pl.ds(pl.multiple_of(i * 384, 128), 384)
            matrix = weight(2, lax.div(i, 4), lax.rem(i, 4))
            for at in range(0, tok, 128):
                rows = slice(at, at + 128)
                pre = dot(normed[rows], matrix)
                square = pre * pre
                root = math.sqrt(2.0 / math.pi)
                bent = jnp.tanh(root * (pre + 0.044715 * (square * pre)))
                value = (0.5 * pre * (1.0 + bent)).astype(bf16)
                hidden[rows, columns] = value
                hidden_turned[0, columns, rows] = value.T
                slope[rows, columns] = (
                    0.5 * (1.0 + bent)
                    + 0.5 * pre * (1.0 - bent * bent) * (root * (1.0 + 3 * 0.044715 * square))
                ).astype(bf16)

    def gate(j):
        def action(rows):
            value = cotangent[rows].astype(f32) if j == 2 else grad[rows]
            if j == 2:
                grad[rows] = value
            else:
                count(j, 2, rows, value * branch[j, rows].astype(f32))
            gated[j, rows] = (mod_part(j, 2, rows) * value).astype(bf16)

        by_rows(action)
        gated_copy(j).start()

    def own_columns(first, width_of_half):
        return pl.ds(pl.multiple_of(core * width_of_half + first, 128), 384)

    def down_terms(z):
        scatter = scatters[0]
        rows = slice(768 * z, 768 * z + 768)
        value = dot(hidden_turned[0, rows], gated[2, :, own_columns(0, 384)]) + dot(
            hidden_turned[1, rows], gated_twin[2]
        )
        value = value.astype(bf16).reshape(4, 4, 48, 384)
        for plane in range(4):
            sums[0, pl.ds(scatter.place(4 * z + plane, 0), 3)] = value[plane, :3]
            sums[0, scatter.place(4 * z + plane, 3)] = value[plane, 3]

    def column_terms(n, chunk, left, right, right_twin):
        value = dot(turned[left, 0], right) + dot(turned[left, 1], right_twin)
        value = value.astype(bf16).reshape(16, 48, 384)
        for chip in range(16):
            sums[n % 2, scatters[n].place(chip, chunk)] = value[chip]

    def up_terms(chunk):
        column_terms(
            1,
            chunk,
            4,
            slope[:, own_columns(384 * chunk, 1536)],
            grad_pre_twin[:, 384 * chunk : 384 * chunk + 384],
        )

    def out_terms(j):
        column_terms(3 - j, 3, 2 * j + 1, gated[j, :, own_columns(0, 384)], gated_twin[j])

    def qkv_terms(j, chunk):
        column_terms(
            3 - j,
            chunk,
            2 * j,
            grad_qkv[:, own_columns(384 * chunk, 1152)],
            grad_qkv_twin[j, :, 384 * chunk : 384 * chunk + 384],
        )

    def contract():
        @pl.loop(0, 2)
        def _(half):
            columns = pl.ds(pl.multiple_of(half * 384, 128), 384)
            matrix = held[3, half].reshape(3072, 384)
            normed[:, columns] = dot(hidden[...], matrix).astype(bf16)

    def close():
        def action(rows):
            value = normed[rows].astype(f32)
            o_layer[rows] = (stream[rows] + mod_part(2, 2, rows) * value).astype(bf16)
            count(2, 2, rows, cotangent[rows].astype(f32) * value)

        by_rows(action)

    def grad_hidden(step):
        first = 2 * lax.rem(step + 2 - 2 * core, 4)

        @pl.loop(0, 2)
        def _(part):
            i = first + part
            columns = pl.ds(pl.multiple_of(i * 384, 128), 384)
            value = sum(
                contract_cols(
                    gated[2, :, 384 * half : 384 * half + 384],
                    held[3, half, pl.ds(2 * i, 2)].reshape(384, 384),
                )
                for half in range(2)
            )
            slope[:, columns] = (slope[:, columns].astype(f32) * value).astype(bf16)

    def back_project(g, chunks, source, first, last):
        @pl.loop(first, last)
        def _(i):
            columns = pl.ds(pl.multiple_of(i * 384, 128), 384)
            value = contract_cols(
                source[:, columns], weight(g, lax.div(i, chunks), lax.rem(i, chunks))
            )

            @pl.when(i == 0)
            def _():
                grad_normed[...] = value

            @pl.when(i > 0)
            def _():
                grad_normed[...] += value

    def norm_back(j):
        def action(rows):
            value, unit = grad_normed[rows], xhat[j, rows].astype(f32)
            count(j, 0, rows, value)
            count(j, 1, rows, value * unit)
            scaled = value * (1.0 + mod_part(j, 1, rows))
            inner = jnp.mean(scaled * unit, axis=-1, keepdims=True)
            scaled = scaled - jnp.mean(scaled, axis=-1, keepdims=True)
            total = grad[rows] + deviation[rows, j : j + 1] * (scaled - unit * inner)
            if j == 0:
                o_tokens[rows] = total
            else:
                grad[rows] = total

        by_rows(action)

    def split(j):
        value = sum(
            contract_cols(gated[j, :, 384 * half : 384 * half + 384], weight(j, half, 3))
            for half in range(2)
        )
        grad_attended[...] = value.astype(bf16)

    def attend_back(j, first, last):
        @pl.loop(first, last)
        def _(pair):
            at_q, at_k, at_v = head_columns(pair)
            queries, keys, values = qkv[j, :, at_q], qkv[j, :, at_k], qkv[j, :, at_v]
            given = grad_attended[:, at_q]
            grad_q, grad_k, grad_v = [], 0.0, 0.0
            for head, lanes in enumerate(head_lanes()):
                part = jnp.where(lanes, given, 0.0).astype(bf16)
                low = probs[j, 2 * pair + head]
                product = low.astype(f32) * contract_cols(part, values)
                total = jnp.sum(product, axis=-1, keepdims=True)
                scores = ((product - low.astype(f32) * total) * 0.125).astype(bf16)
                grad_v += contract_rows(low, part)
                grad_k += contract_rows(scores, jnp.where(lanes, queries, 0.0).astype(bf16))
                grad_q.append(dot(scores, keys))
            grad_qkv[:, at_q] = jnp.where(head_lanes()[0], grad_q[0], grad_q[1]).astype(bf16)
            grad_qkv[:, at_k] = grad_k.astype(bf16)
            grad_qkv[:, at_v] = grad_v.astype(bf16)

    def each_twin_copy():
        for i in range(5):
            yield turned_copy(i)
        for i in range(4):
            yield hidden_copy(i)
        for j in range(3):
            yield gated_copy(j)
        yield grad_pre_copy()

    def forward_drain():
        steps_drain()
        for part in mod_parts:
            part.drain()
        for gather in gathers:
            gather.swap().wait_send()

    def send_hidden(i):
        if i == 0:
            forward_drain()
        hidden_copy(i).start()

    def need_hidden(i):
        if i == 0:
            gated_copy(2).wait_recv()
        hidden_copy(i).wait_recv()

    def retire(n):
        scatters[n].store(puts[n])
        scatters[n].drain()
        if n < 2:
            scatters[n].release()

    def swap(n):
        scatters[n].swap().start()

    def need(copy, *indices):
        copy(*indices).wait_recv()

    steps_of = {
        DO_STEPS: (steps_line, steps_mates),
        DO_COND: make_cond,
        DO_MODT: lambda part: mod_parts[part].for_twin(),
        DO_MODZ: lambda part: mod_parts[part].for_line(),
        DO_MODM: lambda part: mod_parts[part].for_mates(),
        DO_MODROWS: lambda part: mod_parts[part].done(),
        DO_OWN: lambda g: gathers[g].own(),
        DO_GZ: lambda g, k: gathers[g].pass_on(k),
        DO_GS: lambda g, k: gathers[g].spread(k),
        DO_GX: lambda g, k: gathers[g].along_first(k),
        DO_GY: lambda g, k: gathers[g].along_second(k),
        DO_LX: lambda g: gathers[g].last_along_first(),
        DO_LY: lambda g: gathers[g].last_along_second(),
        DO_LP: lambda g, k: gathers[g].line.pass_on(k),
        DO_LZ: lambda g, k: gathers[g].last_along_z(k),
        DO_LANDED: lambda g: gathers[g].landed(),
        DO_CWAIT: lambda n: scatters[n].wait_credit(),
        DO_SS: lambda n, k: scatters[n].second_copy(k).start(),
        DO_SY: lambda n, k: scatters[n].add_second(k),
        DO_SX: lambda n, k: scatters[n].add_first(k),
        DO_SZ: lambda n, k: scatters[n].line.send_middle(k),
        DO_SFIN: lambda n: scatters[n].finish(),
        DO_TE: lambda n, k: scatters[n].last_line.send_end(k),
        DO_TZ: lambda n, k: scatters[n].last_line.send_middle(k),
        DO_TTOT: lambda n: scatters[n].last_total(),
        DO_TY: lambda n: scatters[n].last_add_second(),
        DO_TX: lambda n: scatters[n].last_finish(),
        DO_SWAP: swap,
        DO_RETIRE: retire,
        DO_ROWM: lambda part: row_parts[part].for_mates(),
        DO_ROWZ: lambda part: row_parts[part].for_line(),
        DO_ROWT: lambda part: row_parts[part].for_twin(),
        DO_ROWD: lambda part: row_parts[part].done(),
        DO_MASKS: masks,
        DO_STANDARDIZE: standardize,
        DO_MODULATE: modulate,
        DO_PROJECT: project,
        DO_TURNN: lambda j: turn(2 * j, normed),
        DO_TURNA: lambda j: turn(2 * j + 1, attended),
        DO_ATTEND: lambda j, i: attend(j, 2 * i, 2 * i + 2),
        DO_JOIN: join,
        DO_ADD: add_branch,
        DO_GATE: gate,
        DO_EXPAND: lambda i: expand(2 * i, 2 * i + 2),
        DO_SENDH: send_hidden,
        DO_NEEDH: need_hidden,
        DO_DOWNT: down_terms,
        DO_GHID: grad_hidden,
        DO_SENDP: lambda: grad_pre_copy().start(),
        DO_CONTRACT: contract,
        DO_CLOSE: close,
        DO_NEEDP: lambda: (need(grad_pre_copy), need(turned_copy, 4)),
        DO_UPT: up_terms,
        DO_BACK2: lambda i: back_project(2, 4, slope, 2 * i, 2 * i + 2),
        DO_NORMB: norm_back,
        DO_SPLIT: split,
        DO_ATTB: lambda j, i: attend_back(j, 2 * i, 2 * i + 2),
        DO_SENDQ: lambda j: grad_qkv_copy(j).start(),
        DO_NEEDG: lambda j: (need(turned_copy, 2 * j + 1), need(gated_copy, j)),
        DO_NEEDQ: lambda j: (
            need(turned_copy, 2 * j),
            need(grad_qkv_copy, j),
        ),
        DO_OUTT: out_terms,
        DO_QKVT: qkv_terms,
        DO_BACK: lambda j, i: back_project(j, 3, grad_qkv, 2 * i, 2 * i + 2),
        DO_SENTQ: lambda j: grad_qkv_copy(j).wait_send(),
    }
    for g, gather in enumerate(gathers):
        gather.open(pieces[g])
    steps_open()
    for name, *indices in ORDER:
        step = steps_of[name]
        if isinstance(step, tuple):
            step[indices[0]]()
        else:
            step(*indices)
    for part in row_parts:
        part.drain()
    for gather in gathers:
        gather.drain()
    for copy in each_twin_copy():
        copy.wait_send()


def finish_kernel(cond, all_rows_mod, *refs):
    sources, o_ada, o_bias = refs[:8], refs[8], refs[9]
    results, held, total, sem = refs[10:18], refs[18:26], refs[26], refs[27]

    def copies(first, second, kind):
        return [
            pltpu.make_async_copy(src, dst, sem.at[kind, i])
            for i, (src, dst) in enumerate(zip(first, second, strict=True))
        ]

    arriving, leaving = copies(sources, held, 0), copies(held, results, 1)
    for copy in arriving:
        copy.start()
    total[...] = jnp.zeros_like(total)
    for j in range(3):
        for half in range(2):
            for chunk in range(3):
                at = 2304 * j + 1152 * half + 384 * chunk
                part = all_rows_mod[:, :, j, :, 384 * chunk : 384 * chunk + 384].astype(jnp.float32)
                part = part[:, :, 8 * half : 8 * half + 8].reshape(64, 384)
                low = part.astype(jnp.bfloat16)
                o_ada[:, at : at + 384] = contract_rows(cond[...], low)[:24]
                total[0:1, at : at + 384] = jnp.sum(part, axis=0, keepdims=True)
        if j == 0:
            for copy, onward in zip(arriving, leaving, strict=True):
                copy.wait()
                onward.start()
    place = lax.axis_index("wide") * 2 + lax.axis_index("narrow")
    share, columns = o_bias.shape[1], total.shape[1]
    turned = pltpu.roll(total[...], lax.rem(columns - place * share, columns), 1)
    o_bias[...] = turned[0:1, :share]
    for copy in leaving:
        copy.wait()


def layer(tokens, cotangent, steps, seg_ids, frame_ids, patch_ids, b_ada, w_ada, *shards):
    f32, bf16 = jnp.float32, jnp.bfloat16
    tok, width = tokens.shape
    block = (4, 48, 384)
    dma, vmem = pltpu.SemaphoreType.DMA, pltpu.VMEM
    in_vmem, in_hbm = pl.BlockSpec(memory_space=vmem), pl.BlockSpec(memory_space=pltpu.HBM)
    outs = pl.pallas_call(
        layer_kernel,
        out_shape=[
            jax.ShapeDtypeStruct((tok, width), bf16),
            jax.ShapeDtypeStruct((tok, width), f32),
            jax.ShapeDtypeStruct((64, 128), bf16),
            jax.ShapeDtypeStruct((2, 4, 3, 16, 1152), bf16),
        ]
        + [jax.ShapeDtypeStruct(shard.shape, f32) for shard in shards],
        in_specs=[in_vmem] * 2 + [pl.BlockSpec(memory_space=pltpu.SMEM)] + [in_vmem] * 11,
        out_specs=[in_vmem] * 10,
        scratch_shapes=[
            vmem((4, 2, 16) + block, bf16),
            vmem((4,) + block, f32),
            vmem((3, 4, 24, 384), f32),
            vmem((2, 48, 384), f32),
            vmem((2, 64, 48, 384), bf16),
            vmem((2, 4, 6, 48, 384), bf16),
            vmem((2, 4, 3, 48, 384), bf16),
            vmem((2, 5, 3, 48, 384), bf16),
            vmem((2, 2, 48, 384), bf16),
            vmem((2, 48, 384), bf16),
            vmem((2, 5) + block, bf16),
            vmem((4, 4, 2, 8, 128), f32),
            vmem((8, w_ada.shape[1]), f32),
            vmem((tok, 8), f32),
            vmem((8, 6912), f32),
            vmem((8, 6912), f32),
            vmem((4, 3, 16, 1152), bf16),
            vmem((3, tok, width), bf16),
            vmem((tok, 128), f32),
            vmem((tok, width), bf16),
            vmem((tok, width), bf16),
            vmem((5, 2, width, tok), bf16),
            vmem((2, 4 * width, tok), bf16),
            vmem((2, tok, 3 * width), bf16),
            vmem((2, HEADS, tok, tok), bf16),
            vmem((2, tok, width), bf16),
            vmem((tok, width), f32),
            vmem((tok, width), f32),
            vmem((tok, 4 * width), bf16),
            vmem((tok, 4 * width), bf16),
            vmem((tok, 2 * width), bf16),
            vmem((3, tok, width), bf16),
            vmem((3, tok, width // 2), bf16),
            vmem((tok, width), bf16),
            vmem((2, tok, 3 * width // 2), bf16),
            vmem((2, tok, tok), f32),
            dma((4, 2)),
            dma((4, 33)),
            dma((4, 31)),
            dma((4, 17)),
            dma((4, 21)),
            pltpu.SemaphoreType.REGULAR((2, 4)),
            dma((16,)),
            dma((16,)),
            dma((7,)),
            dma((12,)),
            dma((2, 7)),
            dma((2, 12)),
            dma((2, 7)),
            dma((2, 12)),
        ],
        compiler_params=pltpu.CompilerParams(
            collective_id=0, has_side_effects=True, vmem_limit_bytes=64 * 2**20
        ),
    )(tokens, cotangent, steps, seg_ids, frame_ids, patch_ids, b_ada, w_ada, *shards)
    sources = (*outs[:2], *outs[4:])
    return pl.pallas_call(
        finish_kernel,
        out_shape=[
            jax.ShapeDtypeStruct(w_ada.shape, f32),
            jax.ShapeDtypeStruct((1, w_ada.shape[1] // 32), f32),
        ]
        + [jax.ShapeDtypeStruct(source.shape, source.dtype) for source in sources],
        in_specs=[in_vmem] * 2 + [in_hbm] * 8,
        out_specs=[in_vmem] * 2 + [in_hbm] * 8,
        scratch_shapes=[vmem(source.shape, source.dtype) for source in sources]
        + [vmem((8, w_ada.shape[1]), f32), dma((2, 8))],
        compiler_params=pltpu.CompilerParams(vmem_limit_bytes=60 * 2**20),
    )(outs[2], outs[3], *sources)


def on_grid(
    tokens,
    seg_ids,
    frame_ids,
    patch_ids,
    timesteps,
    w_ada,
    b_ada,
    w_qkv_spatial,
    w_out_spatial,
    w_qkv_temporal,
    w_out_temporal,
    w_up,
    w_down,
    cotangent,
):
    shards = (w_qkv_spatial, w_out_spatial, w_qkv_temporal, w_out_temporal, w_up, w_down)
    grad_ada, grad_bias, out, grad_tokens, *grads = layer(
        tokens,
        cotangent,
        timesteps[None],
        seg_ids[None],
        frame_ids[None],
        patch_ids[None],
        b_ada[None],
        w_ada,
        *shards,
    )
    return (out, grad_tokens, grad_ada, grad_bias.reshape(-1), *grads)


def on_device(
    tokens,
    seg_ids,
    frame_ids,
    patch_ids,
    timesteps,
    w_ada,
    b_ada,
    w_qkv_spatial,
    w_out_spatial,
    w_qkv_temporal,
    w_out_temporal,
    w_up,
    w_down,
    cotangent,
):
    axes = ("wide", "narrow")
    gathered = (
        None,
        None,
        lax.all_gather(w_qkv_spatial, axes, axis=0, tiled=True),
        lax.all_gather(w_out_spatial, axes, axis=0, tiled=True),
        lax.all_gather(w_qkv_temporal, axes, axis=0, tiled=True),
        lax.all_gather(w_out_temporal, axes, axis=0, tiled=True),
        lax.all_gather(w_up, axes, axis=0, tiled=True),
        lax.all_gather(w_down, axes, axis=0, tiled=True),
    )
    width = tokens.shape[1]
    head_count = HEADS
    clip_count = timesteps.shape[0]
    row_count = w_ada.shape[0]
    place = lax.axis_index(axes)
    all_steps = lax.all_gather(timesteps, axes, axis=0, tiled=True)
    cond_all = jax.nn.silu(time_embed(all_steps, width)).astype(jnp.bfloat16)
    cond_rows = lax.dynamic_slice_in_dim(cond_all, place * row_count, row_count, axis=1)
    all_bias = lax.all_gather(b_ada, axes, axis=0, tiled=True)
    modulation = lax.psum_scatter(
        jnp.dot(cond_rows, w_ada, preferred_element_type=jnp.float32),
        axes,
        scatter_dimension=0,
        tiled=True,
    ) + all_bias.astype(jnp.float32)
    one_hot = (seg_ids[:, None] == jnp.arange(clip_count, dtype=jnp.int32)[None, :]).astype(
        jnp.float32
    )
    offset_first, scale_first, gate_a = sublayer_mod(one_hot, modulation, 0, width)
    offset_second, scale_second, gate_b = sublayer_mod(one_hot, modulation, 1, width)
    offset_third, scale_third, gate_c = sublayer_mod(one_hot, modulation, 2, width)
    same_clip = seg_ids[:, None] == seg_ids[None, :]
    spatial_mask = same_clip & (frame_ids[:, None] == frame_ids[None, :])
    temporal_mask = same_clip & (patch_ids[:, None] == patch_ids[None, :])
    residual_first = tokens.astype(jnp.float32)
    standardized_first, inverse_deviation_first = layer_norm_apply(residual_first)
    normalized_first = (standardized_first * (1.0 + scale_first) + offset_first).astype(
        jnp.bfloat16
    )
    branch_a, qkv_a, merged_a = attention_forward(
        normalized_first, gathered[2], gathered[3], spatial_mask, head_count
    )
    residual_second = residual_first + gate_a * branch_a
    standardized_second, inverse_deviation_second = layer_norm_apply(residual_second)
    normalized_second = (standardized_second * (1.0 + scale_second) + offset_second).astype(
        jnp.bfloat16
    )
    branch_b, qkv_b, merged_b = attention_forward(
        normalized_second, gathered[4], gathered[5], temporal_mask, head_count
    )
    residual_third = residual_second + gate_b * branch_b
    standardized_third, inverse_deviation_third = layer_norm_apply(residual_third)
    normalized_third = (standardized_third * (1.0 + scale_third) + offset_third).astype(
        jnp.bfloat16
    )
    pre_act = jnp.dot(normalized_third, gathered[6], preferred_element_type=jnp.float32)
    act_out, gelu_pull = jax.vjp(jax.nn.gelu, pre_act)
    hidden = act_out.astype(jnp.bfloat16)
    branch_c = jnp.dot(hidden, gathered[7], preferred_element_type=jnp.float32)
    result = residual_third + gate_c * branch_c
    back_weights = gathered
    output_gradient = cotangent.astype(jnp.float32)
    gate_gradient_third = output_gradient * branch_c
    grad_branch_c = (gate_c * output_gradient).astype(jnp.bfloat16)
    grad_hidden = contract_cols(grad_branch_c, back_weights[7])
    grad_pre = gelu_pull(grad_hidden)[0].astype(jnp.bfloat16)
    normalized_gradient_third = contract_cols(grad_pre, back_weights[6])
    residual_gradient = output_gradient + layer_norm_reverse(
        normalized_gradient_third, standardized_third, inverse_deviation_third, scale_third
    )
    gate_gradient_second = residual_gradient * branch_b
    grad_branch_b = (gate_b * residual_gradient).astype(jnp.bfloat16)
    normalized_gradient_second, grad_qkv_t = attention_backward(
        grad_branch_b, qkv_b, back_weights[4], back_weights[5], temporal_mask, head_count
    )
    residual_gradient = residual_gradient + layer_norm_reverse(
        normalized_gradient_second, standardized_second, inverse_deviation_second, scale_second
    )
    gate_gradient_first = residual_gradient * branch_a
    grad_branch_a = (gate_a * residual_gradient).astype(jnp.bfloat16)
    normalized_gradient_first, grad_qkv_s = attention_backward(
        grad_branch_a, qkv_a, back_weights[2], back_weights[3], spatial_mask, head_count
    )
    residual_gradient = residual_gradient + layer_norm_reverse(
        normalized_gradient_first, standardized_first, inverse_deviation_first, scale_first
    )
    grad_mod = jnp.concatenate(
        [
            exact_rows(
                one_hot,
                jnp.concatenate(
                    [
                        normalized_gradient_first,
                        normalized_gradient_first * standardized_first,
                        gate_gradient_first,
                    ],
                    axis=1,
                ),
            ),
            exact_rows(
                one_hot,
                jnp.concatenate(
                    [
                        normalized_gradient_second,
                        normalized_gradient_second * standardized_second,
                        gate_gradient_second,
                    ],
                    axis=1,
                ),
            ),
            exact_rows(
                one_hot,
                jnp.concatenate(
                    [
                        normalized_gradient_third,
                        normalized_gradient_third * standardized_third,
                        gate_gradient_third,
                    ],
                    axis=1,
                ),
            ),
        ],
        axis=1,
    )
    grad_mod_low = grad_mod.astype(jnp.bfloat16)
    all_grad_mod = lax.all_gather(grad_mod_low, axes, axis=0, tiled=True)
    bias_share = lax.psum_scatter(
        jnp.sum(grad_mod, axis=0), axes, scatter_dimension=0, tiled=True
    )

    def share(left, right):
        return lax.psum_scatter(
            contract_rows(left, right).astype(jnp.bfloat16),
            axes,
            scatter_dimension=0,
            tiled=True,
        ).astype(jnp.float32)

    return (
        result.astype(jnp.bfloat16),
        residual_gradient,
        contract_rows(cond_rows, all_grad_mod),
        bias_share,
        share(normalized_first, grad_qkv_s),
        share(merged_a, grad_branch_a),
        share(normalized_second, grad_qkv_t),
        share(merged_b, grad_branch_b),
        share(normalized_third, grad_pre),
        share(hidden, grad_branch_c),
    )


def solution(mesh):
    placed = (
        P(("wide", "narrow"), None),
        P(("wide", "narrow")),
        P(("wide", "narrow")),
        P(("wide", "narrow")),
        P(("wide", "narrow")),
        P(("wide", "narrow"), None),
        P(("wide", "narrow")),
        P(("wide", "narrow"), None),
        P(("wide", "narrow"), None),
        P(("wide", "narrow"), None),
        P(("wide", "narrow"), None),
        P(("wide", "narrow"), None),
        P(("wide", "narrow"), None),
        P(("wide", "narrow"), None),
    )
    grid = dict(mesh.shape) == {"wide": 16, "narrow": 2}
    return jax.shard_map(
        on_grid if grid else on_device,
        mesh=mesh,
        in_specs=placed,
        out_specs=(
            P(("wide", "narrow"), None),
            P(("wide", "narrow"), None),
            P(("wide", "narrow"), None),
            P(("wide", "narrow")),
            P(("wide", "narrow"), None),
            P(("wide", "narrow"), None),
            P(("wide", "narrow"), None),
            P(("wide", "narrow"), None),
            P(("wide", "narrow"), None),
            P(("wide", "narrow"), None),
        ),
        check_vma=False,
    )
```

```python
from functools import partial
import math

import jax
import jax.numpy as jnp
from jax import lax
from jax.experimental import pallas as pl
from jax.experimental.pallas import tpu as pltpu
from jax.sharding import PartitionSpec as P

HEADS = 12


EPSILON = 1e-06
FREQ_BASE = 10000.0
MASKED = -1e30


def time_embed(step_ids, width):
    half_width = width // 2
    frequency = jnp.exp(
        -math.log(FREQ_BASE) * jnp.arange(half_width, dtype=jnp.float32) / half_width
    )
    angles = step_ids.astype(jnp.float32)[:, None] * frequency[None, :]
    return jnp.concatenate([jnp.cos(angles), jnp.sin(angles)], axis=1)


def contract_rows(left, right):
    return lax.dot_general(
        left, right, (((0,), (0,)), ((), ())), preferred_element_type=jnp.float32
    )


def contract_cols(left, right):
    return lax.dot_general(
        left, right, (((1,), (1,)), ((), ())), preferred_element_type=jnp.float32
    )


def exact_rows(left, right):
    return lax.dot_general(
        left,
        right,
        (((0,), (0,)), ((), ())),
        precision=lax.Precision.HIGHEST,
        preferred_element_type=jnp.float32,
    )


def layer_norm_apply(stream):
    center = stream - jnp.mean(stream, axis=-1, keepdims=True)
    inverse_deviation = lax.rsqrt(jnp.mean(center * center, axis=-1, keepdims=True) + EPSILON)
    return (center * inverse_deviation, inverse_deviation)


def layer_norm_reverse(normalized_gradient, standardized_input, inverse_deviation, row_scales):
    input_gradient = normalized_gradient * (1.0 + row_scales)
    mean_removed = input_gradient - jnp.mean(input_gradient, axis=-1, keepdims=True)
    return inverse_deviation * (
        mean_removed
        - standardized_input * jnp.mean(input_gradient * standardized_input, axis=-1, keepdims=True)
    )


def sublayer_mod(one_hot, modulation, sublayer, width):
    table = modulation[:, 3 * width * sublayer : 3 * width * (sublayer + 1)]
    rows_mod = jnp.dot(
        one_hot, table, precision=lax.Precision.HIGHEST, preferred_element_type=jnp.float32
    )
    return (rows_mod[:, :width], rows_mod[:, width : 2 * width], rows_mod[:, 2 * width :])


def head_probs(allowed, scale, queries, key_vecs):
    scores = contract_cols(queries, key_vecs) * scale
    scores = jnp.where(allowed, scores, MASKED)
    return jax.nn.softmax(scores, axis=-1)


def head_forward(allowed, scale, item):
    queries, key_vecs, val_vecs = item
    attn_prob = head_probs(allowed, scale, queries, key_vecs)
    return jnp.dot(attn_prob.astype(jnp.bfloat16), val_vecs, preferred_element_type=jnp.float32)


def head_backward(allowed, scale, item):
    queries, key_vecs, val_vecs, grad_att = item
    attn_prob = head_probs(allowed, scale, queries, key_vecs)
    grad_val = contract_rows(attn_prob.astype(jnp.bfloat16), grad_att)
    grad_prob = contract_cols(grad_att, val_vecs)
    grad_score = attn_prob * (grad_prob - jnp.sum(attn_prob * grad_prob, axis=-1, keepdims=True))
    score_low = grad_score.astype(jnp.bfloat16)
    grad_query = jnp.dot(score_low, key_vecs, preferred_element_type=jnp.float32) * scale
    grad_key = contract_rows(score_low, queries) * scale
    return (grad_query, grad_key, grad_val)


def split_heads(qkv_rows, head_count):
    row_count = qkv_rows.shape[0]
    return qkv_rows.reshape(row_count, 3, head_count, -1).transpose(1, 2, 0, 3)


def attention_forward(normed, w_qkv, w_out, allowed, head_count):
    row_count = normed.shape[0]
    qkv_rows = jnp.dot(normed, w_qkv, preferred_element_type=jnp.float32).astype(jnp.bfloat16)
    split_qkv = split_heads(qkv_rows, head_count)
    scale = split_qkv.shape[-1] ** (-0.5)
    attended = lax.map(
        partial(head_forward, allowed, scale), (split_qkv[0], split_qkv[1], split_qkv[2])
    )
    merged = attended.transpose(1, 0, 2).reshape(row_count, -1).astype(jnp.bfloat16)
    branch = jnp.dot(merged, w_out, preferred_element_type=jnp.float32)
    return (branch, qkv_rows, merged)


def attention_backward(grad_branch, qkv_rows, w_qkv, w_out, allowed, head_count):
    row_count = qkv_rows.shape[0]
    grad_merged = contract_cols(grad_branch, w_out).astype(jnp.bfloat16)
    grad_heads = grad_merged.reshape(row_count, head_count, -1).transpose(1, 0, 2)
    split_qkv = split_heads(qkv_rows, head_count)
    scale = split_qkv.shape[-1] ** (-0.5)
    grad_query, grad_key, grad_val = lax.map(
        partial(head_backward, allowed, scale),
        (split_qkv[0], split_qkv[1], split_qkv[2], grad_heads),
    )
    grad_qkv = (
        jnp.stack([grad_query, grad_key, grad_val])
        .transpose(2, 0, 1, 3)
        .reshape(row_count, -1)
        .astype(jnp.bfloat16)
    )
    normalized_gradient = contract_cols(grad_qkv, w_qkv)
    return (normalized_gradient, grad_qkv)


MESH = pl.DeviceIdType.MESH


class Spot:
    def __init__(self):
        chip = lax.axis_index("wide")
        core = lax.axis_index("narrow")
        z, y, x = lax.div(chip, 4), lax.rem(lax.div(chip, 2), 2), lax.rem(chip, 2)
        half = lax.div(z, 2)
        toward = 1 - 2 * half
        self.chip, self.core, self.z, self.y, self.x = chip, core, z, y, x
        self.half = half
        self.middle = z + half * (3 - 2 * z)
        self.is_middle = self.middle == 1
        self.is_end = self.middle == 0
        self.plane = 2 * y + x
        self.inner = ((z + toward) * 4 + self.plane, core)
        self.outer = ((z - toward) * 4 + self.plane, core)
        self.first_plane = 2 * lax.rem(y + core, 2) + lax.rem(x + 1 - core, 2)
        self.second_plane = 2 * lax.rem(y + 1 - core, 2) + lax.rem(x + core, 2)
        self.far_plane = 3 - self.plane
        self.first = (z * 4 + self.first_plane, core)
        self.second = (z * 4 + self.second_plane, core)
        self.far = (z * 4 + self.far_plane, core)
        self.twin = (chip, 1 - core)
        self.mates = (
            (self.first_plane, self.first),
            (self.second_plane, self.second),
            (self.far_plane, self.far),
        )
        self.line = [
            (lax.rem(z + j, 4), (lax.rem(z + j, 4) * 4 + self.plane, core)) for j in (1, 2, 3)
        ]

    def layer(self, mirrored):
        return mirrored + self.half * (3 - 2 * mirrored)

    def arrival(self, k):
        return (self.z, self.layer(1 - self.middle), self.layer(2), self.layer(3))[k]


def greet(spot):
    barrier = pltpu.get_barrier_semaphore()
    for device in [spot.twin] + [device for _, device in spot.mates + tuple(spot.line)]:
        pl.semaphore_signal(barrier, inc=1, device_id=device, device_id_type=MESH)
    pl.semaphore_wait(barrier, 7)


def remote(src, dst, send, recv, device):
    return pltpu.make_async_remote_copy(
        src_ref=src,
        dst_ref=dst,
        send_sem=send,
        recv_sem=recv,
        device_id=device,
        device_id_type=MESH,
    )


class Exchange:
    def __init__(self, places, mine, src, dst, send, recv):
        self.places, self.mine = places, mine
        self.src, self.dst = src, dst
        self.send, self.recv = send, recv

    def copy(self, i):
        place, device = self.places[i]
        return remote(
            self.src(place), self.dst(self.mine), self.send.at[i], self.recv.at[self.mine], device
        )

    def start(self):
        for i in range(3):
            self.copy(i).start()

    def arrive(self):
        for place, device in self.places:
            ref = self.dst(place)
            remote(ref, ref, self.send.at[0], self.recv.at[place], device).wait_recv()

    def drain(self):
        for i in range(3):
            self.copy(i).wait_send()


class LineSum:
    def __init__(self, spot, part, slot, send, recv):
        self.spot, self.part, self.slot = spot, part, slot
        self.send, self.recv = send, recv

    def layer(self, k):
        spot = self.spot
        return (spot.layer(3), spot.layer(2), spot.layer(1 - spot.middle), spot.z)[k]

    def copy(self, k, slot, device):
        return remote(
            self.part(self.layer(k)), self.slot(slot), self.send.at[k], self.recv.at[slot], device
        )

    def from_end(self, k):
        return self.copy(k, k, self.spot.inner)

    def from_middle(self, k):
        return self.copy(k, 3 + k, self.spot.inner) if k < 2 else self.copy(2, 3, self.spot.outer)

    def arrived(self, slot):
        self.copy(0, slot, self.spot.inner).wait_recv()
        return self.slot(slot)

    def send_end(self, k):
        pl.when(self.spot.is_end)(lambda: self.from_end(k).start())

    def send_middle(self, k):
        @pl.when(self.spot.is_middle)
        def _():
            source, part = self.arrived((0, 1, 3)[k]), self.part(self.layer(k))
            for i in range(part.shape[0]):
                part[i] += source[i]
            self.from_middle(k).start()

    def total(self, put):
        def add(*slots):
            sources = [self.arrived(slot) for slot in slots]
            part = self.part(self.spot.z)
            for i in range(part.shape[0]):
                value = part[i].astype(jnp.float32)
                for source in sources:
                    value += source[i].astype(jnp.float32)
                put(i, value)

        pl.when(self.spot.is_end)(lambda: add(3))
        pl.when(self.spot.is_middle)(lambda: add(2, 4))

    def drain(self):
        for k in range(3):
            self.from_end(k).wait_send()


class LineGather:
    def __init__(self, spot, part, send, recv):
        self.spot, self.part = spot, part
        self.send, self.recv = send, recv

    def copy(self, z, send, device):
        ref = self.part(z)
        return remote(ref, ref, self.send.at[send], self.recv.at[z], device)

    def own(self, inward):
        spot = self.spot
        return self.copy(spot.z, 0 if inward else 1, spot.inner if inward else spot.outer)

    def onward(self, k):
        spot = self.spot
        return self.copy(spot.arrival(k), 1 + k, spot.inner if k == 1 else spot.outer)

    def open(self):
        self.own(True).start()
        pl.when(self.spot.is_middle)(lambda: self.own(False).start())

    def get(self, k):
        self.copy(self.spot.arrival(k), 0, self.spot.inner).wait_recv()

    def pass_on(self, k):
        @pl.when(self.spot.is_middle)
        def _():
            self.get(k)
            self.onward(k).start()

    def take(self, k):
        pl.when(self.spot.is_end)(lambda: self.get(k))

    def drain(self):
        self.own(True).wait_send()

        @pl.when(self.spot.is_middle)
        def _():
            self.own(False).wait_send()
            for k in (1, 2, 3):
                self.onward(k).wait_send()


class Gather:
    def __init__(self, spot, held, stage, apart, swap_sems, send, recv, count):
        self.spot, self.held, self.count = spot, held, count
        self.split = count < 4
        self.stage, self.apart, self.swap_sems = stage, apart, swap_sems
        self.send, self.recv = send, recv
        self.whole = apart.shape[1] == 48
        self.line = LineGather(
            spot,
            lambda z: self.last_layer(spot.core, z),
            send.at[pl.ds(24, 5)],
            recv.at[pl.ds(23, 4)],
        )

    def block(self, z, plane):
        return self.held.at[self.spot.core, z * 4 + plane, 0 : self.count]

    def last_layer(self, half, z):
        return self.held.at[half, pl.ds(z * 4, 4), 3]

    def last(self, plane):
        return self.held.at[self.spot.core, self.spot.z * 4 + plane, 3]

    def copy(self, ref, send, recv, device):
        return remote(ref, ref, self.send.at[send], self.recv.at[recv], device)

    def mine(self):
        core = self.spot.core
        if self.whole:
            return self.stage.at[pl.ds(2 * core, 2)]
        return self.stage.at[:, pl.ds(pl.multiple_of(core * 24, 8), 24), :]

    def swap(self):
        return remote(
            self.apart, self.mine(), self.swap_sems.at[0], self.swap_sems.at[1], self.spot.twin
        )

    def open(self, piece):
        core = self.spot.core
        for chunk in range(self.apart.shape[0]):
            self.apart[chunk] = piece(1 - core, chunk).astype(jnp.float32)
        self.swap().start()
        place = self.mine()
        for chunk in range(self.apart.shape[0]):
            place[chunk] = piece(core, chunk).astype(jnp.float32)

    def own(self):
        spot = self.spot
        self.swap().wait_recv()
        self.held[spot.core, spot.chip] = self.stage[...].astype(jnp.bfloat16)
        self.z_own(True).start()
        pl.when(spot.is_middle)(lambda: self.z_own(False).start())
        if self.split:
            self.last_first().start()
            self.last_second(False).start()

    def z_own(self, inward):
        spot = self.spot
        return self.copy(
            self.block(spot.z, spot.plane),
            0 if inward else 1,
            spot.z,
            spot.inner if inward else spot.outer,
        )

    def z_pass(self, k):
        spot = self.spot
        z = spot.arrival(k)
        return self.copy(
            self.block(z, spot.plane), 1 + k, z, spot.inner if k == 1 else spot.outer
        )

    def first_copy(self, k):
        z = self.spot.arrival(k)
        return self.copy(self.block(z, self.spot.plane), 5 + k, 4 + z, self.spot.first)

    def second_copy(self, k):
        z = self.spot.arrival(k)
        return self.copy(self.block(z, self.spot.plane), 9 + k, 8 + z, self.spot.second)

    def second_pass(self, k):
        z = self.spot.arrival(k)
        return self.copy(self.block(z, self.spot.first_plane), 13 + k, 12 + z, self.spot.second)

    def twin_copy(self, half, k):
        z = self.spot.arrival(k)
        ref = self.held.at[half, pl.ds(z * 4, 4), 0 : self.count]
        return self.copy(ref, 17 + k, 16 + z, self.spot.twin)

    def last_first(self):
        return self.copy(self.last(self.spot.plane), 21, 20, self.spot.first)

    def last_second(self, onward):
        spot = self.spot
        plane = spot.first_plane if onward else spot.plane
        return self.copy(self.last(plane), 23 if onward else 22, 22 if onward else 21, spot.second)

    def last_twin(self, half, k):
        z = self.spot.arrival(k)
        ref = self.last_layer(half, z)
        return self.copy(ref, 29 + k, 27 + z, self.spot.twin)

    def get(self, k):
        spot = self.spot
        z = spot.arrival(k)
        self.copy(self.block(z, spot.plane), 0, z, spot.inner).wait_recv()

    def pass_on(self, k):
        @pl.when(self.spot.is_middle)
        def _():
            self.get(k)
            self.z_pass(k).start()

    def spread(self, k):
        if k:
            pl.when(self.spot.is_end)(lambda: self.get(k))
        self.first_copy(k).start()
        self.second_copy(k).start()

    def along_first(self, k):
        spot = self.spot
        z = spot.arrival(k)
        self.copy(self.block(z, spot.first_plane), 0, 4 + z, spot.first).wait_recv()
        self.second_pass(k).start()

    def along_second(self, k):
        spot = self.spot
        z = spot.arrival(k)
        self.copy(self.block(z, spot.second_plane), 0, 8 + z, spot.second).wait_recv()
        self.copy(self.block(z, spot.far_plane), 0, 12 + z, spot.second).wait_recv()
        self.twin_copy(spot.core, k).start()

    def last_along_first(self):
        spot = self.spot
        self.copy(self.last(spot.first_plane), 0, 20, spot.first).wait_recv()
        self.last_second(True).start()

    def last_along_second(self):
        spot = self.spot
        self.copy(self.last(spot.second_plane), 0, 21, spot.second).wait_recv()
        self.copy(self.last(spot.far_plane), 0, 22, spot.second).wait_recv()
        self.line.open()
        self.last_twin(spot.core, 0).start()

    def last_along_z(self, k):
        self.line.take(k)
        self.last_twin(self.spot.core, k).start()

    def landed(self):
        for k in range(4):
            self.twin_copy(1 - self.spot.core, k).wait_recv()
            if self.split:
                self.last_twin(1 - self.spot.core, k).wait_recv()

    def drain(self):
        spot = self.spot
        self.z_own(True).wait_send()

        @pl.when(spot.is_middle)
        def _():
            self.z_own(False).wait_send()
            for k in (1, 2, 3):
                self.z_pass(k).wait_send()

        for k in range(4):
            self.first_copy(k).wait_send()
            self.second_copy(k).wait_send()
            self.second_pass(k).wait_send()
            self.twin_copy(spot.core, k).wait_send()
            if self.split:
                self.last_twin(spot.core, k).wait_send()
        if self.split:
            self.last_first().wait_send()
            self.last_second(False).wait_send()
            self.last_second(True).wait_send()
            self.line.drain()


class Scatter:
    def __init__(
        self, spot, sums, from_second, from_first, from_z, last_pair, last_one, last_z, final,
        theirs, send, recv, credit, owed,
    ):
        self.spot, self.sums = spot, sums
        self.from_second, self.from_first = from_second, from_first
        self.last_pair, self.last_one = last_pair, last_one
        self.final, self.theirs = final, theirs
        self.send, self.recv, self.credit = send, recv, credit
        self.owed, self.whole = owed, theirs.shape[1] == 48
        self.line = LineSum(
            spot,
            lambda z: sums.at[4 * z, 0:3],
            lambda i: from_z.at[i],
            send.at[pl.ds(8, 3)],
            recv.at[pl.ds(8, 5)],
        )
        self.last_line = LineSum(
            spot,
            lambda z: sums.at[pl.ds(4 * z, 4), 3],
            lambda i: last_z.at[i],
            send.at[pl.ds(12, 3)],
            recv.at[pl.ds(14, 5)],
        )

    def place(self, chip):
        spot = self.spot
        z, y, x = chip // 4, (chip // 2) % 2, chip % 2
        other_y, other_x = lax.rem(spot.y + y, 2), lax.rem(spot.x + x, 2)
        second = other_y * (1 - spot.core) + other_x * spot.core
        first = other_x * (1 - spot.core) + other_y * spot.core
        return 4 * z + 2 * second + first

    def second_copy(self, k):
        z = self.line.layer(k)
        return remote(
            self.sums.at[pl.ds(4 * z + 2, 2), 0:3],
            self.from_second.at[z],
            self.send.at[k],
            self.recv.at[z],
            self.spot.second,
        )

    def first_copy(self, k):
        z = self.line.layer(k)
        return remote(
            self.sums.at[4 * z + 1, 0:3],
            self.from_first.at[z],
            self.send.at[4 + k],
            self.recv.at[4 + z],
            self.spot.first,
        )

    def last_second_copy(self):
        return remote(
            self.sums.at[pl.ds(4 * self.spot.z + 2, 2), 3],
            self.last_pair,
            self.send.at[15],
            self.recv.at[19],
            self.spot.second,
        )

    def last_first_copy(self):
        return remote(
            self.sums.at[4 * self.spot.z + 1, 3],
            self.last_one,
            self.send.at[16],
            self.recv.at[20],
            self.spot.first,
        )

    def swap(self):
        core = self.spot.core
        if self.whole:
            src = self.final.at[pl.ds(2 * (1 - core), 2)]
        else:
            src = self.final.at[:, pl.ds(pl.multiple_of((1 - core) * 24, 8), 24), :]
        return remote(src, self.theirs, self.send.at[11], self.recv.at[13], self.spot.twin)

    def wait_credit(self):
        spot = self.spot
        if self.owed:
            for kind in range(3):
                pl.semaphore_wait(self.credit.at[kind], 1)
            pl.when(spot.is_middle)(lambda: pl.semaphore_wait(self.credit.at[3], 1))

    def add_second(self, k):
        z = self.line.layer(k)
        self.second_copy(k).wait_recv()
        for first in (1, 0):
            for chunk in range(3):
                self.sums[4 * z + first, chunk] += self.from_second[z, first, chunk]
            if first:
                self.first_copy(k).start()

    def add_first(self, k):
        z = self.line.layer(k)
        self.first_copy(k).wait_recv()
        for chunk in range(3):
            self.sums[4 * z, chunk] += self.from_first[z, chunk]
        if k < 3:
            self.line.send_end(k)

    def finish(self):
        def put(i, value):
            self.final[i] = value

        self.line.total(put)

    def last_total(self):
        at = 4 * self.spot.z

        def put(i, value):
            self.sums[at + i, 3] = value.astype(jnp.bfloat16)

        self.last_line.total(put)
        self.last_second_copy().start()

    def last_add_second(self):
        at = 4 * self.spot.z
        self.last_second_copy().wait_recv()
        self.sums[at + 1, 3] += self.last_pair[1]
        self.last_first_copy().start()
        self.sums[at, 3] += self.last_pair[0]

    def last_finish(self):
        self.last_first_copy().wait_recv()
        self.final[3] = self.sums[4 * self.spot.z, 3].astype(jnp.float32) + self.last_one[
            ...
        ].astype(jnp.float32)

    def store(self, put):
        core = self.spot.core
        for chunk in range(self.theirs.shape[0]):
            if self.whole:
                mine = self.final[2 * core + chunk]
            else:
                mine = self.final[chunk, pl.ds(pl.multiple_of(core * 24, 8), 24), :]
            put(core, chunk, mine)
        self.swap().wait_recv()
        for chunk in range(self.theirs.shape[0]):
            put(1 - core, chunk, self.theirs[chunk])
        self.swap().wait_send()

    def drain(self):
        for k in range(4):
            self.second_copy(k).wait_send()
            self.first_copy(k).wait_send()
        self.line.drain()
        self.last_line.drain()
        self.last_second_copy().wait_send()
        self.last_first_copy().wait_send()

    def release(self):
        spot, credit = self.spot, self.credit

        def tell(kind, device):
            pl.semaphore_signal(credit.at[kind], inc=1, device_id=device, device_id_type=MESH)

        tell(0, spot.second)
        tell(1, spot.first)

        @pl.when(spot.is_end)
        def _():
            tell(3, spot.inner)

        @pl.when(spot.is_middle)
        def _():
            tell(2, spot.inner)
            tell(2, spot.outer)


(
    DO_STEPS, DO_COND, DO_MODT, DO_MODZ, DO_MODS, DO_MODM, DO_MODROWS, DO_OWN, DO_GZ, DO_GS, DO_GX,
    DO_GY, DO_LX, DO_LY, DO_LP, DO_LZ, DO_LANDED, DO_CWAIT, DO_SS, DO_SY, DO_SX, DO_SZ, DO_SFIN,
    DO_TE, DO_TZ, DO_TTOT, DO_TY, DO_TX, DO_SWAP, DO_RETIRE, DO_ROWM, DO_ROWZ, DO_ROWP, DO_ROWT,
    DO_ROWD, DO_MASKS, DO_STANDARDIZE, DO_MODULATE, DO_PROJECT, DO_TURNN, DO_TURNA, DO_ATTEND,
    DO_JOIN, DO_ADD, DO_GATE, DO_EXPAND, DO_SENDH, DO_NEEDH, DO_DOWNT, DO_GHID, DO_SENDP,
    DO_CONTRACT, DO_CLOSE, DO_NEEDP, DO_UPT, DO_BACK2, DO_NORMB, DO_SPLIT, DO_ATTB, DO_SENDQ,
    DO_NEEDG, DO_NEEDQ, DO_OUTT, DO_QKVT, DO_BACK, DO_SENTQ,
) = range(66)

ORDER = (
    (DO_CWAIT, 0), (DO_CWAIT, 1), (DO_MASKS,), (DO_STANDARDIZE, 0), (DO_STEPS, 0), (DO_OWN, 0), (DO_GS, 0, 0),
    (DO_OWN, 1), (DO_GS, 1, 0), (DO_STEPS, 1), (DO_LX, 0), (DO_GZ, 0, 1), (DO_GZ, 0, 2), (DO_GS, 0, 1), (DO_GZ, 1, 1),
    (DO_GZ, 1, 2), (DO_GX, 0, 0), (DO_LY, 0), (DO_GS, 0, 2), (DO_GZ, 0, 3), (DO_COND,), (DO_MODT, 0), (DO_MODT, 1),
    (DO_MODZ, 0), (DO_GX, 0, 1), (DO_GZ, 1, 3), (DO_GS, 1, 1), (DO_MODZ, 1), (DO_GY, 0, 0), (DO_LP, 0, 1),
    (DO_LP, 0, 2), (DO_LZ, 0, 1), (DO_GX, 0, 2), (DO_GY, 0, 1), (DO_GS, 1, 2), (DO_MODS, 0), (DO_GS, 0, 3),
    (DO_MODS, 1), (DO_MODM, 0), (DO_GY, 0, 2), (DO_LP, 0, 3), (DO_GX, 1, 0), (DO_MODS, 2), (DO_GX, 0, 3),
    (DO_GS, 1, 3), (DO_LZ, 0, 2), (DO_MODROWS, 0), (DO_MODULATE, 0), (DO_GY, 1, 0), (DO_OWN, 2), (DO_GX, 1, 1),
    (DO_LZ, 0, 3), (DO_GY, 0, 3), (DO_MODM, 1), (DO_LANDED, 0), (DO_PROJECT, 0), (DO_OWN, 3), (DO_GZ, 2, 1),
    (DO_GZ, 2, 2), (DO_GX, 1, 2), (DO_LX, 2), (DO_TURNN, 0), (DO_ATTEND, 0, 0), (DO_GX, 1, 3), (DO_GY, 1, 1),
    (DO_ATTEND, 0, 1), (DO_MODROWS, 1), (DO_GZ, 3, 1), (DO_GZ, 3, 2), (DO_GS, 2, 0), (DO_GY, 1, 2), (DO_LX, 3),
    (DO_ATTEND, 0, 2), (DO_LY, 2), (DO_GZ, 2, 3), (DO_GS, 2, 1), (DO_GY, 1, 3), (DO_JOIN, 0), (DO_ADD, 0),
    (DO_GS, 2, 2), (DO_TURNA, 0), (DO_STANDARDIZE, 1), (DO_GZ, 3, 3), (DO_MODULATE, 1), (DO_GATE, 2), (DO_GX, 2, 0),
    (DO_LANDED, 1), (DO_PROJECT, 1), (DO_LP, 2, 1), (DO_LP, 2, 2), (DO_GX, 2, 1), (DO_LZ, 2, 1), (DO_TURNN, 1),
    (DO_GS, 3, 0), (DO_ATTEND, 1, 0), (DO_LY, 3), (DO_GS, 2, 3), (DO_GY, 2, 0), (DO_ATTEND, 1, 1), (DO_GX, 2, 2),
    (DO_GY, 2, 1), (DO_ATTEND, 1, 2), (DO_LP, 2, 3), (DO_GS, 3, 1), (DO_JOIN, 1), (DO_LZ, 2, 2), (DO_ADD, 1),
    (DO_GX, 2, 3), (DO_LP, 3, 1), (DO_TURNA, 1), (DO_STANDARDIZE, 2), (DO_LP, 3, 2), (DO_MODULATE, 2), (DO_GS, 3, 2),
    (DO_GY, 2, 2), (DO_LZ, 3, 1), (DO_TURNN, 2), (DO_GS, 3, 3), (DO_LZ, 2, 3), (DO_GY, 2, 3), (DO_LP, 3, 3),
    (DO_GX, 3, 0), (DO_LANDED, 2), (DO_EXPAND, 0), (DO_GX, 3, 1), (DO_LZ, 3, 2), (DO_SENDH, 0), (DO_EXPAND, 1),
    (DO_GX, 3, 2), (DO_SENDH, 1), (DO_GX, 3, 3), (DO_EXPAND, 2), (DO_GY, 3, 0), (DO_LZ, 3, 3), (DO_SENDH, 2),
    (DO_EXPAND, 3), (DO_GY, 3, 1), (DO_SENDH, 3), (DO_NEEDH, 0), (DO_DOWNT, 0), (DO_GY, 3, 2), (DO_NEEDH, 1),
    (DO_DOWNT, 1), (DO_GY, 3, 3), (DO_NEEDH, 2), (DO_DOWNT, 2), (DO_NEEDH, 3), (DO_DOWNT, 3), (DO_TE, 0, 0),
    (DO_SS, 0, 0), (DO_LANDED, 3), (DO_GHID, 0), (DO_GHID, 1), (DO_TE, 0, 1), (DO_SS, 0, 1), (DO_SENDP,),
    (DO_GHID, 2), (DO_GHID, 3), (DO_SS, 0, 2), (DO_NEEDP,), (DO_UPT, 3), (DO_TE, 0, 2), (DO_UPT, 0), (DO_SY, 0, 0),
    (DO_TZ, 0, 0), (DO_UPT, 1), (DO_UPT, 2), (DO_SS, 0, 3), (DO_SY, 0, 1), (DO_TE, 1, 0), (DO_CONTRACT,),
    (DO_TZ, 0, 1), (DO_CLOSE,), (DO_BACK2, 0), (DO_SX, 0, 0), (DO_SS, 1, 0), (DO_SY, 0, 2), (DO_TZ, 0, 2),
    (DO_BACK2, 1), (DO_BACK2, 2), (DO_SX, 0, 1), (DO_BACK2, 3), (DO_NORMB, 2), (DO_TE, 1, 1), (DO_SS, 1, 1),
    (DO_TZ, 1, 0), (DO_SY, 0, 3), (DO_GATE, 1), (DO_SX, 0, 2), (DO_SPLIT, 1), (DO_SZ, 0, 0), (DO_SY, 1, 0),
    (DO_TTOT, 0), (DO_ATTB, 1, 0), (DO_SZ, 0, 1), (DO_SS, 1, 2), (DO_ATTB, 1, 1), (DO_SX, 0, 3), (DO_TE, 1, 2),
    (DO_SY, 1, 1), (DO_NEEDG, 1), (DO_OUTT, 1), (DO_SX, 1, 0), (DO_SS, 1, 3), (DO_TZ, 1, 1), (DO_TY, 0),
    (DO_SZ, 0, 2), (DO_TZ, 1, 2), (DO_ATTB, 1, 2), (DO_SENDQ, 1), (DO_BACK, 1, 0), (DO_SY, 1, 2), (DO_SX, 1, 1),
    (DO_NEEDQ, 1), (DO_QKVT, 1, 0), (DO_TX, 0), (DO_QKVT, 1, 1), (DO_SFIN, 0), (DO_SWAP, 0), (DO_QKVT, 1, 2),
    (DO_SY, 1, 3), (DO_RETIRE, 0), (DO_SZ, 1, 0), (DO_CWAIT, 2), (DO_SX, 1, 2), (DO_SS, 2, 0), (DO_BACK, 1, 1),
    (DO_TE, 2, 0), (DO_TTOT, 1), (DO_BACK, 1, 2), (DO_SZ, 1, 1), (DO_NORMB, 1), (DO_SX, 1, 3), (DO_TE, 2, 1),
    (DO_SS, 2, 1), (DO_ROWM, 1), (DO_SENTQ, 1), (DO_GATE, 0), (DO_SZ, 1, 2), (DO_SY, 2, 0), (DO_SPLIT, 0), (DO_TY, 1),
    (DO_ATTB, 0, 0), (DO_TE, 2, 2), (DO_TZ, 2, 0), (DO_ATTB, 0, 1), (DO_SFIN, 1), (DO_SS, 2, 2), (DO_SY, 2, 1),
    (DO_NEEDG, 0), (DO_OUTT, 0), (DO_TZ, 2, 1), (DO_ROWZ, 1), (DO_ATTB, 0, 2), (DO_SX, 2, 0), (DO_SS, 2, 3),
    (DO_TX, 1), (DO_TZ, 2, 2), (DO_SWAP, 1), (DO_SENDQ, 0), (DO_BACK, 0, 0), (DO_RETIRE, 1), (DO_SX, 2, 1),
    (DO_CWAIT, 3), (DO_ROWP, 1, 1), (DO_NEEDQ, 0), (DO_QKVT, 0, 0), (DO_TE, 3, 0), (DO_SY, 2, 2), (DO_QKVT, 0, 1),
    (DO_QKVT, 0, 2), (DO_SS, 3, 0), (DO_SZ, 2, 0), (DO_BACK, 0, 1), (DO_SY, 2, 3), (DO_TE, 3, 1), (DO_ROWP, 1, 2),
    (DO_TTOT, 2), (DO_BACK, 0, 2), (DO_SZ, 2, 1), (DO_SX, 2, 2), (DO_ROWP, 1, 3), (DO_NORMB, 0), (DO_SS, 3, 1),
    (DO_ROWM, 0), (DO_SENTQ, 0), (DO_SZ, 2, 2), (DO_TZ, 3, 0), (DO_SY, 3, 0), (DO_SX, 2, 3), (DO_TY, 2), (DO_ROWT, 1),
    (DO_TE, 3, 2), (DO_SS, 3, 2), (DO_ROWD, 1), (DO_TZ, 3, 1), (DO_SX, 3, 0), (DO_SS, 3, 3), (DO_SFIN, 2),
    (DO_TZ, 3, 2), (DO_SY, 3, 1), (DO_TX, 2), (DO_ROWZ, 0), (DO_SWAP, 2), (DO_RETIRE, 2), (DO_SY, 3, 2),
    (DO_SX, 3, 1), (DO_SZ, 3, 0), (DO_TTOT, 3), (DO_ROWP, 0, 1), (DO_ROWP, 0, 2), (DO_SY, 3, 3), (DO_SX, 3, 2),
    (DO_TY, 3), (DO_SZ, 3, 1), (DO_SZ, 3, 2), (DO_ROWP, 0, 3), (DO_SX, 3, 3), (DO_TX, 3), (DO_SFIN, 3), (DO_SWAP, 3),
    (DO_ROWT, 0), (DO_RETIRE, 3), (DO_ROWD, 0),
)


def dot(left, right):
    return jnp.dot(left, right, preferred_element_type=jnp.float32)


GATHER_CHUNKS = (3, 4, 3, 3)


def layer_kernel(
    tokens,
    cotangent,
    steps,
    seg_ids,
    frame_ids,
    patch_ids,
    b_ada,
    w_ada,
    w_qkv_s,
    w_out_s,
    w_qkv_t,
    w_out_t,
    w_up,
    w_down,
    o_layer,
    o_tokens,
    cond,
    all_rows_mod,
    o_qkv_s,
    o_out_s,
    o_qkv_t,
    o_out_t,
    o_up,
    o_down,
    held,
    stage,
    apart,
    apart_down,
    sums,
    from_second,
    from_first,
    from_z,
    last_pair,
    last_one,
    last_z,
    all_steps,
    bias,
    ids,
    mod,
    tally,
    rows_mod,
    xhat,
    deviation,
    normed,
    attended,
    turned,
    hidden_turned,
    qkv,
    probs,
    branch,
    stream,
    grad,
    hidden,
    slope,
    grad_pre_twin,
    gated,
    gated_twin,
    grad_attended,
    grad_qkv_twin,
    disallowed,
    swap_sems,
    gather_send,
    gather_recv,
    scatter_send,
    scatter_recv,
    credit,
    twin_send,
    twin_recv,
    step_send,
    step_recv,
    mod_send,
    mod_recv,
    row_send,
    row_recv,
):
    width, tok = tokens.shape[1], tokens.shape[0]
    f32, bf16 = jnp.float32, jnp.bfloat16
    spot = Spot()
    core = spot.core
    grad_qkv, grad_normed = hidden, stream
    greet(spot)

    def attention_piece(w_qkv, w_out):
        def piece(half, chunk):
            if chunk < 3:
                return w_qkv[:, pl.ds(pl.multiple_of(half * 1152 + chunk * 384, 128), 384)]
            return w_out[:, pl.ds(pl.multiple_of(half * 384, 128), 384)]

        return piece

    def up_piece(half, chunk):
        return w_up[:, pl.ds(pl.multiple_of(half * 1536 + chunk * 384, 128), 384)]

    def down_piece(half, chunk):
        return w_down[chunk * 48 : chunk * 48 + 48, pl.ds(pl.multiple_of(half * 384, 128), 384)]

    pieces = (
        attention_piece(w_qkv_s, w_out_s),
        attention_piece(w_qkv_t, w_out_t),
        up_piece,
        down_piece,
    )
    gathers = [
        Gather(
            spot,
            held.at[g],
            stage.at[g],
            apart.at[g] if g < 3 else apart_down,
            swap_sems.at[g],
            gather_send.at[g],
            gather_recv.at[g],
            GATHER_CHUNKS[g],
        )
        for g in range(4)
    ]
    scatters = [
        Scatter(
            spot,
            held.at[2, n - 2] if n >= 2 else sums.at[n],
            from_second.at[n % 2],
            from_first.at[n % 2],
            from_z.at[n % 2],
            last_pair.at[n % 2],
            last_one.at[n % 2],
            last_z.at[n % 2],
            stage.at[3 - n],
            apart_down if n == 0 else apart.at[3 - n],
            scatter_send.at[n],
            scatter_recv.at[n],
            credit.at[n % 2],
            n >= 2,
        )
        for n in range(4)
    ]

    def put_attention(o_qkv, o_out):
        def put(half, chunk, rows):
            if chunk < 3:
                o_qkv[:, pl.ds(pl.multiple_of(half * 1152 + chunk * 384, 128), 384)] = rows
            else:
                o_out[:, pl.ds(pl.multiple_of(half * 384, 128), 384)] = rows

        return put

    def put_up(half, chunk, rows):
        o_up[:, pl.ds(pl.multiple_of(half * 1536 + chunk * 384, 128), 384)] = rows

    def put_down(half, chunk, rows):
        o_down[chunk * 48 : chunk * 48 + 48, pl.ds(pl.multiple_of(half * 384, 128), 384)] = rows

    puts = (put_down, put_up, put_attention(o_qkv_t, o_out_t), put_attention(o_qkv_s, o_out_s))

    def to_twin(index, src, dst):
        return remote(src, dst, twin_send.at[index], twin_recv.at[index], spot.twin)

    def turned_copy(i):
        return to_twin(i, turned.at[i, 0], turned.at[i, 1])

    def hidden_copy(i):
        rows = pl.ds(768 * i, 768)
        return to_twin(12 + i, hidden_turned.at[0, rows], hidden_turned.at[1, rows])

    def gated_copy(j):
        theirs = pl.multiple_of((1 - core) * 384, 128)
        return to_twin(6 + j, gated.at[j, :, pl.ds(theirs, 384)], gated_twin.at[j])

    def grad_pre_copy():
        theirs = pl.multiple_of((1 - core) * 1536, 128)
        return to_twin(9, slope.at[:, pl.ds(theirs, 1536)], grad_pre_twin)

    def grad_qkv_copy(j):
        theirs = pl.multiple_of((1 - core) * 1152, 128)
        return to_twin(10 + j, grad_qkv.at[:, pl.ds(theirs, 1152)], grad_qkv_twin.at[j])

    def step_twin(owner):
        ref = all_steps.at[spot.z, spot.plane, owner]
        return remote(ref, ref, step_send.at[0], step_recv.at[0], spot.twin)

    step_line = Exchange(
        spot.line,
        spot.z,
        lambda z: all_steps.at[spot.z, spot.plane],
        lambda z: all_steps.at[z, spot.plane],
        step_send.at[pl.ds(1, 3)],
        step_recv.at[pl.ds(4, 4)],
    )
    step_mates = Exchange(
        spot.mates,
        spot.plane,
        lambda plane: all_steps.at[:, spot.plane],
        lambda plane: all_steps.at[:, plane],
        step_send.at[pl.ds(4, 3)],
        step_recv.at[pl.ds(8, 4)],
    )

    def steps_open():
        row = lax.broadcasted_iota(jnp.int32, (8, 128), 0)
        value = jnp.where(row == 0, steps[0, 0], jnp.where(row == 1, steps[0, 1], 0))
        all_steps[spot.z, spot.plane, core] = value.astype(f32)
        step_twin(core).start()

    def steps_line():
        step_twin(1 - core).wait_recv()
        step_line.start()

    def steps_mates():
        step_line.arrive()
        step_mates.start()

    def steps_drain():
        step_twin(core).wait_send()
        step_line.drain()
        step_mates.drain()

    def make_cond():
        step_mates.arrive()
        flat = all_steps[...].reshape(256, 128)
        clip = lax.broadcasted_iota(jnp.int32, (64, 256), 0)
        column = lax.broadcasted_iota(jnp.int32, (64, 256), 1)
        wanted = 64 * ((clip >> 3) & 3) + 16 * ((clip >> 1) & 3) + 8 * (clip >> 5) + (clip & 1)
        times = jnp.dot(
            (column == wanted).astype(f32),
            flat,
            precision=lax.Precision.HIGHEST,
            preferred_element_type=f32,
        )
        first = (spot.chip * 2 + core) * 24
        half_width = width // 2
        feature = first + lax.broadcasted_iota(jnp.int32, (64, 128), 1)
        place = jnp.where(feature < half_width, feature, feature - half_width).astype(f32)
        angle = times * jnp.exp(-math.log(FREQ_BASE) * place / half_width)
        value = jnp.where(feature < half_width, jnp.cos(angle), jnp.sin(angle))
        cond[...] = (value / (1.0 + jnp.exp(-value))).astype(bf16)

    parts = (range(0, 1), range(1, 3))

    def columns_of(j, half, chunk):
        at = 2304 * j + 1152 * half + 384 * chunk
        return slice(at, at + 384)

    def rows_of(chunk):
        return slice(16 * chunk, 16 * chunk + 16)

    class ModPart:
        def __init__(self, part):
            self.part, self.n = part, len(parts[part])
            n, base = self.n, 6 * part

            def region(i):
                return pl.ds(base + n * i, n)

            self.out, self.into, self.sum = (sums.at[1, region(i)] for i in range(3))
            self.own = sums.at[1, 5, pl.ds(part, n)]
            if part:
                self.line = LineSum(
                    spot,
                    lambda z: sums.at[1, region(2), z],
                    lambda i: sums.at[1, region(3), i] if i < 4 else self.own,
                    mod_send.at[part, pl.ds(1, 3)],
                    mod_recv.at[part, pl.ds(1, 5)],
                )
            else:
                self.line = Exchange(
                    spot.line,
                    spot.z,
                    lambda z: sums.at[1, region(2), z],
                    lambda z: sums.at[1, region(3), z],
                    mod_send.at[part, pl.ds(1, 3)],
                    mod_recv.at[part, pl.ds(1, 4)],
                )
            self.mates = Exchange(
                spot.mates,
                spot.plane,
                lambda plane: self.own,
                lambda plane: sums.at[1, region(4), plane],
                mod_send.at[part, pl.ds(4, 3)],
                mod_recv.at[part, pl.ds(6, 4)],
            )

        def swap(self):
            part = self.part
            return remote(self.out, self.into, mod_send.at[part, 0], mod_recv.at[part, 0], spot.twin)

        def terms(self, owner):
            rows = cond[pl.ds(pl.multiple_of(32 * owner, 32), 32), :24]
            for i, j in enumerate(parts[self.part]):
                for chunk in range(3):
                    left, right = (
                        dot(rows, w_ada[:, columns_of(j, half, chunk)])
                        + bias[0:1, columns_of(j, half, chunk)]
                        for half in range(2)
                    )
                    for z in range(4):
                        own = slice(8 * z, 8 * z + 8)
                        block = jnp.concatenate([left[own], right[own]], axis=0)
                        yield (i, z, rows_of(chunk)), block

        def for_twin(self):
            for at, value in self.terms(1 - core):
                self.out[at] = value.astype(bf16)
            self.swap().start()

        def for_line(self):
            self.swap().wait_recv()
            for at, value in self.terms(core):
                self.sum[at] = (value + self.into[at].astype(f32)).astype(bf16)
            if self.part:
                for k in range(3):
                    self.line.send_end(k)
            else:
                self.line.start()

        def for_mates(self):
            def put(i, value):
                self.own[i] = value.astype(bf16)

            if self.part:
                self.line.total(put)
            else:
                self.line.arrive()
                for i in range(self.n):
                    value = self.line.src(spot.z)[i].astype(f32)
                    for z, _ in spot.line:
                        value += self.line.dst(z)[i].astype(f32)
                    put(i, value)
            self.mates.start()

        def done(self):
            self.mates.arrive()
            row = lax.broadcasted_iota(jnp.int32, (16, 384), 0)
            for i, j in enumerate(parts[self.part]):
                for chunk in range(3):
                    value = self.own[i, rows_of(chunk)].astype(f32)
                    for plane, _ in spot.mates:
                        value += self.mates.dst(plane)[i, rows_of(chunk)].astype(f32)
                    for clip in range(2):
                        for half in range(2):
                            chosen = row == 8 * half + 2 * spot.plane + clip
                            mod[clip : clip + 1, columns_of(j, half, chunk)] = jnp.sum(
                                jnp.where(chosen, value, 0.0), axis=0, keepdims=True
                            )

        def drain(self):
            self.swap().wait_send()
            self.line.drain()
            self.mates.drain()

    class RowPart:
        def __init__(self, part):
            self.part, n = part, len(parts[part])
            self.subs = subs = pl.ds(parts[part][0], n)
            self.mates = Exchange(
                spot.mates,
                spot.plane,
                lambda plane: rows_mod.at[spot.plane, subs],
                lambda plane: rows_mod.at[plane, subs],
                row_send.at[part, pl.ds(1, 3)],
                row_recv.at[part, pl.ds(1, 4)],
            )
            self.line = LineGather(
                spot,
                lambda z: all_rows_mod.at[core, z, subs],
                row_send.at[part, pl.ds(4, 5)],
                row_recv.at[part, pl.ds(5, 4)],
            )

        def swap(self, owner):
            ref = all_rows_mod.at[owner, :, self.subs]
            return remote(ref, ref, row_send.at[self.part, 0], row_recv.at[self.part, 0], spot.twin)

        def for_mates(self):
            row = lax.broadcasted_iota(jnp.int32, (16, 384), 0)
            for j in parts[self.part]:
                for chunk in range(3):
                    value = 0.0
                    for clip in range(2):
                        for half in range(2):
                            chosen = row == 8 * half + 2 * spot.plane + clip
                            own = tally[clip : clip + 1, columns_of(j, half, chunk)]
                            value += jnp.where(chosen, own, 0.0)
                    rows_mod[spot.plane, j, :, 384 * chunk : 384 * chunk + 384] = value.astype(bf16)
            self.mates.start()

        def for_line(self):
            self.mates.arrive()
            for j in parts[self.part]:
                all_rows_mod[core, spot.z, j] = (rows_mod[0, j] + rows_mod[1, j]) + (
                    rows_mod[2, j] + rows_mod[3, j]
                )
            self.line.open()

        def for_twin(self):
            for k in (1, 2, 3):
                self.line.take(k)
            self.swap(core).start()

        def done(self):
            self.swap(1 - core).wait_recv()

        def drain(self):
            self.swap(core).wait_send()
            self.mates.drain()
            self.line.drain()

    mod_parts = [ModPart(part) for part in range(2)]
    row_parts = [RowPart(part) for part in range(2)]

    def by_rows(action):
        @pl.loop(0, tok // 64)
        def _(i):
            action(pl.ds(pl.multiple_of(i * 64, 64), 64))

    def mod_part(j, component, rows):
        at = (3 * j + component) * width
        second = ids[rows, 2:3] == 1.0
        return jnp.where(second, mod[1:2, at : at + width], mod[0:1, at : at + width])

    def count(j, component, rows, value):
        at = (3 * j + component) * width
        second = ids[rows, 2:3] == 1.0
        tally[0:1, at : at + width] += jnp.sum(jnp.where(second, 0.0, value), axis=0, keepdims=True)
        tally[1:2, at : at + width] += jnp.sum(jnp.where(second, value, 0.0), axis=0, keepdims=True)

    def masks():
        spatial = (seg_ids[...] * 16 + frame_ids[...]).astype(f32)
        temporal = (seg_ids[...] * 16 + patch_ids[...]).astype(f32)
        row = lax.broadcasted_iota(jnp.int32, (8, tok), 0)
        second = seg_ids[...].astype(f32)
        stacked = jnp.where(row == 0, spatial, jnp.where(row == 1, temporal, second))
        ids[...] = stacked.T
        for j, keys in enumerate((spatial, temporal)):
            disallowed[j] = jnp.where(ids[:, j : j + 1] == keys, 0.0, MASKED)
        tally[...] = jnp.zeros_like(tally)
        share = b_ada.shape[1]
        bias[...] = jnp.zeros_like(bias)
        bias[0:1, :share] = b_ada[...].astype(f32)
        bias[...] = pltpu.roll(bias[...], (2 * spot.chip + core) * share, 1)

    def standardize(j):
        def action(rows):
            if j == 0:
                stream[rows] = tokens[rows].astype(f32)
            value = stream[rows]
            center = value - jnp.mean(value, axis=-1, keepdims=True)
            inverse = lax.rsqrt(jnp.mean(center * center, axis=-1, keepdims=True) + EPSILON)
            xhat[j, rows] = (center * inverse).astype(bf16)
            deviation[rows, j : j + 1] = inverse

        by_rows(action)

    def modulate(j):
        def action(rows):
            normed[rows] = (
                xhat[j, rows].astype(f32) * (1.0 + mod_part(j, 1, rows)) + mod_part(j, 0, rows)
            ).astype(bf16)

        by_rows(action)

    def turn(i, source):
        for at in range(0, tok, 128):
            turned[i, 0, :, at : at + 128] = source[at : at + 128, :].T
        turned_copy(i).start()

    def weight(g, half, chunk):
        return held[g, half, :, chunk].reshape(width, 384)

    def project(j):
        @pl.loop(0, 6)
        def _(i):
            half, chunk = lax.div(i, 3), lax.rem(i, 3)
            columns = pl.ds(pl.multiple_of(i * 384, 128), 384)
            qkv[j, :, columns] = dot(normed[...], weight(j, half, chunk)).astype(bf16)

    def head_lanes():
        lane = lax.broadcasted_iota(jnp.int32, (1, 128), 1)
        return lane < 64, lane >= 64

    def head_columns(pair):
        return [pl.ds(pl.multiple_of(part * 768 + pair * 128, 128), 128) for part in range(3)]

    def attend(j, first, last):
        @pl.loop(first, last)
        def _(pair):
            at_q, at_k, at_v = head_columns(pair)
            queries, keys, values = qkv[j, :, at_q], qkv[j, :, at_k], qkv[j, :, at_v]
            results = []
            for head, lanes in enumerate(head_lanes()):
                scaled = jnp.where(lanes, queries, 0.0) * bf16(0.125)
                scores = contract_cols(scaled, keys) + disallowed[j]
                scores = jnp.exp(scores - jnp.max(scores, axis=-1, keepdims=True))
                low = (scores * (1.0 / jnp.sum(scores, axis=-1, keepdims=True))).astype(bf16)
                probs[j, 2 * pair + head] = low
                results.append(dot(low, values))
            attended[:, at_q] = jnp.where(head_lanes()[0], results[0], results[1]).astype(bf16)

    def join(j):
        @pl.loop(0, 2)
        def _(half):
            columns = pl.ds(pl.multiple_of(half * 384, 128), 384)
            branch[j, :, columns] = dot(attended[...], weight(j, half, 3)).astype(bf16)

    def add_branch(j):
        def action(rows):
            stream[rows] += mod_part(j, 2, rows) * branch[j, rows].astype(f32)

        by_rows(action)

    def expand(first, last):
        @pl.loop(first, last)
        def _(i):
            columns = pl.ds(pl.multiple_of(i * 384, 128), 384)
            matrix = weight(2, lax.div(i, 4), lax.rem(i, 4))
            for at in range(0, tok, 128):
                rows = slice(at, at + 128)
                pre = dot(normed[rows], matrix)
                square = pre * pre
                root = math.sqrt(2.0 / math.pi)
                bent = jnp.tanh(root * (pre + 0.044715 * (square * pre)))
                value = (0.5 * pre * (1.0 + bent)).astype(bf16)
                hidden[rows, columns] = value
                hidden_turned[0, columns, rows] = value.T
                slope[rows, columns] = (
                    0.5 * (1.0 + bent)
                    + 0.5 * pre * (1.0 - bent * bent) * (root * (1.0 + 3 * 0.044715 * square))
                ).astype(bf16)

    def gate(j):
        def action(rows):
            value = cotangent[rows].astype(f32) if j == 2 else grad[rows]
            if j == 2:
                grad[rows] = value
            else:
                count(j, 2, rows, value * branch[j, rows].astype(f32))
            gated[j, rows] = (mod_part(j, 2, rows) * value).astype(bf16)

        by_rows(action)
        gated_copy(j).start()

    def own_columns(first, width_of_half):
        return pl.ds(pl.multiple_of(core * width_of_half + first, 128), 384)

    def down_terms(z):
        scatter = scatters[0]
        rows = slice(768 * z, 768 * z + 768)
        value = dot(hidden_turned[0, rows], gated[2, :, own_columns(0, 384)]) + dot(
            hidden_turned[1, rows], gated_twin[2]
        )
        value = value.astype(bf16).reshape(4, 4, 48, 384)
        for plane in range(4):
            scatter.sums[scatter.place(4 * z + plane)] = value[plane]

    def column_terms(n, chunk, left, right, right_twin):
        value = dot(turned[left, 0], right) + dot(turned[left, 1], right_twin)
        value = value.astype(bf16).reshape(16, 48, 384)
        for chip in range(16):
            scatters[n].sums[scatters[n].place(chip), chunk] = value[chip]

    def up_terms(chunk):
        column_terms(
            1,
            chunk,
            4,
            slope[:, own_columns(384 * chunk, 1536)],
            grad_pre_twin[:, 384 * chunk : 384 * chunk + 384],
        )

    def out_terms(j):
        column_terms(3 - j, 3, 2 * j + 1, gated[j, :, own_columns(0, 384)], gated_twin[j])

    def qkv_terms(j, chunk):
        column_terms(
            3 - j,
            chunk,
            2 * j,
            grad_qkv[:, own_columns(384 * chunk, 1152)],
            grad_qkv_twin[j, :, 384 * chunk : 384 * chunk + 384],
        )

    def contract():
        @pl.loop(0, 2)
        def _(half):
            columns = pl.ds(pl.multiple_of(half * 384, 128), 384)
            matrix = held[3, half].reshape(3072, 384)
            normed[:, columns] = dot(hidden[...], matrix).astype(bf16)

    def close():
        def action(rows):
            value = normed[rows].astype(f32)
            o_layer[rows] = (stream[rows] + mod_part(2, 2, rows) * value).astype(bf16)
            count(2, 2, rows, cotangent[rows].astype(f32) * value)

        by_rows(action)

    def grad_hidden(step):
        first = 2 * lax.rem(step + 2 - 2 * core, 4)

        @pl.loop(0, 2)
        def _(part):
            i = first + part
            columns = pl.ds(pl.multiple_of(i * 384, 128), 384)
            value = sum(
                contract_cols(
                    gated[2, :, 384 * half : 384 * half + 384],
                    held[3, half, pl.ds(2 * i, 2)].reshape(384, 384),
                )
                for half in range(2)
            )
            slope[:, columns] = (slope[:, columns].astype(f32) * value).astype(bf16)

    def back_project(g, chunks, source, first, last):
        @pl.loop(first, last)
        def _(i):
            columns = pl.ds(pl.multiple_of(i * 384, 128), 384)
            value = contract_cols(
                source[:, columns], weight(g, lax.div(i, chunks), lax.rem(i, chunks))
            )

            @pl.when(i == 0)
            def _():
                grad_normed[...] = value

            @pl.when(i > 0)
            def _():
                grad_normed[...] += value

    def norm_back(j):
        def action(rows):
            value, unit = grad_normed[rows], xhat[j, rows].astype(f32)
            count(j, 0, rows, value)
            count(j, 1, rows, value * unit)
            scaled = value * (1.0 + mod_part(j, 1, rows))
            inner = jnp.mean(scaled * unit, axis=-1, keepdims=True)
            scaled = scaled - jnp.mean(scaled, axis=-1, keepdims=True)
            total = grad[rows] + deviation[rows, j : j + 1] * (scaled - unit * inner)
            if j == 0:
                o_tokens[rows] = total
            else:
                grad[rows] = total

        by_rows(action)

    def split(j):
        value = sum(
            contract_cols(gated[j, :, 384 * half : 384 * half + 384], weight(j, half, 3))
            for half in range(2)
        )
        grad_attended[...] = value.astype(bf16)

    def attend_back(j, first, last):
        @pl.loop(first, last)
        def _(pair):
            at_q, at_k, at_v = head_columns(pair)
            queries, keys, values = qkv[j, :, at_q], qkv[j, :, at_k], qkv[j, :, at_v]
            given = grad_attended[:, at_q]
            grad_q, grad_k, grad_v = [], 0.0, 0.0
            for head, lanes in enumerate(head_lanes()):
                part = jnp.where(lanes, given, 0.0).astype(bf16)
                low = probs[j, 2 * pair + head]
                product = low.astype(f32) * contract_cols(part, values)
                total = jnp.sum(product, axis=-1, keepdims=True)
                scores = ((product - low.astype(f32) * total) * 0.125).astype(bf16)
                grad_v += contract_rows(low, part)
                grad_k += contract_rows(scores, jnp.where(lanes, queries, 0.0).astype(bf16))
                grad_q.append(dot(scores, keys))
            grad_qkv[:, at_q] = jnp.where(head_lanes()[0], grad_q[0], grad_q[1]).astype(bf16)
            grad_qkv[:, at_k] = grad_k.astype(bf16)
            grad_qkv[:, at_v] = grad_v.astype(bf16)

    def each_twin_copy():
        for i in range(5):
            yield turned_copy(i)
        for i in range(4):
            yield hidden_copy(i)
        for j in range(3):
            yield gated_copy(j)
        yield grad_pre_copy()

    def forward_drain():
        steps_drain()
        for part in mod_parts:
            part.drain()
        for gather in gathers:
            gather.swap().wait_send()

    def send_hidden(i):
        if i == 0:
            forward_drain()
        hidden_copy(i).start()

    def need_hidden(i):
        if i == 0:
            gated_copy(2).wait_recv()
        hidden_copy(i).wait_recv()

    def need_gated(j):
        if j == 1:
            gathers[2].drain()
        need(turned_copy, 2 * j + 1)
        need(gated_copy, j)

    def retire(n):
        scatters[n].store(puts[n])
        scatters[n].drain()
        if n < 2:
            scatters[n].release()

    def swap(n):
        scatters[n].swap().start()

    def need(copy, *indices):
        copy(*indices).wait_recv()

    steps_of = {
        DO_STEPS: (steps_line, steps_mates),
        DO_COND: make_cond,
        DO_MODT: lambda part: mod_parts[part].for_twin(),
        DO_MODZ: lambda part: mod_parts[part].for_line(),
        DO_MODS: lambda k: mod_parts[1].line.send_middle(k),
        DO_MODM: lambda part: mod_parts[part].for_mates(),
        DO_MODROWS: lambda part: mod_parts[part].done(),
        DO_OWN: lambda g: gathers[g].own(),
        DO_GZ: lambda g, k: gathers[g].pass_on(k),
        DO_GS: lambda g, k: gathers[g].spread(k),
        DO_GX: lambda g, k: gathers[g].along_first(k),
        DO_GY: lambda g, k: gathers[g].along_second(k),
        DO_LX: lambda g: gathers[g].last_along_first(),
        DO_LY: lambda g: gathers[g].last_along_second(),
        DO_LP: lambda g, k: gathers[g].line.pass_on(k),
        DO_LZ: lambda g, k: gathers[g].last_along_z(k),
        DO_LANDED: lambda g: gathers[g].landed(),
        DO_CWAIT: lambda n: scatters[n].wait_credit(),
        DO_SS: lambda n, k: scatters[n].second_copy(k).start(),
        DO_SY: lambda n, k: scatters[n].add_second(k),
        DO_SX: lambda n, k: scatters[n].add_first(k),
        DO_SZ: lambda n, k: scatters[n].line.send_middle(k),
        DO_SFIN: lambda n: scatters[n].finish(),
        DO_TE: lambda n, k: scatters[n].last_line.send_end(k),
        DO_TZ: lambda n, k: scatters[n].last_line.send_middle(k),
        DO_TTOT: lambda n: scatters[n].last_total(),
        DO_TY: lambda n: scatters[n].last_add_second(),
        DO_TX: lambda n: scatters[n].last_finish(),
        DO_SWAP: swap,
        DO_RETIRE: retire,
        DO_ROWM: lambda part: row_parts[part].for_mates(),
        DO_ROWZ: lambda part: row_parts[part].for_line(),
        DO_ROWP: lambda part, k: row_parts[part].line.pass_on(k),
        DO_ROWT: lambda part: row_parts[part].for_twin(),
        DO_ROWD: lambda part: row_parts[part].done(),
        DO_MASKS: masks,
        DO_STANDARDIZE: standardize,
        DO_MODULATE: modulate,
        DO_PROJECT: project,
        DO_TURNN: lambda j: turn(2 * j, normed),
        DO_TURNA: lambda j: turn(2 * j + 1, attended),
        DO_ATTEND: lambda j, i: attend(j, 2 * i, 2 * i + 2),
        DO_JOIN: join,
        DO_ADD: add_branch,
        DO_GATE: gate,
        DO_EXPAND: lambda i: expand(2 * i, 2 * i + 2),
        DO_SENDH: send_hidden,
        DO_NEEDH: need_hidden,
        DO_DOWNT: down_terms,
        DO_GHID: grad_hidden,
        DO_SENDP: lambda: grad_pre_copy().start(),
        DO_CONTRACT: contract,
        DO_CLOSE: close,
        DO_NEEDP: lambda: (need(grad_pre_copy), need(turned_copy, 4)),
        DO_UPT: up_terms,
        DO_BACK2: lambda i: back_project(2, 4, slope, 2 * i, 2 * i + 2),
        DO_NORMB: norm_back,
        DO_SPLIT: split,
        DO_ATTB: lambda j, i: attend_back(j, 2 * i, 2 * i + 2),
        DO_SENDQ: lambda j: grad_qkv_copy(j).start(),
        DO_NEEDG: need_gated,
        DO_NEEDQ: lambda j: (
            need(turned_copy, 2 * j),
            need(grad_qkv_copy, j),
        ),
        DO_OUTT: out_terms,
        DO_QKVT: qkv_terms,
        DO_BACK: lambda j, i: back_project(j, 3, grad_qkv, 2 * i, 2 * i + 2),
        DO_SENTQ: lambda j: grad_qkv_copy(j).wait_send(),
    }
    for g, gather in enumerate(gathers):
        gather.open(pieces[g])
    steps_open()
    for name, *indices in ORDER:
        step = steps_of[name]
        if isinstance(step, tuple):
            step[indices[0]]()
        else:
            step(*indices)
    for part in row_parts:
        part.drain()
    for g in (0, 1, 3):
        gathers[g].drain()
    for copy in each_twin_copy():
        copy.wait_send()


def finish_kernel(cond, all_rows_mod, *refs):
    sources, o_ada, o_bias = refs[:8], refs[8], refs[9]
    results, held, total, sem = refs[10:18], refs[18:26], refs[26], refs[27]

    def copies(first, second, kind):
        return [
            pltpu.make_async_copy(src, dst, sem.at[kind, i])
            for i, (src, dst) in enumerate(zip(first, second, strict=True))
        ]

    arriving, leaving = copies(sources, held, 0), copies(held, results, 1)
    for copy in arriving:
        copy.start()
    total[...] = jnp.zeros_like(total)
    for j in range(3):
        for half in range(2):
            for chunk in range(3):
                at = 2304 * j + 1152 * half + 384 * chunk
                part = all_rows_mod[:, :, j, :, 384 * chunk : 384 * chunk + 384].astype(jnp.float32)
                part = part[:, :, 8 * half : 8 * half + 8].reshape(64, 384)
                low = part.astype(jnp.bfloat16)
                o_ada[:, at : at + 384] = contract_rows(cond[...], low)[:24]
                total[0:1, at : at + 384] = jnp.sum(part, axis=0, keepdims=True)
        if j == 0:
            for copy, onward in zip(arriving, leaving, strict=True):
                copy.wait()
                onward.start()
    place = lax.axis_index("wide") * 2 + lax.axis_index("narrow")
    share, columns = o_bias.shape[1], total.shape[1]
    turned = pltpu.roll(total[...], lax.rem(columns - place * share, columns), 1)
    o_bias[...] = turned[0:1, :share]
    for copy in leaving:
        copy.wait()


def layer(tokens, cotangent, steps, seg_ids, frame_ids, patch_ids, b_ada, w_ada, *shards):
    f32, bf16 = jnp.float32, jnp.bfloat16
    tok, width = tokens.shape
    block = (4, 48, 384)
    dma, vmem = pltpu.SemaphoreType.DMA, pltpu.VMEM
    in_vmem, in_hbm = pl.BlockSpec(memory_space=vmem), pl.BlockSpec(memory_space=pltpu.HBM)
    outs = pl.pallas_call(
        layer_kernel,
        out_shape=[
            jax.ShapeDtypeStruct((tok, width), bf16),
            jax.ShapeDtypeStruct((tok, width), f32),
            jax.ShapeDtypeStruct((64, 128), bf16),
            jax.ShapeDtypeStruct((2, 4, 3, 16, 1152), bf16),
        ]
        + [jax.ShapeDtypeStruct(shard.shape, f32) for shard in shards],
        in_specs=[in_vmem] * 2 + [pl.BlockSpec(memory_space=pltpu.SMEM)] + [in_vmem] * 11,
        out_specs=[in_vmem] * 10,
        scratch_shapes=[
            vmem((4, 2, 16) + block, bf16),
            vmem((4,) + block, f32),
            vmem((3, 4, 24, 384), f32),
            vmem((2, 48, 384), f32),
            vmem((2, 16) + block, bf16),
            vmem((2, 4, 2, 3, 48, 384), bf16),
            vmem((2, 4, 3, 48, 384), bf16),
            vmem((2, 5, 3, 48, 384), bf16),
            vmem((2, 2, 48, 384), bf16),
            vmem((2, 48, 384), bf16),
            vmem((2, 5) + block, bf16),
            vmem((4, 4, 2, 8, 128), f32),
            vmem((8, w_ada.shape[1]), f32),
            vmem((tok, 8), f32),
            vmem((8, 6912), f32),
            vmem((8, 6912), f32),
            vmem((4, 3, 16, 1152), bf16),
            vmem((3, tok, width), bf16),
            vmem((tok, 128), f32),
            vmem((tok, width), bf16),
            vmem((tok, width), bf16),
            vmem((5, 2, width, tok), bf16),
            vmem((2, 4 * width, tok), bf16),
            vmem((2, tok, 3 * width), bf16),
            vmem((2, HEADS, tok, tok), bf16),
            vmem((2, tok, width), bf16),
            vmem((tok, width), f32),
            vmem((tok, width), f32),
            vmem((tok, 4 * width), bf16),
            vmem((tok, 4 * width), bf16),
            vmem((tok, 2 * width), bf16),
            vmem((3, tok, width), bf16),
            vmem((3, tok, width // 2), bf16),
            vmem((tok, width), bf16),
            vmem((2, tok, 3 * width // 2), bf16),
            vmem((2, tok, tok), f32),
            dma((4, 2)),
            dma((4, 33)),
            dma((4, 31)),
            dma((4, 17)),
            dma((4, 21)),
            pltpu.SemaphoreType.REGULAR((2, 4)),
            dma((16,)),
            dma((16,)),
            dma((7,)),
            dma((12,)),
            dma((2, 7)),
            dma((2, 10)),
            dma((2, 9)),
            dma((2, 9)),
        ],
        compiler_params=pltpu.CompilerParams(
            collective_id=0, has_side_effects=True, vmem_limit_bytes=64 * 2**20
        ),
    )(tokens, cotangent, steps, seg_ids, frame_ids, patch_ids, b_ada, w_ada, *shards)
    sources = (*outs[:2], *outs[4:])
    return pl.pallas_call(
        finish_kernel,
        out_shape=[
            jax.ShapeDtypeStruct(w_ada.shape, f32),
            jax.ShapeDtypeStruct((1, w_ada.shape[1] // 32), f32),
        ]
        + [jax.ShapeDtypeStruct(source.shape, source.dtype) for source in sources],
        in_specs=[in_vmem] * 2 + [in_hbm] * 8,
        out_specs=[in_vmem] * 2 + [in_hbm] * 8,
        scratch_shapes=[vmem(source.shape, source.dtype) for source in sources]
        + [vmem((8, w_ada.shape[1]), f32), dma((2, 8))],
        compiler_params=pltpu.CompilerParams(vmem_limit_bytes=60 * 2**20),
    )(outs[2], outs[3], *sources)


def on_grid(
    tokens,
    seg_ids,
    frame_ids,
    patch_ids,
    timesteps,
    w_ada,
    b_ada,
    w_qkv_spatial,
    w_out_spatial,
    w_qkv_temporal,
    w_out_temporal,
    w_up,
    w_down,
    cotangent,
):
    shards = (w_qkv_spatial, w_out_spatial, w_qkv_temporal, w_out_temporal, w_up, w_down)
    grad_ada, grad_bias, out, grad_tokens, *grads = layer(
        tokens,
        cotangent,
        timesteps[None],
        seg_ids[None],
        frame_ids[None],
        patch_ids[None],
        b_ada[None],
        w_ada,
        *shards,
    )
    return (out, grad_tokens, grad_ada, grad_bias.reshape(-1), *grads)


def on_device(
    tokens,
    seg_ids,
    frame_ids,
    patch_ids,
    timesteps,
    w_ada,
    b_ada,
    w_qkv_spatial,
    w_out_spatial,
    w_qkv_temporal,
    w_out_temporal,
    w_up,
    w_down,
    cotangent,
):
    axes = ("wide", "narrow")
    gathered = (
        None,
        None,
        lax.all_gather(w_qkv_spatial, axes, axis=0, tiled=True),
        lax.all_gather(w_out_spatial, axes, axis=0, tiled=True),
        lax.all_gather(w_qkv_temporal, axes, axis=0, tiled=True),
        lax.all_gather(w_out_temporal, axes, axis=0, tiled=True),
        lax.all_gather(w_up, axes, axis=0, tiled=True),
        lax.all_gather(w_down, axes, axis=0, tiled=True),
    )
    width = tokens.shape[1]
    head_count = HEADS
    clip_count = timesteps.shape[0]
    row_count = w_ada.shape[0]
    place = lax.axis_index(axes)
    all_steps = lax.all_gather(timesteps, axes, axis=0, tiled=True)
    cond_all = jax.nn.silu(time_embed(all_steps, width)).astype(jnp.bfloat16)
    cond_rows = lax.dynamic_slice_in_dim(cond_all, place * row_count, row_count, axis=1)
    all_bias = lax.all_gather(b_ada, axes, axis=0, tiled=True)
    modulation = lax.psum_scatter(
        jnp.dot(cond_rows, w_ada, preferred_element_type=jnp.float32),
        axes,
        scatter_dimension=0,
        tiled=True,
    ) + all_bias.astype(jnp.float32)
    one_hot = (seg_ids[:, None] == jnp.arange(clip_count, dtype=jnp.int32)[None, :]).astype(
        jnp.float32
    )
    offset_first, scale_first, gate_a = sublayer_mod(one_hot, modulation, 0, width)
    offset_second, scale_second, gate_b = sublayer_mod(one_hot, modulation, 1, width)
    offset_third, scale_third, gate_c = sublayer_mod(one_hot, modulation, 2, width)
    same_clip = seg_ids[:, None] == seg_ids[None, :]
    spatial_mask = same_clip & (frame_ids[:, None] == frame_ids[None, :])
    temporal_mask = same_clip & (patch_ids[:, None] == patch_ids[None, :])
    residual_first = tokens.astype(jnp.float32)
    standardized_first, inverse_deviation_first = layer_norm_apply(residual_first)
    normalized_first = (standardized_first * (1.0 + scale_first) + offset_first).astype(
        jnp.bfloat16
    )
    branch_a, qkv_a, merged_a = attention_forward(
        normalized_first, gathered[2], gathered[3], spatial_mask, head_count
    )
    residual_second = residual_first + gate_a * branch_a
    standardized_second, inverse_deviation_second = layer_norm_apply(residual_second)
    normalized_second = (standardized_second * (1.0 + scale_second) + offset_second).astype(
        jnp.bfloat16
    )
    branch_b, qkv_b, merged_b = attention_forward(
        normalized_second, gathered[4], gathered[5], temporal_mask, head_count
    )
    residual_third = residual_second + gate_b * branch_b
    standardized_third, inverse_deviation_third = layer_norm_apply(residual_third)
    normalized_third = (standardized_third * (1.0 + scale_third) + offset_third).astype(
        jnp.bfloat16
    )
    pre_act = jnp.dot(normalized_third, gathered[6], preferred_element_type=jnp.float32)
    act_out, gelu_pull = jax.vjp(jax.nn.gelu, pre_act)
    hidden = act_out.astype(jnp.bfloat16)
    branch_c = jnp.dot(hidden, gathered[7], preferred_element_type=jnp.float32)
    result = residual_third + gate_c * branch_c
    back_weights = gathered
    output_gradient = cotangent.astype(jnp.float32)
    gate_gradient_third = output_gradient * branch_c
    grad_branch_c = (gate_c * output_gradient).astype(jnp.bfloat16)
    grad_hidden = contract_cols(grad_branch_c, back_weights[7])
    grad_pre = gelu_pull(grad_hidden)[0].astype(jnp.bfloat16)
    normalized_gradient_third = contract_cols(grad_pre, back_weights[6])
    residual_gradient = output_gradient + layer_norm_reverse(
        normalized_gradient_third, standardized_third, inverse_deviation_third, scale_third
    )
    gate_gradient_second = residual_gradient * branch_b
    grad_branch_b = (gate_b * residual_gradient).astype(jnp.bfloat16)
    normalized_gradient_second, grad_qkv_t = attention_backward(
        grad_branch_b, qkv_b, back_weights[4], back_weights[5], temporal_mask, head_count
    )
    residual_gradient = residual_gradient + layer_norm_reverse(
        normalized_gradient_second, standardized_second, inverse_deviation_second, scale_second
    )
    gate_gradient_first = residual_gradient * branch_a
    grad_branch_a = (gate_a * residual_gradient).astype(jnp.bfloat16)
    normalized_gradient_first, grad_qkv_s = attention_backward(
        grad_branch_a, qkv_a, back_weights[2], back_weights[3], spatial_mask, head_count
    )
    residual_gradient = residual_gradient + layer_norm_reverse(
        normalized_gradient_first, standardized_first, inverse_deviation_first, scale_first
    )
    grad_mod = jnp.concatenate(
        [
            exact_rows(
                one_hot,
                jnp.concatenate(
                    [
                        normalized_gradient_first,
                        normalized_gradient_first * standardized_first,
                        gate_gradient_first,
                    ],
                    axis=1,
                ),
            ),
            exact_rows(
                one_hot,
                jnp.concatenate(
                    [
                        normalized_gradient_second,
                        normalized_gradient_second * standardized_second,
                        gate_gradient_second,
                    ],
                    axis=1,
                ),
            ),
            exact_rows(
                one_hot,
                jnp.concatenate(
                    [
                        normalized_gradient_third,
                        normalized_gradient_third * standardized_third,
                        gate_gradient_third,
                    ],
                    axis=1,
                ),
            ),
        ],
        axis=1,
    )
    grad_mod_low = grad_mod.astype(jnp.bfloat16)
    all_grad_mod = lax.all_gather(grad_mod_low, axes, axis=0, tiled=True)
    bias_share = lax.psum_scatter(
        jnp.sum(grad_mod, axis=0), axes, scatter_dimension=0, tiled=True
    )

    def share(left, right):
        return lax.psum_scatter(
            contract_rows(left, right).astype(jnp.bfloat16),
            axes,
            scatter_dimension=0,
            tiled=True,
        ).astype(jnp.float32)

    return (
        result.astype(jnp.bfloat16),
        residual_gradient,
        contract_rows(cond_rows, all_grad_mod),
        bias_share,
        share(normalized_first, grad_qkv_s),
        share(merged_a, grad_branch_a),
        share(normalized_second, grad_qkv_t),
        share(merged_b, grad_branch_b),
        share(normalized_third, grad_pre),
        share(hidden, grad_branch_c),
    )


def solution(mesh):
    placed = (
        P(("wide", "narrow"), None),
        P(("wide", "narrow")),
        P(("wide", "narrow")),
        P(("wide", "narrow")),
        P(("wide", "narrow")),
        P(("wide", "narrow"), None),
        P(("wide", "narrow")),
        P(("wide", "narrow"), None),
        P(("wide", "narrow"), None),
        P(("wide", "narrow"), None),
        P(("wide", "narrow"), None),
        P(("wide", "narrow"), None),
        P(("wide", "narrow"), None),
        P(("wide", "narrow"), None),
    )
    grid = dict(mesh.shape) == {"wide": 16, "narrow": 2}
    return jax.shard_map(
        on_grid if grid else on_device,
        mesh=mesh,
        in_specs=placed,
        out_specs=(
            P(("wide", "narrow"), None),
            P(("wide", "narrow"), None),
            P(("wide", "narrow"), None),
            P(("wide", "narrow")),
            P(("wide", "narrow"), None),
            P(("wide", "narrow"), None),
            P(("wide", "narrow"), None),
            P(("wide", "narrow"), None),
            P(("wide", "narrow"), None),
            P(("wide", "narrow"), None),
        ),
        check_vma=False,
    )
```

```python
from functools import partial
import math

import jax
import jax.numpy as jnp
from jax import lax
from jax.experimental import pallas as pl
from jax.experimental.pallas import tpu as pltpu
from jax.sharding import PartitionSpec as P

HEADS = 12


EPSILON = 1e-06
FREQ_BASE = 10000.0
MASKED = -1e30


def time_embed(step_ids, width):
    half_width = width // 2
    frequency = jnp.exp(
        -math.log(FREQ_BASE) * jnp.arange(half_width, dtype=jnp.float32) / half_width
    )
    angles = step_ids.astype(jnp.float32)[:, None] * frequency[None, :]
    return jnp.concatenate([jnp.cos(angles), jnp.sin(angles)], axis=1)


def contract_rows(left, right):
    return lax.dot_general(
        left, right, (((0,), (0,)), ((), ())), preferred_element_type=jnp.float32
    )


def contract_cols(left, right):
    return lax.dot_general(
        left, right, (((1,), (1,)), ((), ())), preferred_element_type=jnp.float32
    )


def exact_rows(left, right):
    return lax.dot_general(
        left,
        right,
        (((0,), (0,)), ((), ())),
        precision=lax.Precision.HIGHEST,
        preferred_element_type=jnp.float32,
    )


def layer_norm_apply(stream):
    center = stream - jnp.mean(stream, axis=-1, keepdims=True)
    inverse_deviation = lax.rsqrt(jnp.mean(center * center, axis=-1, keepdims=True) + EPSILON)
    return (center * inverse_deviation, inverse_deviation)


def layer_norm_reverse(normalized_gradient, standardized_input, inverse_deviation, row_scales):
    input_gradient = normalized_gradient * (1.0 + row_scales)
    mean_removed = input_gradient - jnp.mean(input_gradient, axis=-1, keepdims=True)
    return inverse_deviation * (
        mean_removed
        - standardized_input * jnp.mean(input_gradient * standardized_input, axis=-1, keepdims=True)
    )


def sublayer_mod(one_hot, modulation, sublayer, width):
    table = modulation[:, 3 * width * sublayer : 3 * width * (sublayer + 1)]
    rows_mod = jnp.dot(
        one_hot, table, precision=lax.Precision.HIGHEST, preferred_element_type=jnp.float32
    )
    return (rows_mod[:, :width], rows_mod[:, width : 2 * width], rows_mod[:, 2 * width :])


def head_probs(allowed, scale, queries, key_vecs):
    scores = contract_cols(queries, key_vecs) * scale
    scores = jnp.where(allowed, scores, MASKED)
    return jax.nn.softmax(scores, axis=-1)


def head_forward(allowed, scale, item):
    queries, key_vecs, val_vecs = item
    attn_prob = head_probs(allowed, scale, queries, key_vecs)
    return jnp.dot(attn_prob.astype(jnp.bfloat16), val_vecs, preferred_element_type=jnp.float32)


def head_backward(allowed, scale, item):
    queries, key_vecs, val_vecs, grad_att = item
    attn_prob = head_probs(allowed, scale, queries, key_vecs)
    grad_val = contract_rows(attn_prob.astype(jnp.bfloat16), grad_att)
    grad_prob = contract_cols(grad_att, val_vecs)
    grad_score = attn_prob * (grad_prob - jnp.sum(attn_prob * grad_prob, axis=-1, keepdims=True))
    score_low = grad_score.astype(jnp.bfloat16)
    grad_query = jnp.dot(score_low, key_vecs, preferred_element_type=jnp.float32) * scale
    grad_key = contract_rows(score_low, queries) * scale
    return (grad_query, grad_key, grad_val)


def split_heads(qkv_rows, head_count):
    row_count = qkv_rows.shape[0]
    return qkv_rows.reshape(row_count, 3, head_count, -1).transpose(1, 2, 0, 3)


def attention_forward(normed, w_qkv, w_out, allowed, head_count):
    row_count = normed.shape[0]
    qkv_rows = jnp.dot(normed, w_qkv, preferred_element_type=jnp.float32).astype(jnp.bfloat16)
    split_qkv = split_heads(qkv_rows, head_count)
    scale = split_qkv.shape[-1] ** (-0.5)
    attended = lax.map(
        partial(head_forward, allowed, scale), (split_qkv[0], split_qkv[1], split_qkv[2])
    )
    merged = attended.transpose(1, 0, 2).reshape(row_count, -1).astype(jnp.bfloat16)
    branch = jnp.dot(merged, w_out, preferred_element_type=jnp.float32)
    return (branch, qkv_rows, merged)


def attention_backward(grad_branch, qkv_rows, w_qkv, w_out, allowed, head_count):
    row_count = qkv_rows.shape[0]
    grad_merged = contract_cols(grad_branch, w_out).astype(jnp.bfloat16)
    grad_heads = grad_merged.reshape(row_count, head_count, -1).transpose(1, 0, 2)
    split_qkv = split_heads(qkv_rows, head_count)
    scale = split_qkv.shape[-1] ** (-0.5)
    grad_query, grad_key, grad_val = lax.map(
        partial(head_backward, allowed, scale),
        (split_qkv[0], split_qkv[1], split_qkv[2], grad_heads),
    )
    grad_qkv = (
        jnp.stack([grad_query, grad_key, grad_val])
        .transpose(2, 0, 1, 3)
        .reshape(row_count, -1)
        .astype(jnp.bfloat16)
    )
    normalized_gradient = contract_cols(grad_qkv, w_qkv)
    return (normalized_gradient, grad_qkv)


MESH = pl.DeviceIdType.MESH


class Spot:
    def __init__(self):
        chip = lax.axis_index("wide")
        core = lax.axis_index("narrow")
        z, y, x = lax.div(chip, 4), lax.rem(lax.div(chip, 2), 2), lax.rem(chip, 2)
        half = lax.div(z, 2)
        toward = 1 - 2 * half
        self.chip, self.core, self.z, self.y, self.x = chip, core, z, y, x
        self.half = half
        self.middle = z + half * (3 - 2 * z)
        self.is_middle = self.middle == 1
        self.is_end = self.middle == 0
        self.plane = 2 * y + x
        self.inner = ((z + toward) * 4 + self.plane, core)
        self.outer = ((z - toward) * 4 + self.plane, core)
        self.first_plane = 2 * lax.rem(y + core, 2) + lax.rem(x + 1 - core, 2)
        self.second_plane = 2 * lax.rem(y + 1 - core, 2) + lax.rem(x + core, 2)
        self.far_plane = 3 - self.plane
        self.first = (z * 4 + self.first_plane, core)
        self.second = (z * 4 + self.second_plane, core)
        self.far = (z * 4 + self.far_plane, core)
        self.twin = (chip, 1 - core)
        self.mates = (
            (self.first_plane, self.first),
            (self.second_plane, self.second),
            (self.far_plane, self.far),
        )
        self.line = [
            (lax.rem(z + j, 4), (lax.rem(z + j, 4) * 4 + self.plane, core)) for j in (1, 2, 3)
        ]

    def layer(self, mirrored):
        return mirrored + self.half * (3 - 2 * mirrored)

    def arrival(self, k):
        return (self.z, self.layer(1 - self.middle), self.layer(2), self.layer(3))[k]


def greet(spot, meanwhile):
    barrier = pltpu.get_barrier_semaphore()
    for device in [spot.twin] + [device for _, device in spot.mates + tuple(spot.line)]:
        pl.semaphore_signal(barrier, inc=1, device_id=device, device_id_type=MESH)
    meanwhile()
    pl.semaphore_wait(barrier, 7)


def remote(src, dst, send, recv, device):
    return pltpu.make_async_remote_copy(
        src_ref=src,
        dst_ref=dst,
        send_sem=send,
        recv_sem=recv,
        device_id=device,
        device_id_type=MESH,
    )


class Exchange:
    def __init__(self, places, mine, src, dst, send, recv):
        self.places, self.mine = places, mine
        self.src, self.dst = src, dst
        self.send, self.recv = send, recv

    def copy(self, i):
        place, device = self.places[i]
        return remote(
            self.src(place), self.dst(self.mine), self.send.at[i], self.recv.at[self.mine], device
        )

    def start(self):
        for i in range(3):
            self.copy(i).start()

    def arrive(self):
        for place, device in self.places:
            ref = self.dst(place)
            remote(ref, ref, self.send.at[0], self.recv.at[place], device).wait_recv()

    def drain(self):
        for i in range(3):
            self.copy(i).wait_send()


class LineSum:
    def __init__(self, spot, part, slot, send, recv):
        self.spot, self.part, self.slot = spot, part, slot
        self.send, self.recv = send, recv

    def layer(self, k):
        spot = self.spot
        return (spot.layer(3), spot.layer(2), spot.layer(1 - spot.middle), spot.z)[k]

    def copy(self, k, slot, device):
        return remote(
            self.part(self.layer(k)), self.slot(slot), self.send.at[k], self.recv.at[slot], device
        )

    def from_end(self, k):
        return self.copy(k, k, self.spot.inner)

    def from_middle(self, k):
        return self.copy(k, 3 + k, self.spot.inner) if k < 2 else self.copy(2, 3, self.spot.outer)

    def arrived(self, slot):
        self.copy(0, slot, self.spot.inner).wait_recv()
        return self.slot(slot)

    def send_end(self, k):
        pl.when(self.spot.is_end)(lambda: self.from_end(k).start())

    def send_middle(self, k):
        @pl.when(self.spot.is_middle)
        def _():
            source, part = self.arrived((0, 1, 3)[k]), self.part(self.layer(k))
            for i in range(part.shape[0]):
                part[i] += source[i]
            self.from_middle(k).start()

    def total(self, put):
        def add(*slots):
            sources = [self.arrived(slot) for slot in slots]
            part = self.part(self.spot.z)
            for i in range(part.shape[0]):
                value = part[i].astype(jnp.float32)
                for source in sources:
                    value += source[i].astype(jnp.float32)
                put(i, value)

        pl.when(self.spot.is_end)(lambda: add(3))
        pl.when(self.spot.is_middle)(lambda: add(2, 4))

    def drain(self):
        for k in range(3):
            self.from_end(k).wait_send()


class LineGather:
    def __init__(self, spot, part, send, recv):
        self.spot, self.part = spot, part
        self.send, self.recv = send, recv

    def copy(self, z, send, device):
        ref = self.part(z)
        return remote(ref, ref, self.send.at[send], self.recv.at[z], device)

    def own(self, inward):
        spot = self.spot
        return self.copy(spot.z, 0 if inward else 1, spot.inner if inward else spot.outer)

    def onward(self, k):
        spot = self.spot
        return self.copy(spot.arrival(k), 1 + k, spot.inner if k == 1 else spot.outer)

    def open(self):
        self.own(True).start()
        pl.when(self.spot.is_middle)(lambda: self.own(False).start())

    def get(self, k):
        self.copy(self.spot.arrival(k), 0, self.spot.inner).wait_recv()

    def pass_on(self, k):
        @pl.when(self.spot.is_middle)
        def _():
            self.get(k)
            self.onward(k).start()

    def take(self, k):
        pl.when(self.spot.is_end)(lambda: self.get(k))

    def drain(self):
        self.own(True).wait_send()

        @pl.when(self.spot.is_middle)
        def _():
            self.own(False).wait_send()
            for k in (1, 2, 3):
                self.onward(k).wait_send()


class Gather:
    def __init__(self, spot, held, stage, apart, swap_sems, send, recv, count):
        self.spot, self.held, self.count = spot, held, count
        self.split = count < 4
        self.stage, self.apart, self.swap_sems = stage, apart, swap_sems
        self.send, self.recv = send, recv
        self.whole = apart.shape[1] == 48
        self.line = LineGather(
            spot,
            lambda z: self.last_layer(spot.core, z),
            send.at[pl.ds(24, 5)],
            recv.at[pl.ds(23, 4)],
        )

    def block(self, z, plane):
        return self.held.at[self.spot.core, z * 4 + plane, 0 : self.count]

    def last_layer(self, half, z):
        return self.held.at[half, pl.ds(z * 4, 4), 3]

    def last(self, plane):
        return self.held.at[self.spot.core, self.spot.z * 4 + plane, 3]

    def copy(self, ref, send, recv, device):
        return remote(ref, ref, self.send.at[send], self.recv.at[recv], device)

    def mine(self):
        core = self.spot.core
        if self.whole:
            return self.stage.at[pl.ds(2 * core, 2)]
        return self.stage.at[:, pl.ds(pl.multiple_of(core * 24, 8), 24), :]

    def swap(self):
        return remote(
            self.apart, self.mine(), self.swap_sems.at[0], self.swap_sems.at[1], self.spot.twin
        )

    def open(self, piece):
        core = self.spot.core
        for chunk in range(self.apart.shape[0]):
            self.apart[chunk] = piece(1 - core, chunk).astype(jnp.float32)
        place = self.mine()
        for chunk in range(self.apart.shape[0]):
            place[chunk] = piece(core, chunk).astype(jnp.float32)

    def own(self):
        spot = self.spot
        self.swap().wait_recv()
        self.held[spot.core, spot.chip] = self.stage[...].astype(jnp.bfloat16)
        self.z_own(True).start()
        pl.when(spot.is_middle)(lambda: self.z_own(False).start())
        if self.split:
            self.last_first().start()
            self.last_second(False).start()

    def z_own(self, inward):
        spot = self.spot
        return self.copy(
            self.block(spot.z, spot.plane),
            0 if inward else 1,
            spot.z,
            spot.inner if inward else spot.outer,
        )

    def z_pass(self, k):
        spot = self.spot
        z = spot.arrival(k)
        return self.copy(
            self.block(z, spot.plane), 1 + k, z, spot.inner if k == 1 else spot.outer
        )

    def first_copy(self, k):
        z = self.spot.arrival(k)
        return self.copy(self.block(z, self.spot.plane), 5 + k, 4 + z, self.spot.first)

    def second_copy(self, k):
        z = self.spot.arrival(k)
        return self.copy(self.block(z, self.spot.plane), 9 + k, 8 + z, self.spot.second)

    def second_pass(self, k):
        z = self.spot.arrival(k)
        return self.copy(self.block(z, self.spot.first_plane), 13 + k, 12 + z, self.spot.second)

    def twin_copy(self, half, k):
        z = self.spot.arrival(k)
        ref = self.held.at[half, pl.ds(z * 4, 4), 0 : self.count]
        return self.copy(ref, 17 + k, 16 + z, self.spot.twin)

    def last_first(self):
        return self.copy(self.last(self.spot.plane), 21, 20, self.spot.first)

    def last_second(self, onward):
        spot = self.spot
        plane = spot.first_plane if onward else spot.plane
        return self.copy(self.last(plane), 23 if onward else 22, 22 if onward else 21, spot.second)

    def last_twin(self, half, k):
        z = self.spot.arrival(k)
        ref = self.last_layer(half, z)
        return self.copy(ref, 29 + k, 27 + z, self.spot.twin)

    def get(self, k):
        spot = self.spot
        z = spot.arrival(k)
        self.copy(self.block(z, spot.plane), 0, z, spot.inner).wait_recv()

    def pass_on(self, k):
        @pl.when(self.spot.is_middle)
        def _():
            self.get(k)
            self.z_pass(k).start()

    def spread(self, k):
        if k:
            pl.when(self.spot.is_end)(lambda: self.get(k))
        self.first_copy(k).start()
        self.second_copy(k).start()

    def along_first(self, k):
        spot = self.spot
        z = spot.arrival(k)
        self.copy(self.block(z, spot.first_plane), 0, 4 + z, spot.first).wait_recv()
        self.second_pass(k).start()

    def along_second(self, k):
        spot = self.spot
        z = spot.arrival(k)
        self.copy(self.block(z, spot.second_plane), 0, 8 + z, spot.second).wait_recv()
        self.copy(self.block(z, spot.far_plane), 0, 12 + z, spot.second).wait_recv()
        self.twin_copy(spot.core, k).start()

    def last_along_first(self):
        spot = self.spot
        self.copy(self.last(spot.first_plane), 0, 20, spot.first).wait_recv()
        self.last_second(True).start()

    def last_along_second(self):
        spot = self.spot
        self.copy(self.last(spot.second_plane), 0, 21, spot.second).wait_recv()
        self.copy(self.last(spot.far_plane), 0, 22, spot.second).wait_recv()
        self.line.open()
        self.last_twin(spot.core, 0).start()

    def last_along_z(self, k):
        self.line.take(k)
        self.last_twin(self.spot.core, k).start()

    def landed(self):
        for k in range(4):
            self.twin_copy(1 - self.spot.core, k).wait_recv()
            if self.split:
                self.last_twin(1 - self.spot.core, k).wait_recv()

    def drain(self):
        spot = self.spot
        self.z_own(True).wait_send()

        @pl.when(spot.is_middle)
        def _():
            self.z_own(False).wait_send()
            for k in (1, 2, 3):
                self.z_pass(k).wait_send()

        for k in range(4):
            self.first_copy(k).wait_send()
            self.second_copy(k).wait_send()
            self.second_pass(k).wait_send()
            self.twin_copy(spot.core, k).wait_send()
            if self.split:
                self.last_twin(spot.core, k).wait_send()
        if self.split:
            self.last_first().wait_send()
            self.last_second(False).wait_send()
            self.last_second(True).wait_send()
            self.line.drain()


class Scatter:
    def __init__(
        self, spot, sums, from_second, from_first, from_z, last_pair, last_one, last_z, final,
        theirs, send, recv, credit, owed,
    ):
        self.spot, self.sums = spot, sums
        self.from_second, self.from_first = from_second, from_first
        self.last_pair, self.last_one = last_pair, last_one
        self.final, self.theirs = final, theirs
        self.send, self.recv, self.credit = send, recv, credit
        self.owed, self.whole = owed, theirs.shape[1] == 48
        self.line = LineSum(
            spot,
            lambda z: sums.at[4 * z, 0:3],
            lambda i: from_z.at[i],
            send.at[pl.ds(8, 3)],
            recv.at[pl.ds(8, 5)],
        )
        self.last_line = LineSum(
            spot,
            lambda z: sums.at[pl.ds(4 * z, 4), 3],
            lambda i: last_z.at[i],
            send.at[pl.ds(12, 3)],
            recv.at[pl.ds(14, 5)],
        )

    def place(self, chip):
        spot = self.spot
        z, y, x = chip // 4, (chip // 2) % 2, chip % 2
        other_y, other_x = lax.rem(spot.y + y, 2), lax.rem(spot.x + x, 2)
        second = other_y * (1 - spot.core) + other_x * spot.core
        first = other_x * (1 - spot.core) + other_y * spot.core
        return 4 * z + 2 * second + first

    def second_copy(self, k):
        z = self.line.layer(k)
        return remote(
            self.sums.at[pl.ds(4 * z + 2, 2), 0:3],
            self.from_second.at[z],
            self.send.at[k],
            self.recv.at[z],
            self.spot.second,
        )

    def first_copy(self, k):
        z = self.line.layer(k)
        return remote(
            self.sums.at[4 * z + 1, 0:3],
            self.from_first.at[z],
            self.send.at[4 + k],
            self.recv.at[4 + z],
            self.spot.first,
        )

    def last_second_copy(self):
        return remote(
            self.sums.at[pl.ds(4 * self.spot.z + 2, 2), 3],
            self.last_pair,
            self.send.at[15],
            self.recv.at[19],
            self.spot.second,
        )

    def last_first_copy(self):
        return remote(
            self.sums.at[4 * self.spot.z + 1, 3],
            self.last_one,
            self.send.at[16],
            self.recv.at[20],
            self.spot.first,
        )

    def swap(self):
        core = self.spot.core
        if self.whole:
            src = self.final.at[pl.ds(2 * (1 - core), 2)]
        else:
            src = self.final.at[:, pl.ds(pl.multiple_of((1 - core) * 24, 8), 24), :]
        return remote(src, self.theirs, self.send.at[11], self.recv.at[13], self.spot.twin)

    def wait_credit(self):
        spot = self.spot
        if self.owed:
            for kind in range(3):
                pl.semaphore_wait(self.credit.at[kind], 1)
            pl.when(spot.is_middle)(lambda: pl.semaphore_wait(self.credit.at[3], 1))

    def add_second(self, k):
        z = self.line.layer(k)
        self.second_copy(k).wait_recv()
        for first in (1, 0):
            for chunk in range(3):
                self.sums[4 * z + first, chunk] += self.from_second[z, first, chunk]
            if first:
                self.first_copy(k).start()

    def add_first(self, k):
        z = self.line.layer(k)
        self.first_copy(k).wait_recv()
        for chunk in range(3):
            self.sums[4 * z, chunk] += self.from_first[z, chunk]
        if k < 3:
            self.line.send_end(k)

    def finish(self):
        def put(i, value):
            self.final[i] = value

        self.line.total(put)

    def last_total(self):
        at = 4 * self.spot.z

        def put(i, value):
            self.sums[at + i, 3] = value.astype(jnp.bfloat16)

        self.last_line.total(put)
        self.last_second_copy().start()

    def last_add_second(self):
        at = 4 * self.spot.z
        self.last_second_copy().wait_recv()
        self.sums[at + 1, 3] += self.last_pair[1]
        self.last_first_copy().start()
        self.sums[at, 3] += self.last_pair[0]

    def last_finish(self):
        self.last_first_copy().wait_recv()
        self.final[3] = self.sums[4 * self.spot.z, 3].astype(jnp.float32) + self.last_one[
            ...
        ].astype(jnp.float32)

    def store(self, put):
        core = self.spot.core
        for chunk in range(self.theirs.shape[0]):
            if self.whole:
                mine = self.final[2 * core + chunk]
            else:
                mine = self.final[chunk, pl.ds(pl.multiple_of(core * 24, 8), 24), :]
            put(core, chunk, mine)
        self.swap().wait_recv()
        for chunk in range(self.theirs.shape[0]):
            put(1 - core, chunk, self.theirs[chunk])
        self.swap().wait_send()

    def drain(self):
        for k in range(4):
            self.second_copy(k).wait_send()
            self.first_copy(k).wait_send()
        self.line.drain()
        self.last_line.drain()
        self.last_second_copy().wait_send()
        self.last_first_copy().wait_send()

    def release(self):
        spot, credit = self.spot, self.credit

        def tell(kind, device):
            pl.semaphore_signal(credit.at[kind], inc=1, device_id=device, device_id_type=MESH)

        tell(0, spot.second)
        tell(1, spot.first)

        @pl.when(spot.is_end)
        def _():
            tell(3, spot.inner)

        @pl.when(spot.is_middle)
        def _():
            tell(2, spot.inner)
            tell(2, spot.outer)


(
    DO_STEPS, DO_COND, DO_MODT, DO_MODZ, DO_MODS, DO_MODM, DO_MODROWS, DO_OWN, DO_GZ, DO_GS, DO_GX,
    DO_GY, DO_LX, DO_LY, DO_LP, DO_LZ, DO_LANDED, DO_CWAIT, DO_SS, DO_SY, DO_SX, DO_SZ, DO_SFIN,
    DO_TE, DO_TZ, DO_TTOT, DO_TY, DO_TX, DO_SWAP, DO_RETIRE, DO_ROWM, DO_ROWZ, DO_ROWP, DO_ROWT,
    DO_ROWD, DO_MASKS, DO_STANDARDIZE, DO_MODULATE, DO_PROJECT, DO_TURNN, DO_TURNA, DO_ATTEND,
    DO_JOIN, DO_ADD, DO_GATE, DO_EXPAND, DO_SENDH, DO_NEEDH, DO_DOWNT, DO_GHID, DO_SENDP,
    DO_CONTRACT, DO_CLOSE, DO_NEEDP, DO_UPT, DO_BACK2, DO_NORMB, DO_SPLIT, DO_ATTB, DO_SENDQ,
    DO_NEEDG, DO_NEEDQ, DO_OUTT, DO_QKVT, DO_BACK, DO_SENTQ,
) = range(66)

ORDER = (
    (DO_CWAIT, 0), (DO_CWAIT, 1), (DO_MASKS,), (DO_STANDARDIZE, 0), (DO_STEPS, 0), (DO_OWN, 0), (DO_GS, 0, 0),
    (DO_OWN, 1), (DO_GS, 1, 0), (DO_STEPS, 1), (DO_GZ, 0, 1), (DO_GS, 0, 1), (DO_GZ, 0, 2), (DO_LX, 1), (DO_GX, 0, 0),
    (DO_GZ, 1, 1), (DO_GZ, 1, 2), (DO_GS, 1, 1), (DO_COND,), (DO_MODT, 0), (DO_MODT, 1), (DO_GZ, 0, 3), (DO_GS, 0, 2),
    (DO_MODZ, 0), (DO_GZ, 1, 3), (DO_MODZ, 1), (DO_GX, 0, 1), (DO_GY, 0, 0), (DO_GS, 1, 2), (DO_LY, 1), (DO_GS, 0, 3),
    (DO_MODS, 0), (DO_MODM, 0), (DO_MODS, 1), (DO_GX, 0, 2), (DO_OWN, 2), (DO_GY, 0, 1), (DO_LP, 1, 2), (DO_GX, 0, 3),
    (DO_MODS, 2), (DO_LP, 1, 1), (DO_LZ, 1, 1), (DO_LX, 2), (DO_GS, 1, 3), (DO_MODROWS, 0), (DO_MODULATE, 0),
    (DO_GZ, 2, 1), (DO_GY, 0, 2), (DO_GZ, 2, 2), (DO_GX, 1, 0), (DO_LZ, 1, 2), (DO_GX, 1, 1), (DO_GY, 0, 3),
    (DO_LP, 1, 3), (DO_MODM, 1), (DO_LY, 2), (DO_GX, 1, 2), (DO_LANDED, 0), (DO_PROJECT, 0), (DO_GY, 1, 0),
    (DO_GZ, 2, 3), (DO_GX, 1, 3), (DO_TURNN, 0), (DO_MODROWS, 1), (DO_GY, 1, 1), (DO_GS, 2, 0), (DO_ATTEND, 0, 0),
    (DO_GY, 1, 2), (DO_LZ, 1, 3), (DO_LP, 2, 1), (DO_LP, 2, 2), (DO_GS, 2, 1), (DO_ATTEND, 0, 1), (DO_GY, 1, 3),
    (DO_LZ, 2, 1), (DO_GS, 2, 2), (DO_OWN, 3), (DO_ATTEND, 0, 2), (DO_GS, 2, 3), (DO_JOIN, 0), (DO_ADD, 0),
    (DO_LP, 2, 3), (DO_TURNA, 0), (DO_GX, 2, 0), (DO_STANDARDIZE, 1), (DO_MODULATE, 1), (DO_LZ, 2, 2), (DO_GZ, 3, 1),
    (DO_GZ, 3, 2), (DO_GATE, 2), (DO_GX, 2, 1), (DO_LX, 3), (DO_LANDED, 1), (DO_PROJECT, 1), (DO_GX, 2, 2),
    (DO_TURNN, 1), (DO_GY, 2, 0), (DO_GX, 2, 3), (DO_ATTEND, 1, 0), (DO_GY, 2, 1), (DO_LZ, 2, 3), (DO_GZ, 3, 3),
    (DO_GS, 3, 0), (DO_LY, 3), (DO_ATTEND, 1, 1), (DO_GY, 2, 2), (DO_GS, 3, 1), (DO_GY, 2, 3), (DO_ATTEND, 1, 2),
    (DO_GS, 3, 2), (DO_JOIN, 1), (DO_ADD, 1), (DO_GS, 3, 3), (DO_TURNA, 1), (DO_LP, 3, 1), (DO_LP, 3, 2),
    (DO_STANDARDIZE, 2), (DO_MODULATE, 2), (DO_GX, 3, 0), (DO_TURNN, 2), (DO_LZ, 3, 1), (DO_LANDED, 2),
    (DO_EXPAND, 0), (DO_SENDH, 0), (DO_GX, 3, 1), (DO_EXPAND, 1), (DO_GX, 3, 2), (DO_SENDH, 1), (DO_EXPAND, 2),
    (DO_LP, 3, 3), (DO_LZ, 3, 2), (DO_GX, 3, 3), (DO_SENDH, 2), (DO_EXPAND, 3), (DO_GY, 3, 0), (DO_SENDH, 3),
    (DO_GY, 3, 1), (DO_NEEDH, 0), (DO_DOWNT, 0), (DO_NEEDH, 1), (DO_DOWNT, 1), (DO_GY, 3, 2), (DO_NEEDH, 2),
    (DO_DOWNT, 2), (DO_GY, 3, 3), (DO_NEEDH, 3), (DO_DOWNT, 3), (DO_TE, 0, 0), (DO_SS, 0, 0), (DO_TE, 0, 1),
    (DO_LZ, 3, 3), (DO_LANDED, 3), (DO_SS, 0, 1), (DO_GHID, 0), (DO_GHID, 1), (DO_SENDP,), (DO_GHID, 2),
    (DO_TE, 0, 2), (DO_SS, 0, 2), (DO_GHID, 3), (DO_SY, 0, 0), (DO_NEEDP,), (DO_UPT, 3), (DO_TZ, 0, 0), (DO_UPT, 0),
    (DO_TE, 1, 0), (DO_UPT, 1), (DO_SY, 0, 1), (DO_UPT, 2), (DO_SS, 0, 3), (DO_CONTRACT,), (DO_SX, 0, 0),
    (DO_TZ, 0, 1), (DO_CLOSE,), (DO_SY, 0, 2), (DO_BACK2, 0), (DO_TE, 1, 1), (DO_TZ, 0, 2), (DO_SX, 0, 1),
    (DO_SS, 1, 0), (DO_BACK2, 1), (DO_BACK2, 2), (DO_SY, 0, 3), (DO_BACK2, 3), (DO_TZ, 1, 0), (DO_SX, 0, 2),
    (DO_SS, 1, 1), (DO_NORMB, 2), (DO_GATE, 1), (DO_SZ, 0, 0), (DO_SS, 1, 2), (DO_SPLIT, 1), (DO_SY, 1, 0),
    (DO_TTOT, 0), (DO_ATTB, 1, 0), (DO_SX, 0, 3), (DO_SY, 1, 1), (DO_TE, 1, 2), (DO_TZ, 1, 1), (DO_TZ, 1, 2),
    (DO_ATTB, 1, 1), (DO_SZ, 0, 1), (DO_SZ, 0, 2), (DO_SX, 1, 0), (DO_SS, 1, 3), (DO_NEEDG, 1), (DO_OUTT, 1),
    (DO_ATTB, 1, 2), (DO_SY, 1, 2), (DO_SX, 1, 1), (DO_TY, 0), (DO_SENDQ, 1), (DO_BACK, 1, 0), (DO_TTOT, 1),
    (DO_NEEDQ, 1), (DO_QKVT, 1, 0), (DO_SY, 1, 3), (DO_SFIN, 0), (DO_QKVT, 1, 1), (DO_SZ, 1, 0), (DO_SX, 1, 2),
    (DO_TX, 0), (DO_SWAP, 0), (DO_QKVT, 1, 2), (DO_TY, 1), (DO_BACK, 1, 1), (DO_SZ, 1, 1), (DO_RETIRE, 0),
    (DO_SX, 1, 3), (DO_CWAIT, 2), (DO_TE, 2, 0), (DO_SS, 2, 0), (DO_BACK, 1, 2), (DO_TE, 2, 1), (DO_TX, 1),
    (DO_NORMB, 1), (DO_SZ, 1, 2), (DO_ROWM, 1), (DO_SS, 2, 1), (DO_SENTQ, 1), (DO_GATE, 0), (DO_TE, 2, 2),
    (DO_SPLIT, 0), (DO_ATTB, 0, 0), (DO_SY, 2, 0), (DO_TZ, 2, 0), (DO_ATTB, 0, 1), (DO_ROWZ, 1), (DO_SY, 2, 1),
    (DO_TZ, 2, 1), (DO_SFIN, 1), (DO_SWAP, 1), (DO_SS, 2, 2), (DO_NEEDG, 0), (DO_OUTT, 0), (DO_SX, 2, 0),
    (DO_RETIRE, 1), (DO_ATTB, 0, 2), (DO_CWAIT, 3), (DO_TE, 3, 0), (DO_TZ, 2, 2), (DO_SS, 2, 3), (DO_SENDQ, 0),
    (DO_SX, 2, 1), (DO_BACK, 0, 0), (DO_ROWP, 1, 1), (DO_ROWP, 1, 2), (DO_NEEDQ, 0), (DO_SY, 2, 2), (DO_QKVT, 0, 0),
    (DO_QKVT, 0, 1), (DO_SZ, 2, 0), (DO_QKVT, 0, 2), (DO_TE, 3, 1), (DO_SS, 3, 0), (DO_BACK, 0, 1), (DO_BACK, 0, 2),
    (DO_SY, 2, 3), (DO_SX, 2, 2), (DO_TZ, 3, 0), (DO_TTOT, 2), (DO_SS, 3, 1), (DO_ROWP, 1, 3), (DO_NORMB, 0),
    (DO_ROWM, 0), (DO_SZ, 2, 1), (DO_TE, 3, 2), (DO_SENTQ, 0), (DO_SZ, 2, 2), (DO_SY, 3, 0), (DO_SX, 2, 3),
    (DO_SS, 3, 2), (DO_TY, 2), (DO_ROWT, 1), (DO_TZ, 3, 1), (DO_TZ, 3, 2), (DO_ROWD, 1), (DO_SS, 3, 3), (DO_SX, 3, 0),
    (DO_SFIN, 2), (DO_SY, 3, 1), (DO_ROWZ, 0), (DO_TX, 2), (DO_SWAP, 2), (DO_RETIRE, 2), (DO_SY, 3, 2), (DO_TTOT, 3),
    (DO_SZ, 3, 0), (DO_SX, 3, 1), (DO_ROWP, 0, 1), (DO_ROWP, 0, 2), (DO_SY, 3, 3), (DO_SX, 3, 2), (DO_TY, 3),
    (DO_SZ, 3, 1), (DO_SZ, 3, 2), (DO_ROWP, 0, 3), (DO_SX, 3, 3), (DO_TX, 3), (DO_SFIN, 3), (DO_SWAP, 3),
    (DO_ROWT, 0), (DO_RETIRE, 3), (DO_ROWD, 0),
)


def dot(left, right):
    return jnp.dot(left, right, preferred_element_type=jnp.float32)


GATHER_CHUNKS = (4, 3, 3, 3)


def layer_kernel(
    tokens,
    cotangent,
    steps,
    seg_ids,
    frame_ids,
    patch_ids,
    b_ada,
    w_ada,
    w_qkv_s,
    w_out_s,
    w_qkv_t,
    w_out_t,
    w_up,
    w_down,
    r_layer,
    r_tokens,
    cond,
    all_rows_mod,
    r_qkv_s,
    r_out_s,
    r_qkv_t,
    r_out_t,
    r_up,
    r_down,
    o_layer,
    o_tokens,
    o_qkv_s,
    o_out_s,
    o_qkv_t,
    o_out_t,
    o_up,
    o_down,
    leave_sems,
    held,
    stage,
    apart,
    apart_down,
    sums,
    from_second,
    from_first,
    from_z,
    last_pair,
    last_one,
    last_z,
    all_steps,
    bias,
    ids,
    mod,
    tally,
    xhat,
    deviation,
    normed,
    attended,
    turned,
    hidden_turned,
    qkv,
    probs,
    branch,
    stream,
    grad,
    hidden,
    slope,
    grad_pre_twin,
    gated,
    gated_twin,
    grad_attended,
    grad_qkv_twin,
    disallowed,
    swap_sems,
    gather_send,
    gather_recv,
    scatter_send,
    scatter_recv,
    credit,
    twin_send,
    twin_recv,
    step_send,
    step_recv,
    mod_send,
    mod_recv,
    row_send,
    row_recv,
):
    width, tok = tokens.shape[1], tokens.shape[0]
    f32, bf16 = jnp.float32, jnp.bfloat16
    spot = Spot()
    core = spot.core
    grad_qkv, grad_normed = hidden, stream

    def attention_piece(w_qkv, w_out):
        def piece(half, chunk):
            if chunk < 3:
                return w_qkv[:, pl.ds(pl.multiple_of(half * 1152 + chunk * 384, 128), 384)]
            return w_out[:, pl.ds(pl.multiple_of(half * 384, 128), 384)]

        return piece

    def up_piece(half, chunk):
        return w_up[:, pl.ds(pl.multiple_of(half * 1536 + chunk * 384, 128), 384)]

    def down_piece(half, chunk):
        return w_down[chunk * 48 : chunk * 48 + 48, pl.ds(pl.multiple_of(half * 384, 128), 384)]

    pieces = (
        attention_piece(w_qkv_s, w_out_s),
        attention_piece(w_qkv_t, w_out_t),
        up_piece,
        down_piece,
    )
    gathers = [
        Gather(
            spot,
            held.at[g],
            stage.at[g],
            apart.at[g] if g < 3 else apart_down,
            swap_sems.at[g],
            gather_send.at[g],
            gather_recv.at[g],
            GATHER_CHUNKS[g],
        )
        for g in range(4)
    ]
    scatters = [
        Scatter(
            spot,
            held.at[2, n - 2] if n >= 2 else sums.at[n],
            from_second.at[n % 2],
            from_first.at[n % 2],
            from_z.at[n % 2],
            last_pair.at[n % 2],
            last_one.at[n % 2],
            last_z.at[n % 2],
            stage.at[3 - n],
            apart_down if n == 0 else apart.at[3 - n],
            scatter_send.at[n],
            scatter_recv.at[n],
            credit.at[n % 2],
            n >= 2,
        )
        for n in range(4)
    ]

    def put_attention(o_qkv, o_out):
        def put(half, chunk, rows):
            if chunk < 3:
                o_qkv[:, pl.ds(pl.multiple_of(half * 1152 + chunk * 384, 128), 384)] = rows
            else:
                o_out[:, pl.ds(pl.multiple_of(half * 384, 128), 384)] = rows

        return put

    def put_up(half, chunk, rows):
        o_up[:, pl.ds(pl.multiple_of(half * 1536 + chunk * 384, 128), 384)] = rows

    def put_down(half, chunk, rows):
        o_down[chunk * 48 : chunk * 48 + 48, pl.ds(pl.multiple_of(half * 384, 128), 384)] = rows

    puts = (put_down, put_up, put_attention(o_qkv_t, o_out_t), put_attention(o_qkv_s, o_out_s))

    def to_twin(index, src, dst):
        return remote(src, dst, twin_send.at[index], twin_recv.at[index], spot.twin)

    def turned_copy(i):
        return to_twin(i, turned.at[i, 0], turned.at[i, 1])

    def hidden_copy(i):
        rows = pl.ds(768 * i, 768)
        return to_twin(12 + i, hidden_turned.at[0, rows], hidden_turned.at[1, rows])

    def gated_copy(j):
        theirs = pl.multiple_of((1 - core) * 384, 128)
        return to_twin(6 + j, gated.at[j, :, pl.ds(theirs, 384)], gated_twin.at[j])

    def grad_pre_copy():
        theirs = pl.multiple_of((1 - core) * 1536, 128)
        return to_twin(9, slope.at[:, pl.ds(theirs, 1536)], grad_pre_twin)

    def grad_qkv_copy(j):
        theirs = pl.multiple_of((1 - core) * 1152, 128)
        return to_twin(10 + j, grad_qkv.at[:, pl.ds(theirs, 1152)], grad_qkv_twin.at[j])

    def step_twin(owner):
        ref = all_steps.at[spot.z, spot.plane, owner]
        return remote(ref, ref, step_send.at[0], step_recv.at[0], spot.twin)

    step_line = Exchange(
        spot.line,
        spot.z,
        lambda z: all_steps.at[spot.z, spot.plane],
        lambda z: all_steps.at[z, spot.plane],
        step_send.at[pl.ds(1, 3)],
        step_recv.at[pl.ds(4, 4)],
    )
    step_mates = Exchange(
        spot.mates,
        spot.plane,
        lambda plane: all_steps.at[:, spot.plane],
        lambda plane: all_steps.at[:, plane],
        step_send.at[pl.ds(4, 3)],
        step_recv.at[pl.ds(8, 4)],
    )

    def steps_prepare():
        row = lax.broadcasted_iota(jnp.int32, (8, 128), 0)
        value = jnp.where(row == 0, steps[0, 0], jnp.where(row == 1, steps[0, 1], 0))
        all_steps[spot.z, spot.plane, core] = value.astype(f32)

    def steps_line():
        step_twin(1 - core).wait_recv()
        step_line.start()

    def steps_mates():
        step_line.arrive()
        step_mates.start()

    def steps_drain():
        step_twin(core).wait_send()
        step_line.drain()
        step_mates.drain()

    def make_cond():
        step_mates.arrive()
        flat = all_steps[...].reshape(256, 128)
        clip = lax.broadcasted_iota(jnp.int32, (64, 256), 0)
        column = lax.broadcasted_iota(jnp.int32, (64, 256), 1)
        wanted = 64 * ((clip >> 3) & 3) + 16 * ((clip >> 1) & 3) + 8 * (clip >> 5) + (clip & 1)
        times = jnp.dot(
            (column == wanted).astype(f32),
            flat,
            precision=lax.Precision.HIGHEST,
            preferred_element_type=f32,
        )
        first = (spot.chip * 2 + core) * 24
        half_width = width // 2
        feature = first + lax.broadcasted_iota(jnp.int32, (64, 128), 1)
        place = jnp.where(feature < half_width, feature, feature - half_width).astype(f32)
        angle = times * jnp.exp(-math.log(FREQ_BASE) * place / half_width)
        value = jnp.where(feature < half_width, jnp.cos(angle), jnp.sin(angle))
        cond[...] = (value / (1.0 + jnp.exp(-value))).astype(bf16)

    parts = (range(0, 1), range(1, 3))

    def columns_of(j, half, chunk):
        at = 2304 * j + 1152 * half + 384 * chunk
        return slice(at, at + 384)

    def rows_of(chunk):
        return slice(16 * chunk, 16 * chunk + 16)

    class ModPart:
        def __init__(self, part):
            self.part, self.n = part, len(parts[part])
            n, base = self.n, 6 * part

            def region(i):
                return pl.ds(base + n * i, n)

            self.out, self.into, self.sum = (sums.at[1, region(i)] for i in range(3))
            self.own = sums.at[1, 5, pl.ds(part, n)]
            if part:
                self.line = LineSum(
                    spot,
                    lambda z: sums.at[1, region(2), z],
                    lambda i: sums.at[1, region(3), i] if i < 4 else self.own,
                    mod_send.at[part, pl.ds(1, 3)],
                    mod_recv.at[part, pl.ds(1, 5)],
                )
            else:
                self.line = Exchange(
                    spot.line,
                    spot.z,
                    lambda z: sums.at[1, region(2), z],
                    lambda z: sums.at[1, region(3), z],
                    mod_send.at[part, pl.ds(1, 3)],
                    mod_recv.at[part, pl.ds(1, 4)],
                )
            self.mates = Exchange(
                spot.mates,
                spot.plane,
                lambda plane: sums.at[1, region(4), plane, 16:32],
                lambda plane: sums.at[1, region(4), plane, 0:16],
                mod_send.at[part, pl.ds(4, 3)],
                mod_recv.at[part, pl.ds(6, 4)],
            )

        def swap(self):
            part = self.part
            return remote(self.out, self.into, mod_send.at[part, 0], mod_recv.at[part, 0], spot.twin)

        def terms(self, owner):
            rows = cond[pl.ds(pl.multiple_of(32 * owner, 32), 32), :24]
            for i, j in enumerate(parts[self.part]):
                for chunk in range(3):
                    left, right = (
                        dot(rows, w_ada[:, columns_of(j, half, chunk)])
                        + bias[0:1, columns_of(j, half, chunk)]
                        for half in range(2)
                    )
                    for z in range(4):
                        own = slice(8 * z, 8 * z + 8)
                        block = jnp.concatenate([left[own], right[own]], axis=0)
                        yield (i, z, rows_of(chunk)), block

        def for_twin(self):
            for at, value in self.terms(1 - core):
                self.out[at] = value.astype(bf16)
            self.swap().start()

        def for_line(self):
            self.swap().wait_recv()
            for at, value in self.terms(core):
                self.sum[at] = (value + self.into[at].astype(f32)).astype(bf16)
            if self.part:
                for k in range(3):
                    self.line.send_end(k)
            else:
                self.line.start()

        def for_mates(self):
            def put(i, value):
                self.own[i] = value.astype(bf16)

            if self.part:
                self.line.total(put)
            else:
                self.line.arrive()
                for i in range(self.n):
                    value = self.line.src(spot.z)[i].astype(f32)
                    for z, _ in spot.line:
                        value += self.line.dst(z)[i].astype(f32)
                    put(i, value)
            for plane, _ in spot.mates:
                self.mates.src(plane)[...] = self.picked(plane).astype(bf16)
            self.mates.start()

        def picked(self, plane):
            to = lax.broadcasted_iota(jnp.int32, (16, 48), 0)
            at = lax.broadcasted_iota(jnp.int32, (16, 48), 1)
            wanted = 16 * (to >> 2) + 8 * ((to >> 1) & 1) + 2 * plane + (to & 1)
            pick = (at == wanted).astype(bf16)
            return jnp.stack([dot(pick, self.own[i]) for i in range(self.n)])

        def done(self):
            self.mates.arrive()
            total = self.picked(spot.plane)
            for plane, _ in spot.mates:
                total += self.mates.dst(plane)[...].astype(f32)
            for i, j in enumerate(parts[self.part]):
                for chunk in range(3):
                    for half in range(2):
                        for clip in range(2):
                            row = 4 * chunk + 2 * half + clip
                            mod[clip : clip + 1, columns_of(j, half, chunk)] = total[i, row : row + 1]

        def drain(self):
            self.swap().wait_send()
            self.line.drain()
            self.mates.drain()

    class RowPart:
        def __init__(self, part):
            self.part, n = part, len(parts[part])
            self.subs = subs = pl.ds(parts[part][0], n)
            self.mates = Exchange(
                spot.mates,
                spot.plane,
                lambda plane: all_rows_mod.at[core, spot.z, subs, spot.plane],
                lambda plane: all_rows_mod.at[core, spot.z, subs, plane],
                row_send.at[part, pl.ds(1, 3)],
                row_recv.at[part, pl.ds(1, 4)],
            )
            self.line = LineGather(
                spot,
                lambda z: all_rows_mod.at[core, z, subs],
                row_send.at[part, pl.ds(4, 5)],
                row_recv.at[part, pl.ds(5, 4)],
            )

        def swap(self, owner):
            ref = all_rows_mod.at[owner, :, self.subs]
            return remote(ref, ref, row_send.at[self.part, 0], row_recv.at[self.part, 0], spot.twin)

        def for_mates(self):
            row = lax.broadcasted_iota(jnp.int32, (16, 384), 0)
            for j in parts[self.part]:
                value = 0.0
                for chunk in range(3):
                    for half in range(2):
                        for clip in range(2):
                            own = tally[clip : clip + 1, columns_of(j, half, chunk)]
                            value += jnp.where(row == 4 * chunk + 2 * half + clip, own, 0.0)
                all_rows_mod[core, spot.z, j, spot.plane] = value.astype(bf16)
            self.mates.start()

        def for_line(self):
            self.mates.arrive()
            self.line.open()

        def for_twin(self):
            for k in (1, 2, 3):
                self.line.take(k)
            self.swap(core).start()

        def done(self):
            self.swap(1 - core).wait_recv()

        def drain(self):
            self.swap(core).wait_send()
            self.mates.drain()
            self.line.drain()

    mod_parts = [ModPart(part) for part in range(2)]
    row_parts = [RowPart(part) for part in range(2)]

    def by_rows(action):
        @pl.loop(0, tok // 64)
        def _(i):
            action(pl.ds(pl.multiple_of(i * 64, 64), 64))

    def mod_part(j, component, rows):
        at = (3 * j + component) * width
        second = ids[rows, 2:3] == 1.0
        return jnp.where(second, mod[1:2, at : at + width], mod[0:1, at : at + width])

    def count(j, component, rows, value):
        at = (3 * j + component) * width
        second = ids[rows, 2:3] == 1.0
        tally[0:1, at : at + width] += jnp.sum(jnp.where(second, 0.0, value), axis=0, keepdims=True)
        tally[1:2, at : at + width] += jnp.sum(jnp.where(second, value, 0.0), axis=0, keepdims=True)

    def masks():
        spatial = (seg_ids[...] * 16 + frame_ids[...]).astype(f32)
        temporal = (seg_ids[...] * 16 + patch_ids[...]).astype(f32)
        row = lax.broadcasted_iota(jnp.int32, (8, tok), 0)
        second = seg_ids[...].astype(f32)
        stacked = jnp.where(row == 0, spatial, jnp.where(row == 1, temporal, second))
        ids[...] = stacked.T
        for j, keys in enumerate((spatial, temporal)):
            disallowed[j] = jnp.where(ids[:, j : j + 1] == keys, 0.0, MASKED)
        tally[...] = jnp.zeros_like(tally)
        share = b_ada.shape[0]
        bias[...] = jnp.zeros_like(bias)
        bias[0:1, :share] = b_ada[...].astype(f32).reshape(1, share)
        bias[...] = pltpu.roll(bias[...], (2 * spot.chip + core) * share, 1)

    def standardize(j):
        def action(rows):
            if j == 0:
                stream[rows] = tokens[rows].astype(f32)
            value = stream[rows]
            center = value - jnp.mean(value, axis=-1, keepdims=True)
            inverse = lax.rsqrt(jnp.mean(center * center, axis=-1, keepdims=True) + EPSILON)
            xhat[j, rows] = (center * inverse).astype(bf16)
            deviation[rows, j : j + 1] = inverse

        by_rows(action)

    def modulate(j):
        def action(rows):
            normed[rows] = (
                xhat[j, rows].astype(f32) * (1.0 + mod_part(j, 1, rows)) + mod_part(j, 0, rows)
            ).astype(bf16)

        by_rows(action)

    def turn(i, source):
        for at in range(0, tok, 128):
            turned[i, 0, :, at : at + 128] = source[at : at + 128, :].T
        turned_copy(i).start()

    def weight(g, half, chunk):
        return held[g, half, :, chunk].reshape(width, 384)

    def project(j):
        @pl.loop(0, 6)
        def _(i):
            half, chunk = lax.div(i, 3), lax.rem(i, 3)
            columns = pl.ds(pl.multiple_of(i * 384, 128), 384)
            qkv[j, :, columns] = dot(normed[...], weight(j, half, chunk)).astype(bf16)

    def head_lanes():
        lane = lax.broadcasted_iota(jnp.int32, (1, 128), 1)
        return lane < 64, lane >= 64

    def head_columns(pair):
        return [pl.ds(pl.multiple_of(part * 768 + pair * 128, 128), 128) for part in range(3)]

    def attend(j, first, last):
        @pl.loop(first, last)
        def _(pair):
            at_q, at_k, at_v = head_columns(pair)
            queries, keys, values = qkv[j, :, at_q], qkv[j, :, at_k], qkv[j, :, at_v]
            results = []
            for head, lanes in enumerate(head_lanes()):
                scaled = jnp.where(lanes, queries, 0.0) * bf16(0.125)
                scores = contract_cols(scaled, keys) + disallowed[j]
                scores = jnp.exp(scores - jnp.max(scores, axis=-1, keepdims=True))
                low = (scores * (1.0 / jnp.sum(scores, axis=-1, keepdims=True))).astype(bf16)
                probs[j, 2 * pair + head] = low
                results.append(dot(low, values))
            attended[:, at_q] = jnp.where(head_lanes()[0], results[0], results[1]).astype(bf16)

    def join(j):
        @pl.loop(0, 2)
        def _(half):
            columns = pl.ds(pl.multiple_of(half * 384, 128), 384)
            branch[j, :, columns] = dot(attended[...], weight(j, half, 3)).astype(bf16)

    def add_branch(j):
        def action(rows):
            stream[rows] += mod_part(j, 2, rows) * branch[j, rows].astype(f32)

        by_rows(action)

    def expand(first, last):
        @pl.loop(first, last)
        def _(i):
            columns = pl.ds(pl.multiple_of(i * 384, 128), 384)
            matrix = weight(2, lax.div(i, 4), lax.rem(i, 4))
            for at in range(0, tok, 128):
                rows = slice(at, at + 128)
                pre = dot(normed[rows], matrix)
                square = pre * pre
                root = math.sqrt(2.0 / math.pi)
                bent = jnp.tanh(root * (pre + 0.044715 * (square * pre)))
                value = (0.5 * pre * (1.0 + bent)).astype(bf16)
                hidden[rows, columns] = value
                hidden_turned[0, columns, rows] = value.T
                slope[rows, columns] = (
                    0.5 * (1.0 + bent)
                    + 0.5 * pre * (1.0 - bent * bent) * (root * (1.0 + 3 * 0.044715 * square))
                ).astype(bf16)

    def gate(j):
        def action(rows):
            value = cotangent[rows].astype(f32) if j == 2 else grad[rows]
            if j == 2:
                grad[rows] = value
            else:
                count(j, 2, rows, value * branch[j, rows].astype(f32))
            gated[j, rows] = (mod_part(j, 2, rows) * value).astype(bf16)

        by_rows(action)
        gated_copy(j).start()

    def own_columns(first, width_of_half):
        return pl.ds(pl.multiple_of(core * width_of_half + first, 128), 384)

    def down_terms(z):
        scatter = scatters[0]
        rows = slice(768 * z, 768 * z + 768)
        value = dot(hidden_turned[0, rows], gated[2, :, own_columns(0, 384)]) + dot(
            hidden_turned[1, rows], gated_twin[2]
        )
        value = value.astype(bf16).reshape(4, 4, 48, 384)
        for plane in range(4):
            scatter.sums[scatter.place(4 * z + plane)] = value[plane]

    def column_terms(n, chunk, left, right, right_twin):
        value = dot(turned[left, 0], right) + dot(turned[left, 1], right_twin)
        value = value.astype(bf16).reshape(16, 48, 384)
        for chip in range(16):
            scatters[n].sums[scatters[n].place(chip), chunk] = value[chip]

    def up_terms(chunk):
        column_terms(
            1,
            chunk,
            4,
            slope[:, own_columns(384 * chunk, 1536)],
            grad_pre_twin[:, 384 * chunk : 384 * chunk + 384],
        )

    def out_terms(j):
        column_terms(3 - j, 3, 2 * j + 1, gated[j, :, own_columns(0, 384)], gated_twin[j])

    def qkv_terms(j, chunk):
        column_terms(
            3 - j,
            chunk,
            2 * j,
            grad_qkv[:, own_columns(384 * chunk, 1152)],
            grad_qkv_twin[j, :, 384 * chunk : 384 * chunk + 384],
        )

    def contract():
        @pl.loop(0, 2)
        def _(half):
            columns = pl.ds(pl.multiple_of(half * 384, 128), 384)
            matrix = held[3, half].reshape(3072, 384)
            normed[:, columns] = dot(hidden[...], matrix).astype(bf16)

    def close():
        def action(rows):
            value = normed[rows].astype(f32)
            o_layer[rows] = (stream[rows] + mod_part(2, 2, rows) * value).astype(bf16)
            count(2, 2, rows, cotangent[rows].astype(f32) * value)

        by_rows(action)

    def grad_hidden(step):
        first = 2 * lax.rem(step + 2 - 2 * core, 4)

        @pl.loop(0, 2)
        def _(part):
            i = first + part
            columns = pl.ds(pl.multiple_of(i * 384, 128), 384)
            value = sum(
                contract_cols(
                    gated[2, :, 384 * half : 384 * half + 384],
                    held[3, half, pl.ds(2 * i, 2)].reshape(384, 384),
                )
                for half in range(2)
            )
            slope[:, columns] = (slope[:, columns].astype(f32) * value).astype(bf16)

    def back_project(g, chunks, source, first, last):
        @pl.loop(first, last)
        def _(i):
            columns = pl.ds(pl.multiple_of(i * 384, 128), 384)
            value = contract_cols(
                source[:, columns], weight(g, lax.div(i, chunks), lax.rem(i, chunks))
            )

            @pl.when(i == 0)
            def _():
                grad_normed[...] = value

            @pl.when(i > 0)
            def _():
                grad_normed[...] += value

    def norm_back(j):
        def action(rows):
            value, unit = grad_normed[rows], xhat[j, rows].astype(f32)
            count(j, 0, rows, value)
            count(j, 1, rows, value * unit)
            scaled = value * (1.0 + mod_part(j, 1, rows))
            inner = jnp.mean(scaled * unit, axis=-1, keepdims=True)
            scaled = scaled - jnp.mean(scaled, axis=-1, keepdims=True)
            total = grad[rows] + deviation[rows, j : j + 1] * (scaled - unit * inner)
            if j == 0:
                o_tokens[rows] = total
            else:
                grad[rows] = total

        by_rows(action)

    def split(j):
        value = sum(
            contract_cols(gated[j, :, 384 * half : 384 * half + 384], weight(j, half, 3))
            for half in range(2)
        )
        grad_attended[...] = value.astype(bf16)

    def attend_back(j, first, last):
        @pl.loop(first, last)
        def _(pair):
            at_q, at_k, at_v = head_columns(pair)
            queries, keys, values = qkv[j, :, at_q], qkv[j, :, at_k], qkv[j, :, at_v]
            given = grad_attended[:, at_q]
            grad_q, grad_k, grad_v = [], 0.0, 0.0
            for head, lanes in enumerate(head_lanes()):
                part = jnp.where(lanes, given, 0.0).astype(bf16)
                low = probs[j, 2 * pair + head]
                product = low.astype(f32) * contract_cols(part, values)
                total = jnp.sum(product, axis=-1, keepdims=True)
                scores = ((product - low.astype(f32) * total) * 0.125).astype(bf16)
                grad_v += contract_rows(low, part)
                grad_k += contract_rows(scores, jnp.where(lanes, queries, 0.0).astype(bf16))
                grad_q.append(dot(scores, keys))
            grad_qkv[:, at_q] = jnp.where(head_lanes()[0], grad_q[0], grad_q[1]).astype(bf16)
            grad_qkv[:, at_k] = grad_k.astype(bf16)
            grad_qkv[:, at_v] = grad_v.astype(bf16)

    def each_twin_copy():
        for i in range(5):
            yield turned_copy(i)
        for i in range(4):
            yield hidden_copy(i)
        for j in range(3):
            yield gated_copy(j)
        yield grad_pre_copy()

    def forward_drain():
        steps_drain()
        for part in mod_parts:
            part.drain()
        for gather in gathers:
            gather.swap().wait_send()

    def send_hidden(i):
        if i == 0:
            forward_drain()
        hidden_copy(i).start()

    def need_hidden(i):
        if i == 0:
            gated_copy(2).wait_recv()
        hidden_copy(i).wait_recv()

    def need_gated(j):
        if j == 1:
            gathers[2].drain()
        need(turned_copy, 2 * j + 1)
        need(gated_copy, j)

    leaving = [
        pltpu.make_async_copy(src, dst, leave_sems.at[i])
        for i, (src, dst) in enumerate(
            (
                (o_layer, r_layer),
                (o_tokens, r_tokens),
                (o_down, r_down),
                (o_up, r_up),
                (o_qkv_t, r_qkv_t),
                (o_out_t, r_out_t),
                (o_qkv_s, r_qkv_s),
                (o_out_s, r_out_s),
            )
        )
    ]
    of_group = (leaving[2:3], leaving[3:4], leaving[4:6], leaving[6:8])

    def retire(n):
        scatters[n].store(puts[n])
        for copy in of_group[n]:
            copy.start()
        scatters[n].drain()
        if n < 2:
            scatters[n].release()

    def swap(n):
        scatters[n].swap().start()

    def need(copy, *indices):
        copy(*indices).wait_recv()

    steps_of = {
        DO_STEPS: (steps_line, steps_mates),
        DO_COND: make_cond,
        DO_MODT: lambda part: mod_parts[part].for_twin(),
        DO_MODZ: lambda part: mod_parts[part].for_line(),
        DO_MODS: lambda k: mod_parts[1].line.send_middle(k),
        DO_MODM: lambda part: mod_parts[part].for_mates(),
        DO_MODROWS: lambda part: mod_parts[part].done(),
        DO_OWN: lambda g: gathers[g].own(),
        DO_GZ: lambda g, k: gathers[g].pass_on(k),
        DO_GS: lambda g, k: gathers[g].spread(k),
        DO_GX: lambda g, k: gathers[g].along_first(k),
        DO_GY: lambda g, k: gathers[g].along_second(k),
        DO_LX: lambda g: gathers[g].last_along_first(),
        DO_LY: lambda g: gathers[g].last_along_second(),
        DO_LP: lambda g, k: gathers[g].line.pass_on(k),
        DO_LZ: lambda g, k: gathers[g].last_along_z(k),
        DO_LANDED: lambda g: gathers[g].landed(),
        DO_CWAIT: lambda n: scatters[n].wait_credit(),
        DO_SS: lambda n, k: scatters[n].second_copy(k).start(),
        DO_SY: lambda n, k: scatters[n].add_second(k),
        DO_SX: lambda n, k: scatters[n].add_first(k),
        DO_SZ: lambda n, k: scatters[n].line.send_middle(k),
        DO_SFIN: lambda n: scatters[n].finish(),
        DO_TE: lambda n, k: scatters[n].last_line.send_end(k),
        DO_TZ: lambda n, k: scatters[n].last_line.send_middle(k),
        DO_TTOT: lambda n: scatters[n].last_total(),
        DO_TY: lambda n: scatters[n].last_add_second(),
        DO_TX: lambda n: scatters[n].last_finish(),
        DO_SWAP: swap,
        DO_RETIRE: retire,
        DO_ROWM: lambda part: row_parts[part].for_mates(),
        DO_ROWZ: lambda part: row_parts[part].for_line(),
        DO_ROWP: lambda part, k: row_parts[part].line.pass_on(k),
        DO_ROWT: lambda part: row_parts[part].for_twin(),
        DO_ROWD: lambda part: row_parts[part].done(),
        DO_MASKS: masks,
        DO_STANDARDIZE: standardize,
        DO_MODULATE: modulate,
        DO_PROJECT: project,
        DO_TURNN: lambda j: turn(2 * j, normed),
        DO_TURNA: lambda j: turn(2 * j + 1, attended),
        DO_ATTEND: lambda j, i: attend(j, 2 * i, 2 * i + 2),
        DO_JOIN: join,
        DO_ADD: add_branch,
        DO_GATE: gate,
        DO_EXPAND: lambda i: expand(2 * i, 2 * i + 2),
        DO_SENDH: send_hidden,
        DO_NEEDH: need_hidden,
        DO_DOWNT: down_terms,
        DO_GHID: grad_hidden,
        DO_SENDP: lambda: grad_pre_copy().start(),
        DO_CONTRACT: contract,
        DO_CLOSE: lambda: (close(), leaving[0].start()),
        DO_NEEDP: lambda: (need(grad_pre_copy), need(turned_copy, 4)),
        DO_UPT: up_terms,
        DO_BACK2: lambda i: back_project(2, 4, slope, 2 * i, 2 * i + 2),
        DO_NORMB: norm_back,
        DO_SPLIT: split,
        DO_ATTB: lambda j, i: attend_back(j, 2 * i, 2 * i + 2),
        DO_SENDQ: lambda j: grad_qkv_copy(j).start(),
        DO_NEEDG: need_gated,
        DO_NEEDQ: lambda j: (
            need(turned_copy, 2 * j),
            need(grad_qkv_copy, j),
        ),
        DO_OUTT: out_terms,
        DO_QKVT: qkv_terms,
        DO_BACK: lambda j, i: back_project(j, 3, grad_qkv, 2 * i, 2 * i + 2),
        DO_SENTQ: lambda j: (grad_qkv_copy(j).wait_send(), j == 0 and leaving[1].start()),
    }
    def prepare():
        for g, gather in enumerate(gathers):
            gather.open(pieces[g])
        steps_prepare()

    greet(spot, prepare)
    gathers[0].swap().start()
    step_twin(core).start()
    for gather in gathers[1:]:
        gather.swap().start()
    for name, *indices in ORDER:
        step = steps_of[name]
        if isinstance(step, tuple):
            step[indices[0]]()
        else:
            step(*indices)
    for part in row_parts:
        part.drain()
    for g in (0, 1, 3):
        gathers[g].drain()
    for copy in each_twin_copy():
        copy.wait_send()
    for copy in leaving:
        copy.wait()


def finish_kernel(cond, all_rows_mod, *refs):
    sources, o_ada, o_bias = refs[:8], refs[8], refs[9]
    results, held, total, sem = refs[10:18], refs[18:26], refs[26], refs[27]

    def copies(first, second, kind):
        return [
            pltpu.make_async_copy(src, dst, sem.at[kind, i])
            for i, (src, dst) in enumerate(zip(first, second, strict=True))
        ]

    arriving, leaving = copies(sources, held, 0), copies(held, results, 1)
    for copy in arriving:
        copy.start()
    total[...] = jnp.zeros_like(total)
    clip = lax.broadcasted_iota(jnp.int32, (64, 512), 0)
    at = lax.broadcasted_iota(jnp.int32, (64, 512), 1)
    spread = (clip == 2 * (at >> 4) + (at & 1)).astype(jnp.bfloat16)
    weights = contract_rows(cond[...], spread)[:32]
    row = lax.broadcasted_iota(jnp.int32, (32, 512), 0)
    kind = (lax.broadcasted_iota(jnp.int32, (32, 512), 1) & 15) >> 1
    weights = jnp.where(row == 24, 1.0, weights)
    for j in range(3):
        values = all_rows_mod[:, :, j].reshape(512, 384)
        for half in range(2):
            for chunk in range(3):
                columns = slice(2304 * j + 1152 * half + 384 * chunk, 2304 * j + 1152 * half + 384 * chunk + 384)
                own = jnp.where(kind == 2 * chunk + half, weights, 0.0).astype(jnp.bfloat16)
                product = dot(own, values)
                o_ada[:, columns] = product[:24]
                total[0:1, columns] = product[24:25]
        if j == 0:
            for copy, onward in zip(arriving, leaving, strict=True):
                copy.wait()
                onward.start()
    place = lax.axis_index("wide") * 2 + lax.axis_index("narrow")
    share, columns = o_bias.shape[1], total.shape[1]
    turned = pltpu.roll(total[...], lax.rem(columns - place * share, columns), 1)
    o_bias[...] = turned[0:1, :share]
    for copy in leaving:
        copy.wait()


def layer(tokens, cotangent, steps, seg_ids, frame_ids, patch_ids, b_ada, w_ada, *shards):
    f32, bf16 = jnp.float32, jnp.bfloat16
    tok, width = tokens.shape
    block = (4, 48, 384)
    dma, vmem = pltpu.SemaphoreType.DMA, pltpu.VMEM
    in_vmem, in_hbm = pl.BlockSpec(memory_space=vmem), pl.BlockSpec(memory_space=pltpu.HBM)
    outs = pl.pallas_call(
        layer_kernel,
        out_shape=[
            jax.ShapeDtypeStruct((tok, width), bf16),
            jax.ShapeDtypeStruct((tok, width), f32),
            jax.ShapeDtypeStruct((64, 128), bf16),
            jax.ShapeDtypeStruct((2, 4, 3, 4, 16, 384), bf16),
        ]
        + [jax.ShapeDtypeStruct(shard.shape, f32) for shard in shards],
        in_specs=[in_vmem] * 2 + [pl.BlockSpec(memory_space=pltpu.SMEM)] + [in_vmem] * 11,
        out_specs=[in_hbm] * 2 + [in_vmem] * 2 + [in_hbm] * 6,
        scratch_shapes=[
            vmem((tok, width), bf16),
            vmem((tok, width), f32),
            *(vmem(shard.shape, f32) for shard in shards),
            dma((8,)),
            vmem((4, 2, 16) + block, bf16),
            vmem((4,) + block, f32),
            vmem((3, 4, 24, 384), f32),
            vmem((2, 48, 384), f32),
            vmem((2, 16) + block, bf16),
            vmem((2, 4, 2, 3, 48, 384), bf16),
            vmem((2, 4, 3, 48, 384), bf16),
            vmem((2, 5, 3, 48, 384), bf16),
            vmem((2, 2, 48, 384), bf16),
            vmem((2, 48, 384), bf16),
            vmem((2, 5) + block, bf16),
            vmem((4, 4, 2, 8, 128), f32),
            vmem((8, w_ada.shape[1]), f32),
            vmem((tok, 8), f32),
            vmem((8, 6912), f32),
            vmem((8, 6912), f32),
            vmem((3, tok, width), bf16),
            vmem((tok, 128), f32),
            vmem((tok, width), bf16),
            vmem((tok, width), bf16),
            vmem((5, 2, width, tok), bf16),
            vmem((2, 4 * width, tok), bf16),
            vmem((2, tok, 3 * width), bf16),
            vmem((2, HEADS, tok, tok), bf16),
            vmem((2, tok, width), bf16),
            vmem((tok, width), f32),
            vmem((tok, width), f32),
            vmem((tok, 4 * width), bf16),
            vmem((tok, 4 * width), bf16),
            vmem((tok, 2 * width), bf16),
            vmem((3, tok, width), bf16),
            vmem((3, tok, width // 2), bf16),
            vmem((tok, width), bf16),
            vmem((2, tok, 3 * width // 2), bf16),
            vmem((2, tok, tok), f32),
            dma((4, 2)),
            dma((4, 33)),
            dma((4, 31)),
            dma((4, 17)),
            dma((4, 21)),
            pltpu.SemaphoreType.REGULAR((2, 4)),
            dma((16,)),
            dma((16,)),
            dma((7,)),
            dma((12,)),
            dma((2, 7)),
            dma((2, 10)),
            dma((2, 9)),
            dma((2, 9)),
        ],
        compiler_params=pltpu.CompilerParams(
            collective_id=0, has_side_effects=True, vmem_limit_bytes=64 * 2**20
        ),
    )(tokens, cotangent, steps, seg_ids, frame_ids, patch_ids, b_ada, w_ada, *shards)
    sources = (*outs[:2], *outs[4:])
    return pl.pallas_call(
        finish_kernel,
        out_shape=[
            jax.ShapeDtypeStruct(w_ada.shape, f32),
            jax.ShapeDtypeStruct((1, w_ada.shape[1] // 32), f32),
        ]
        + [jax.ShapeDtypeStruct(source.shape, source.dtype) for source in sources],
        in_specs=[in_vmem] * 2 + [in_hbm] * 8,
        out_specs=[in_vmem] * 2 + [in_hbm] * 8,
        scratch_shapes=[vmem(source.shape, source.dtype) for source in sources]
        + [vmem((8, w_ada.shape[1]), f32), dma((2, 8))],
        compiler_params=pltpu.CompilerParams(vmem_limit_bytes=60 * 2**20),
    )(outs[2], outs[3], *sources)


def on_grid(
    tokens,
    seg_ids,
    frame_ids,
    patch_ids,
    timesteps,
    w_ada,
    b_ada,
    w_qkv_spatial,
    w_out_spatial,
    w_qkv_temporal,
    w_out_temporal,
    w_up,
    w_down,
    cotangent,
):
    shards = (w_qkv_spatial, w_out_spatial, w_qkv_temporal, w_out_temporal, w_up, w_down)
    grad_ada, grad_bias, out, grad_tokens, *grads = layer(
        tokens,
        cotangent,
        timesteps[None],
        seg_ids[None],
        frame_ids[None],
        patch_ids[None],
        b_ada,
        w_ada,
        *shards,
    )
    return (out, grad_tokens, grad_ada, grad_bias.reshape(-1), *grads)


def on_device(
    tokens,
    seg_ids,
    frame_ids,
    patch_ids,
    timesteps,
    w_ada,
    b_ada,
    w_qkv_spatial,
    w_out_spatial,
    w_qkv_temporal,
    w_out_temporal,
    w_up,
    w_down,
    cotangent,
):
    axes = ("wide", "narrow")
    gathered = (
        None,
        None,
        lax.all_gather(w_qkv_spatial, axes, axis=0, tiled=True),
        lax.all_gather(w_out_spatial, axes, axis=0, tiled=True),
        lax.all_gather(w_qkv_temporal, axes, axis=0, tiled=True),
        lax.all_gather(w_out_temporal, axes, axis=0, tiled=True),
        lax.all_gather(w_up, axes, axis=0, tiled=True),
        lax.all_gather(w_down, axes, axis=0, tiled=True),
    )
    width = tokens.shape[1]
    head_count = HEADS
    clip_count = timesteps.shape[0]
    row_count = w_ada.shape[0]
    place = lax.axis_index(axes)
    all_steps = lax.all_gather(timesteps, axes, axis=0, tiled=True)
    cond_all = jax.nn.silu(time_embed(all_steps, width)).astype(jnp.bfloat16)
    cond_rows = lax.dynamic_slice_in_dim(cond_all, place * row_count, row_count, axis=1)
    all_bias = lax.all_gather(b_ada, axes, axis=0, tiled=True)
    modulation = lax.psum_scatter(
        jnp.dot(cond_rows, w_ada, preferred_element_type=jnp.float32),
        axes,
        scatter_dimension=0,
        tiled=True,
    ) + all_bias.astype(jnp.float32)
    one_hot = (seg_ids[:, None] == jnp.arange(clip_count, dtype=jnp.int32)[None, :]).astype(
        jnp.float32
    )
    offset_first, scale_first, gate_a = sublayer_mod(one_hot, modulation, 0, width)
    offset_second, scale_second, gate_b = sublayer_mod(one_hot, modulation, 1, width)
    offset_third, scale_third, gate_c = sublayer_mod(one_hot, modulation, 2, width)
    same_clip = seg_ids[:, None] == seg_ids[None, :]
    spatial_mask = same_clip & (frame_ids[:, None] == frame_ids[None, :])
    temporal_mask = same_clip & (patch_ids[:, None] == patch_ids[None, :])
    residual_first = tokens.astype(jnp.float32)
    standardized_first, inverse_deviation_first = layer_norm_apply(residual_first)
    normalized_first = (standardized_first * (1.0 + scale_first) + offset_first).astype(
        jnp.bfloat16
    )
    branch_a, qkv_a, merged_a = attention_forward(
        normalized_first, gathered[2], gathered[3], spatial_mask, head_count
    )
    residual_second = residual_first + gate_a * branch_a
    standardized_second, inverse_deviation_second = layer_norm_apply(residual_second)
    normalized_second = (standardized_second * (1.0 + scale_second) + offset_second).astype(
        jnp.bfloat16
    )
    branch_b, qkv_b, merged_b = attention_forward(
        normalized_second, gathered[4], gathered[5], temporal_mask, head_count
    )
    residual_third = residual_second + gate_b * branch_b
    standardized_third, inverse_deviation_third = layer_norm_apply(residual_third)
    normalized_third = (standardized_third * (1.0 + scale_third) + offset_third).astype(
        jnp.bfloat16
    )
    pre_act = jnp.dot(normalized_third, gathered[6], preferred_element_type=jnp.float32)
    act_out, gelu_pull = jax.vjp(jax.nn.gelu, pre_act)
    hidden = act_out.astype(jnp.bfloat16)
    branch_c = jnp.dot(hidden, gathered[7], preferred_element_type=jnp.float32)
    result = residual_third + gate_c * branch_c
    back_weights = gathered
    output_gradient = cotangent.astype(jnp.float32)
    gate_gradient_third = output_gradient * branch_c
    grad_branch_c = (gate_c * output_gradient).astype(jnp.bfloat16)
    grad_hidden = contract_cols(grad_branch_c, back_weights[7])
    grad_pre = gelu_pull(grad_hidden)[0].astype(jnp.bfloat16)
    normalized_gradient_third = contract_cols(grad_pre, back_weights[6])
    residual_gradient = output_gradient + layer_norm_reverse(
        normalized_gradient_third, standardized_third, inverse_deviation_third, scale_third
    )
    gate_gradient_second = residual_gradient * branch_b
    grad_branch_b = (gate_b * residual_gradient).astype(jnp.bfloat16)
    normalized_gradient_second, grad_qkv_t = attention_backward(
        grad_branch_b, qkv_b, back_weights[4], back_weights[5], temporal_mask, head_count
    )
    residual_gradient = residual_gradient + layer_norm_reverse(
        normalized_gradient_second, standardized_second, inverse_deviation_second, scale_second
    )
    gate_gradient_first = residual_gradient * branch_a
    grad_branch_a = (gate_a * residual_gradient).astype(jnp.bfloat16)
    normalized_gradient_first, grad_qkv_s = attention_backward(
        grad_branch_a, qkv_a, back_weights[2], back_weights[3], spatial_mask, head_count
    )
    residual_gradient = residual_gradient + layer_norm_reverse(
        normalized_gradient_first, standardized_first, inverse_deviation_first, scale_first
    )
    grad_mod = jnp.concatenate(
        [
            exact_rows(
                one_hot,
                jnp.concatenate(
                    [
                        normalized_gradient_first,
                        normalized_gradient_first * standardized_first,
                        gate_gradient_first,
                    ],
                    axis=1,
                ),
            ),
            exact_rows(
                one_hot,
                jnp.concatenate(
                    [
                        normalized_gradient_second,
                        normalized_gradient_second * standardized_second,
                        gate_gradient_second,
                    ],
                    axis=1,
                ),
            ),
            exact_rows(
                one_hot,
                jnp.concatenate(
                    [
                        normalized_gradient_third,
                        normalized_gradient_third * standardized_third,
                        gate_gradient_third,
                    ],
                    axis=1,
                ),
            ),
        ],
        axis=1,
    )
    grad_mod_low = grad_mod.astype(jnp.bfloat16)
    all_grad_mod = lax.all_gather(grad_mod_low, axes, axis=0, tiled=True)
    bias_share = lax.psum_scatter(
        jnp.sum(grad_mod, axis=0), axes, scatter_dimension=0, tiled=True
    )

    def share(left, right):
        return lax.psum_scatter(
            contract_rows(left, right).astype(jnp.bfloat16),
            axes,
            scatter_dimension=0,
            tiled=True,
        ).astype(jnp.float32)

    return (
        result.astype(jnp.bfloat16),
        residual_gradient,
        contract_rows(cond_rows, all_grad_mod),
        bias_share,
        share(normalized_first, grad_qkv_s),
        share(merged_a, grad_branch_a),
        share(normalized_second, grad_qkv_t),
        share(merged_b, grad_branch_b),
        share(normalized_third, grad_pre),
        share(hidden, grad_branch_c),
    )


def solution(mesh):
    placed = (
        P(("wide", "narrow"), None),
        P(("wide", "narrow")),
        P(("wide", "narrow")),
        P(("wide", "narrow")),
        P(("wide", "narrow")),
        P(("wide", "narrow"), None),
        P(("wide", "narrow")),
        P(("wide", "narrow"), None),
        P(("wide", "narrow"), None),
        P(("wide", "narrow"), None),
        P(("wide", "narrow"), None),
        P(("wide", "narrow"), None),
        P(("wide", "narrow"), None),
        P(("wide", "narrow"), None),
    )
    grid = dict(mesh.shape) == {"wide": 16, "narrow": 2}
    return jax.shard_map(
        on_grid if grid else on_device,
        mesh=mesh,
        in_specs=placed,
        out_specs=(
            P(("wide", "narrow"), None),
            P(("wide", "narrow"), None),
            P(("wide", "narrow"), None),
            P(("wide", "narrow")),
            P(("wide", "narrow"), None),
            P(("wide", "narrow"), None),
            P(("wide", "narrow"), None),
            P(("wide", "narrow"), None),
            P(("wide", "narrow"), None),
            P(("wide", "narrow"), None),
        ),
        check_vma=False,
    )
```

```python
from functools import partial
import math

import jax
import jax.numpy as jnp
from jax import lax
from jax.experimental import pallas as pl
from jax.experimental.pallas import tpu as pltpu
from jax.sharding import PartitionSpec as P

HEADS = 12


EPSILON = 1e-06
FREQ_BASE = 10000.0
MASKED = -1e30


def time_embed(step_ids, width):
    half_width = width // 2
    frequency = jnp.exp(
        -math.log(FREQ_BASE) * jnp.arange(half_width, dtype=jnp.float32) / half_width
    )
    angles = step_ids.astype(jnp.float32)[:, None] * frequency[None, :]
    return jnp.concatenate([jnp.cos(angles), jnp.sin(angles)], axis=1)


def contract_rows(left, right):
    return lax.dot_general(
        left, right, (((0,), (0,)), ((), ())), preferred_element_type=jnp.float32
    )


def contract_cols(left, right):
    return lax.dot_general(
        left, right, (((1,), (1,)), ((), ())), preferred_element_type=jnp.float32
    )


def exact_rows(left, right):
    return lax.dot_general(
        left,
        right,
        (((0,), (0,)), ((), ())),
        precision=lax.Precision.HIGHEST,
        preferred_element_type=jnp.float32,
    )


def layer_norm_apply(stream):
    center = stream - jnp.mean(stream, axis=-1, keepdims=True)
    inverse_deviation = lax.rsqrt(jnp.mean(center * center, axis=-1, keepdims=True) + EPSILON)
    return (center * inverse_deviation, inverse_deviation)


def layer_norm_reverse(normalized_gradient, standardized_input, inverse_deviation, row_scales):
    input_gradient = normalized_gradient * (1.0 + row_scales)
    mean_removed = input_gradient - jnp.mean(input_gradient, axis=-1, keepdims=True)
    return inverse_deviation * (
        mean_removed
        - standardized_input * jnp.mean(input_gradient * standardized_input, axis=-1, keepdims=True)
    )


def sublayer_mod(one_hot, modulation, sublayer, width):
    table = modulation[:, 3 * width * sublayer : 3 * width * (sublayer + 1)]
    rows_mod = jnp.dot(
        one_hot, table, precision=lax.Precision.HIGHEST, preferred_element_type=jnp.float32
    )
    return (rows_mod[:, :width], rows_mod[:, width : 2 * width], rows_mod[:, 2 * width :])


def head_probs(allowed, scale, queries, key_vecs):
    scores = contract_cols(queries, key_vecs) * scale
    scores = jnp.where(allowed, scores, MASKED)
    return jax.nn.softmax(scores, axis=-1)


def head_forward(allowed, scale, item):
    queries, key_vecs, val_vecs = item
    attn_prob = head_probs(allowed, scale, queries, key_vecs)
    return jnp.dot(attn_prob.astype(jnp.bfloat16), val_vecs, preferred_element_type=jnp.float32)


def head_backward(allowed, scale, item):
    queries, key_vecs, val_vecs, grad_att = item
    attn_prob = head_probs(allowed, scale, queries, key_vecs)
    grad_val = contract_rows(attn_prob.astype(jnp.bfloat16), grad_att)
    grad_prob = contract_cols(grad_att, val_vecs)
    grad_score = attn_prob * (grad_prob - jnp.sum(attn_prob * grad_prob, axis=-1, keepdims=True))
    score_low = grad_score.astype(jnp.bfloat16)
    grad_query = jnp.dot(score_low, key_vecs, preferred_element_type=jnp.float32) * scale
    grad_key = contract_rows(score_low, queries) * scale
    return (grad_query, grad_key, grad_val)


def split_heads(qkv_rows, head_count):
    row_count = qkv_rows.shape[0]
    return qkv_rows.reshape(row_count, 3, head_count, -1).transpose(1, 2, 0, 3)


def attention_forward(normed, w_qkv, w_out, allowed, head_count):
    row_count = normed.shape[0]
    qkv_rows = jnp.dot(normed, w_qkv, preferred_element_type=jnp.float32).astype(jnp.bfloat16)
    split_qkv = split_heads(qkv_rows, head_count)
    scale = split_qkv.shape[-1] ** (-0.5)
    attended = lax.map(
        partial(head_forward, allowed, scale), (split_qkv[0], split_qkv[1], split_qkv[2])
    )
    merged = attended.transpose(1, 0, 2).reshape(row_count, -1).astype(jnp.bfloat16)
    branch = jnp.dot(merged, w_out, preferred_element_type=jnp.float32)
    return (branch, qkv_rows, merged)


def attention_backward(grad_branch, qkv_rows, w_qkv, w_out, allowed, head_count):
    row_count = qkv_rows.shape[0]
    grad_merged = contract_cols(grad_branch, w_out).astype(jnp.bfloat16)
    grad_heads = grad_merged.reshape(row_count, head_count, -1).transpose(1, 0, 2)
    split_qkv = split_heads(qkv_rows, head_count)
    scale = split_qkv.shape[-1] ** (-0.5)
    grad_query, grad_key, grad_val = lax.map(
        partial(head_backward, allowed, scale),
        (split_qkv[0], split_qkv[1], split_qkv[2], grad_heads),
    )
    grad_qkv = (
        jnp.stack([grad_query, grad_key, grad_val])
        .transpose(2, 0, 1, 3)
        .reshape(row_count, -1)
        .astype(jnp.bfloat16)
    )
    normalized_gradient = contract_cols(grad_qkv, w_qkv)
    return (normalized_gradient, grad_qkv)


MESH = pl.DeviceIdType.MESH


class Spot:
    def __init__(self):
        chip = lax.axis_index("wide")
        core = lax.axis_index("narrow")
        z, y, x = lax.div(chip, 4), lax.rem(lax.div(chip, 2), 2), lax.rem(chip, 2)
        half = lax.div(z, 2)
        toward = 1 - 2 * half
        self.chip, self.core, self.z, self.y, self.x = chip, core, z, y, x
        self.half = half
        self.middle = z + half * (3 - 2 * z)
        self.is_middle = self.middle == 1
        self.is_end = self.middle == 0
        self.plane = 2 * y + x
        self.inner = ((z + toward) * 4 + self.plane, core)
        self.outer = ((z - toward) * 4 + self.plane, core)
        self.first_plane = 2 * lax.rem(y + core, 2) + lax.rem(x + 1 - core, 2)
        self.second_plane = 2 * lax.rem(y + 1 - core, 2) + lax.rem(x + core, 2)
        self.far_plane = 3 - self.plane
        self.first = (z * 4 + self.first_plane, core)
        self.second = (z * 4 + self.second_plane, core)
        self.far = (z * 4 + self.far_plane, core)
        self.twin = (chip, 1 - core)
        self.mates = (
            (self.first_plane, self.first),
            (self.second_plane, self.second),
            (self.far_plane, self.far),
        )
        self.line = [
            (lax.rem(z + j, 4), (lax.rem(z + j, 4) * 4 + self.plane, core)) for j in (1, 2, 3)
        ]

    def layer(self, mirrored):
        return mirrored + self.half * (3 - 2 * mirrored)

    def arrival(self, k):
        return (self.z, self.layer(1 - self.middle), self.layer(2), self.layer(3))[k]


def greet(spot, meanwhile):
    barrier = pltpu.get_barrier_semaphore()
    for device in [spot.twin] + [device for _, device in spot.mates + tuple(spot.line)]:
        pl.semaphore_signal(barrier, inc=1, device_id=device, device_id_type=MESH)
    meanwhile()
    pl.semaphore_wait(barrier, 7)


def remote(src, dst, send, recv, device):
    return pltpu.make_async_remote_copy(
        src_ref=src,
        dst_ref=dst,
        send_sem=send,
        recv_sem=recv,
        device_id=device,
        device_id_type=MESH,
    )


class Exchange:
    def __init__(self, places, mine, src, dst, send, recv):
        self.places, self.mine = places, mine
        self.src, self.dst = src, dst
        self.send, self.recv = send, recv

    def copy(self, i):
        place, device = self.places[i]
        return remote(
            self.src(place), self.dst(self.mine), self.send.at[i], self.recv.at[self.mine], device
        )

    def start(self):
        for i in range(3):
            self.copy(i).start()

    def arrive(self):
        for place, device in self.places:
            ref = self.dst(place)
            remote(ref, ref, self.send.at[0], self.recv.at[place], device).wait_recv()

    def drain(self):
        for i in range(3):
            self.copy(i).wait_send()


class LineSum:
    def __init__(self, spot, part, slot, send, recv):
        self.spot, self.part, self.slot = spot, part, slot
        self.send, self.recv = send, recv

    def layer(self, k):
        spot = self.spot
        return (spot.layer(3), spot.layer(2), spot.layer(1 - spot.middle), spot.z)[k]

    def copy(self, k, slot, device):
        return remote(
            self.part(self.layer(k)), self.slot(slot), self.send.at[k], self.recv.at[slot], device
        )

    def from_end(self, k):
        return self.copy(k, k, self.spot.inner)

    def from_middle(self, k):
        return self.copy(k, 3 + k, self.spot.inner) if k < 2 else self.copy(2, 3, self.spot.outer)

    def arrived(self, slot):
        self.copy(0, slot, self.spot.inner).wait_recv()
        return self.slot(slot)

    def send_end(self, k):
        pl.when(self.spot.is_end)(lambda: self.from_end(k).start())

    def send_middle(self, k):
        @pl.when(self.spot.is_middle)
        def _():
            source, part = self.arrived((0, 1, 3)[k]), self.part(self.layer(k))
            for i in range(part.shape[0]):
                part[i] += source[i]
            self.from_middle(k).start()

    def total(self, put):
        def add(*slots):
            sources = [self.arrived(slot) for slot in slots]
            part = self.part(self.spot.z)
            for i in range(part.shape[0]):
                value = part[i].astype(jnp.float32)
                for source in sources:
                    value += source[i].astype(jnp.float32)
                put(i, value)

        pl.when(self.spot.is_end)(lambda: add(3))
        pl.when(self.spot.is_middle)(lambda: add(2, 4))

    def drain(self):
        for k in range(3):
            self.from_end(k).wait_send()


class LineGather:
    def __init__(self, spot, part, send, recv):
        self.spot, self.part = spot, part
        self.send, self.recv = send, recv

    def copy(self, z, send, device):
        ref = self.part(z)
        return remote(ref, ref, self.send.at[send], self.recv.at[z], device)

    def own(self, inward):
        spot = self.spot
        return self.copy(spot.z, 0 if inward else 1, spot.inner if inward else spot.outer)

    def onward(self, k):
        spot = self.spot
        return self.copy(spot.arrival(k), 1 + k, spot.inner if k == 1 else spot.outer)

    def open(self):
        self.own(True).start()
        pl.when(self.spot.is_middle)(lambda: self.own(False).start())

    def get(self, k):
        self.copy(self.spot.arrival(k), 0, self.spot.inner).wait_recv()

    def pass_on(self, k):
        @pl.when(self.spot.is_middle)
        def _():
            self.get(k)
            self.onward(k).start()

    def take(self, k):
        pl.when(self.spot.is_end)(lambda: self.get(k))

    def drain(self):
        self.own(True).wait_send()

        @pl.when(self.spot.is_middle)
        def _():
            self.own(False).wait_send()
            for k in (1, 2, 3):
                self.onward(k).wait_send()


class Gather:
    def __init__(self, spot, held, stage, apart, swap_sems, send, recv, count):
        self.spot, self.held, self.count = spot, held, count
        self.split = count < 4
        self.stage, self.apart, self.swap_sems = stage, apart, swap_sems
        self.send, self.recv = send, recv
        self.whole = apart.shape[1] == 48
        self.line = LineGather(
            spot,
            lambda z: self.last_layer(spot.core, z),
            send.at[pl.ds(24, 5)],
            recv.at[pl.ds(23, 4)],
        )

    def block(self, z, plane):
        return self.held.at[self.spot.core, z * 4 + plane, 0 : self.count]

    def last_layer(self, half, z):
        return self.held.at[half, pl.ds(z * 4, 4), 3]

    def last(self, plane):
        return self.held.at[self.spot.core, self.spot.z * 4 + plane, 3]

    def copy(self, ref, send, recv, device):
        return remote(ref, ref, self.send.at[send], self.recv.at[recv], device)

    def mine(self):
        core = self.spot.core
        if self.whole:
            return self.stage.at[pl.ds(2 * core, 2)]
        return self.stage.at[:, pl.ds(pl.multiple_of(core * 24, 8), 24), :]

    def swap(self):
        return remote(
            self.apart, self.mine(), self.swap_sems.at[0], self.swap_sems.at[1], self.spot.twin
        )

    def open(self, piece):
        core = self.spot.core
        for chunk in range(self.apart.shape[0]):
            self.apart[chunk] = piece(1 - core, chunk).astype(jnp.float32)
        place = self.mine()
        for chunk in range(self.apart.shape[0]):
            place[chunk] = piece(core, chunk).astype(jnp.float32)

    def own(self):
        spot = self.spot
        self.swap().wait_recv()
        self.held[spot.core, spot.chip] = self.stage[...].astype(jnp.bfloat16)
        self.z_own(True).start()
        pl.when(spot.is_middle)(lambda: self.z_own(False).start())
        if self.split:
            self.last_first().start()
            self.last_second(False).start()

    def z_own(self, inward):
        spot = self.spot
        return self.copy(
            self.block(spot.z, spot.plane),
            0 if inward else 1,
            spot.z,
            spot.inner if inward else spot.outer,
        )

    def z_pass(self, k):
        spot = self.spot
        z = spot.arrival(k)
        return self.copy(
            self.block(z, spot.plane), 1 + k, z, spot.inner if k == 1 else spot.outer
        )

    def first_copy(self, k):
        z = self.spot.arrival(k)
        return self.copy(self.block(z, self.spot.plane), 5 + k, 4 + z, self.spot.first)

    def second_copy(self, k):
        z = self.spot.arrival(k)
        return self.copy(self.block(z, self.spot.plane), 9 + k, 8 + z, self.spot.second)

    def second_pass(self, k):
        z = self.spot.arrival(k)
        return self.copy(self.block(z, self.spot.first_plane), 13 + k, 12 + z, self.spot.second)

    def twin_copy(self, half, k):
        z = self.spot.arrival(k)
        ref = self.held.at[half, pl.ds(z * 4, 4), 0 : self.count]
        return self.copy(ref, 17 + k, 16 + z, self.spot.twin)

    def last_first(self):
        return self.copy(self.last(self.spot.plane), 21, 20, self.spot.first)

    def last_second(self, onward):
        spot = self.spot
        plane = spot.first_plane if onward else spot.plane
        return self.copy(self.last(plane), 23 if onward else 22, 22 if onward else 21, spot.second)

    def last_twin(self, half, k):
        z = self.spot.arrival(k)
        ref = self.last_layer(half, z)
        return self.copy(ref, 29 + k, 27 + z, self.spot.twin)

    def get(self, k):
        spot = self.spot
        z = spot.arrival(k)
        self.copy(self.block(z, spot.plane), 0, z, spot.inner).wait_recv()

    def pass_on(self, k):
        @pl.when(self.spot.is_middle)
        def _():
            self.get(k)
            self.z_pass(k).start()

    def spread(self, k):
        if k:
            pl.when(self.spot.is_end)(lambda: self.get(k))
        self.first_copy(k).start()
        self.second_copy(k).start()

    def along_first(self, k):
        spot = self.spot
        z = spot.arrival(k)
        self.copy(self.block(z, spot.first_plane), 0, 4 + z, spot.first).wait_recv()
        self.second_pass(k).start()

    def along_second(self, k):
        spot = self.spot
        z = spot.arrival(k)
        self.copy(self.block(z, spot.second_plane), 0, 8 + z, spot.second).wait_recv()
        self.copy(self.block(z, spot.far_plane), 0, 12 + z, spot.second).wait_recv()
        self.twin_copy(spot.core, k).start()

    def last_along_first(self):
        spot = self.spot
        self.copy(self.last(spot.first_plane), 0, 20, spot.first).wait_recv()
        self.last_second(True).start()

    def last_along_second(self):
        spot = self.spot
        self.copy(self.last(spot.second_plane), 0, 21, spot.second).wait_recv()
        self.copy(self.last(spot.far_plane), 0, 22, spot.second).wait_recv()
        self.line.open()
        self.last_twin(spot.core, 0).start()

    def last_along_z(self, k):
        self.line.take(k)
        self.last_twin(self.spot.core, k).start()

    def landed(self):
        for k in range(4):
            self.twin_copy(1 - self.spot.core, k).wait_recv()
            if self.split:
                self.last_twin(1 - self.spot.core, k).wait_recv()

    def drain(self):
        spot = self.spot
        self.z_own(True).wait_send()

        @pl.when(spot.is_middle)
        def _():
            self.z_own(False).wait_send()
            for k in (1, 2, 3):
                self.z_pass(k).wait_send()

        for k in range(4):
            self.first_copy(k).wait_send()
            self.second_copy(k).wait_send()
            self.second_pass(k).wait_send()
            self.twin_copy(spot.core, k).wait_send()
            if self.split:
                self.last_twin(spot.core, k).wait_send()
        if self.split:
            self.last_first().wait_send()
            self.last_second(False).wait_send()
            self.last_second(True).wait_send()
            self.line.drain()


class Scatter:
    def __init__(
        self, spot, sums, from_second, from_first, from_z, last_pair, last_one, last_z, final,
        theirs, send, recv, credit, owed,
    ):
        self.spot, self.sums = spot, sums
        self.from_second, self.from_first = from_second, from_first
        self.last_pair, self.last_one = last_pair, last_one
        self.final, self.theirs = final, theirs
        self.send, self.recv, self.credit = send, recv, credit
        self.owed, self.whole = owed, theirs.shape[1] == 48
        self.line = LineSum(
            spot,
            lambda z: sums.at[4 * z, 0:3],
            lambda i: from_z.at[i],
            send.at[pl.ds(8, 3)],
            recv.at[pl.ds(8, 5)],
        )
        self.last_line = LineSum(
            spot,
            lambda z: sums.at[pl.ds(4 * z, 4), 3],
            lambda i: last_z.at[i],
            send.at[pl.ds(12, 3)],
            recv.at[pl.ds(14, 5)],
        )

    def place(self, chip):
        spot = self.spot
        z, y, x = chip // 4, (chip // 2) % 2, chip % 2
        other_y, other_x = lax.rem(spot.y + y, 2), lax.rem(spot.x + x, 2)
        second = other_y * (1 - spot.core) + other_x * spot.core
        first = other_x * (1 - spot.core) + other_y * spot.core
        return 4 * z + 2 * second + first

    def second_copy(self, k):
        z = self.line.layer(k)
        return remote(
            self.sums.at[pl.ds(4 * z + 2, 2), 0:3],
            self.from_second.at[z],
            self.send.at[k],
            self.recv.at[z],
            self.spot.second,
        )

    def first_copy(self, k):
        z = self.line.layer(k)
        return remote(
            self.sums.at[4 * z + 1, 0:3],
            self.from_first.at[z],
            self.send.at[4 + k],
            self.recv.at[4 + z],
            self.spot.first,
        )

    def last_second_copy(self):
        return remote(
            self.sums.at[pl.ds(4 * self.spot.z + 2, 2), 3],
            self.last_pair,
            self.send.at[15],
            self.recv.at[19],
            self.spot.second,
        )

    def last_first_copy(self):
        return remote(
            self.sums.at[4 * self.spot.z + 1, 3],
            self.last_one,
            self.send.at[16],
            self.recv.at[20],
            self.spot.first,
        )

    def swap(self):
        core = self.spot.core
        if self.whole:
            src = self.final.at[pl.ds(2 * (1 - core), 2)]
        else:
            src = self.final.at[:, pl.ds(pl.multiple_of((1 - core) * 24, 8), 24), :]
        return remote(src, self.theirs, self.send.at[11], self.recv.at[13], self.spot.twin)

    def wait_credit(self):
        spot = self.spot
        if self.owed:
            for kind in range(3):
                pl.semaphore_wait(self.credit.at[kind], 1)
            pl.when(spot.is_middle)(lambda: pl.semaphore_wait(self.credit.at[3], 1))

    def add_second(self, k):
        z = self.line.layer(k)
        self.second_copy(k).wait_recv()
        for first in (1, 0):
            for chunk in range(3):
                self.sums[4 * z + first, chunk] += self.from_second[z, first, chunk]
            if first:
                self.first_copy(k).start()

    def add_first(self, k):
        z = self.line.layer(k)
        self.first_copy(k).wait_recv()
        for chunk in range(3):
            self.sums[4 * z, chunk] += self.from_first[z, chunk]
        if k < 3:
            self.line.send_end(k)

    def finish(self):
        def put(i, value):
            self.final[i] = value

        self.line.total(put)

    def last_total(self):
        at = 4 * self.spot.z

        def put(i, value):
            self.sums[at + i, 3] = value.astype(jnp.bfloat16)

        self.last_line.total(put)
        self.last_second_copy().start()

    def last_add_second(self):
        at = 4 * self.spot.z
        self.last_second_copy().wait_recv()
        self.sums[at + 1, 3] += self.last_pair[1]
        self.last_first_copy().start()
        self.sums[at, 3] += self.last_pair[0]

    def last_finish(self):
        self.last_first_copy().wait_recv()
        self.final[3] = self.sums[4 * self.spot.z, 3].astype(jnp.float32) + self.last_one[
            ...
        ].astype(jnp.float32)

    def store(self, put):
        core = self.spot.core
        for chunk in range(self.theirs.shape[0]):
            if self.whole:
                mine = self.final[2 * core + chunk]
            else:
                mine = self.final[chunk, pl.ds(pl.multiple_of(core * 24, 8), 24), :]
            put(core, chunk, mine)
        self.swap().wait_recv()
        for chunk in range(self.theirs.shape[0]):
            put(1 - core, chunk, self.theirs[chunk])
        self.swap().wait_send()

    def drain(self):
        for k in range(4):
            self.second_copy(k).wait_send()
            self.first_copy(k).wait_send()
        self.line.drain()
        self.last_line.drain()
        self.last_second_copy().wait_send()
        self.last_first_copy().wait_send()

    def release(self):
        spot, credit = self.spot, self.credit

        def tell(kind, device):
            pl.semaphore_signal(credit.at[kind], inc=1, device_id=device, device_id_type=MESH)

        tell(0, spot.second)
        tell(1, spot.first)

        @pl.when(spot.is_end)
        def _():
            tell(3, spot.inner)

        @pl.when(spot.is_middle)
        def _():
            tell(2, spot.inner)
            tell(2, spot.outer)


(
    DO_STEPS, DO_COND, DO_MODT, DO_MODZ, DO_MODS, DO_MODM, DO_MODROWS, DO_OWN, DO_GZ, DO_GS, DO_GX,
    DO_GY, DO_LX, DO_LY, DO_LP, DO_LZ, DO_LANDED, DO_CWAIT, DO_SS, DO_SY, DO_SX, DO_SZ, DO_SFIN,
    DO_TE, DO_TZ, DO_TTOT, DO_TY, DO_TX, DO_SWAP, DO_RETIRE, DO_ROWM, DO_ROWZ, DO_ROWP, DO_ROWT,
    DO_ROWD, DO_MASKS, DO_STANDARDIZE, DO_MODULATE, DO_PROJECT, DO_TURNN, DO_TURNA, DO_ATTEND,
    DO_JOIN, DO_ADD, DO_GATE, DO_EXPAND, DO_SENDH, DO_NEEDH, DO_DOWNT, DO_GHID, DO_SENDP,
    DO_CONTRACT, DO_CLOSE, DO_NEEDP, DO_UPT, DO_BACK2, DO_NORMB, DO_SPLIT, DO_ATTB, DO_SENDQ,
    DO_NEEDG, DO_NEEDQ, DO_OUTT, DO_QKVT, DO_BACK, DO_SENTQ,
) = range(66)

ORDER = (
    (DO_CWAIT, 0), (DO_CWAIT, 1), (DO_MASKS,), (DO_STANDARDIZE, 0), (DO_STEPS, 0), (DO_OWN, 0), (DO_GS, 0, 0),
    (DO_OWN, 1), (DO_GS, 1, 0), (DO_STEPS, 1), (DO_GZ, 0, 1), (DO_GS, 0, 1), (DO_GZ, 0, 2), (DO_LX, 1), (DO_GX, 0, 0),
    (DO_GZ, 1, 1), (DO_GZ, 1, 2), (DO_GS, 1, 1), (DO_COND,), (DO_MODT, 0), (DO_MODT, 1), (DO_GZ, 0, 3), (DO_GS, 0, 2),
    (DO_MODZ, 0), (DO_GZ, 1, 3), (DO_MODZ, 1), (DO_GX, 0, 1), (DO_GY, 0, 0), (DO_GS, 1, 2), (DO_LY, 1), (DO_GS, 0, 3),
    (DO_MODS, 0), (DO_MODM, 0), (DO_MODS, 1), (DO_GX, 0, 2), (DO_OWN, 2), (DO_GY, 0, 1), (DO_LP, 1, 2), (DO_GX, 0, 3),
    (DO_MODS, 2), (DO_LP, 1, 1), (DO_LZ, 1, 1), (DO_LX, 2), (DO_GS, 1, 3), (DO_MODROWS, 0), (DO_MODULATE, 0),
    (DO_GZ, 2, 1), (DO_GY, 0, 2), (DO_GZ, 2, 2), (DO_GX, 1, 0), (DO_LZ, 1, 2), (DO_GX, 1, 1), (DO_GY, 0, 3),
    (DO_LP, 1, 3), (DO_MODM, 1), (DO_LY, 2), (DO_GX, 1, 2), (DO_LANDED, 0), (DO_PROJECT, 0), (DO_GY, 1, 0),
    (DO_GZ, 2, 3), (DO_GX, 1, 3), (DO_TURNN, 0), (DO_MODROWS, 1), (DO_GY, 1, 1), (DO_GS, 2, 0), (DO_ATTEND, 0, 0),
    (DO_GY, 1, 2), (DO_LZ, 1, 3), (DO_LP, 2, 1), (DO_LP, 2, 2), (DO_GS, 2, 1), (DO_ATTEND, 0, 1), (DO_GY, 1, 3),
    (DO_LZ, 2, 1), (DO_GS, 2, 2), (DO_OWN, 3), (DO_ATTEND, 0, 2), (DO_GS, 2, 3), (DO_JOIN, 0), (DO_ADD, 0),
    (DO_LP, 2, 3), (DO_TURNA, 0), (DO_GX, 2, 0), (DO_STANDARDIZE, 1), (DO_MODULATE, 1), (DO_LZ, 2, 2), (DO_GZ, 3, 1),
    (DO_GZ, 3, 2), (DO_GATE, 2), (DO_GX, 2, 1), (DO_LX, 3), (DO_LANDED, 1), (DO_PROJECT, 1), (DO_GX, 2, 2),
    (DO_TURNN, 1), (DO_GY, 2, 0), (DO_GX, 2, 3), (DO_ATTEND, 1, 0), (DO_GY, 2, 1), (DO_LZ, 2, 3), (DO_GZ, 3, 3),
    (DO_GS, 3, 0), (DO_LY, 3), (DO_ATTEND, 1, 1), (DO_GY, 2, 2), (DO_GS, 3, 1), (DO_GY, 2, 3), (DO_ATTEND, 1, 2),
    (DO_GS, 3, 2), (DO_JOIN, 1), (DO_ADD, 1), (DO_GS, 3, 3), (DO_TURNA, 1), (DO_LP, 3, 1), (DO_LP, 3, 2),
    (DO_STANDARDIZE, 2), (DO_MODULATE, 2), (DO_GX, 3, 0), (DO_TURNN, 2), (DO_LZ, 3, 1), (DO_LANDED, 2),
    (DO_EXPAND, 0), (DO_SENDH, 0), (DO_GX, 3, 1), (DO_EXPAND, 1), (DO_GX, 3, 2), (DO_SENDH, 1), (DO_EXPAND, 2),
    (DO_LP, 3, 3), (DO_LZ, 3, 2), (DO_GX, 3, 3), (DO_SENDH, 2), (DO_EXPAND, 3), (DO_GY, 3, 0), (DO_SENDH, 3),
    (DO_GY, 3, 1), (DO_NEEDH, 0), (DO_DOWNT, 0), (DO_NEEDH, 1), (DO_DOWNT, 1), (DO_GY, 3, 2), (DO_NEEDH, 2),
    (DO_DOWNT, 2), (DO_GY, 3, 3), (DO_NEEDH, 3), (DO_DOWNT, 3), (DO_TE, 0, 0), (DO_SS, 0, 0), (DO_TE, 0, 1),
    (DO_LZ, 3, 3), (DO_LANDED, 3), (DO_SS, 0, 1), (DO_GHID, 0), (DO_GHID, 1), (DO_SENDP,), (DO_GHID, 2),
    (DO_TE, 0, 2), (DO_SS, 0, 2), (DO_GHID, 3), (DO_SY, 0, 0), (DO_NEEDP,), (DO_UPT, 3), (DO_TZ, 0, 0), (DO_UPT, 0),
    (DO_TE, 1, 0), (DO_UPT, 1), (DO_SY, 0, 1), (DO_UPT, 2), (DO_SS, 0, 3), (DO_CONTRACT,), (DO_SX, 0, 0),
    (DO_TZ, 0, 1), (DO_CLOSE,), (DO_SY, 0, 2), (DO_BACK2, 0), (DO_TE, 1, 1), (DO_TZ, 0, 2), (DO_SX, 0, 1),
    (DO_SS, 1, 0), (DO_BACK2, 1), (DO_BACK2, 2), (DO_SY, 0, 3), (DO_BACK2, 3), (DO_TZ, 1, 0), (DO_SX, 0, 2),
    (DO_SS, 1, 1), (DO_NORMB, 2), (DO_GATE, 1), (DO_SZ, 0, 0), (DO_SS, 1, 2), (DO_SPLIT, 1), (DO_SY, 1, 0),
    (DO_TTOT, 0), (DO_ATTB, 1, 0), (DO_SX, 0, 3), (DO_SY, 1, 1), (DO_TE, 1, 2), (DO_TZ, 1, 1), (DO_TZ, 1, 2),
    (DO_ATTB, 1, 1), (DO_SZ, 0, 1), (DO_SZ, 0, 2), (DO_SX, 1, 0), (DO_SS, 1, 3), (DO_NEEDG, 1), (DO_OUTT, 1),
    (DO_ATTB, 1, 2), (DO_SY, 1, 2), (DO_SX, 1, 1), (DO_TY, 0), (DO_SENDQ, 1), (DO_BACK, 1, 0), (DO_TTOT, 1),
    (DO_NEEDQ, 1), (DO_QKVT, 1, 0), (DO_SY, 1, 3), (DO_SFIN, 0), (DO_QKVT, 1, 1), (DO_SZ, 1, 0), (DO_SX, 1, 2),
    (DO_TX, 0), (DO_SWAP, 0), (DO_QKVT, 1, 2), (DO_TY, 1), (DO_BACK, 1, 1), (DO_SZ, 1, 1), (DO_RETIRE, 0),
    (DO_SX, 1, 3), (DO_CWAIT, 2), (DO_TE, 2, 0), (DO_SS, 2, 0), (DO_BACK, 1, 2), (DO_TE, 2, 1), (DO_TX, 1),
    (DO_NORMB, 1), (DO_SZ, 1, 2), (DO_ROWM, 1), (DO_SS, 2, 1), (DO_SENTQ, 1), (DO_GATE, 0), (DO_TE, 2, 2),
    (DO_SPLIT, 0), (DO_ATTB, 0, 0), (DO_SY, 2, 0), (DO_TZ, 2, 0), (DO_ATTB, 0, 1), (DO_ROWZ, 1), (DO_SY, 2, 1),
    (DO_TZ, 2, 1), (DO_SFIN, 1), (DO_SWAP, 1), (DO_SS, 2, 2), (DO_NEEDG, 0), (DO_OUTT, 0), (DO_SX, 2, 0),
    (DO_RETIRE, 1), (DO_ATTB, 0, 2), (DO_CWAIT, 3), (DO_TE, 3, 0), (DO_TZ, 2, 2), (DO_SS, 2, 3), (DO_SENDQ, 0),
    (DO_SX, 2, 1), (DO_BACK, 0, 0), (DO_ROWP, 1, 1), (DO_ROWP, 1, 2), (DO_NEEDQ, 0), (DO_SY, 2, 2), (DO_QKVT, 0, 0),
    (DO_QKVT, 0, 1), (DO_SZ, 2, 0), (DO_QKVT, 0, 2), (DO_TE, 3, 1), (DO_SS, 3, 0), (DO_BACK, 0, 1), (DO_BACK, 0, 2),
    (DO_SY, 2, 3), (DO_SX, 2, 2), (DO_TZ, 3, 0), (DO_TTOT, 2), (DO_SS, 3, 1), (DO_ROWP, 1, 3), (DO_NORMB, 0),
    (DO_ROWM, 0), (DO_SZ, 2, 1), (DO_TE, 3, 2), (DO_SENTQ, 0), (DO_SZ, 2, 2), (DO_SY, 3, 0), (DO_SX, 2, 3),
    (DO_SS, 3, 2), (DO_TY, 2), (DO_ROWT, 1), (DO_TZ, 3, 1), (DO_TZ, 3, 2), (DO_ROWD, 1), (DO_SS, 3, 3), (DO_SX, 3, 0),
    (DO_SFIN, 2), (DO_SY, 3, 1), (DO_ROWZ, 0), (DO_TX, 2), (DO_SWAP, 2), (DO_RETIRE, 2), (DO_SY, 3, 2), (DO_TTOT, 3),
    (DO_SZ, 3, 0), (DO_SX, 3, 1), (DO_ROWP, 0, 1), (DO_ROWP, 0, 2), (DO_SY, 3, 3), (DO_SX, 3, 2), (DO_TY, 3),
    (DO_SZ, 3, 1), (DO_SZ, 3, 2), (DO_ROWP, 0, 3), (DO_SX, 3, 3), (DO_TX, 3), (DO_SFIN, 3), (DO_SWAP, 3),
    (DO_ROWT, 0), (DO_RETIRE, 3), (DO_ROWD, 0),
)


def dot(left, right):
    return jnp.dot(left, right, preferred_element_type=jnp.float32)


GATHER_CHUNKS = (4, 3, 3, 3)


def layer_kernel(
    tokens,
    cotangent,
    steps,
    seg_ids,
    frame_ids,
    patch_ids,
    b_ada,
    w_ada,
    w_qkv_s,
    w_out_s,
    w_qkv_t,
    w_out_t,
    w_up,
    w_down,
    r_layer,
    r_tokens,
    cond,
    all_rows_mod,
    r_qkv_s,
    r_out_s,
    r_qkv_t,
    r_out_t,
    r_up,
    r_down,
    o_layer,
    o_tokens,
    o_qkv_s,
    o_out_s,
    o_qkv_t,
    o_out_t,
    o_up,
    o_down,
    leave_sems,
    held,
    stage,
    apart,
    apart_down,
    sums,
    from_second,
    from_first,
    from_z,
    last_pair,
    last_one,
    last_z,
    all_steps,
    bias,
    ids,
    mod,
    tally,
    xhat,
    deviation,
    normed,
    attended,
    turned,
    hidden_turned,
    qkv,
    probs,
    branch,
    stream,
    grad,
    hidden,
    slope,
    grad_pre_twin,
    gated,
    gated_twin,
    grad_attended,
    grad_qkv_twin,
    disallowed,
    swap_sems,
    gather_send,
    gather_recv,
    scatter_send,
    scatter_recv,
    credit,
    twin_send,
    twin_recv,
    step_send,
    step_recv,
    mod_send,
    mod_recv,
    row_send,
    row_recv,
):
    width, tok = tokens.shape[1], tokens.shape[0]
    f32, bf16 = jnp.float32, jnp.bfloat16
    spot = Spot()
    core = spot.core
    grad_qkv, grad_normed = hidden, stream

    def attention_piece(w_qkv, w_out):
        def piece(half, chunk):
            if chunk < 3:
                return w_qkv[:, pl.ds(pl.multiple_of(half * 1152 + chunk * 384, 128), 384)]
            return w_out[:, pl.ds(pl.multiple_of(half * 384, 128), 384)]

        return piece

    def up_piece(half, chunk):
        return w_up[:, pl.ds(pl.multiple_of(half * 1536 + chunk * 384, 128), 384)]

    def down_piece(half, chunk):
        return w_down[chunk * 48 : chunk * 48 + 48, pl.ds(pl.multiple_of(half * 384, 128), 384)]

    pieces = (
        attention_piece(w_qkv_s, w_out_s),
        attention_piece(w_qkv_t, w_out_t),
        up_piece,
        down_piece,
    )
    gathers = [
        Gather(
            spot,
            held.at[g],
            stage.at[g],
            apart.at[g] if g < 3 else apart_down,
            swap_sems.at[g],
            gather_send.at[g],
            gather_recv.at[g],
            GATHER_CHUNKS[g],
        )
        for g in range(4)
    ]
    scatters = [
        Scatter(
            spot,
            held.at[2, n - 2] if n >= 2 else sums.at[n],
            from_second.at[n % 2],
            from_first.at[n % 2],
            from_z.at[n % 2],
            last_pair.at[n % 2],
            last_one.at[n % 2],
            last_z.at[n % 2],
            stage.at[3 - n],
            apart_down if n == 0 else apart.at[3 - n],
            scatter_send.at[n],
            scatter_recv.at[n],
            credit.at[n % 2],
            n >= 2,
        )
        for n in range(4)
    ]

    def put_attention(o_qkv, o_out):
        def put(half, chunk, rows):
            if chunk < 3:
                o_qkv[:, pl.ds(pl.multiple_of(half * 1152 + chunk * 384, 128), 384)] = rows
            else:
                o_out[:, pl.ds(pl.multiple_of(half * 384, 128), 384)] = rows

        return put

    def put_up(half, chunk, rows):
        o_up[:, pl.ds(pl.multiple_of(half * 1536 + chunk * 384, 128), 384)] = rows

    def put_down(half, chunk, rows):
        o_down[chunk * 48 : chunk * 48 + 48, pl.ds(pl.multiple_of(half * 384, 128), 384)] = rows

    puts = (put_down, put_up, put_attention(o_qkv_t, o_out_t), put_attention(o_qkv_s, o_out_s))

    def to_twin(index, src, dst):
        return remote(src, dst, twin_send.at[index], twin_recv.at[index], spot.twin)

    def turned_copy(i):
        return to_twin(i, turned.at[i, 0], turned.at[i, 1])

    def hidden_copy(i):
        rows = pl.ds(768 * i, 768)
        return to_twin(12 + i, hidden_turned.at[0, rows], hidden_turned.at[1, rows])

    def gated_copy(j):
        theirs = pl.multiple_of((1 - core) * 384, 128)
        return to_twin(6 + j, gated.at[j, :, pl.ds(theirs, 384)], gated_twin.at[j])

    def grad_pre_copy():
        theirs = pl.multiple_of((1 - core) * 1536, 128)
        return to_twin(9, slope.at[:, pl.ds(theirs, 1536)], grad_pre_twin)

    def grad_qkv_copy(j):
        theirs = pl.multiple_of((1 - core) * 1152, 128)
        return to_twin(10 + j, grad_qkv.at[:, pl.ds(theirs, 1152)], grad_qkv_twin.at[j])

    def step_twin(owner):
        ref = all_steps.at[spot.z, spot.plane, owner]
        return remote(ref, ref, step_send.at[0], step_recv.at[0], spot.twin)

    step_line = Exchange(
        spot.line,
        spot.z,
        lambda z: all_steps.at[spot.z, spot.plane],
        lambda z: all_steps.at[z, spot.plane],
        step_send.at[pl.ds(1, 3)],
        step_recv.at[pl.ds(4, 4)],
    )
    step_mates = Exchange(
        spot.mates,
        spot.plane,
        lambda plane: all_steps.at[:, spot.plane],
        lambda plane: all_steps.at[:, plane],
        step_send.at[pl.ds(4, 3)],
        step_recv.at[pl.ds(8, 4)],
    )

    def steps_prepare():
        row = lax.broadcasted_iota(jnp.int32, (8, 128), 0)
        value = jnp.where(row == 0, steps[0, 0], jnp.where(row == 1, steps[0, 1], 0))
        all_steps[spot.z, spot.plane, core] = value.astype(f32)

    def steps_line():
        step_twin(1 - core).wait_recv()
        step_line.start()

    def steps_mates():
        step_line.arrive()
        step_mates.start()

    def steps_drain():
        step_twin(core).wait_send()
        step_line.drain()
        step_mates.drain()

    def make_cond():
        step_mates.arrive()
        flat = all_steps[...].reshape(256, 128)
        clip = lax.broadcasted_iota(jnp.int32, (64, 256), 0)
        column = lax.broadcasted_iota(jnp.int32, (64, 256), 1)
        wanted = 64 * ((clip >> 3) & 3) + 16 * ((clip >> 1) & 3) + 8 * (clip >> 5) + (clip & 1)
        times = jnp.dot(
            (column == wanted).astype(f32),
            flat,
            precision=lax.Precision.HIGHEST,
            preferred_element_type=f32,
        )
        first = (spot.chip * 2 + core) * 24
        half_width = width // 2
        feature = first + lax.broadcasted_iota(jnp.int32, (64, 128), 1)
        place = jnp.where(feature < half_width, feature, feature - half_width).astype(f32)
        angle = times * jnp.exp(-math.log(FREQ_BASE) * place / half_width)
        value = jnp.where(feature < half_width, jnp.cos(angle), jnp.sin(angle))
        cond[...] = (value / (1.0 + jnp.exp(-value))).astype(bf16)

    parts = (range(0, 1), range(1, 3))

    def columns_of(j, half, chunk):
        at = 2304 * j + 1152 * half + 384 * chunk
        return slice(at, at + 384)

    def rows_of(chunk):
        return slice(16 * chunk, 16 * chunk + 16)

    class ModPart:
        def __init__(self, part):
            self.part, self.n = part, len(parts[part])
            n, base = self.n, 6 * part

            def region(i):
                return pl.ds(base + n * i, n)

            self.out, self.into, self.sum = (sums.at[1, region(i)] for i in range(3))
            self.own = sums.at[1, 5, pl.ds(part, n)]
            if part:
                self.line = LineSum(
                    spot,
                    lambda z: sums.at[1, region(2), z],
                    lambda i: sums.at[1, region(3), i] if i < 4 else self.own,
                    mod_send.at[part, pl.ds(1, 3)],
                    mod_recv.at[part, pl.ds(1, 5)],
                )
            else:
                self.line = Exchange(
                    spot.line,
                    spot.z,
                    lambda z: sums.at[1, region(2), z],
                    lambda z: sums.at[1, region(3), z],
                    mod_send.at[part, pl.ds(1, 3)],
                    mod_recv.at[part, pl.ds(1, 4)],
                )
            self.mates = Exchange(
                spot.mates,
                spot.plane,
                lambda plane: sums.at[1, region(4), plane, 16:32],
                lambda plane: sums.at[1, region(4), plane, 0:16],
                mod_send.at[part, pl.ds(4, 3)],
                mod_recv.at[part, pl.ds(6, 4)],
            )

        def swap(self):
            part = self.part
            return remote(self.out, self.into, mod_send.at[part, 0], mod_recv.at[part, 0], spot.twin)

        def terms(self, owner):
            rows = cond[pl.ds(pl.multiple_of(32 * owner, 32), 32), :24]
            for i, j in enumerate(parts[self.part]):
                for chunk in range(3):
                    left, right = (
                        dot(rows, w_ada[:, columns_of(j, half, chunk)])
                        + bias[0:1, columns_of(j, half, chunk)]
                        for half in range(2)
                    )
                    for z in range(4):
                        own = slice(8 * z, 8 * z + 8)
                        block = jnp.concatenate([left[own], right[own]], axis=0)
                        yield (i, z, rows_of(chunk)), block

        def for_twin(self):
            for at, value in self.terms(1 - core):
                self.out[at] = value.astype(bf16)
            self.swap().start()

        def for_line(self):
            self.swap().wait_recv()
            for at, value in self.terms(core):
                self.sum[at] = (value + self.into[at].astype(f32)).astype(bf16)
            if self.part:
                for k in range(3):
                    self.line.send_end(k)
            else:
                self.line.start()

        def for_mates(self):
            def put(i, value):
                self.own[i] = value.astype(bf16)

            if self.part:
                self.line.total(put)
            else:
                self.line.arrive()
                for i in range(self.n):
                    value = self.line.src(spot.z)[i].astype(f32)
                    for z, _ in spot.line:
                        value += self.line.dst(z)[i].astype(f32)
                    put(i, value)
            for plane, _ in spot.mates:
                self.mates.src(plane)[...] = self.picked(plane).astype(bf16)
            self.mates.start()

        def picked(self, plane):
            to = lax.broadcasted_iota(jnp.int32, (16, 48), 0)
            at = lax.broadcasted_iota(jnp.int32, (16, 48), 1)
            wanted = 16 * (to >> 2) + 8 * ((to >> 1) & 1) + 2 * plane + (to & 1)
            pick = (at == wanted).astype(bf16)
            return jnp.stack([dot(pick, self.own[i]) for i in range(self.n)])

        def done(self):
            self.mates.arrive()
            total = self.picked(spot.plane)
            for plane, _ in spot.mates:
                total += self.mates.dst(plane)[...].astype(f32)
            for i, j in enumerate(parts[self.part]):
                for chunk in range(3):
                    for half in range(2):
                        for clip in range(2):
                            row = 4 * chunk + 2 * half + clip
                            mod[clip : clip + 1, columns_of(j, half, chunk)] = total[i, row : row + 1]

        def drain(self):
            self.swap().wait_send()
            self.line.drain()
            self.mates.drain()

    class RowPart:
        def __init__(self, part):
            self.part, n = part, len(parts[part])
            self.subs = subs = pl.ds(parts[part][0], n)
            self.mates = Exchange(
                spot.mates,
                spot.plane,
                lambda plane: all_rows_mod.at[core, spot.z, subs, spot.plane],
                lambda plane: all_rows_mod.at[core, spot.z, subs, plane],
                row_send.at[part, pl.ds(1, 3)],
                row_recv.at[part, pl.ds(1, 4)],
            )
            self.line = LineGather(
                spot,
                lambda z: all_rows_mod.at[core, z, subs],
                row_send.at[part, pl.ds(4, 5)],
                row_recv.at[part, pl.ds(5, 4)],
            )

        def swap(self, owner):
            ref = all_rows_mod.at[owner, :, self.subs]
            return remote(ref, ref, row_send.at[self.part, 0], row_recv.at[self.part, 0], spot.twin)

        def for_mates(self):
            row = lax.broadcasted_iota(jnp.int32, (16, 384), 0)
            for j in parts[self.part]:
                value = 0.0
                for chunk in range(3):
                    for half in range(2):
                        for clip in range(2):
                            own = tally[clip : clip + 1, columns_of(j, half, chunk)]
                            value += jnp.where(row == 4 * chunk + 2 * half + clip, own, 0.0)
                all_rows_mod[core, spot.z, j, spot.plane] = value.astype(bf16)
            self.mates.start()

        def for_line(self):
            self.mates.arrive()
            self.line.open()

        def for_twin(self):
            for k in (1, 2, 3):
                self.line.take(k)
            self.swap(core).start()

        def done(self):
            self.swap(1 - core).wait_recv()

        def drain(self):
            self.swap(core).wait_send()
            self.mates.drain()
            self.line.drain()

    mod_parts = [ModPart(part) for part in range(2)]
    row_parts = [RowPart(part) for part in range(2)]

    def by_rows(action):
        @pl.loop(0, tok // 64)
        def _(i):
            action(pl.ds(pl.multiple_of(i * 64, 64), 64))

    def mod_part(j, component, rows):
        at = (3 * j + component) * width
        second = ids[rows, 2:3] == 1.0
        return jnp.where(second, mod[1:2, at : at + width], mod[0:1, at : at + width])

    def count(j, component, rows, value):
        at = (3 * j + component) * width
        second = ids[rows, 2:3] == 1.0
        tally[0:1, at : at + width] += jnp.sum(jnp.where(second, 0.0, value), axis=0, keepdims=True)
        tally[1:2, at : at + width] += jnp.sum(jnp.where(second, value, 0.0), axis=0, keepdims=True)

    def masks():
        spatial = (seg_ids[...] * 16 + frame_ids[...]).astype(f32)
        temporal = (seg_ids[...] * 16 + patch_ids[...]).astype(f32)
        row = lax.broadcasted_iota(jnp.int32, (8, tok), 0)
        second = seg_ids[...].astype(f32)
        stacked = jnp.where(row == 0, spatial, jnp.where(row == 1, temporal, second))
        ids[...] = stacked.T
        for j, keys in enumerate((spatial, temporal)):
            disallowed[j] = jnp.where(ids[:, j : j + 1] == keys, 0.0, MASKED)
        tally[...] = jnp.zeros_like(tally)
        share = b_ada.shape[0]
        bias[...] = jnp.zeros_like(bias)
        bias[0:1, :share] = b_ada[...].astype(f32).reshape(1, share)
        bias[...] = pltpu.roll(bias[...], (2 * spot.chip + core) * share, 1)

    def standardize(j):
        def action(rows):
            if j == 0:
                stream[rows] = tokens[rows].astype(f32)
            value = stream[rows]
            center = value - jnp.mean(value, axis=-1, keepdims=True)
            inverse = lax.rsqrt(jnp.mean(center * center, axis=-1, keepdims=True) + EPSILON)
            xhat[j, rows] = (center * inverse).astype(bf16)
            deviation[rows, j : j + 1] = inverse

        by_rows(action)

    def modulate(j):
        def action(rows):
            normed[rows] = (
                xhat[j, rows].astype(f32) * (1.0 + mod_part(j, 1, rows)) + mod_part(j, 0, rows)
            ).astype(bf16)

        by_rows(action)

    def turn(i, source):
        for at in range(0, tok, 128):
            turned[i, 0, :, at : at + 128] = source[at : at + 128, :].T
        turned_copy(i).start()

    def weight(g, half, chunk):
        return held[g, half, :, chunk].reshape(width, 384)

    def project(j):
        @pl.loop(0, 6)
        def _(i):
            half, chunk = lax.div(i, 3), lax.rem(i, 3)
            columns = pl.ds(pl.multiple_of(i * 384, 128), 384)
            qkv[j, :, columns] = dot(normed[...], weight(j, half, chunk)).astype(bf16)

    def head_lanes():
        lane = lax.broadcasted_iota(jnp.int32, (1, 128), 1)
        return lane < 64, lane >= 64

    def head_columns(pair):
        return [pl.ds(pl.multiple_of(part * 768 + pair * 128, 128), 128) for part in range(3)]

    def attend(j, first, last):
        @pl.loop(first, last)
        def _(pair):
            at_q, at_k, at_v = head_columns(pair)
            queries, keys, values = qkv[j, :, at_q], qkv[j, :, at_k], qkv[j, :, at_v]
            results = []
            for head, lanes in enumerate(head_lanes()):
                scaled = jnp.where(lanes, queries, 0.0) * bf16(0.125)
                scores = contract_cols(scaled, keys) + disallowed[j]
                scores = jnp.exp(scores - jnp.max(scores, axis=-1, keepdims=True))
                low = (scores * (1.0 / jnp.sum(scores, axis=-1, keepdims=True))).astype(bf16)
                probs[j, 2 * pair + head] = low
                results.append(dot(low, values))
            attended[:, at_q] = jnp.where(head_lanes()[0], results[0], results[1]).astype(bf16)

    def join(j):
        @pl.loop(0, 2)
        def _(half):
            columns = pl.ds(pl.multiple_of(half * 384, 128), 384)
            branch[j, :, columns] = dot(attended[...], weight(j, half, 3)).astype(bf16)

    def add_branch(j):
        def action(rows):
            stream[rows] += mod_part(j, 2, rows) * branch[j, rows].astype(f32)

        by_rows(action)

    def expand(first, last):
        @pl.loop(first, last)
        def _(i):
            columns = pl.ds(pl.multiple_of(i * 384, 128), 384)
            matrix = weight(2, lax.div(i, 4), lax.rem(i, 4))
            for at in range(0, tok, 128):
                rows = slice(at, at + 128)
                pre = dot(normed[rows], matrix)
                square = pre * pre
                root = math.sqrt(2.0 / math.pi)
                bent = jnp.tanh(root * (pre + 0.044715 * (square * pre)))
                value = (0.5 * pre * (1.0 + bent)).astype(bf16)
                hidden[rows, columns] = value
                hidden_turned[0, columns, rows] = value.T
                slope[rows, columns] = (
                    0.5 * (1.0 + bent)
                    + 0.5 * pre * (1.0 - bent * bent) * (root * (1.0 + 3 * 0.044715 * square))
                ).astype(bf16)

    def gate(j):
        def action(rows):
            value = cotangent[rows].astype(f32) if j == 2 else grad[rows]
            if j == 2:
                grad[rows] = value
            else:
                count(j, 2, rows, value * branch[j, rows].astype(f32))
            gated[j, rows] = (mod_part(j, 2, rows) * value).astype(bf16)

        by_rows(action)
        gated_copy(j).start()

    def own_columns(first, width_of_half):
        return pl.ds(pl.multiple_of(core * width_of_half + first, 128), 384)

    def down_terms(z):
        scatter = scatters[0]
        rows = slice(768 * z, 768 * z + 768)
        value = dot(hidden_turned[0, rows], gated[2, :, own_columns(0, 384)]) + dot(
            hidden_turned[1, rows], gated_twin[2]
        )
        value = value.astype(bf16).reshape(4, 4, 48, 384)
        for plane in range(4):
            scatter.sums[scatter.place(4 * z + plane)] = value[plane]

    def column_terms(n, chunk, left, right, right_twin):
        value = dot(turned[left, 0], right) + dot(turned[left, 1], right_twin)
        value = value.astype(bf16).reshape(16, 48, 384)
        for chip in range(16):
            scatters[n].sums[scatters[n].place(chip), chunk] = value[chip]

    def up_terms(chunk):
        column_terms(
            1,
            chunk,
            4,
            slope[:, own_columns(384 * chunk, 1536)],
            grad_pre_twin[:, 384 * chunk : 384 * chunk + 384],
        )

    def out_terms(j):
        column_terms(3 - j, 3, 2 * j + 1, gated[j, :, own_columns(0, 384)], gated_twin[j])

    def qkv_terms(j, chunk):
        column_terms(
            3 - j,
            chunk,
            2 * j,
            grad_qkv[:, own_columns(384 * chunk, 1152)],
            grad_qkv_twin[j, :, 384 * chunk : 384 * chunk + 384],
        )

    def contract():
        @pl.loop(0, 2)
        def _(half):
            columns = pl.ds(pl.multiple_of(half * 384, 128), 384)
            matrix = held[3, half].reshape(3072, 384)
            normed[:, columns] = dot(hidden[...], matrix).astype(bf16)

    def close():
        def action(rows):
            value = normed[rows].astype(f32)
            o_layer[rows] = (stream[rows] + mod_part(2, 2, rows) * value).astype(bf16)
            count(2, 2, rows, cotangent[rows].astype(f32) * value)

        by_rows(action)

    def grad_hidden(step):
        first = 2 * lax.rem(step + 2 - 2 * core, 4)

        @pl.loop(0, 2)
        def _(part):
            i = first + part
            columns = pl.ds(pl.multiple_of(i * 384, 128), 384)
            value = sum(
                contract_cols(
                    gated[2, :, 384 * half : 384 * half + 384],
                    held[3, half, pl.ds(2 * i, 2)].reshape(384, 384),
                )
                for half in range(2)
            )
            slope[:, columns] = (slope[:, columns].astype(f32) * value).astype(bf16)

    def back_project(g, chunks, source, first, last):
        @pl.loop(first, last)
        def _(i):
            columns = pl.ds(pl.multiple_of(i * 384, 128), 384)
            value = contract_cols(
                source[:, columns], weight(g, lax.div(i, chunks), lax.rem(i, chunks))
            )

            @pl.when(i == 0)
            def _():
                grad_normed[...] = value

            @pl.when(i > 0)
            def _():
                grad_normed[...] += value

    def norm_back(j):
        def action(rows):
            value, unit = grad_normed[rows], xhat[j, rows].astype(f32)
            count(j, 0, rows, value)
            count(j, 1, rows, value * unit)
            scaled = value * (1.0 + mod_part(j, 1, rows))
            inner = jnp.mean(scaled * unit, axis=-1, keepdims=True)
            scaled = scaled - jnp.mean(scaled, axis=-1, keepdims=True)
            total = grad[rows] + deviation[rows, j : j + 1] * (scaled - unit * inner)
            if j == 0:
                o_tokens[rows] = total
            else:
                grad[rows] = total

        by_rows(action)

    def split(j):
        value = sum(
            contract_cols(gated[j, :, 384 * half : 384 * half + 384], weight(j, half, 3))
            for half in range(2)
        )
        grad_attended[...] = value.astype(bf16)

    def attend_back(j, first, last):
        @pl.loop(first, last)
        def _(pair):
            at_q, at_k, at_v = head_columns(pair)
            queries, keys, values = qkv[j, :, at_q], qkv[j, :, at_k], qkv[j, :, at_v]
            given = grad_attended[:, at_q]
            grad_q, grad_k, grad_v = [], 0.0, 0.0
            for head, lanes in enumerate(head_lanes()):
                part = jnp.where(lanes, given, 0.0).astype(bf16)
                low = probs[j, 2 * pair + head]
                product = low.astype(f32) * contract_cols(part, values)
                total = jnp.sum(product, axis=-1, keepdims=True)
                scores = ((product - low.astype(f32) * total) * 0.125).astype(bf16)
                grad_v += contract_rows(low, part)
                grad_k += contract_rows(scores, jnp.where(lanes, queries, 0.0).astype(bf16))
                grad_q.append(dot(scores, keys))
            grad_qkv[:, at_q] = jnp.where(head_lanes()[0], grad_q[0], grad_q[1]).astype(bf16)
            grad_qkv[:, at_k] = grad_k.astype(bf16)
            grad_qkv[:, at_v] = grad_v.astype(bf16)

    def each_twin_copy():
        for i in range(5):
            yield turned_copy(i)
        for i in range(4):
            yield hidden_copy(i)
        for j in range(3):
            yield gated_copy(j)
        yield grad_pre_copy()

    def forward_drain():
        steps_drain()
        for part in mod_parts:
            part.drain()
        for gather in gathers:
            gather.swap().wait_send()

    def send_hidden(i):
        if i == 0:
            forward_drain()
        hidden_copy(i).start()

    def need_hidden(i):
        if i == 0:
            gated_copy(2).wait_recv()
        hidden_copy(i).wait_recv()

    def need_gated(j):
        if j == 1:
            gathers[2].drain()
        need(turned_copy, 2 * j + 1)
        need(gated_copy, j)

    leaving = [
        pltpu.make_async_copy(src, dst, leave_sems.at[i])
        for i, (src, dst) in enumerate(
            (
                (o_layer, r_layer),
                (o_tokens, r_tokens),
                (o_down, r_down),
                (o_up, r_up),
                (o_qkv_t, r_qkv_t),
                (o_out_t, r_out_t),
                (o_qkv_s, r_qkv_s),
                (o_out_s, r_out_s),
            )
        )
    ]
    of_group = (leaving[2:3], leaving[3:4], leaving[4:6], leaving[6:8])

    def retire(n):
        scatters[n].store(puts[n])
        for copy in of_group[n]:
            copy.start()
        scatters[n].drain()
        if n < 2:
            scatters[n].release()

    def swap(n):
        scatters[n].swap().start()

    def need(copy, *indices):
        copy(*indices).wait_recv()

    steps_of = {
        DO_STEPS: (steps_line, steps_mates),
        DO_COND: make_cond,
        DO_MODT: lambda part: mod_parts[part].for_twin(),
        DO_MODZ: lambda part: mod_parts[part].for_line(),
        DO_MODS: lambda k: mod_parts[1].line.send_middle(k),
        DO_MODM: lambda part: mod_parts[part].for_mates(),
        DO_MODROWS: lambda part: mod_parts[part].done(),
        DO_OWN: lambda g: gathers[g].own(),
        DO_GZ: lambda g, k: gathers[g].pass_on(k),
        DO_GS: lambda g, k: gathers[g].spread(k),
        DO_GX: lambda g, k: gathers[g].along_first(k),
        DO_GY: lambda g, k: gathers[g].along_second(k),
        DO_LX: lambda g: gathers[g].last_along_first(),
        DO_LY: lambda g: gathers[g].last_along_second(),
        DO_LP: lambda g, k: gathers[g].line.pass_on(k),
        DO_LZ: lambda g, k: gathers[g].last_along_z(k),
        DO_LANDED: lambda g: gathers[g].landed(),
        DO_CWAIT: lambda n: scatters[n].wait_credit(),
        DO_SS: lambda n, k: scatters[n].second_copy(k).start(),
        DO_SY: lambda n, k: scatters[n].add_second(k),
        DO_SX: lambda n, k: scatters[n].add_first(k),
        DO_SZ: lambda n, k: scatters[n].line.send_middle(k),
        DO_SFIN: lambda n: scatters[n].finish(),
        DO_TE: lambda n, k: scatters[n].last_line.send_end(k),
        DO_TZ: lambda n, k: scatters[n].last_line.send_middle(k),
        DO_TTOT: lambda n: scatters[n].last_total(),
        DO_TY: lambda n: scatters[n].last_add_second(),
        DO_TX: lambda n: scatters[n].last_finish(),
        DO_SWAP: swap,
        DO_RETIRE: retire,
        DO_ROWM: lambda part: row_parts[part].for_mates(),
        DO_ROWZ: lambda part: row_parts[part].for_line(),
        DO_ROWP: lambda part, k: row_parts[part].line.pass_on(k),
        DO_ROWT: lambda part: row_parts[part].for_twin(),
        DO_ROWD: lambda part: row_parts[part].done(),
        DO_MASKS: masks,
        DO_STANDARDIZE: standardize,
        DO_MODULATE: modulate,
        DO_PROJECT: project,
        DO_TURNN: lambda j: turn(2 * j, normed),
        DO_TURNA: lambda j: turn(2 * j + 1, attended),
        DO_ATTEND: lambda j, i: attend(j, 2 * i, 2 * i + 2),
        DO_JOIN: join,
        DO_ADD: add_branch,
        DO_GATE: gate,
        DO_EXPAND: lambda i: expand(2 * i, 2 * i + 2),
        DO_SENDH: send_hidden,
        DO_NEEDH: need_hidden,
        DO_DOWNT: down_terms,
        DO_GHID: grad_hidden,
        DO_SENDP: lambda: grad_pre_copy().start(),
        DO_CONTRACT: contract,
        DO_CLOSE: lambda: (close(), leaving[0].start()),
        DO_NEEDP: lambda: (need(grad_pre_copy), need(turned_copy, 4)),
        DO_UPT: up_terms,
        DO_BACK2: lambda i: back_project(2, 4, slope, 2 * i, 2 * i + 2),
        DO_NORMB: norm_back,
        DO_SPLIT: split,
        DO_ATTB: lambda j, i: attend_back(j, 2 * i, 2 * i + 2),
        DO_SENDQ: lambda j: grad_qkv_copy(j).start(),
        DO_NEEDG: need_gated,
        DO_NEEDQ: lambda j: (
            need(turned_copy, 2 * j),
            need(grad_qkv_copy, j),
        ),
        DO_OUTT: out_terms,
        DO_QKVT: qkv_terms,
        DO_BACK: lambda j, i: back_project(j, 3, grad_qkv, 2 * i, 2 * i + 2),
        DO_SENTQ: lambda j: (grad_qkv_copy(j).wait_send(), j == 0 and leaving[1].start()),
    }
    def prepare():
        for g, gather in enumerate(gathers):
            gather.open(pieces[g])
        steps_prepare()

    greet(spot, prepare)
    gathers[0].swap().start()
    step_twin(core).start()
    for gather in gathers[1:]:
        gather.swap().start()
    for name, *indices in ORDER:
        step = steps_of[name]
        if isinstance(step, tuple):
            step[indices[0]]()
        else:
            step(*indices)
    for part in row_parts:
        part.drain()
    for g in (0, 1, 3):
        gathers[g].drain()
    for copy in each_twin_copy():
        copy.wait_send()
    for copy in leaving:
        copy.wait()


def finish_kernel(*refs):
    sources, r_ada, o_bias, results = refs[:10], refs[10], refs[11], refs[12:20]
    held, o_ada, total, sem, ada_sem = refs[20:30], refs[30], refs[31], refs[32], refs[33]
    cond, all_rows_mod = held[:2]

    def copies(first, second, kind):
        return [
            pltpu.make_async_copy(src, dst, sem.at[kind, i])
            for i, (src, dst) in enumerate(zip(first, second, strict=True))
        ]

    arriving, leaving = copies(sources, held, 0), copies(held[2:], results, 1)
    for copy in arriving:
        copy.start()
    total[...] = jnp.zeros_like(total)
    clip = lax.broadcasted_iota(jnp.int32, (64, 512), 0)
    at = lax.broadcasted_iota(jnp.int32, (64, 512), 1)
    spread = (clip == 2 * (at >> 4) + (at & 1)).astype(jnp.bfloat16)
    arriving[0].wait()
    weights = contract_rows(cond[...], spread)[:32]
    row = lax.broadcasted_iota(jnp.int32, (32, 512), 0)
    kind = (lax.broadcasted_iota(jnp.int32, (32, 512), 1) & 15) >> 1
    weights = jnp.where(row == 24, 1.0, weights)
    for copy, onward in zip(arriving[2:], leaving, strict=True):
        copy.wait()
        onward.start()
    arriving[1].wait()
    for j in range(3):
        values = all_rows_mod[:, :, j].reshape(512, 384)
        for half in range(2):
            for chunk in range(3):
                columns = slice(2304 * j + 1152 * half + 384 * chunk, 2304 * j + 1152 * half + 384 * chunk + 384)
                own = jnp.where(kind == 2 * chunk + half, weights, 0.0).astype(jnp.bfloat16)
                product = dot(own, values)
                o_ada[:, columns] = product[:24]
                total[0:1, columns] = product[24:25]
        part = slice(2304 * j, 2304 * j + 2304)
        leaving.append(pltpu.make_async_copy(o_ada.at[:, part], r_ada.at[:, part], ada_sem.at[j]))
        leaving[-1].start()
    place = lax.axis_index("wide") * 2 + lax.axis_index("narrow")
    share, columns = o_bias.shape[1], total.shape[1]
    turned = pltpu.roll(total[...], lax.rem(columns - place * share, columns), 1)
    o_bias[...] = turned[0:1, :share]
    for copy in leaving:
        copy.wait()


def layer(tokens, cotangent, steps, seg_ids, frame_ids, patch_ids, b_ada, w_ada, *shards):
    f32, bf16 = jnp.float32, jnp.bfloat16
    tok, width = tokens.shape
    block = (4, 48, 384)
    dma, vmem = pltpu.SemaphoreType.DMA, pltpu.VMEM
    in_vmem, in_hbm = pl.BlockSpec(memory_space=vmem), pl.BlockSpec(memory_space=pltpu.HBM)
    outs = pl.pallas_call(
        layer_kernel,
        out_shape=[
            jax.ShapeDtypeStruct((tok, width), bf16),
            jax.ShapeDtypeStruct((tok, width), f32),
            jax.ShapeDtypeStruct((64, 128), bf16),
            jax.ShapeDtypeStruct((2, 4, 3, 4, 16, 384), bf16),
        ]
        + [jax.ShapeDtypeStruct(shard.shape, f32) for shard in shards],
        in_specs=[in_vmem] * 2 + [pl.BlockSpec(memory_space=pltpu.SMEM)] + [in_vmem] * 11,
        out_specs=[in_hbm] * 2 + [in_vmem] * 2 + [in_hbm] * 6,
        scratch_shapes=[
            vmem((tok, width), bf16),
            vmem((tok, width), f32),
            *(vmem(shard.shape, f32) for shard in shards),
            dma((8,)),
            vmem((4, 2, 16) + block, bf16),
            vmem((4,) + block, f32),
            vmem((3, 4, 24, 384), f32),
            vmem((2, 48, 384), f32),
            vmem((2, 16) + block, bf16),
            vmem((2, 4, 2, 3, 48, 384), bf16),
            vmem((2, 4, 3, 48, 384), bf16),
            vmem((2, 5, 3, 48, 384), bf16),
            vmem((2, 2, 48, 384), bf16),
            vmem((2, 48, 384), bf16),
            vmem((2, 5) + block, bf16),
            vmem((4, 4, 2, 8, 128), f32),
            vmem((8, w_ada.shape[1]), f32),
            vmem((tok, 8), f32),
            vmem((8, 6912), f32),
            vmem((8, 6912), f32),
            vmem((3, tok, width), bf16),
            vmem((tok, 128), f32),
            vmem((tok, width), bf16),
            vmem((tok, width), bf16),
            vmem((5, 2, width, tok), bf16),
            vmem((2, 4 * width, tok), bf16),
            vmem((2, tok, 3 * width), bf16),
            vmem((2, HEADS, tok, tok), bf16),
            vmem((2, tok, width), bf16),
            vmem((tok, width), f32),
            vmem((tok, width), f32),
            vmem((tok, 4 * width), bf16),
            vmem((tok, 4 * width), bf16),
            vmem((tok, 2 * width), bf16),
            vmem((3, tok, width), bf16),
            vmem((3, tok, width // 2), bf16),
            vmem((tok, width), bf16),
            vmem((2, tok, 3 * width // 2), bf16),
            vmem((2, tok, tok), f32),
            dma((4, 2)),
            dma((4, 33)),
            dma((4, 31)),
            dma((4, 17)),
            dma((4, 21)),
            pltpu.SemaphoreType.REGULAR((2, 4)),
            dma((16,)),
            dma((16,)),
            dma((7,)),
            dma((12,)),
            dma((2, 7)),
            dma((2, 10)),
            dma((2, 9)),
            dma((2, 9)),
        ],
        compiler_params=pltpu.CompilerParams(
            collective_id=0, has_side_effects=True, vmem_limit_bytes=64 * 2**20
        ),
    )(tokens, cotangent, steps, seg_ids, frame_ids, patch_ids, b_ada, w_ada, *shards)
    sources = (*outs[:2], *outs[4:])
    return pl.pallas_call(
        finish_kernel,
        out_shape=[
            jax.ShapeDtypeStruct(w_ada.shape, f32),
            jax.ShapeDtypeStruct((1, w_ada.shape[1] // 32), f32),
        ]
        + [jax.ShapeDtypeStruct(source.shape, source.dtype) for source in sources],
        in_specs=[in_hbm] * 10,
        out_specs=[in_hbm, in_vmem] + [in_hbm] * 8,
        scratch_shapes=[vmem(source.shape, source.dtype) for source in (outs[2], outs[3], *sources)]
        + [vmem(w_ada.shape, f32), vmem((8, w_ada.shape[1]), f32), dma((2, 10)), dma((3,))],
        compiler_params=pltpu.CompilerParams(vmem_limit_bytes=60 * 2**20),
    )(outs[2], outs[3], *sources)


def on_grid(
    tokens,
    seg_ids,
    frame_ids,
    patch_ids,
    timesteps,
    w_ada,
    b_ada,
    w_qkv_spatial,
    w_out_spatial,
    w_qkv_temporal,
    w_out_temporal,
    w_up,
    w_down,
    cotangent,
):
    shards = (w_qkv_spatial, w_out_spatial, w_qkv_temporal, w_out_temporal, w_up, w_down)
    grad_ada, grad_bias, out, grad_tokens, *grads = layer(
        tokens,
        cotangent,
        timesteps[None],
        seg_ids[None],
        frame_ids[None],
        patch_ids[None],
        b_ada,
        w_ada,
        *shards,
    )
    return (out, grad_tokens, grad_ada, grad_bias.reshape(-1), *grads)


def on_device(
    tokens,
    seg_ids,
    frame_ids,
    patch_ids,
    timesteps,
    w_ada,
    b_ada,
    w_qkv_spatial,
    w_out_spatial,
    w_qkv_temporal,
    w_out_temporal,
    w_up,
    w_down,
    cotangent,
):
    axes = ("wide", "narrow")
    gathered = (
        None,
        None,
        lax.all_gather(w_qkv_spatial, axes, axis=0, tiled=True),
        lax.all_gather(w_out_spatial, axes, axis=0, tiled=True),
        lax.all_gather(w_qkv_temporal, axes, axis=0, tiled=True),
        lax.all_gather(w_out_temporal, axes, axis=0, tiled=True),
        lax.all_gather(w_up, axes, axis=0, tiled=True),
        lax.all_gather(w_down, axes, axis=0, tiled=True),
    )
    width = tokens.shape[1]
    head_count = HEADS
    clip_count = timesteps.shape[0]
    row_count = w_ada.shape[0]
    place = lax.axis_index(axes)
    all_steps = lax.all_gather(timesteps, axes, axis=0, tiled=True)
    cond_all = jax.nn.silu(time_embed(all_steps, width)).astype(jnp.bfloat16)
    cond_rows = lax.dynamic_slice_in_dim(cond_all, place * row_count, row_count, axis=1)
    all_bias = lax.all_gather(b_ada, axes, axis=0, tiled=True)
    modulation = lax.psum_scatter(
        jnp.dot(cond_rows, w_ada, preferred_element_type=jnp.float32),
        axes,
        scatter_dimension=0,
        tiled=True,
    ) + all_bias.astype(jnp.float32)
    one_hot = (seg_ids[:, None] == jnp.arange(clip_count, dtype=jnp.int32)[None, :]).astype(
        jnp.float32
    )
    offset_first, scale_first, gate_a = sublayer_mod(one_hot, modulation, 0, width)
    offset_second, scale_second, gate_b = sublayer_mod(one_hot, modulation, 1, width)
    offset_third, scale_third, gate_c = sublayer_mod(one_hot, modulation, 2, width)
    same_clip = seg_ids[:, None] == seg_ids[None, :]
    spatial_mask = same_clip & (frame_ids[:, None] == frame_ids[None, :])
    temporal_mask = same_clip & (patch_ids[:, None] == patch_ids[None, :])
    residual_first = tokens.astype(jnp.float32)
    standardized_first, inverse_deviation_first = layer_norm_apply(residual_first)
    normalized_first = (standardized_first * (1.0 + scale_first) + offset_first).astype(
        jnp.bfloat16
    )
    branch_a, qkv_a, merged_a = attention_forward(
        normalized_first, gathered[2], gathered[3], spatial_mask, head_count
    )
    residual_second = residual_first + gate_a * branch_a
    standardized_second, inverse_deviation_second = layer_norm_apply(residual_second)
    normalized_second = (standardized_second * (1.0 + scale_second) + offset_second).astype(
        jnp.bfloat16
    )
    branch_b, qkv_b, merged_b = attention_forward(
        normalized_second, gathered[4], gathered[5], temporal_mask, head_count
    )
    residual_third = residual_second + gate_b * branch_b
    standardized_third, inverse_deviation_third = layer_norm_apply(residual_third)
    normalized_third = (standardized_third * (1.0 + scale_third) + offset_third).astype(
        jnp.bfloat16
    )
    pre_act = jnp.dot(normalized_third, gathered[6], preferred_element_type=jnp.float32)
    act_out, gelu_pull = jax.vjp(jax.nn.gelu, pre_act)
    hidden = act_out.astype(jnp.bfloat16)
    branch_c = jnp.dot(hidden, gathered[7], preferred_element_type=jnp.float32)
    result = residual_third + gate_c * branch_c
    back_weights = gathered
    output_gradient = cotangent.astype(jnp.float32)
    gate_gradient_third = output_gradient * branch_c
    grad_branch_c = (gate_c * output_gradient).astype(jnp.bfloat16)
    grad_hidden = contract_cols(grad_branch_c, back_weights[7])
    grad_pre = gelu_pull(grad_hidden)[0].astype(jnp.bfloat16)
    normalized_gradient_third = contract_cols(grad_pre, back_weights[6])
    residual_gradient = output_gradient + layer_norm_reverse(
        normalized_gradient_third, standardized_third, inverse_deviation_third, scale_third
    )
    gate_gradient_second = residual_gradient * branch_b
    grad_branch_b = (gate_b * residual_gradient).astype(jnp.bfloat16)
    normalized_gradient_second, grad_qkv_t = attention_backward(
        grad_branch_b, qkv_b, back_weights[4], back_weights[5], temporal_mask, head_count
    )
    residual_gradient = residual_gradient + layer_norm_reverse(
        normalized_gradient_second, standardized_second, inverse_deviation_second, scale_second
    )
    gate_gradient_first = residual_gradient * branch_a
    grad_branch_a = (gate_a * residual_gradient).astype(jnp.bfloat16)
    normalized_gradient_first, grad_qkv_s = attention_backward(
        grad_branch_a, qkv_a, back_weights[2], back_weights[3], spatial_mask, head_count
    )
    residual_gradient = residual_gradient + layer_norm_reverse(
        normalized_gradient_first, standardized_first, inverse_deviation_first, scale_first
    )
    grad_mod = jnp.concatenate(
        [
            exact_rows(
                one_hot,
                jnp.concatenate(
                    [
                        normalized_gradient_first,
                        normalized_gradient_first * standardized_first,
                        gate_gradient_first,
                    ],
                    axis=1,
                ),
            ),
            exact_rows(
                one_hot,
                jnp.concatenate(
                    [
                        normalized_gradient_second,
                        normalized_gradient_second * standardized_second,
                        gate_gradient_second,
                    ],
                    axis=1,
                ),
            ),
            exact_rows(
                one_hot,
                jnp.concatenate(
                    [
                        normalized_gradient_third,
                        normalized_gradient_third * standardized_third,
                        gate_gradient_third,
                    ],
                    axis=1,
                ),
            ),
        ],
        axis=1,
    )
    grad_mod_low = grad_mod.astype(jnp.bfloat16)
    all_grad_mod = lax.all_gather(grad_mod_low, axes, axis=0, tiled=True)
    bias_share = lax.psum_scatter(
        jnp.sum(grad_mod, axis=0), axes, scatter_dimension=0, tiled=True
    )

    def share(left, right):
        return lax.psum_scatter(
            contract_rows(left, right).astype(jnp.bfloat16),
            axes,
            scatter_dimension=0,
            tiled=True,
        ).astype(jnp.float32)

    return (
        result.astype(jnp.bfloat16),
        residual_gradient,
        contract_rows(cond_rows, all_grad_mod),
        bias_share,
        share(normalized_first, grad_qkv_s),
        share(merged_a, grad_branch_a),
        share(normalized_second, grad_qkv_t),
        share(merged_b, grad_branch_b),
        share(normalized_third, grad_pre),
        share(hidden, grad_branch_c),
    )


def solution(mesh):
    placed = (
        P(("wide", "narrow"), None),
        P(("wide", "narrow")),
        P(("wide", "narrow")),
        P(("wide", "narrow")),
        P(("wide", "narrow")),
        P(("wide", "narrow"), None),
        P(("wide", "narrow")),
        P(("wide", "narrow"), None),
        P(("wide", "narrow"), None),
        P(("wide", "narrow"), None),
        P(("wide", "narrow"), None),
        P(("wide", "narrow"), None),
        P(("wide", "narrow"), None),
        P(("wide", "narrow"), None),
    )
    grid = dict(mesh.shape) == {"wide": 16, "narrow": 2}
    return jax.shard_map(
        on_grid if grid else on_device,
        mesh=mesh,
        in_specs=placed,
        out_specs=(
            P(("wide", "narrow"), None),
            P(("wide", "narrow"), None),
            P(("wide", "narrow"), None),
            P(("wide", "narrow")),
            P(("wide", "narrow"), None),
            P(("wide", "narrow"), None),
            P(("wide", "narrow"), None),
            P(("wide", "narrow"), None),
            P(("wide", "narrow"), None),
            P(("wide", "narrow"), None),
        ),
        check_vma=False,
    )
```
